128 devices in a mesh: dp: 32 (over z_hi, y, x), tensor: 4 (over z_lo, core).
Axes of the slice: x: 4, y: 4, z: 4 (z_hi: 2, z_lo: 2; z = z_hi * 2 + z_lo), core: 2. Of those that a mesh axis runs over, the one named last changes fastest.
Arguments:
- layer_input: bfloat16 [16384, 1536], P(('dp', 'tensor')), may hold values from -6 to 6
- q_weight: bfloat16 [1536, 1536], P('dp', 'tensor'), may hold values from -0.15625 to 0.15625
- kv_weight: bfloat16 [2, 1536, 256], P(None, ('dp', 'tensor')), may hold values from -0.15625 to 0.15625
- o_weight: bfloat16 [1536, 1536], P('tensor', 'dp'), may hold values from -0.625 to 0.625
- norm_gains: bfloat16 [2, 1536], P(None, ('dp', 'tensor')), may hold values from 0.5 to 1.5
- qkv_bias: bfloat16 [2048], P(('dp', 'tensor')), may hold values from -3 to 3
- gate_up: bfloat16 [2, 1536, 8960], P(None, 'dp', 'tensor'), may hold values from -0.15625 to 0.15625
- down_weight: bfloat16 [8960, 1536], P('tensor', 'dp'), may hold values from -0.0625 to 0.0625
- cotangent: bfloat16 [16384, 1536], P(('dp', 'tensor')), may hold values from -6 to 6
- lengths: int32 [32, 3], P('dp'), may hold values from 0 to 512, as said below
Outputs:
- layer_output: bfloat16 [16384, 1536], P(('dp', 'tensor'))
- input_grad: float32 [16384, 1536], P(('dp', 'tensor'))
- q_weight_grad: float32 [1536, 1536], P('dp', 'tensor')
- kv_weight_grad: float32 [2, 1536, 256], P(None, ('dp', 'tensor'))
- o_weight_grad: float32 [1536, 1536], P('tensor', 'dp')
- gains_grad: float32 [2, 1536], P(None, ('dp', 'tensor'))
- bias_grad: float32 [1792], P(('dp', 'tensor'))
- value_bias_grad: float32 [256], P(('dp', 'tensor'))
- gate_up_grad: float32 [2, 1536, 8960], P(None, 'dp', 'tensor')
- down_grad: float32 [8960, 1536], P('tensor', 'dp')
The draws below stay inside these ranges and needn't reach their ends.
Inputs may be any that keep to these rules, and one draw needn't show every extreme that they name: `lengths`: row g lists the sequences of group g in order from the group's first row; its entries sum to at most 512, the rows after the last sequence are padding, and one entry of every row is greater than 384.
All inputs are finite; a program needn't handle non-finite values.
Results may differ from the reference program's by a relative error of at most 0.025.
Values may be sent and summed in bfloat16 or wider, within the bound.
No kernel may reach another device: no remote copies, remote signals or barrier semaphores. Data moves between devices by JAX's collectives and lax.ppermute only.
A program may use at most 192 MiB of HBM per device.

```python
import jax
import jax.numpy as jnp
from jax import lax

D = 1536
HQ = 12
KVH = 2
HD = 128
FF = 8960
TOK_DEV = 128
SEQS = 3
GROUP = 512
GROUPS = 32
TOKENS = 16384
N_TENSOR = 4


def draw_lengths(key, part):
    key = jax.random.fold_in(key, 7)
    keys = jax.random.split(key, 4)
    longest = jax.random.randint(keys[0], (GROUPS,), GROUP - TOK_DEV + 1, GROUP + 1)
    filled = jax.random.randint(keys[1], (), 0, GROUPS)
    longest = jnp.where(jnp.arange(GROUPS) == filled, GROUP, longest)
    leftover = GROUP - longest
    others = jax.random.randint(keys[2], (GROUPS, SEQS - 1), 0, leftover[:, None] // (SEQS - 1) + 1)
    placed = jax.random.randint(keys[3], (GROUPS, 1), 0, SEQS)
    column = jnp.arange(SEQS, dtype=jnp.int32)[None, :]
    source = jnp.clip(column - (column > placed).astype(jnp.int32), 0, SEQS - 2)
    picked = jnp.take_along_axis(others, source, axis=1)
    return jnp.where(column == placed, longest[:, None], picked).astype(jnp.int32)


def level_of(own_key, shape, shards, least, top_value):
    level = 1.0
    for axis_at, parts in shards:
        steps = jax.random.uniform(jax.random.fold_in(jax.random.fold_in(own_key, 6), axis_at), (parts,), jnp.float32, least / len(shards), top_value / len(shards))
        level = level * jnp.repeat(jnp.exp(steps), shape[axis_at] // parts).reshape((-1,) + (1,) * (len(shape) - 1 - axis_at))
    return level


def centred(stream_key, shape, deviation, most, shards=(), kind=jnp.bfloat16):
    values = deviation * jax.random.normal(stream_key, shape, jnp.float32)
    if shards:
        values = values * level_of(stream_key, shape, shards, -0.22, 0.18)
    return jnp.clip(values, -most, most).astype(kind)


def setup_inputs(seed: int = 0) -> dict:
    splits = jax.random.split(jax.random.key(seed), 11)
    return {
        "layer_input": centred(splits[0], (TOKENS, D), 1.0, 6.0, ((0, 128),)),
        "q_weight": centred(splits[1], (D, HQ * HD), D ** -0.5, 0.15625, ((0, 32), (1, 4))),
        "kv_weight": centred(splits[2], (2, D, KVH * HD), D ** -0.5, 0.15625, ((1, 128),)),
        "o_weight": centred(splits[3], (HQ * HD, D), (HQ * HD // 16) ** -0.5, 0.625, ((0, 4), (1, 32))),
        "norm_gains": jnp.clip(1.0 + 0.1 * jax.random.normal(splits[4], (2, D), jnp.float32), 0.5, 1.5).astype(jnp.bfloat16),
        "qkv_bias": centred(splits[5], (HQ * HD + 2 * KVH * HD,), 0.5, 3.0, ((0, 128),)),
        "gate_up": centred(splits[6], (2, D, FF), D ** -0.5, 0.15625, ((1, 32), (2, 4))),
        "down_weight": centred(splits[7], (FF, D), FF ** -0.5, 0.0625, ((0, 4), (1, 32))),
        "cotangent": centred(splits[8], (TOKENS, D), 1.0, 6.0, ((0, 128),)),
        "lengths": draw_lengths(jax.random.fold_in(splits[10], 71), 0),
    }


@jax.custom_vjp
def low(v):
    return lax.optimization_barrier(v.astype(jnp.bfloat16)).astype(jnp.float32)

@jax.custom_vjp
def low_back(v):
    return v

def low_keep(v):
    return (low(v), None)

def low_pass(kept, grad):
    return (grad,)

def back_keep(v):
    return (v, None)

def back_low(kept, grad):
    return (low(grad),)
low.defvjp(low_keep, low_pass)
low_back.defvjp(back_keep, back_low)
EPSILON = 1e-06
THETA = 1000000.0
HIGHEST = lax.Precision.HIGHEST

def segment_table(seq_lengths, row_count):
    seq_ends = jnp.cumsum(seq_lengths).astype(jnp.int32)
    places = jnp.arange(row_count, dtype=jnp.int32)
    passed = seq_ends[None, :] <= places[:, None]
    segment = lax.optimization_barrier(jnp.sum(passed.astype(jnp.int32), axis=1)).astype(jnp.int32)
    starts = lax.optimization_barrier(jnp.sum(jnp.where(passed, seq_lengths[None, :], 0), axis=1)).astype(jnp.int32)
    living = places < seq_ends[-1]
    return (segment, places - starts, living)

def rotate(vectors, cos_table, sin_table):
    middle = vectors.shape[-1] // 2
    first_half = vectors[..., :middle]
    second_half = vectors[..., middle:]
    return jnp.concatenate([first_half * cos_table - second_half * sin_table, second_half * cos_table + first_half * sin_table], axis=-1)

def group_forward(params, inputs, cos_table, sin_table, allowed):
    q_weight, kv_weight, o_weight, norm_gains, qkv_bias, gate_up, down_weight = params
    row_count = inputs.shape[0]
    per_group = HQ // N_TENSOR
    heads_per_kv = HQ // KVH
    score_scale = HD ** (-0.5)
    first_scale = lax.rsqrt(lax.optimization_barrier(jnp.mean(inputs * inputs, axis=-1, keepdims=True)) + EPSILON)
    normed = low(inputs * first_scale * norm_gains[0])
    query_pre = low_back(jnp.dot(normed, q_weight, precision=HIGHEST) + qkv_bias[:HQ * HD])
    key_pre = jnp.dot(normed, kv_weight[0], precision=HIGHEST) + qkv_bias[HQ * HD:HQ * HD + KVH * HD]
    value_pre = jnp.dot(normed, kv_weight[1], precision=HIGHEST) + qkv_bias[HQ * HD + KVH * HD:]
    queries = low(rotate(query_pre.reshape(row_count, HQ, HD), cos_table[:, None, :], sin_table[:, None, :]))
    pieces = []
    for tensor_group in range(N_TENSOR):
        kv_head = tensor_group * per_group // heads_per_kv
        keys_group = low(rotate(low_back(key_pre[:, kv_head * HD:(kv_head + 1) * HD]), cos_table, sin_table))
        values_group = low(low_back(value_pre[:, kv_head * HD:(kv_head + 1) * HD]))
        queries_group = queries[:, tensor_group * per_group:(tensor_group + 1) * per_group, :]
        scores = low_back(jnp.einsum('qhd,kd->hqk', queries_group, keys_group, precision=HIGHEST) * score_scale)
        scores = jnp.where(allowed[None], scores, -1e+30)
        shifted = jnp.exp(scores - lax.optimization_barrier(jnp.max(scores, axis=-1, keepdims=True)))
        probabilities = shifted / lax.optimization_barrier(jnp.sum(shifted, axis=-1, keepdims=True))
        mixed_heads = jnp.einsum('hqk,kd->qhd', low(probabilities), values_group, precision=HIGHEST)
        pieces.append(mixed_heads.reshape(row_count, per_group * HD))
    attended = low(low_back(jnp.concatenate(pieces, axis=1)))
    residual = inputs + low_back(jnp.dot(attended, o_weight, precision=HIGHEST))
    second_scale = lax.rsqrt(lax.optimization_barrier(jnp.mean(residual * residual, axis=-1, keepdims=True)) + EPSILON)
    normed_mlp = low(residual * second_scale * norm_gains[1])
    gate_pre = low_back(jnp.dot(normed_mlp, gate_up[0], precision=HIGHEST))
    up_pre = low_back(jnp.dot(normed_mlp, gate_up[1], precision=HIGHEST))
    hidden = low(gate_pre * jax.nn.sigmoid(gate_pre) * up_pre)
    return residual + jnp.dot(hidden, down_weight, precision=HIGHEST)

def reference(layer_input, q_weight, kv_weight, o_weight, norm_gains, qkv_bias, gate_up, down_weight, cotangent, lengths):
    params = tuple((weight.astype(jnp.float32) for weight in (q_weight, kv_weight, o_weight, norm_gains, qkv_bias, gate_up, down_weight)))
    inputs_all = layer_input.astype(jnp.float32).reshape(GROUPS, GROUP, D)
    cot_all = cotangent.astype(jnp.float32).reshape(GROUPS, GROUP, D)
    inverse = THETA ** (-(2.0 * jnp.arange(HD // 2, dtype=jnp.float32)) / HD)
    places = jnp.arange(GROUP, dtype=jnp.int32)

    def one_group(totals, item):
        inputs, cot_group, seq_lengths = item
        segment, relative, living = segment_table(seq_lengths, GROUP)
        angles = relative.astype(jnp.float32)[:, None] * inverse[None, :]
        cos_table = jnp.cos(angles)
        sin_table = jnp.sin(angles)
        allowed = (segment[:, None] == segment[None, :]) & (places[:, None] >= places[None, :])

        def forward(weights, block_inputs):
            return group_forward(weights, block_inputs, cos_table, sin_table, allowed)
        outputs, pull_back = jax.vjp(forward, params, inputs)
        grads, input_grad = pull_back(cot_group * living[:, None].astype(jnp.float32))
        totals = jax.tree.map(lambda running, adding: running + adding, totals, grads)
        return (totals, (outputs.astype(jnp.bfloat16), input_grad))
    zeros = jax.tree.map(jnp.zeros_like, params)
    totals, (outputs, input_grads) = lax.scan(one_group, zeros, (inputs_all, cot_all, lengths))
    split_at = (HQ + KVH) * HD
    return (outputs.reshape(TOKENS, D), input_grads.reshape(TOKENS, D), totals[0], totals[1], totals[2], totals[3], totals[4][:split_at], totals[4][split_at:], totals[5], totals[6])
```

```python
import jax
import jax.numpy as jnp
from jax import lax
from jax.sharding import Mesh, PartitionSpec as P

HQ = 12
KVH = 2
HD = 128
EPSILON = 1e-06
THETA = 1000000.0

AXES = ("zh", "y", "x", "zl", "core")
SIZES = (2, 4, 4, 2, 2)
ZRING = ("zh", "zl")
PIECES = ((0, 640), (640, 1152))
HALF = 1152
BF = jnp.bfloat16
F32 = jnp.float32


def shift(block, axis, by):
    return lax.ppermute(block, axis, [(i, (i + by) % 4) for i in range(4)])


def swap(block, axis):
    return lax.ppermute(block, axis, [(0, 1), (1, 0)])


def halves(block, dim):
    middle = block.shape[dim] // 2
    return (
        lax.slice_in_dim(block, 0, middle, axis=dim),
        lax.slice_in_dim(block, middle, block.shape[dim], axis=dim),
    )


def ring_gather(block, axis, dim):
    after = shift(block, axis, -1)
    before = shift(block, axis, 1)
    far_low = shift(halves(after, dim)[0], axis, -1)
    far_high = shift(halves(before, dim)[1], axis, 1)
    return [(0, 0, block), (1, 0, after), (3, 0, before), (2, 0, far_low), (2, 1, far_high)]


def place(buffer, pieces, rank, dim, split_dim, fixed):
    for distance, half, array in pieces:
        start = [0] * buffer.ndim
        for at, value in fixed.items():
            start[at] = value
        start[dim] = (rank + distance) % 4
        if half:
            start[split_dim] = array.shape[split_dim]
        buffer = lax.dynamic_update_slice(buffer, array, start)
    return buffer


def plane_gather(buffer, block, zsel, first):
    k, r, w = block.shape
    ry, rx = lax.axis_index("y"), lax.axis_index("x")
    order = (("x", rx, 3), ("y", ry, 2)) if first == "x" else (("y", ry, 2), ("x", rx, 3))
    (axis1, rank1, _), (axis2, rank2, dim2) = order
    parts = ring_gather(block, axis1, 1)
    parts = [(d, h, a[:, None]) for d, h, a in parts]
    line = place(jnp.zeros((k, 4, r, w), block.dtype), parts, rank1, 1, 2, {})
    other = 5 - dim2
    parts = ring_gather(line, axis2, 1)
    parts = [(d, h, jnp.expand_dims(a, (1, dim2))) for d, h, a in parts]
    return place(buffer, parts, rank2, dim2, other, {1: zsel})


def ring_scatter(terms, axis, rank, dim):
    def block(distance):
        return lax.dynamic_index_in_dim(terms, (rank + distance) % 4, dim, keepdims=False)

    far_low, far_high = halves(block(2), dim)
    near_low, near_high = halves(block(1), dim)
    back_low, back_high = halves(block(3), dim)
    got_low = shift(far_low, axis, 1)
    got_high = shift(far_high, axis, -1)
    after = jnp.concatenate([add(near_low, got_low), near_high], axis=dim)
    before = jnp.concatenate([back_low, add(back_high, got_high)], axis=dim)
    return add(block(0), shift(after, axis, 1), shift(before, axis, -1))


def add(*terms):
    total = terms[0].astype(F32)
    for term in terms[1:]:
        total = total + term.astype(F32)
    return total.astype(terms[0].dtype)


def plane_scatter(terms, first):
    ry, rx = lax.axis_index("y"), lax.axis_index("x")
    if first == "y":
        return ring_scatter(ring_scatter(terms, "y", ry, 1), "x", rx, 1)
    return ring_scatter(ring_scatter(terms, "x", rx, 2), "y", ry, 1)


def z_gather(block):
    spread = jnp.broadcast_to(block[None], (4,) + block.shape)
    return lax.all_to_all(spread, ZRING, split_axis=0, concat_axis=0, tiled=True)


def z_scatter(terms):
    got = lax.all_to_all(terms, ZRING, split_axis=0, concat_axis=0, tiled=True)
    return jnp.sum(got.astype(F32), axis=0)


def rows_gather(block):
    mine = z_gather(block)
    return jnp.stack([mine, swap(mine, "core")]).reshape(8 * block.shape[0], block.shape[1])


def rows_scatter(partial):
    rows, columns = partial.shape
    parts = partial.astype(BF).reshape(2, 4, rows // 8, columns)
    return z_scatter(add(parts[0], swap(parts[1], "core")))


def rotate(vectors, cos_table, sin_table):
    middle = vectors.shape[-1] // 2
    first_half = vectors[..., :middle]
    second_half = vectors[..., middle:]
    return jnp.concatenate(
        [
            first_half * cos_table - second_half * sin_table,
            second_half * cos_table + first_half * sin_table,
        ],
        axis=-1,
    )


def dot(a, b):
    return jnp.dot(a, b, preferred_element_type=F32)


def dot_t(a, b):
    return lax.dot_general(a, b, (((1,), (1,)), ((), ())), preferred_element_type=F32)


def t_dot(a, b):
    return lax.dot_general(a, b, (((0,), (0,)), ((), ())), preferred_element_type=F32)


def pick(index, low, high):
    return jnp.where(index == 0, low, high)


def shards(
    layer_input,
    q_weight,
    kv_weight,
    o_weight,
    norm_gains,
    qkv_bias,
    gate_up,
    down_weight,
    cotangent,
    lengths,
):
    zh, zl, core = (lax.axis_index(a) for a in ("zh", "zl", "core"))
    width = layer_input.shape[1]
    rows = layer_input.shape[0]
    heads = HQ // 2
    scale = HD ** (-0.5)

    small = jnp.concatenate([norm_gains.reshape(-1), qkv_bias, jnp.zeros((88,), BF)]).astype(F32)
    small = lax.all_to_all(
        jnp.broadcast_to(small[None], (128, 128)), AXES, split_axis=0, concat_axis=0, tiled=True
    )
    gain_attn = small[:, 0:12].reshape(width)
    gain_mlp = small[:, 12:24].reshape(width)
    bias_full = small[:, 24:40].reshape(2048)
    bias = jnp.concatenate(
        [
            pick(core, bias_full[:768], bias_full[768:1536]),
            pick(core, bias_full[1536:1664], bias_full[1664:1792]),
            pick(core, bias_full[1792:1920], bias_full[1920:2048]),
        ]
    )

    kv_rows = kv_weight.reshape(48, 128)
    packed = jnp.concatenate([q_weight, o_weight.T, kv_rows], axis=1)
    packed = z_gather(packed).reshape(2, 2, 48, 896)
    qo = packed[..., :768]
    kv_all = packed[..., 768:].reshape(2, 2, 2, 12, 2, HD)
    keep = lax.dynamic_index_in_dim(qo, core, 1, keepdims=False)
    give = lax.dynamic_index_in_dim(qo, 1 - core, 1, keepdims=False)
    kv_keep = lax.dynamic_index_in_dim(kv_all, core, 4, keepdims=False)
    kv_give = lax.dynamic_index_in_dim(kv_all, 1 - core, 4, keepdims=False)
    got = swap(jnp.concatenate([give, kv_give.reshape(2, 48, HD)], axis=-1), "core")
    qo_got = got[..., :768]
    kv_got = got[..., 768:].reshape(2, 2, 2, 12, HD)
    first = pick(core, keep, qo_got)
    second = pick(core, qo_got, keep)
    q_part = jnp.concatenate([first[..., :384], second[..., :384]], axis=-1)
    o_part = jnp.concatenate([first[..., 384:], second[..., 384:]], axis=-1)
    kv_pair = jnp.stack([pick(core, kv_keep, kv_got), pick(core, kv_got, kv_keep)], axis=2)
    kv_part = kv_pair.transpose(0, 1, 2, 4, 3, 5).reshape(2, 48, 2 * HD)
    qkv_part = jnp.concatenate([q_part, kv_part], axis=-1)

    def plane_both(part):
        own = lax.dynamic_index_in_dim(part, zh, 0, keepdims=True)
        other = lax.dynamic_index_in_dim(part, 1 - zh, 0, keepdims=True)
        buffer = jnp.zeros((1, 2, 4, 4) + part.shape[1:], part.dtype)
        buffer = plane_gather(buffer, own, zh, "x")
        buffer = plane_gather(buffer, other, 1 - zh, "y")
        return buffer.reshape(width, part.shape[-1])

    qkv_full = plane_both(qkv_part)
    o_full = plane_both(o_part)

    mlp = jnp.concatenate([gate_up, down_weight.T[None]], axis=0)
    mlp = jnp.pad(mlp, ((0, 0), (0, 0), (0, 2 * HALF - mlp.shape[2])))
    mlp_own = pick(zh, mlp[..., :HALF], mlp[..., HALF:])
    mlp_other = pick(zh, mlp[..., HALF:], mlp[..., :HALF])
    mlp_full = []
    for low, high in PIECES:
        got = swap(mlp_other[..., low:high], "zh")
        buffer = jnp.zeros((3, 2, 4, 4, 48, high - low), BF)
        buffer = plane_gather(buffer, mlp_own[..., low:high], zh, "x")
        buffer = plane_gather(buffer, got, 1 - zh, "y")
        mlp_full.append(buffer.reshape(3, width, high - low))

    ends = jnp.cumsum(lengths[0])
    ranks = jnp.stack(
        [2 * zl + core, 2 * zl + 1 - core, 2 * (1 - zl) + core, 2 * (1 - zl) + 1 - core]
    )
    places = (ranks[:, None] * rows + jnp.arange(rows, dtype=jnp.int32)[None, :]).reshape(4 * rows)
    passed = ends[None, :] <= places[:, None]
    segment = jnp.sum(passed.astype(jnp.int32), axis=1)
    starts = jnp.sum(jnp.where(passed, lengths[0][None, :], 0), axis=1)
    relative = places - starts
    chip = 2 * rows
    allowed = (segment[:chip, None] == segment[None, :]) & (places[:chip, None] >= places[None, :])
    inverse = THETA ** (-(2.0 * jnp.arange(HD // 2, dtype=F32)) / HD)
    angles = relative[:chip].astype(F32)[:, None] * inverse[None, :]
    cos_table = jnp.cos(angles)
    sin_table = jnp.sin(angles)

    living = (places[:rows] < ends[-1])[:, None]
    cot_local = jnp.where(living, cotangent, jnp.zeros((), BF))
    cot_all = rows_gather(cot_local)

    inputs = layer_input.astype(F32)
    first_scale = lax.rsqrt(jnp.mean(inputs * inputs, axis=-1, keepdims=True) + EPSILON)
    normed = (inputs * first_scale * gain_attn).astype(BF)
    normed_chip = jnp.concatenate([normed, swap(normed, "core")], axis=0)
    qkv = dot(normed_chip, qkv_full) + bias
    queries = rotate(
        qkv[:, :768].reshape(chip, heads, HD), cos_table[:, None, :], sin_table[:, None, :]
    ).astype(BF)
    kv_own = jnp.concatenate(
        [rotate(qkv[:, 768:896], cos_table, sin_table), qkv[:, 896:]], axis=-1
    ).astype(BF)
    kv_rot = jnp.concatenate([kv_own, swap(kv_own, "zl")], axis=0)
    keys, values = kv_rot[:, :HD], kv_rot[:, HD:]
    scores = jnp.einsum("qhd,kd->hqk", queries, keys, preferred_element_type=F32) * scale
    scores = jnp.where(allowed[None], scores, -1e30)
    peak = jnp.max(scores, axis=-1, keepdims=True)
    shifted = jnp.exp(scores - peak)
    total = jnp.sum(shifted, axis=-1, keepdims=True)
    probs = shifted / total
    attended = (
        jnp.einsum("hqk,kd->qhd", probs.astype(BF), values, preferred_element_type=F32)
        .reshape(chip, heads * HD)
        .astype(BF)
    )
    o_partial = dot_t(attended, o_full)
    residual = inputs + o_partial[:rows] + swap(o_partial[rows:].astype(BF), "core").astype(F32)
    second_scale = lax.rsqrt(jnp.mean(residual * residual, axis=-1, keepdims=True) + EPSILON)
    normed_mlp = (residual * second_scale * gain_mlp).astype(BF)

    normed_all = rows_gather(normed_mlp)
    out_partial = 0.0
    back_partial = 0.0
    mlp_grads = []
    for (low, high), weights in zip(PIECES, mlp_full):
        gate = dot(normed_all, weights[0])
        up = dot(normed_all, weights[1])
        hidden_grad = dot(cot_all, weights[2])
        sigma = jax.nn.sigmoid(gate)
        act = gate * sigma
        hidden = (act * up).astype(BF)
        gate_grad = (hidden_grad * up * sigma * (1.0 + gate * (1.0 - sigma))).astype(BF)
        up_grad = (hidden_grad * act).astype(BF)
        back_partial = back_partial + dot_t(gate_grad, weights[0]) + dot_t(up_grad, weights[1])
        out_partial = out_partial + dot_t(hidden, weights[2])
        grads = jnp.stack(
            [
                t_dot(normed_all, gate_grad).astype(BF),
                t_dot(normed_all, up_grad).astype(BF),
                t_dot(cot_all, hidden).astype(BF),
            ]
        )
        mlp_grads.append(grads.reshape(3, 2, 4, 4, 48, high - low))
    normed_mlp_grad = rows_scatter(back_partial)
    layer_output = (residual + rows_scatter(out_partial)).astype(BF)

    own_grads, other_grads = [], []
    for grads in mlp_grads:
        own = lax.dynamic_index_in_dim(grads, zh, 1, keepdims=False)
        other = lax.dynamic_index_in_dim(grads, 1 - zh, 1, keepdims=False)
        own_grads.append(plane_scatter(own, "y"))
        other_grads.append(swap(plane_scatter(other, "x"), "zh"))
    own_grads = jnp.concatenate(own_grads, axis=-1).astype(F32)
    other_grads = jnp.concatenate(other_grads, axis=-1).astype(F32)
    mlp_shard = jnp.concatenate(
        [pick(zh, own_grads, other_grads), pick(zh, other_grads, own_grads)], axis=-1
    )[..., : gate_up.shape[2]]
    gate_up_shard = mlp_shard[:2]
    down_shard = mlp_shard[2].T

    scaled_mlp = normed_mlp_grad * gain_mlp
    gain_mlp_grad = jnp.sum(normed_mlp_grad * residual * second_scale, axis=0)
    residual_grad = (
        cot_local.astype(F32)
        + second_scale * scaled_mlp
        - residual * second_scale**3 * jnp.mean(scaled_mlp * residual, axis=-1, keepdims=True)
    )

    branch = residual_grad.astype(BF)
    branch_chip = jnp.concatenate([branch, swap(branch, "core")], axis=0)
    o_grad = t_dot(branch_chip, attended)
    attended_grad = dot(branch_chip, o_full).astype(BF).reshape(chip, heads, HD)
    prob_grad = jnp.einsum("qhd,kd->hqk", attended_grad, values, preferred_element_type=F32)
    inner = jnp.sum(probs * prob_grad, axis=-1, keepdims=True)
    score_grad = (probs * (prob_grad - inner)).astype(BF)
    query_rot_grad = (
        jnp.einsum("hqk,kd->qhd", score_grad, keys, preferred_element_type=F32) * scale
    )
    key_rot_grad = (
        jnp.einsum("hqk,qhd->kd", score_grad, queries, preferred_element_type=F32) * scale
    )
    value_grad = jnp.einsum(
        "hqk,qhd->kd", probs.astype(BF), attended_grad, preferred_element_type=F32
    )
    kv_grad = jnp.concatenate([key_rot_grad, value_grad], axis=-1)
    kv_grad = kv_grad[:chip] + swap(kv_grad[chip:], "zl")
    query_grad = rotate(query_rot_grad, cos_table[:, None, :], -sin_table[:, None, :]).reshape(
        chip, heads * HD
    )
    key_grad = rotate(kv_grad[:, :HD], cos_table, -sin_table)
    qkv_grad = jnp.concatenate([query_grad, key_grad, kv_grad[:, HD:]], axis=-1).astype(BF)
    normed_partial = dot_t(qkv_grad, qkv_full)
    normed_grad = normed_partial[:rows] + swap(normed_partial[rows:].astype(BF), "core").astype(F32)
    qkv_weight_grad = t_dot(normed_chip, qkv_grad)
    scaled_attn = normed_grad * gain_attn
    gain_attn_grad = jnp.sum(normed_grad * inputs * first_scale, axis=0)
    input_grad = (
        residual_grad
        + first_scale * scaled_attn
        - inputs * first_scale**3 * jnp.mean(scaled_attn * inputs, axis=-1, keepdims=True)
    )

    def plane_sum(grad):
        terms = grad.astype(BF).reshape(2, 4, 4, 48, grad.shape[-1])
        own = lax.dynamic_index_in_dim(terms, zh, 0, keepdims=True)
        other = lax.dynamic_index_in_dim(terms, 1 - zh, 0, keepdims=True)
        own = plane_scatter(own, "y")
        other = plane_scatter(other, "x")
        return jnp.concatenate([pick(zh, own, other), pick(zh, other, own)], axis=0)

    o_sum = plane_sum(o_grad)
    qkv_sum = plane_sum(qkv_weight_grad)
    pair0 = jnp.concatenate([qkv_sum[..., :384], o_sum[..., :384]], axis=-1)
    pair1 = jnp.concatenate([qkv_sum[..., 384:768], o_sum[..., 384:]], axis=-1)
    keep = pick(core, pair0, pair1)
    give = pick(core, pair1, pair0)
    kv_sum = qkv_sum[..., 768:].reshape(2, 2, 2, 12, 2, HD)
    kv_keep = lax.dynamic_index_in_dim(kv_sum, core, 2, keepdims=False)
    kv_give = lax.dynamic_index_in_dim(kv_sum, 1 - core, 2, keepdims=False)
    got = swap(jnp.concatenate([give, kv_give.reshape(2, 48, HD)], axis=-1), "core")
    qo_got = got[..., :768]
    kv_got = got[..., 768:].reshape(2, 2, 12, 2, HD)
    qo_terms = jnp.stack([pick(core, keep, qo_got), pick(core, qo_got, keep)], axis=1)
    kv_terms = jnp.stack([pick(core, kv_keep, kv_got), pick(core, kv_got, kv_keep)], axis=4)
    kv_terms = kv_terms.transpose(0, 1, 3, 2, 4, 5).reshape(2, 2, 48, 128)
    attn_shard = z_scatter(
        jnp.concatenate([qo_terms, kv_terms], axis=-1).reshape(4, 48, 896)
    )
    q_shard = attn_shard[:, :384]
    o_shard = attn_shard[:, 384:768].T
    kv_shard = attn_shard[:, 768:].reshape(2, 12, 2 * HD)

    sums = jnp.sum(qkv_grad.astype(F32), axis=0)
    none = jnp.zeros_like(sums)
    low, high = pick(core, sums, none), pick(core, none, sums)
    bias_grad = jnp.concatenate([low[:768], high[:768], low[768:896], high[768:896]])
    value_bias_grad = jnp.concatenate([low[896:], high[896:]])
    vectors = jnp.concatenate(
        [
            gain_attn_grad.reshape(128, 12),
            gain_mlp_grad.reshape(128, 12),
            bias_grad.reshape(128, 14),
            value_bias_grad.reshape(128, 2),
            jnp.zeros((128, 88), F32),
        ],
        axis=1,
    )
    vectors = lax.all_to_all(vectors, AXES, split_axis=0, concat_axis=0, tiled=True)
    vectors = jnp.sum(vectors, axis=0)
    return (
        layer_output,
        input_grad,
        q_shard,
        kv_shard,
        o_shard,
        vectors[:24].reshape(2, 12),
        vectors[24:38],
        vectors[38:40],
        gate_up_shard,
        down_shard,
    )


def solution(mesh):
    fine = Mesh(mesh.devices.reshape(SIZES), AXES)
    dp = ("zh", "y", "x")
    tensor = ("zl", "core")
    every = dp + tensor
    in_specs = (
        P(every, None),
        P(dp, tensor),
        P(None, every, None),
        P(tensor, dp),
        P(None, every),
        P(every),
        P(None, dp, tensor),
        P(tensor, dp),
        P(every, None),
        P(dp, None),
    )
    out_specs = (
        P(every, None),
        P(every, None),
        P(dp, tensor),
        P(None, every, None),
        P(tensor, dp),
        P(None, every),
        P(every),
        P(every),
        P(None, dp, tensor),
        P(tensor, dp),
    )
    return jax.shard_map(shards, mesh=fine, in_specs=in_specs, out_specs=out_specs, check_vma=False)
```

```python
import functools

import jax
import jax.numpy as jnp
from jax import lax
from jax.experimental import pallas as pl
from jax.experimental.pallas import tpu as pltpu
from jax.sharding import Mesh, PartitionSpec as P

HQ = 12
KVH = 2
HD = 128
EPSILON = 1e-06
THETA = 1000000.0

AXES = ("zh", "y", "x", "zl", "core")
SIZES = (2, 4, 4, 2, 2)
ZRING = ("zh", "zl")
PLANE = ("y", "x")
DATA = ("zh", "y", "x")
HALF = 1152
BF = jnp.bfloat16
F32 = jnp.float32


def swap(block, axis):
    return lax.ppermute(block, axis, [(0, 1), (1, 0)])


def halves(block, dim):
    middle = block.shape[dim] // 2
    return (
        lax.slice_in_dim(block, 0, middle, axis=dim),
        lax.slice_in_dim(block, middle, block.shape[dim], axis=dim),
    )


def add(*terms):
    total = terms[0].astype(F32)
    for term in terms[1:]:
        total = total + term.astype(F32)
    return total.astype(terms[0].dtype)


def exchange(blocks, axes):
    return lax.all_to_all(blocks, axes, split_axis=0, concat_axis=0, tiled=True)


def spread(block, axes, count):
    return exchange(jnp.broadcast_to(block[None], (count,) + block.shape), axes)


def z_shift(block, by):
    return lax.ppermute(block, ZRING, [(i, (i + by) % 4) for i in range(4)])


def token_groups(block):
    near = jnp.concatenate([z_shift(block, -1), z_shift(block, 1)], axis=0)
    far = z_shift(block, 2)
    return [(part, swap(part, "core")) for part in (block, near, far)]


def token_sums(pairs):
    own, near, far = (add(mine, swap(others, "core")) for mine, others in pairs)
    after_rows, before_rows = halves(near, 0)
    terms = (own, z_shift(after_rows, 1), z_shift(before_rows, -1), z_shift(far, 2))
    return sum(term.astype(F32) for term in terms)


def ff_body(
    na, nb, ca, cb, w, m_out, dg_out, du_out, dna_out, dnb_out,
    wbuf, nbuf, cbuf, wsem, nsem, csem, *, tile,
):
    half = na.shape[0]
    weights = [pltpu.make_async_copy(w.at[i], wbuf.at[i], wsem.at[i]) for i in range(3)]
    normed = [
        pltpu.make_async_copy(part, nbuf.at[pl.ds(k * half, half)], nsem.at[k])
        for k, part in enumerate((na, nb))
    ]
    cots = [
        pltpu.make_async_copy(part, cbuf.at[pl.ds(k * half, half)], csem.at[k])
        for k, part in enumerate((ca, cb))
    ]
    for copy in normed + weights[:2] + cots + weights[2:]:
        copy.start()
    for copy in normed + weights[:1]:
        copy.wait()
    tiles = 2 * half // tile
    for i in range(tiles):
        at = pl.ds(i * tile, tile)
        rows = nbuf[at]
        gate = dot(rows, wbuf[0])
        if i == 0:
            weights[1].wait()
        up = dot(rows, wbuf[1])
        if i == 0:
            for copy in cots + weights[2:]:
                copy.wait()
        hidden_grad = dot(cbuf[at], wbuf[2])
        sigma = 1.0 / (1.0 + jnp.exp(-gate))
        act = gate * sigma
        m_out[at] = (act * up).astype(BF)
        up_grad = (hidden_grad * act).astype(BF)
        gate_grad = (hidden_grad * up * sigma * (1.0 + gate * (1.0 - sigma))).astype(BF)
        dg_out[at] = gate_grad
        du_out[at] = up_grad
        back = (dot_t(gate_grad, wbuf[0]) + dot_t(up_grad, wbuf[1])).astype(BF)
        if tiles == 1:
            dna_out[...] = back[:half]
            dnb_out[...] = back[half:]
        else:
            out = dna_out if i < tiles // 2 else dnb_out
            out[pl.ds(i % (tiles // 2) * tile, tile)] = back


def ff_rows(normed, cots, weights, tile=256):
    half, width = normed[0].shape
    units = weights.shape[2]
    anywhere = pl.BlockSpec(memory_space=pl.ANY)
    vmem = pl.BlockSpec(memory_space=pltpu.VMEM)
    return pl.pallas_call(
        functools.partial(ff_body, tile=tile),
        out_shape=[jax.ShapeDtypeStruct((2 * half, units), BF)] * 3
        + [jax.ShapeDtypeStruct((half, width), BF)] * 2,
        in_specs=[anywhere] * 5,
        out_specs=[vmem] * 5,
        scratch_shapes=[
            pltpu.VMEM((3, width, units), BF),
            pltpu.VMEM((2 * half, width), BF),
            pltpu.VMEM((2 * half, width), BF),
            pltpu.SemaphoreType.DMA((3,)),
            pltpu.SemaphoreType.DMA((2,)),
            pltpu.SemaphoreType.DMA((2,)),
        ],
        compiler_params=pltpu.CompilerParams(vmem_limit_bytes=48 * 1024 * 1024),
        cost_estimate=pl.CostEstimate(
            flops=20 * half * width * units,
            bytes_accessed=6 * width * units,
            transcendentals=2 * half * units,
        ),
        name="feed_forward_rows",
    )(*normed, *cots, weights)


def wg_body(*refs, sizes, tile):
    count = len(sizes)
    groups = count // 2
    normed, cots, refs = refs[:count], refs[count : 2 * count], refs[2 * count :]
    hidden, gates, ups = refs[:groups], refs[groups : 2 * groups], refs[2 * groups : 3 * groups]
    out, nbuf, cbuf, mbuf, gbuf, ubuf, sem = refs[3 * groups :]
    pair_sizes = [sizes[2 * i] + sizes[2 * i + 1] for i in range(groups)]

    def copies(at, buffer, sources, lengths):
        result, start = [], 0
        for source, length in zip(sources, lengths):
            target = buffer.at[pl.ds(start, length)]
            result.append(pltpu.make_async_copy(source, target, sem.at[at]))
            start += length
        return result

    def normed_copies():
        return copies(0, nbuf, normed, sizes)

    def cot_copies():
        return copies(1, cbuf, cots, sizes)

    def gate_copies():
        return copies(2, gbuf, gates, pair_sizes)

    def up_copies():
        return copies(3, ubuf, ups, pair_sizes)

    def hidden_copies():
        return copies(4, mbuf, hidden, pair_sizes)

    which, step = pl.program_id(0), pl.program_id(1)

    @pl.when((which == 0) & (step == 0))
    def _():
        first = normed_copies() + gate_copies()
        for copy in first + up_copies() + cot_copies() + hidden_copies():
            copy.start()
        for copy in first:
            copy.wait()

    @pl.when((which == 1) & (step == 0))
    def _():
        for copy in up_copies():
            copy.wait()

    @pl.when((which == 2) & (step == 0))
    def _():
        for copy in cot_copies() + hidden_copies():
            copy.wait()

    columns = pl.ds(pl.multiple_of(step * tile, tile), tile)
    for i, (left, right) in enumerate(((nbuf, gbuf), (nbuf, ubuf), (cbuf, mbuf))):

        @pl.when(which == i)
        def _():
            out[...] = t_dot(left[:, columns], right[...]).astype(BF)


def weight_grads(normed, cots, hidden, gates, ups, tile=768):
    sizes = tuple(part.shape[0] for part in normed)
    rows, width, units = sum(sizes), normed[0].shape[1], hidden[0].shape[1]
    anywhere = pl.BlockSpec(memory_space=pl.ANY)
    return pl.pallas_call(
        functools.partial(wg_body, sizes=sizes, tile=tile),
        grid=(3, width // tile),
        out_shape=jax.ShapeDtypeStruct((3, width, units), BF),
        in_specs=[anywhere] * (2 * len(normed) + 3 * len(hidden)),
        out_specs=pl.BlockSpec((None, tile, units), lambda i, j: (i, j, 0)),
        scratch_shapes=[pltpu.VMEM((rows, width), BF)] * 2
        + [pltpu.VMEM((rows, units), BF)] * 3
        + [pltpu.SemaphoreType.DMA((5,))],
        compiler_params=pltpu.CompilerParams(vmem_limit_bytes=48 * 1024 * 1024),
        cost_estimate=pl.CostEstimate(
            flops=6 * rows * width * units,
            bytes_accessed=6 * width * units + rows * (4 * width + 6 * units),
            transcendentals=0,
        ),
        name="weight_gradients",
    )(*normed, *cots, *hidden, *gates, *ups)


def rotate(vectors, cos_table, sin_table):
    middle = vectors.shape[-1] // 2
    first_half = vectors[..., :middle]
    second_half = vectors[..., middle:]
    return jnp.concatenate(
        [
            first_half * cos_table - second_half * sin_table,
            second_half * cos_table + first_half * sin_table,
        ],
        axis=-1,
    )


def dot(a, b):
    return jnp.dot(a, b, preferred_element_type=F32)


def dot_t(a, b):
    return lax.dot_general(a, b, (((1,), (1,)), ((), ())), preferred_element_type=F32)


def t_dot(a, b):
    return lax.dot_general(a, b, (((0,), (0,)), ((), ())), preferred_element_type=F32)


def pick(index, low, high):
    return jnp.where(index == 0, low, high)


def group_gather(block):
    across = swap(block, "zl")
    return jnp.concatenate([block, swap(block, "core"), across, swap(across, "core")], axis=0)


def group_scatter(partial):
    rows, columns = partial.shape
    parts = partial.reshape(2, 2, rows // 4, columns)
    parts = add(parts[:, 0], swap(parts[:, 1].astype(BF), "core"))
    return parts[0] + swap(parts[1].astype(BF), "zl").astype(F32)


def after(value, *others):
    return lax.optimization_barrier((value,) + others)[0]


def shards(
    layer_input,
    q_weight,
    kv_weight,
    o_weight,
    norm_gains,
    qkv_bias,
    gate_up,
    down_weight,
    cotangent,
    lengths,
):
    zh, zl, core = (lax.axis_index(a) for a in ("zh", "zl", "core"))
    rank = 2 * zl + core
    width = layer_input.shape[1]
    rows = layer_input.shape[0]
    heads = HQ // 4
    scale = HD ** (-0.5)

    small = jnp.concatenate([norm_gains.reshape(-1), qkv_bias, jnp.zeros((88,), BF)]).astype(F32)
    small = spread(small, AXES, 128)
    gain_attn = small[:, 0:12].reshape(width)
    gain_mlp = small[:, 12:24].reshape(width)
    bias_full = small[:, 24:40].reshape(2048)
    bias = jnp.concatenate(
        [
            lax.dynamic_index_in_dim(bias_full[:1536].reshape(4, 384), rank, 0, keepdims=False),
            pick(zl, bias_full[1536:1664], bias_full[1664:1792]),
            pick(zl, bias_full[1792:1920], bias_full[1920:2048]),
        ]
    )

    kv_both = swap(kv_weight, "core")
    kv_both = jnp.stack([pick(core, kv_weight, kv_both), pick(core, kv_both, kv_weight)])
    kv_keep = pick(zl, kv_both[..., :HD], kv_both[..., HD:])
    kv_got = swap(pick(zl, kv_both[..., HD:], kv_both[..., :HD]), "zl")
    kv_rows = jnp.stack([pick(zl, kv_keep, kv_got), pick(zl, kv_got, kv_keep)])
    kv_rows = kv_rows.transpose(0, 1, 3, 2, 4).reshape(48, 2 * HD)
    attn_part = jnp.concatenate([q_weight, kv_rows, o_weight.T], axis=-1)
    attn_full = spread(after(attn_part, small), DATA, 32).reshape(width, 1024)
    qkv_full, o_full = attn_full[:, :640], attn_full[:, 640:]

    mlp = jnp.concatenate([gate_up, down_weight.T[None]], axis=0)
    mlp = jnp.pad(mlp, ((0, 0), (0, 0), (0, 2 * HALF - mlp.shape[2])))
    mlp_own = pick(zh, mlp[..., :HALF], mlp[..., HALF:])
    mlp_other = swap(pick(zh, mlp[..., HALF:], mlp[..., :HALF]), "zh")
    mlp = jnp.stack([pick(zh, mlp_own, mlp_other), pick(zh, mlp_other, mlp_own)], axis=1)
    mlp = lax.all_gather(mlp.reshape(6, 48, HALF), PLANE, axis=1, tiled=True)
    mlp = mlp.reshape(3, width, HALF)

    ends = jnp.cumsum(lengths[0])
    ranks = jnp.stack([rank, 2 * zl + 1 - core, 2 * (1 - zl) + core, 2 * (1 - zl) + 1 - core])
    group = 4 * rows
    places = (ranks[:, None] * rows + jnp.arange(rows, dtype=jnp.int32)[None, :]).reshape(group)
    passed = ends[None, :] <= places[:, None]
    segment = jnp.sum(passed.astype(jnp.int32), axis=1)
    starts = jnp.sum(jnp.where(passed, lengths[0][None, :], 0), axis=1)
    relative = places - starts
    allowed = (segment[:, None] == segment[None, :]) & (places[:, None] >= places[None, :])
    inverse = THETA ** (-(2.0 * jnp.arange(HD // 2, dtype=F32)) / HD)
    angles = relative.astype(F32)[:, None] * inverse[None, :]
    cos_table = jnp.cos(angles)
    sin_table = jnp.sin(angles)

    living = (places[:rows] < ends[-1])[:, None]
    cot_local = jnp.where(living, cotangent, jnp.zeros((), BF))
    cot_all = spread(after(cot_local, attn_full), ZRING, 4)
    z_rank = 2 * zh + zl
    cot_ring = [
        lax.dynamic_index_in_dim(cot_all, (z_rank + k) % 4, 0, keepdims=False) for k in (1, 3, 2)
    ]
    cot_groups = [cot_local, jnp.concatenate(cot_ring[:2], axis=0), cot_ring[2]]
    cot_groups = [(part, swap(part, "core")) for part in cot_groups]

    inputs = layer_input.astype(F32)
    group_inputs = group_gather(layer_input).astype(F32)
    group_scale = lax.rsqrt(
        jnp.mean(group_inputs * group_inputs, axis=-1, keepdims=True) + EPSILON
    )
    first_scale = group_scale[:rows]
    normed_group = (group_inputs * group_scale * gain_attn).astype(BF)
    qkv = dot(normed_group, qkv_full) + bias
    queries = rotate(
        qkv[:, :384].reshape(group, heads, HD), cos_table[:, None, :], sin_table[:, None, :]
    ).astype(BF)
    keys = rotate(qkv[:, 384:512], cos_table, sin_table).astype(BF)
    values = qkv[:, 512:].astype(BF)
    scores = jnp.einsum("qhd,kd->hqk", queries, keys, preferred_element_type=F32) * scale
    scores = jnp.where(allowed[None], scores, -1e30)
    peak = jnp.max(scores, axis=-1, keepdims=True)
    shifted = jnp.exp(scores - peak)
    total = jnp.sum(shifted, axis=-1, keepdims=True)
    probs = shifted / total
    attended = (
        jnp.einsum("hqk,kd->qhd", probs.astype(BF), values, preferred_element_type=F32)
        .reshape(group, heads * HD)
        .astype(BF)
    )
    residual = inputs + group_scatter(dot_t(attended, o_full))
    second_scale = lax.rsqrt(jnp.mean(residual * residual, axis=-1, keepdims=True) + EPSILON)
    normed_mlp = (residual * second_scale * gain_mlp).astype(BF)

    after_rows, before_rows = z_shift(normed_mlp, -1), z_shift(normed_mlp, 1)
    far_rows = z_shift(normed_mlp, 2)
    own = (normed_mlp, swap(normed_mlp, "core"))
    own_out = ff_rows(own, cot_groups[0], mlp)
    after_rows, before_rows, own_out = lax.optimization_barrier((after_rows, before_rows, own_out))
    near = jnp.concatenate([after_rows, before_rows], axis=0)
    near = (near, swap(near, "core"))
    near_out = ff_rows(near, cot_groups[1], mlp)
    far_rows, near_out = lax.optimization_barrier((far_rows, near_out))
    far = (far_rows, swap(far_rows, "core"))
    near_sum = add(near_out[3], swap(near_out[4], "core"))
    far, near_sum = lax.optimization_barrier((far, near_sum))
    near_got = (z_shift(near_sum[:rows], 1), z_shift(near_sum[rows:], -1))
    far_out = ff_rows(far, cot_groups[2], mlp)
    far_sum = add(far_out[3], swap(far_out[4], "core"))
    own_sum = add(own_out[3], swap(own_out[4], "core"))
    far_sum, own_sum, far_out = lax.optimization_barrier((far_sum, own_sum, far_out))
    far_got = z_shift(far_sum, 2)
    results = (own_out, near_out, far_out)
    hidden, gate_grads, up_grads = ([r[i] for r in results] for i in range(3))
    flat_normed = [*own, *near, *far]
    flat_cots = [part for pair in cot_groups for part in pair]
    mlp_grads = weight_grads(flat_normed, flat_cots, hidden, gate_grads, up_grads)
    terms, mlp_grads = lax.optimization_barrier(((own_sum, *near_got, far_got), mlp_grads))
    normed_mlp_grad = sum(term.astype(F32) for term in terms)
    mlp_grads = lax.psum_scatter(
        mlp_grads.reshape(6, width // 2, HALF), PLANE, scatter_dimension=1, tiled=True
    ).reshape(3, 2, 48, HALF)
    own_grads = lax.dynamic_index_in_dim(mlp_grads, zh, 1, keepdims=False)
    other_grads = swap(lax.dynamic_index_in_dim(mlp_grads, 1 - zh, 1, keepdims=False), "zh")
    own_grads, other_grads = own_grads.astype(F32), other_grads.astype(F32)
    mlp_shard = jnp.concatenate(
        [pick(zh, own_grads, other_grads), pick(zh, other_grads, own_grads)], axis=-1
    )[..., : gate_up.shape[2]]
    gate_up_shard = mlp_shard[:2]
    down_shard = mlp_shard[2].T

    scaled_mlp = normed_mlp_grad * gain_mlp
    gain_mlp_grad = jnp.sum(normed_mlp_grad * residual * second_scale, axis=0)
    residual_grad = (
        cot_local.astype(F32)
        + second_scale * scaled_mlp
        - residual * second_scale**3 * jnp.mean(scaled_mlp * residual, axis=-1, keepdims=True)
    )

    branch = group_gather(residual_grad.astype(BF))
    out_pairs = []
    for part in after(hidden, branch):
        out_pairs.append(halves(dot_t(part, mlp[2]).astype(BF), 0))
    layer_output = (residual + token_sums(out_pairs)).astype(BF)
    o_grad = t_dot(branch, attended)
    attended_grad = dot(branch, o_full).astype(BF).reshape(group, heads, HD)
    prob_grad = jnp.einsum("qhd,kd->hqk", attended_grad, values, preferred_element_type=F32)
    inner = jnp.sum(probs * prob_grad, axis=-1, keepdims=True)
    score_grad = (probs * (prob_grad - inner)).astype(BF)
    query_rot_grad = (
        jnp.einsum("hqk,kd->qhd", score_grad, keys, preferred_element_type=F32) * scale
    )
    key_rot_grad = (
        jnp.einsum("hqk,qhd->kd", score_grad, queries, preferred_element_type=F32) * scale
    )
    value_grad = jnp.einsum(
        "hqk,qhd->kd", probs.astype(BF), attended_grad, preferred_element_type=F32
    )
    query_grad = rotate(query_rot_grad, cos_table[:, None, :], -sin_table[:, None, :]).reshape(
        group, heads * HD
    )
    key_grad = rotate(key_rot_grad, cos_table, -sin_table)
    qkv_grad = jnp.concatenate([query_grad, key_grad, value_grad], axis=-1).astype(BF)
    normed_grad = group_scatter(dot_t(qkv_grad, qkv_full))
    qkv_weight_grad = t_dot(normed_group, qkv_grad)
    scaled_attn = normed_grad * gain_attn
    gain_attn_grad = jnp.sum(normed_grad * inputs * first_scale, axis=0)
    input_grad = (
        residual_grad
        + first_scale * scaled_attn
        - inputs * first_scale**3 * jnp.mean(scaled_attn * inputs, axis=-1, keepdims=True)
    )

    terms = jnp.concatenate([qkv_weight_grad, o_grad], axis=-1).astype(BF)
    terms = exchange(terms.reshape(32, 48, 1024), DATA)
    attn_shard = jnp.sum(terms.astype(F32), axis=0)
    q_shard = attn_shard[:, :384]
    o_shard = attn_shard[:, 640:].T
    kv_sum = attn_shard[:, 384:640].reshape(2, 2, 12, 2, HD)
    kv_keep = lax.dynamic_index_in_dim(kv_sum, core, 1, keepdims=False)
    kv_give = lax.dynamic_index_in_dim(kv_sum, 1 - core, 1, keepdims=False)
    kv_sum = kv_keep + swap(kv_give, "core")
    kv_keep = pick(zl, kv_sum[0], kv_sum[1])
    kv_got = swap(pick(zl, kv_sum[1], kv_sum[0]), "zl")
    kv_shard = jnp.concatenate([pick(zl, kv_keep, kv_got), pick(zl, kv_got, kv_keep)], axis=-1)
    kv_shard = kv_shard.transpose(1, 0, 2)

    sums = jnp.sum(qkv_grad.astype(F32), axis=0)
    ranked = jnp.arange(4, dtype=jnp.int32)[:, None]
    headed = ranked[:2]
    bias_grad = jnp.concatenate(
        [
            jnp.where(ranked == rank, sums[None, :384], 0.0).reshape(1536),
            jnp.where(headed == zl, sums[None, 384:512], 0.0).reshape(256),
        ]
    )
    value_bias_grad = jnp.where(headed == zl, sums[None, 512:], 0.0).reshape(256)
    vectors = jnp.concatenate(
        [
            gain_attn_grad.reshape(128, 12),
            gain_mlp_grad.reshape(128, 12),
            bias_grad.reshape(128, 14),
            value_bias_grad.reshape(128, 2),
            jnp.zeros((128, 88), F32),
        ],
        axis=1,
    )
    vectors = exchange(after(vectors, attn_shard), AXES)
    vectors = jnp.sum(vectors, axis=0)
    return (
        layer_output,
        input_grad,
        q_shard,
        kv_shard,
        o_shard,
        vectors[:24].reshape(2, 12),
        vectors[24:38],
        vectors[38:40],
        gate_up_shard,
        down_shard,
    )


def solution(mesh):
    fine = Mesh(mesh.devices.reshape(SIZES), AXES)
    dp = ("zh", "y", "x")
    tensor = ("zl", "core")
    every = dp + tensor
    in_specs = (
        P(every, None),
        P(dp, tensor),
        P(None, every, None),
        P(tensor, dp),
        P(None, every),
        P(every),
        P(None, dp, tensor),
        P(tensor, dp),
        P(every, None),
        P(dp, None),
    )
    out_specs = (
        P(every, None),
        P(every, None),
        P(dp, tensor),
        P(None, every, None),
        P(tensor, dp),
        P(None, every),
        P(every),
        P(every),
        P(None, dp, tensor),
        P(tensor, dp),
    )
    return jax.shard_map(shards, mesh=fine, in_specs=in_specs, out_specs=out_specs, check_vma=False)
```

```python
import functools

import jax
import jax.numpy as jnp
from jax import lax
from jax.experimental import pallas as pl
from jax.experimental.pallas import tpu as pltpu
from jax.sharding import Mesh, PartitionSpec as P

HQ = 12
KVH = 2
HD = 128
EPSILON = 1e-06
THETA = 1000000.0

AXES = ("zh", "y", "x", "zl", "core")
SIZES = (2, 4, 4, 2, 2)
ZRING = ("zh", "zl")
PLANE = ("y", "x")
DATA = ("zh", "y", "x")
HALF = 1152
BF = jnp.bfloat16
F32 = jnp.float32


def swap(block, axis):
    return lax.ppermute(block, axis, [(0, 1), (1, 0)])


def halves(block, dim):
    middle = block.shape[dim] // 2
    return (
        lax.slice_in_dim(block, 0, middle, axis=dim),
        lax.slice_in_dim(block, middle, block.shape[dim], axis=dim),
    )


def add(*terms):
    total = terms[0].astype(F32)
    for term in terms[1:]:
        total = total + term.astype(F32)
    return total.astype(terms[0].dtype)


def exchange(blocks, axes):
    return lax.all_to_all(blocks, axes, split_axis=0, concat_axis=0, tiled=True)


def spread(block, axes, count):
    return exchange(jnp.broadcast_to(block[None], (count,) + block.shape), axes)


def z_shift(block, by):
    return lax.ppermute(block, ZRING, [(i, (i + by) % 4) for i in range(4)])


def token_groups(block):
    near = jnp.concatenate([z_shift(block, -1), z_shift(block, 1)], axis=0)
    far = z_shift(block, 2)
    return [(part, swap(part, "core")) for part in (block, near, far)]


def token_sums(pairs):
    own, near, far = (add(mine, swap(others, "core")) for mine, others in pairs)
    after_rows, before_rows = halves(near, 0)
    terms = (own, z_shift(after_rows, 1), z_shift(before_rows, -1), z_shift(far, 2))
    return sum(term.astype(F32) for term in terms)


def ff_body(
    na, nb, ca, cb, w, _, m_out, dg_out, du_out, dna_out, dnb_out,
    wbuf, nbuf, cbuf, wsem, nsem, csem, *, tile,
):
    half = na.shape[0]
    weights = [pltpu.make_async_copy(w.at[i], wbuf.at[i], wsem.at[i]) for i in range(3)]
    normed = [
        pltpu.make_async_copy(part, nbuf.at[pl.ds(k * half, half)], nsem.at[k])
        for k, part in enumerate((na, nb))
    ]
    cots = [
        pltpu.make_async_copy(part, cbuf.at[pl.ds(k * half, half)], csem.at[k])
        for k, part in enumerate((ca, cb))
    ]
    for copy in normed + weights[:2] + cots + weights[2:]:
        copy.start()
    for copy in normed + weights[:1]:
        copy.wait()
    tiles = 2 * half // tile
    for i in range(tiles):
        at = pl.ds(i * tile, tile)
        rows = nbuf[at]
        gate = dot(rows, wbuf[0])
        if i == 0:
            weights[1].wait()
        up = dot(rows, wbuf[1])
        if i == 0:
            for copy in cots + weights[2:]:
                copy.wait()
        hidden_grad = dot(cbuf[at], wbuf[2])
        sigma = 1.0 / (1.0 + jnp.exp(-gate))
        act = gate * sigma
        m_out[at] = (act * up).astype(BF)
        up_grad = (hidden_grad * act).astype(BF)
        gate_grad = (hidden_grad * up * sigma * (1.0 + gate * (1.0 - sigma))).astype(BF)
        dg_out[at] = gate_grad
        du_out[at] = up_grad
        back = (dot_t(gate_grad, wbuf[0]) + dot_t(up_grad, wbuf[1])).astype(BF)
        if tiles == 1:
            dna_out[...] = back[:half]
            dnb_out[...] = back[half:]
        else:
            out = dna_out if i < tiles // 2 else dnb_out
            out[pl.ds(i % (tiles // 2) * tile, tile)] = back


def ff_rows(normed, cots, weights, order, tile=256):
    half, width = normed[0].shape
    units = weights.shape[2]
    anywhere = pl.BlockSpec(memory_space=pl.ANY)
    vmem = pl.BlockSpec(memory_space=pltpu.VMEM)
    return pl.pallas_call(
        functools.partial(ff_body, tile=tile),
        out_shape=[jax.ShapeDtypeStruct((2 * half, units), BF)] * 3
        + [jax.ShapeDtypeStruct((half, width), BF)] * 2,
        in_specs=[anywhere] * 6,
        out_specs=[vmem] * 5,
        scratch_shapes=[
            pltpu.VMEM((3, width, units), BF),
            pltpu.VMEM((2 * half, width), BF),
            pltpu.VMEM((2 * half, width), BF),
            pltpu.SemaphoreType.DMA((3,)),
            pltpu.SemaphoreType.DMA((2,)),
            pltpu.SemaphoreType.DMA((2,)),
        ],
        compiler_params=pltpu.CompilerParams(vmem_limit_bytes=48 * 1024 * 1024),
        cost_estimate=pl.CostEstimate(
            flops=20 * half * width * units,
            bytes_accessed=6 * width * units,
            transcendentals=2 * half * units,
        ),
        name="feed_forward_rows",
    )(*normed, *cots, weights, order)


def wg_body(*refs, sizes, tile):
    count = len(sizes)
    groups = count // 2
    normed, cots, refs = refs[:count], refs[count : 2 * count], refs[2 * count :]
    hidden, gates, ups = refs[:groups], refs[groups : 2 * groups], refs[2 * groups : 3 * groups]
    out, nbuf, cbuf, mbuf, gbuf, ubuf, sem = refs[3 * groups + 1 :]
    pair_sizes = [sizes[2 * i] + sizes[2 * i + 1] for i in range(groups)]

    def copies(at, buffer, sources, lengths):
        result, start = [], 0
        for source, length in zip(sources, lengths):
            target = buffer.at[pl.ds(start, length)]
            result.append(pltpu.make_async_copy(source, target, sem.at[at]))
            start += length
        return result

    def normed_copies():
        return copies(0, nbuf, normed, sizes)

    def cot_copies():
        return copies(1, cbuf, cots, sizes)

    def gate_copies():
        return copies(2, gbuf, gates, pair_sizes)

    def up_copies():
        return copies(3, ubuf, ups, pair_sizes)

    def hidden_copies():
        return copies(4, mbuf, hidden, pair_sizes)

    which, step = pl.program_id(0), pl.program_id(1)

    @pl.when((which == 0) & (step == 0))
    def _():
        first = normed_copies() + gate_copies()
        for copy in first + up_copies() + cot_copies() + hidden_copies():
            copy.start()
        for copy in first:
            copy.wait()

    @pl.when((which == 1) & (step == 0))
    def _():
        for copy in up_copies():
            copy.wait()

    @pl.when((which == 2) & (step == 0))
    def _():
        for copy in cot_copies() + hidden_copies():
            copy.wait()

    columns = pl.ds(pl.multiple_of(step * tile, tile), tile)
    for i, (left, right) in enumerate(((nbuf, gbuf), (nbuf, ubuf), (cbuf, mbuf))):

        @pl.when(which == i)
        def _():
            out[...] = t_dot(left[:, columns], right[...]).astype(BF)


def weight_grads(normed, cots, hidden, gates, ups, order, tile=768):
    sizes = tuple(part.shape[0] for part in normed)
    rows, width, units = sum(sizes), normed[0].shape[1], hidden[0].shape[1]
    anywhere = pl.BlockSpec(memory_space=pl.ANY)
    return pl.pallas_call(
        functools.partial(wg_body, sizes=sizes, tile=tile),
        grid=(3, width // tile),
        out_shape=jax.ShapeDtypeStruct((3, width, units), BF),
        in_specs=[anywhere] * (2 * len(normed) + 3 * len(hidden) + 1),
        out_specs=pl.BlockSpec((None, tile, units), lambda i, j: (i, j, 0)),
        scratch_shapes=[pltpu.VMEM((rows, width), BF)] * 2
        + [pltpu.VMEM((rows, units), BF)] * 3
        + [pltpu.SemaphoreType.DMA((5,))],
        compiler_params=pltpu.CompilerParams(vmem_limit_bytes=48 * 1024 * 1024),
        cost_estimate=pl.CostEstimate(
            flops=6 * rows * width * units,
            bytes_accessed=6 * width * units + rows * (4 * width + 6 * units),
            transcendentals=0,
        ),
        name="weight_gradients",
    )(*normed, *cots, *hidden, *gates, *ups, order)


def down_body(ha, hb, hc, w, _, *refs, tile):
    outs, (wbuf, sem) = refs[:6], refs[6:]
    copy = pltpu.make_async_copy(w.at[2], wbuf, sem)
    copy.start()
    copy.wait()
    for group, hidden in enumerate((ha, hb, hc)):
        half = hidden.shape[0] // 2
        step = min(tile, 2 * half)
        for start in range(0, 2 * half, step):
            part = dot_t(hidden[pl.ds(start, step)], wbuf[...]).astype(BF)
            if step > half:
                outs[2 * group][...] = part[:half]
                outs[2 * group + 1][...] = part[half:]
            else:
                outs[2 * group + start // half][pl.ds(start % half, step)] = part


def down_rows(hidden, weights, order, tile=256):
    _, width, units = weights.shape
    anywhere = pl.BlockSpec(memory_space=pl.ANY)
    vmem = pl.BlockSpec(memory_space=pltpu.VMEM)
    halved = [part.shape[0] // 2 for part in hidden for _ in range(2)]
    outs = pl.pallas_call(
        functools.partial(down_body, tile=tile),
        out_shape=[jax.ShapeDtypeStruct((rows, width), BF) for rows in halved],
        in_specs=[vmem] * 3 + [anywhere] * 2,
        out_specs=[vmem] * 6,
        scratch_shapes=[pltpu.VMEM((width, units), BF), pltpu.SemaphoreType.DMA],
        compiler_params=pltpu.CompilerParams(vmem_limit_bytes=32 * 1024 * 1024),
        cost_estimate=pl.CostEstimate(
            flops=2 * sum(halved) * width * units,
            bytes_accessed=2 * width * units + 2 * sum(halved) * (width + units),
            transcendentals=0,
        ),
        name="down_rows",
    )(*hidden, weights, order)
    return [(outs[0], outs[1]), (outs[2], outs[3]), (outs[4], outs[5])]


def attn_grads_body(normed, branch, qkv_grad, attended, _, out):
    out[:, :640] = t_dot(normed[...], qkv_grad[...]).astype(BF)
    out[:, 640:] = t_dot(branch[...], attended[...]).astype(BF)


def attn_weight_grads(normed, branch, qkv_grad, attended, order, tile=768):
    rows, width = normed.shape
    return pl.pallas_call(
        attn_grads_body,
        grid=(width // tile,),
        out_shape=jax.ShapeDtypeStruct((width, 1024), BF),
        in_specs=[
            pl.BlockSpec((rows, tile), lambda i: (0, i)),
            pl.BlockSpec((rows, tile), lambda i: (0, i)),
            pl.BlockSpec((rows, 640), lambda i: (0, 0)),
            pl.BlockSpec((rows, 384), lambda i: (0, 0)),
            pl.BlockSpec(memory_space=pl.ANY),
        ],
        out_specs=pl.BlockSpec((tile, 1024), lambda i: (i, 0)),
        compiler_params=pltpu.CompilerParams(vmem_limit_bytes=32 * 1024 * 1024),
        cost_estimate=pl.CostEstimate(
            flops=2 * rows * width * 1024,
            bytes_accessed=2 * width * 1024 + 4 * rows * width + 2 * rows * 1024,
            transcendentals=0,
        ),
        name="attention_weight_gradients",
    )(normed, branch, qkv_grad, attended, order)


def rotate(vectors, cos_table, sin_table):
    middle = vectors.shape[-1] // 2
    first_half = vectors[..., :middle]
    second_half = vectors[..., middle:]
    return jnp.concatenate(
        [
            first_half * cos_table - second_half * sin_table,
            second_half * cos_table + first_half * sin_table,
        ],
        axis=-1,
    )


def dot(a, b):
    return jnp.dot(a, b, preferred_element_type=F32)


def dot_t(a, b):
    return lax.dot_general(a, b, (((1,), (1,)), ((), ())), preferred_element_type=F32)


def t_dot(a, b):
    return lax.dot_general(a, b, (((0,), (0,)), ((), ())), preferred_element_type=F32)


def pick(index, low, high):
    return jnp.where(index == 0, low, high)


def group_gather(block):
    across = swap(block, "zl")
    return jnp.concatenate([block, swap(block, "core"), across, swap(across, "core")], axis=0)


def chip_sums(partial):
    rows, columns = partial.shape
    parts = partial.reshape(2, 2, rows // 4, columns)
    parts = add(parts[:, 0], swap(parts[:, 1].astype(BF), "core"))
    return parts[0], parts[1].astype(BF)


def group_scatter(partial):
    own, other = chip_sums(partial)
    return own + swap(other, "zl").astype(F32)


def shards(
    layer_input,
    q_weight,
    kv_weight,
    o_weight,
    norm_gains,
    qkv_bias,
    gate_up,
    down_weight,
    cotangent,
    lengths,
):
    zh, zl, core = (lax.axis_index(a) for a in ("zh", "zl", "core"))
    rank = 2 * zl + core
    width = layer_input.shape[1]
    rows = layer_input.shape[0]
    heads = HQ // 4
    scale = HD ** (-0.5)

    small = jnp.concatenate([norm_gains.reshape(-1), qkv_bias, jnp.zeros((216,), BF)])
    vectors = jnp.concatenate([kv_weight.reshape(24, 256), small[None], jnp.zeros((7, 256), BF)])
    got = swap(vectors, "core")
    both = jnp.stack([pick(core, vectors, got), pick(core, got, vectors)])
    small_keep = both[:, 24].reshape(2, 2, HD)
    kv_keep = pick(zl, both[:, :24, :HD], both[:, :24, HD:])
    kv_give = pick(zl, both[:, :24, HD:], both[:, :24, :HD])
    got = swap(jnp.concatenate([kv_give, small_keep, jnp.zeros((2, 6, HD), BF)], axis=1), "zl")
    kv_got, small_got = got[:, :24], got[:, 24:26]
    kv_rows = jnp.stack([pick(zl, kv_keep, kv_got), pick(zl, kv_got, kv_keep)])
    kv_rows = kv_rows.reshape(2, 2, 2, 12, HD).transpose(0, 1, 3, 2, 4).reshape(48, 2 * HD)
    small = jnp.stack([pick(zl, small_keep, small_got), pick(zl, small_got, small_keep)])
    small = jnp.concatenate([small.reshape(8, HD), jnp.zeros((40, HD), BF)])
    attn_part = jnp.concatenate([q_weight, kv_rows, small, o_weight.T], axis=-1)
    attn_full = spread(attn_part, DATA, 32)
    small = attn_full[:, :8, 640:768].reshape(128, 256).astype(F32)
    attn_full = attn_full.reshape(width, 1152)
    qkv_full, o_full = attn_full[:, :640], attn_full[:, 768:]
    gain_attn = small[:, 0:12].reshape(width)
    gain_mlp = small[:, 12:24].reshape(width)
    bias_full = small[:, 24:40].reshape(2048)
    bias = jnp.concatenate(
        [
            lax.dynamic_index_in_dim(bias_full[:1536].reshape(4, 384), rank, 0, keepdims=False),
            pick(zl, bias_full[1536:1664], bias_full[1664:1792]),
            pick(zl, bias_full[1792:1920], bias_full[1920:2048]),
        ]
    )

    mlp = jnp.concatenate([gate_up, down_weight.T[None]], axis=0)
    mlp = jnp.pad(mlp, ((0, 0), (0, 0), (0, 2 * HALF - mlp.shape[2])))
    mlp_own = pick(zh, mlp[..., :HALF], mlp[..., HALF:])
    mlp_other = swap(pick(zh, mlp[..., HALF:], mlp[..., :HALF]), "zh")
    mlp = jnp.stack([pick(zh, mlp_own, mlp_other), pick(zh, mlp_other, mlp_own)], axis=1)
    mlp = lax.all_gather(mlp.reshape(6, 48, HALF), PLANE, axis=1, tiled=True)
    mlp = mlp.reshape(3, width, HALF)

    ends = jnp.cumsum(lengths[0])
    ranks = jnp.stack([rank, 2 * zl + 1 - core, 2 * (1 - zl) + core, 2 * (1 - zl) + 1 - core])
    group = 4 * rows
    places = (ranks[:, None] * rows + jnp.arange(rows, dtype=jnp.int32)[None, :]).reshape(group)
    passed = ends[None, :] <= places[:, None]
    segment = jnp.sum(passed.astype(jnp.int32), axis=1)
    starts = jnp.sum(jnp.where(passed, lengths[0][None, :], 0), axis=1)
    relative = places - starts
    allowed = (segment[:, None] == segment[None, :]) & (places[:, None] >= places[None, :])
    inverse = THETA ** (-(2.0 * jnp.arange(HD // 2, dtype=F32)) / HD)
    angles = relative.astype(F32)[:, None] * inverse[None, :]
    cos_table = jnp.cos(angles)
    sin_table = jnp.sin(angles)

    living = (places[:rows] < ends[-1])[:, None]
    cot_local = jnp.where(living, cotangent, jnp.zeros((), BF))
    cot_all = spread(cot_local, ZRING, 4)
    z_rank = 2 * zh + zl
    cot_ring = [
        lax.dynamic_index_in_dim(cot_all, (z_rank + k) % 4, 0, keepdims=False) for k in (1, 3, 2)
    ]
    cot_groups = [cot_local, jnp.concatenate(cot_ring[:2], axis=0), cot_ring[2]]
    cot_groups = [(part, swap(part, "core")) for part in cot_groups]

    inputs = layer_input.astype(F32)
    group_inputs = group_gather(layer_input).astype(F32)
    group_scale = lax.rsqrt(
        jnp.mean(group_inputs * group_inputs, axis=-1, keepdims=True) + EPSILON
    )
    first_scale = group_scale[:rows]
    normed_group = (group_inputs * group_scale * gain_attn).astype(BF)
    qkv = dot(normed_group, qkv_full) + bias
    queries = rotate(
        qkv[:, :384].reshape(group, heads, HD), cos_table[:, None, :], sin_table[:, None, :]
    ).astype(BF)
    keys = rotate(qkv[:, 384:512], cos_table, sin_table).astype(BF)
    values = qkv[:, 512:].astype(BF)
    scores = jnp.einsum("qhd,kd->hqk", queries, keys, preferred_element_type=F32) * scale
    scores = jnp.where(allowed[None], scores, -1e30)
    peak = jnp.max(scores, axis=-1, keepdims=True)
    shifted = jnp.exp(scores - peak)
    total = jnp.sum(shifted, axis=-1, keepdims=True)
    probs = shifted / total
    attended = (
        jnp.einsum("hqk,kd->qhd", probs.astype(BF), values, preferred_element_type=F32)
        .reshape(group, heads * HD)
        .astype(BF)
    )
    residual = inputs + group_scatter(dot_t(attended, o_full))
    second_scale = lax.rsqrt(jnp.mean(residual * residual, axis=-1, keepdims=True) + EPSILON)
    normed_mlp = (residual * second_scale * gain_mlp).astype(BF)

    after_rows, before_rows = z_shift(normed_mlp, -1), z_shift(normed_mlp, 1)
    far_rows = z_shift(normed_mlp, 2)
    own = (normed_mlp, swap(normed_mlp, "core"))
    own_out = ff_rows(own, cot_groups[0], mlp, cot_local)
    near = jnp.concatenate([after_rows, before_rows], axis=0)
    near = (near, swap(near, "core"))
    near_out = ff_rows(near, cot_groups[1], mlp, own_out[0])
    far = (far_rows, swap(far_rows, "core"))
    near_sum = add(near_out[3], swap(near_out[4], "core"))
    near_got = (z_shift(near_sum[:rows], 1), z_shift(near_sum[rows:], -1))
    far_out = ff_rows(far, cot_groups[2], mlp, near_sum)
    far_sum = add(far_out[3], swap(far_out[4], "core"))
    own_sum = add(own_out[3], swap(own_out[4], "core"))
    far_got = z_shift(far_sum, 2)
    results = (own_out, near_out, far_out)
    hidden, gate_grads, up_grads = ([r[i] for r in results] for i in range(3))
    flat_normed = [*own, *near, *far]
    flat_cots = [part for pair in cot_groups for part in pair]
    mlp_grads = weight_grads(flat_normed, flat_cots, hidden, gate_grads, up_grads, far_sum)
    normed_mlp_grad = sum(term.astype(F32) for term in (own_sum, *near_got, far_got))
    mlp_grads = lax.psum_scatter(
        mlp_grads.reshape(6, width // 2, HALF), PLANE, scatter_dimension=1, tiled=True
    ).reshape(3, 2, 48, HALF)
    own_grads = lax.dynamic_index_in_dim(mlp_grads, zh, 1, keepdims=False)
    other_grads = swap(lax.dynamic_index_in_dim(mlp_grads, 1 - zh, 1, keepdims=False), "zh")
    own_grads, other_grads = own_grads.astype(F32), other_grads.astype(F32)
    mlp_shard = jnp.concatenate(
        [pick(zh, own_grads, other_grads), pick(zh, other_grads, own_grads)], axis=-1
    )[..., : gate_up.shape[2]]
    gate_up_shard = mlp_shard[:2]
    down_shard = mlp_shard[2].T

    scaled_mlp = normed_mlp_grad * gain_mlp
    gain_mlp_grad = jnp.sum(normed_mlp_grad * residual * second_scale, axis=0)
    residual_grad = (
        cot_local.astype(F32)
        + second_scale * scaled_mlp
        - residual * second_scale**3 * jnp.mean(scaled_mlp * residual, axis=-1, keepdims=True)
    )

    branch = group_gather(residual_grad.astype(BF))
    out_pairs = down_rows(hidden, mlp, branch)
    layer_output = (residual + token_sums(out_pairs)).astype(BF)
    attended_grad = dot(branch, o_full).astype(BF).reshape(group, heads, HD)
    prob_grad = jnp.einsum("qhd,kd->hqk", attended_grad, values, preferred_element_type=F32)
    inner = jnp.sum(probs * prob_grad, axis=-1, keepdims=True)
    score_grad = (probs * (prob_grad - inner)).astype(BF)
    query_rot_grad = (
        jnp.einsum("hqk,kd->qhd", score_grad, keys, preferred_element_type=F32) * scale
    )
    key_rot_grad = (
        jnp.einsum("hqk,qhd->kd", score_grad, queries, preferred_element_type=F32) * scale
    )
    value_grad = jnp.einsum(
        "hqk,qhd->kd", probs.astype(BF), attended_grad, preferred_element_type=F32
    )
    query_grad = rotate(query_rot_grad, cos_table[:, None, :], -sin_table[:, None, :]).reshape(
        group, heads * HD
    )
    key_grad = rotate(key_rot_grad, cos_table, -sin_table)
    qkv_grad = jnp.concatenate([query_grad, key_grad, value_grad], axis=-1).astype(BF)
    own_grad, other_grad = chip_sums(dot_t(qkv_grad, qkv_full))
    normed_grad = own_grad + swap(other_grad, "zl").astype(F32)
    terms = attn_weight_grads(normed_group, branch, qkv_grad, attended, other_grad)
    scaled_attn = normed_grad * gain_attn
    gain_attn_grad = jnp.sum(normed_grad * inputs * first_scale, axis=0)
    input_grad = (
        residual_grad
        + first_scale * scaled_attn
        - inputs * first_scale**3 * jnp.mean(scaled_attn * inputs, axis=-1, keepdims=True)
    )

    terms = exchange(terms.reshape(32, 48, 1024), DATA)
    attn_shard = jnp.sum(terms.astype(F32), axis=0)
    q_shard = attn_shard[:, :384]
    o_shard = attn_shard[:, 640:].T
    kv_sum = attn_shard[:, 384:640].reshape(2, 2, 12, 2, HD)
    kv_keep = lax.dynamic_index_in_dim(kv_sum, core, 1, keepdims=False)
    kv_give = lax.dynamic_index_in_dim(kv_sum, 1 - core, 1, keepdims=False)
    kv_sum = kv_keep + swap(kv_give, "core")
    kv_keep = pick(zl, kv_sum[0], kv_sum[1])
    kv_got = swap(pick(zl, kv_sum[1], kv_sum[0]), "zl")
    kv_shard = jnp.concatenate([pick(zl, kv_keep, kv_got), pick(zl, kv_got, kv_keep)], axis=-1)
    kv_shard = kv_shard.transpose(1, 0, 2)

    sums = jnp.sum(qkv_grad.astype(F32), axis=0)
    ranked = jnp.arange(4, dtype=jnp.int32)[:, None]
    headed = ranked[:2]
    bias_grad = jnp.concatenate(
        [
            jnp.where(ranked == rank, sums[None, :384], 0.0).reshape(1536),
            jnp.where(headed == zl, sums[None, 384:512], 0.0).reshape(256),
        ]
    )
    value_bias_grad = jnp.where(headed == zl, sums[None, 512:], 0.0).reshape(256)
    vectors = jnp.concatenate(
        [
            gain_attn_grad.reshape(128, 12),
            gain_mlp_grad.reshape(128, 12),
            bias_grad.reshape(128, 14),
            value_bias_grad.reshape(128, 2),
            jnp.zeros((128, 88), F32),
        ],
        axis=1,
    )
    vectors = exchange(vectors, AXES)
    vectors = jnp.sum(vectors, axis=0)
    return (
        layer_output,
        input_grad,
        q_shard,
        kv_shard,
        o_shard,
        vectors[:24].reshape(2, 12),
        vectors[24:38],
        vectors[38:40],
        gate_up_shard,
        down_shard,
    )


def solution(mesh):
    fine = Mesh(mesh.devices.reshape(SIZES), AXES)
    dp = ("zh", "y", "x")
    tensor = ("zl", "core")
    every = dp + tensor
    in_specs = (
        P(every, None),
        P(dp, tensor),
        P(None, every, None),
        P(tensor, dp),
        P(None, every),
        P(every),
        P(None, dp, tensor),
        P(tensor, dp),
        P(every, None),
        P(dp, None),
    )
    out_specs = (
        P(every, None),
        P(every, None),
        P(dp, tensor),
        P(None, every, None),
        P(tensor, dp),
        P(None, every),
        P(every),
        P(every),
        P(None, dp, tensor),
        P(tensor, dp),
    )
    return jax.shard_map(shards, mesh=fine, in_specs=in_specs, out_specs=out_specs, check_vma=False)
```

```python
import functools

import jax
import jax.numpy as jnp
from jax import lax
from jax.experimental import pallas as pl
from jax.experimental.pallas import tpu as pltpu
from jax.sharding import Mesh, PartitionSpec as P

HQ = 12
KVH = 2
HD = 128
EPSILON = 1e-06
THETA = 1000000.0

AXES = ("zh", "y", "x", "zl", "core")
SIZES = (2, 4, 4, 2, 2)
ZRING = ("zh", "zl")
PLANE = ("y", "x")
DATA = ("zh", "y", "x")
HALF = 1152
BF = jnp.bfloat16
WEIGHT = 1000
F32 = jnp.float32


def swap(block, axis):
    return lax.ppermute(block, axis, [(0, 1), (1, 0)])


def halves(block, dim):
    middle = block.shape[dim] // 2
    return (
        lax.slice_in_dim(block, 0, middle, axis=dim),
        lax.slice_in_dim(block, middle, block.shape[dim], axis=dim),
    )


def add(*terms):
    total = terms[0].astype(F32)
    for term in terms[1:]:
        total = total + term.astype(F32)
    return total.astype(terms[0].dtype)


def exchange(blocks, axes):
    return lax.all_to_all(blocks, axes, split_axis=0, concat_axis=0, tiled=True)


def spread(block, axes, count):
    return exchange(jnp.broadcast_to(block[None], (count,) + block.shape), axes)


def z_shift(block, by):
    return lax.ppermute(block, ZRING, [(i, (i + by) % 4) for i in range(4)])


def token_groups(block):
    near = jnp.concatenate([z_shift(block, -1), z_shift(block, 1)], axis=0)
    far = z_shift(block, 2)
    return [(part, swap(part, "core")) for part in (block, near, far)]


def token_sums(pairs):
    own, near, far = (add(mine, swap(others, "core")) for mine, others in pairs)
    after_rows, before_rows = halves(near, 0)
    terms = (own, z_shift(after_rows, 1), z_shift(before_rows, -1), z_shift(far, 2))
    return sum(term.astype(F32) for term in terms)


def ff_body(
    na, nb, ca, cb, w, _, m_out, dg_out, du_out, dna_out, dnb_out,
    wbuf, nbuf, cbuf, wsem, nsem, csem, *, tile,
):
    half = na.shape[0]
    weights = [pltpu.make_async_copy(w.at[i], wbuf.at[i], wsem.at[i]) for i in range(3)]
    normed = [
        pltpu.make_async_copy(part, nbuf.at[pl.ds(k * half, half)], nsem.at[k])
        for k, part in enumerate((na, nb))
    ]
    cots = [
        pltpu.make_async_copy(part, cbuf.at[pl.ds(k * half, half)], csem.at[k])
        for k, part in enumerate((ca, cb))
    ]
    for copy in normed + weights[:2] + cots + weights[2:]:
        copy.start()
    for copy in normed + weights[:1]:
        copy.wait()
    tiles = 2 * half // tile
    for i in range(tiles):
        at = pl.ds(i * tile, tile)
        rows = nbuf[at]
        gate = dot(rows, wbuf[0])
        if i == 0:
            weights[1].wait()
        up = dot(rows, wbuf[1])
        if i == 0:
            for copy in cots + weights[2:]:
                copy.wait()
        hidden_grad = dot(cbuf[at], wbuf[2])
        sigma = 1.0 / (1.0 + jnp.exp(-gate))
        act = gate * sigma
        m_out[at] = (act * up).astype(BF)
        up_grad = (hidden_grad * act).astype(BF)
        gate_grad = (hidden_grad * up * sigma * (1.0 + gate * (1.0 - sigma))).astype(BF)
        dg_out[at] = gate_grad
        du_out[at] = up_grad
        back = (dot_t(gate_grad, wbuf[0]) + dot_t(up_grad, wbuf[1])).astype(BF)
        if tiles == 1:
            dna_out[...] = back[:half]
            dnb_out[...] = back[half:]
        else:
            out = dna_out if i < tiles // 2 else dnb_out
            out[pl.ds(i % (tiles // 2) * tile, tile)] = back


def ff_rows(normed, cots, weights, order, tile=256):
    half, width = normed[0].shape
    units = weights.shape[2]
    anywhere = pl.BlockSpec(memory_space=pl.ANY)
    vmem = pl.BlockSpec(memory_space=pltpu.VMEM)
    return pl.pallas_call(
        functools.partial(ff_body, tile=tile),
        out_shape=[jax.ShapeDtypeStruct((2 * half, units), BF)] * 3
        + [jax.ShapeDtypeStruct((half, width), BF)] * 2,
        in_specs=[anywhere] * 6,
        out_specs=[vmem] * 5,
        scratch_shapes=[
            pltpu.VMEM((3, width, units), BF),
            pltpu.VMEM((2 * half, width), BF),
            pltpu.VMEM((2 * half, width), BF),
            pltpu.SemaphoreType.DMA((3,)),
            pltpu.SemaphoreType.DMA((2,)),
            pltpu.SemaphoreType.DMA((2,)),
        ],
        compiler_params=pltpu.CompilerParams(vmem_limit_bytes=48 * 1024 * 1024),
        cost_estimate=pl.CostEstimate(
            flops=20 * half * width * units,
            bytes_accessed=6 * width * units,
            transcendentals=2 * half * units,
        ),
        name="feed_forward_rows",
    )(*normed, *cots, weights, order)


def wg_body(*refs, sizes, tile):
    count = len(sizes)
    groups = count // 2
    normed, cots, refs = refs[:count], refs[count : 2 * count], refs[2 * count :]
    hidden, gates, ups = refs[:groups], refs[groups : 2 * groups], refs[2 * groups : 3 * groups]
    out, nbuf, cbuf, mbuf, gbuf, ubuf, sem = refs[3 * groups + 1 :]
    pair_sizes = [sizes[2 * i] + sizes[2 * i + 1] for i in range(groups)]

    def copies(at, buffer, sources, lengths):
        result, start = [], 0
        for source, length in zip(sources, lengths):
            target = buffer.at[pl.ds(start, length)]
            result.append(pltpu.make_async_copy(source, target, sem.at[at]))
            start += length
        return result

    def normed_copies():
        return copies(0, nbuf, normed, sizes)

    def cot_copies():
        return copies(1, cbuf, cots, sizes)

    def gate_copies():
        return copies(2, gbuf, gates, pair_sizes)

    def up_copies():
        return copies(3, ubuf, ups, pair_sizes)

    def hidden_copies():
        return copies(4, mbuf, hidden, pair_sizes)

    which, step = pl.program_id(0), pl.program_id(1)

    @pl.when((which == 0) & (step == 0))
    def _():
        first = normed_copies() + gate_copies()
        for copy in first + up_copies() + cot_copies() + hidden_copies():
            copy.start()
        for copy in first:
            copy.wait()

    @pl.when((which == 1) & (step == 0))
    def _():
        for copy in up_copies():
            copy.wait()

    @pl.when((which == 2) & (step == 0))
    def _():
        for copy in cot_copies() + hidden_copies():
            copy.wait()

    columns = pl.ds(pl.multiple_of(step * tile, tile), tile)
    for i, (left, right) in enumerate(((nbuf, gbuf), (nbuf, ubuf), (cbuf, mbuf))):

        @pl.when(which == i)
        def _():
            out[...] = t_dot(left[:, columns], right[...]).astype(BF)


def weight_grads(normed, cots, hidden, gates, ups, order, tile=768):
    sizes = tuple(part.shape[0] for part in normed)
    rows, width, units = sum(sizes), normed[0].shape[1], hidden[0].shape[1]
    anywhere = pl.BlockSpec(memory_space=pl.ANY)
    return pl.pallas_call(
        functools.partial(wg_body, sizes=sizes, tile=tile),
        grid=(3, width // tile),
        out_shape=jax.ShapeDtypeStruct((3, width, units), BF),
        in_specs=[anywhere] * (2 * len(normed) + 3 * len(hidden) + 1),
        out_specs=pl.BlockSpec((None, tile, units), lambda i, j: (i, j, 0)),
        scratch_shapes=[pltpu.VMEM((rows, width), BF)] * 2
        + [pltpu.VMEM((rows, units), BF)] * 3
        + [pltpu.SemaphoreType.DMA((5,))],
        compiler_params=pltpu.CompilerParams(vmem_limit_bytes=48 * 1024 * 1024),
        cost_estimate=pl.CostEstimate(
            flops=6 * rows * width * units,
            bytes_accessed=6 * width * units + rows * (4 * width + 6 * units),
            transcendentals=0,
        ),
        name="weight_gradients",
    )(*normed, *cots, *hidden, *gates, *ups, order)


def down_body(ha, hb, hc, w, _, *refs, tile):
    outs, (wbuf, sem) = refs[:6], refs[6:]
    copy = pltpu.make_async_copy(w.at[2], wbuf, sem)
    copy.start()
    copy.wait()
    for group, hidden in enumerate((ha, hb, hc)):
        half = hidden.shape[0] // 2
        step = min(tile, 2 * half)
        for start in range(0, 2 * half, step):
            part = dot_t(hidden[pl.ds(start, step)], wbuf[...]).astype(BF)
            if step > half:
                outs[2 * group][...] = part[:half]
                outs[2 * group + 1][...] = part[half:]
            else:
                outs[2 * group + start // half][pl.ds(start % half, step)] = part


def down_rows(hidden, weights, order, tile=256):
    _, width, units = weights.shape
    anywhere = pl.BlockSpec(memory_space=pl.ANY)
    vmem = pl.BlockSpec(memory_space=pltpu.VMEM)
    halved = [part.shape[0] // 2 for part in hidden for _ in range(2)]
    outs = pl.pallas_call(
        functools.partial(down_body, tile=tile),
        out_shape=[jax.ShapeDtypeStruct((rows, width), BF) for rows in halved],
        in_specs=[vmem] * 3 + [anywhere] * 2,
        out_specs=[vmem] * 6,
        scratch_shapes=[pltpu.VMEM((width, units), BF), pltpu.SemaphoreType.DMA],
        compiler_params=pltpu.CompilerParams(vmem_limit_bytes=32 * 1024 * 1024),
        cost_estimate=pl.CostEstimate(
            flops=2 * sum(halved) * width * units,
            bytes_accessed=2 * width * units + 2 * sum(halved) * (width + units),
            transcendentals=0,
        ),
        name="down_rows",
    )(*hidden, weights, order)
    return [(outs[0], outs[1]), (outs[2], outs[3]), (outs[4], outs[5])]


def attn_grads_body(normed, branch, qkv_grad, attended, _, out):
    out[:, :640] = t_dot(normed[...], qkv_grad[...]).astype(BF)
    out[:, 640:] = t_dot(branch[...], attended[...]).astype(BF)


def attn_weight_grads(normed, branch, qkv_grad, attended, order, tile=768):
    rows, width = normed.shape
    return pl.pallas_call(
        attn_grads_body,
        grid=(width // tile,),
        out_shape=jax.ShapeDtypeStruct((width, 1024), BF),
        in_specs=[
            pl.BlockSpec((rows, tile), lambda i: (0, i)),
            pl.BlockSpec((rows, tile), lambda i: (0, i)),
            pl.BlockSpec((rows, 640), lambda i: (0, 0)),
            pl.BlockSpec((rows, 384), lambda i: (0, 0)),
            pl.BlockSpec(memory_space=pl.ANY),
        ],
        out_specs=pl.BlockSpec((tile, 1024), lambda i: (i, 0)),
        compiler_params=pltpu.CompilerParams(vmem_limit_bytes=32 * 1024 * 1024),
        cost_estimate=pl.CostEstimate(
            flops=2 * rows * width * 1024,
            bytes_accessed=2 * width * 1024 + 4 * rows * width + 2 * rows * 1024,
            transcendentals=0,
        ),
        name="attention_weight_gradients",
    )(normed, branch, qkv_grad, attended, order)


def down_body(ha, hb, hc, w, _, *refs, tile):
    outs, (wbuf, sem) = refs[:6], refs[6:]
    copy = pltpu.make_async_copy(w.at[2], wbuf, sem)
    copy.start()
    copy.wait()
    for group, hidden in enumerate((ha, hb, hc)):
        half = hidden.shape[0] // 2
        step = min(tile, 2 * half)
        for start in range(0, 2 * half, step):
            part = dot_t(hidden[pl.ds(start, step)], wbuf[...]).astype(BF)
            if step > half:
                outs[2 * group][...] = part[:half]
                outs[2 * group + 1][...] = part[half:]
            else:
                outs[2 * group + start // half][pl.ds(start % half, step)] = part


def down_rows(hidden, weights, order, tile=256):
    _, width, units = weights.shape
    anywhere = pl.BlockSpec(memory_space=pl.ANY)
    vmem = pl.BlockSpec(memory_space=pltpu.VMEM)
    halved = [part.shape[0] // 2 for part in hidden for _ in range(2)]
    outs = pl.pallas_call(
        functools.partial(down_body, tile=tile),
        out_shape=[jax.ShapeDtypeStruct((rows, width), BF) for rows in halved],
        in_specs=[vmem] * 3 + [anywhere] * 2,
        out_specs=[vmem] * 6,
        scratch_shapes=[pltpu.VMEM((width, units), BF), pltpu.SemaphoreType.DMA],
        compiler_params=pltpu.CompilerParams(vmem_limit_bytes=32 * 1024 * 1024),
        cost_estimate=pl.CostEstimate(
            flops=2 * sum(halved) * width * units,
            bytes_accessed=2 * width * units + 2 * sum(halved) * (width + units),
            transcendentals=0,
        ),
        name="down_rows",
    )(*hidden, weights, order)
    return [(outs[0], outs[1]), (outs[2], outs[3]), (outs[4], outs[5])]


def dot(a, b):
    return jnp.dot(a, b, preferred_element_type=F32)


def dot_t(a, b):
    return lax.dot_general(a, b, (((1,), (1,)), ((), ())), preferred_element_type=F32)


def t_dot(a, b):
    return lax.dot_general(a, b, (((0,), (0,)), ((), ())), preferred_element_type=F32)


def pick(index, low, high):
    return jnp.where(index == 0, low, high)


def vmem_call(body, outs, ins, name, order=(), scratch=(), limit=40, flops=0, moved=0):
    vmem = pl.BlockSpec(memory_space=pltpu.VMEM)
    anywhere = pl.BlockSpec(memory_space=pl.ANY)
    count, skipped = len(ins), len(order)

    def kernel(*refs):
        body(*refs[:count], *refs[count + skipped :])

    return pl.pallas_call(
        kernel,
        out_shape=[jax.ShapeDtypeStruct(shape, dtype) for shape, dtype in outs],
        in_specs=[vmem] * count + [anywhere] * skipped,
        out_specs=[vmem] * len(outs),
        scratch_shapes=list(scratch),
        compiler_params=pltpu.CompilerParams(vmem_limit_bytes=limit * 1024 * 1024),
        cost_estimate=pl.CostEstimate(flops=flops, bytes_accessed=moved, transcendentals=0),
        name=name,
    )(*ins, *order)


def copies_body(block, out):
    for i in range(out.shape[0]):
        out[i] = block[...]


def copies(block, count, *order):
    shape = (count,) + block.shape
    moved = 2 * count * block.size
    return vmem_call(
        copies_body, [(shape, block.dtype)], [block], "copies", order, moved=moved
    )[0]


def stack_body(*refs):
    *parts, out = refs
    rows = parts[0].shape[0]
    for i, part in enumerate(parts):
        out[i * rows : (i + 1) * rows] = part[...]


def stacked(parts, *order):
    rows, columns = parts[0].shape
    shape = (len(parts) * rows, columns)
    moved = 4 * shape[0] * columns
    return vmem_call(stack_body, [(shape, BF)], list(parts), "stacked", order, moved=moved)[0]


def turn(vectors, cos2, sin2):
    return vectors * cos2 + pltpu.roll(vectors, HD // 2, 1) * sin2


def masked_scores(queries, keys, allowed):
    return jnp.where(allowed, dot_t(queries, keys) * HD ** (-0.5), -1e30)


def attn_forward_body(
    x0, x1, x2, x3, gain, w, bias, cos2, sin2, seg_c, seg_r, pos_c, pos_r,
    n_out, q_out, kv_out, o_out, lse_out,
):
    rows = x0.shape[0]
    for i, x in enumerate((x0, x1, x2, x3)):
        part = x[...].astype(F32)
        scale = lax.rsqrt(jnp.mean(part * part, axis=-1, keepdims=True) + EPSILON)
        n_out[i * rows : (i + 1) * rows] = (part * scale * gain[...]).astype(BF)
    qkv = dot(n_out[...], w[:, :640]) + bias[...]
    cosines, sines = cos2[...], sin2[...]
    keys = turn(qkv[:, 384:512], cosines, sines).astype(BF)
    values = qkv[:, 512:].astype(BF)
    kv_out[:, :HD] = keys
    kv_out[:, HD:] = values
    allowed = (seg_c[...] == seg_r[...]) & (pos_c[...] >= pos_r[...])
    lses = []
    for h in range(3):
        at = slice(h * HD, (h + 1) * HD)
        queries = turn(qkv[:, at], cosines, sines).astype(BF)
        q_out[:, at] = queries
        scores = masked_scores(queries, keys, allowed)
        peak = jnp.max(scores, axis=-1, keepdims=True)
        shifted = jnp.exp(scores - peak)
        total = jnp.sum(shifted, axis=-1, keepdims=True)
        probs = (shifted / total).astype(BF)
        o_out[:, at] = dot(probs, values).astype(BF)
        lses.append(peak + jnp.log(total))
    lse_out[...] = jnp.concatenate(lses + [jnp.zeros((4 * rows, 125), F32)], axis=1)


def parted(partial, keep, give):
    rows = partial.shape[0] // 4
    keep[0] = partial[:rows].astype(BF)
    give[0] = partial[rows : 2 * rows].astype(BF)
    keep[1] = partial[2 * rows : 3 * rows].astype(BF)
    give[1] = partial[3 * rows :].astype(BF)


def attn_out_body(o, w, keep, give):
    parted(dot_t(o[...], w[...]), keep, give)


def residual_body(x, keep, got, across, gain, h_out, n_out):
    h = x[...].astype(F32) + keep[0].astype(F32) + got[0].astype(F32) + across[...].astype(F32)
    h_out[...] = h
    scale = lax.rsqrt(jnp.mean(h * h, axis=-1, keepdims=True) + EPSILON)
    n_out[...] = (h * scale * gain[...]).astype(BF)


def norm_backward(grad, rows, gain):
    scale = lax.rsqrt(jnp.mean(rows * rows, axis=-1, keepdims=True) + EPSILON)
    scaled = grad * gain
    back = scale * scaled - rows * scale**3 * jnp.mean(scaled * rows, axis=-1, keepdims=True)
    return back, jnp.sum(grad * rows * scale, axis=0, keepdims=True)


def ff_back_body(own_a, own_b, got_a, got_b, got_c, h, cot, gain, grad_out, branch_out, gain_out):
    grad = sum(part[...].astype(F32) for part in (own_a, own_b, got_a, got_b, got_c))
    back, gain_out[...] = norm_backward(grad, h[...], gain[...])
    total = cot[...].astype(F32) + back
    grad_out[...] = total
    branch_out[...] = total.astype(BF)


def attn_back_body(keep, got, across, x, above, gain, grad_out, gain_out):
    grad = keep[0].astype(F32) + got[0].astype(F32) + across[...].astype(F32)
    back, gain_out[...] = norm_backward(grad, x[...].astype(F32), gain[...])
    grad_out[...] = above[...] + back


def attn_backward_body(
    b0, b1, b2, b3, wo, w, q, kv, lse, cos2, sin2, seg_c, seg_r, pos_c, pos_r,
    grads_out, keep, give, sums_out, bbuf,
):
    rows = b0.shape[0]
    for i, part in enumerate((b0, b1, b2, b3)):
        bbuf[i * rows : (i + 1) * rows] = part[...]
    attended_grad = dot(bbuf[...], wo[...]).astype(BF)
    keys, values = kv[:, :HD], kv[:, HD:]
    cosines, sines = cos2[...], -sin2[...]
    allowed = (seg_c[...] == seg_r[...]) & (pos_c[...] >= pos_r[...])
    key_grad = value_grad = 0.0
    for h in range(3):
        at = slice(h * HD, (h + 1) * HD)
        queries, o_grad = q[:, at], attended_grad[:, at]
        probs = jnp.exp(masked_scores(queries, keys, allowed) - lse[:, h : h + 1])
        prob_grad = dot_t(o_grad, values)
        inner = jnp.sum(probs * prob_grad, axis=-1, keepdims=True)
        score_grad = (probs * (prob_grad - inner)).astype(BF)
        query_grad = dot(score_grad, keys) * HD ** (-0.5)
        grads_out[:, at] = turn(query_grad, cosines, sines).astype(BF)
        key_grad = key_grad + t_dot(score_grad, queries)
        value_grad = value_grad + t_dot(probs.astype(BF), o_grad)
    grads_out[:, 384:512] = turn(key_grad * HD ** (-0.5), cosines, sines).astype(BF)
    grads_out[:, 512:] = value_grad.astype(BF)
    grads = grads_out[...]
    sums_out[...] = jnp.sum(grads.astype(F32), axis=0, keepdims=True)
    parted(dot_t(grads, w[:, :640]), keep, give)


def rows_product_body(*refs):
    *rows, right, out, buffer = refs
    size = rows[0].shape[0]
    for i, part in enumerate(rows):
        buffer[i * size : (i + 1) * size] = part[...]
    half = buffer.shape[1] // 2
    for i in range(2):
        grad = t_dot(buffer[:, i * half : (i + 1) * half], right[...]).astype(BF)
        out[16 * i : 16 * (i + 1)] = grad.reshape(16, half // 16, right.shape[1])


def rows_product(rows, right, name, order):
    width, columns = rows[0].shape[1], right.shape[1]
    total = sum(part.shape[0] for part in rows)
    return vmem_call(
        rows_product_body,
        [((32, width // 32, columns), BF)],
        [*rows, right],
        name,
        order,
        [pltpu.VMEM((total, width), BF)],
        flops=2 * total * width * columns,
        moved=2 * (total * width + total * columns + width * columns),
    )[0]


def shards(
    layer_input,
    q_weight,
    kv_weight,
    o_weight,
    norm_gains,
    qkv_bias,
    gate_up,
    down_weight,
    cotangent,
    lengths,
):
    zh, zl, core = (lax.axis_index(a) for a in ("zh", "zl", "core"))
    rank = 2 * zl + core
    width = layer_input.shape[1]
    rows = layer_input.shape[0]

    small = jnp.concatenate([norm_gains.reshape(-1), qkv_bias, jnp.zeros((216,), BF)])
    vectors = jnp.concatenate([kv_weight.reshape(24, 256), small[None], jnp.zeros((7, 256), BF)])
    got = swap(vectors, "core")
    both = jnp.stack([pick(core, vectors, got), pick(core, got, vectors)])
    small_keep = both[:, 24].reshape(2, 2, HD)
    kv_keep = pick(zl, both[:, :24, :HD], both[:, :24, HD:])
    kv_give = pick(zl, both[:, :24, HD:], both[:, :24, :HD])
    got = swap(jnp.concatenate([kv_give, small_keep, jnp.zeros((2, 6, HD), BF)], axis=1), "zl")
    kv_got, small_got = got[:, :24], got[:, 24:26]
    kv_rows = jnp.stack([pick(zl, kv_keep, kv_got), pick(zl, kv_got, kv_keep)])
    kv_rows = kv_rows.reshape(2, 2, 2, 12, HD).transpose(0, 1, 3, 2, 4).reshape(48, 2 * HD)
    small = jnp.stack([pick(zl, small_keep, small_got), pick(zl, small_got, small_keep)])
    small = jnp.concatenate([small.reshape(8, HD), jnp.zeros((40, HD), BF)])
    ends = jnp.cumsum(lengths[0])
    own_places = rank * rows + jnp.arange(rows, dtype=jnp.int32)
    living = (own_places < ends[-1])[:, None]
    cot_local = jnp.where(living, cotangent, jnp.zeros((), BF))
    cot_groups = token_groups(cot_local)

    across = swap(layer_input, "zl")
    group_inputs = (layer_input, swap(layer_input, "core"), across, swap(across, "core"))

    qkv_full = exchange(
        copies(jnp.concatenate([q_weight, kv_rows, small], axis=-1), 32, across), DATA
    )
    o_full = exchange(copies(o_weight.T, 32, qkv_full, cot_groups[1][1], cot_groups[2][1]), DATA).reshape(width, 384)
    small = qkv_full[:, :8, 640:].reshape(128, 256).astype(F32)
    qkv_full = qkv_full.reshape(width, 768)
    gain_attn = small[:, 0:12].reshape(1, width)
    gain_mlp = small[:, 12:24].reshape(1, width)
    bias_full = small[:, 24:40].reshape(2048)
    bias = jnp.concatenate(
        [
            lax.dynamic_index_in_dim(bias_full[:1536].reshape(4, 384), rank, 0, keepdims=False),
            pick(zl, bias_full[1536:1664], bias_full[1664:1792]),
            pick(zl, bias_full[1792:1920], bias_full[1920:2048]),
        ]
    )[None]

    mlp = jnp.concatenate([gate_up, down_weight.T[None]], axis=0)
    mlp = jnp.pad(mlp, ((0, 0), (0, 0), (0, 2 * HALF - mlp.shape[2])))
    mlp_own = pick(zh, mlp[..., :HALF], mlp[..., HALF:])
    mlp_other = swap(pick(zh, mlp[..., HALF:], mlp[..., :HALF]), "zh")
    mlp = jnp.stack([pick(zh, mlp_own, mlp_other), pick(zh, mlp_other, mlp_own)], axis=1)
    mlp = lax.all_gather(mlp.reshape(6, 48, HALF), PLANE, axis=1, tiled=True)
    mlp = mlp.reshape(3, width, HALF)

    ranks = jnp.stack([rank, 2 * zl + 1 - core, 2 * (1 - zl) + core, 2 * (1 - zl) + 1 - core])
    group = 4 * rows
    places = (ranks[:, None] * rows + jnp.arange(rows, dtype=jnp.int32)[None, :]).reshape(group)
    passed = ends[None, :] <= places[:, None]
    segment = jnp.sum(passed.astype(jnp.int32), axis=1)
    starts = jnp.sum(jnp.where(passed, lengths[0][None, :], 0), axis=1)
    relative = places - starts
    inverse = THETA ** (-(2.0 * jnp.arange(HD // 2, dtype=F32)) / HD)
    angles = relative.astype(F32)[:, None] * inverse[None, :]
    cosines, sines = jnp.cos(angles), jnp.sin(angles)
    tables = (
        jnp.concatenate([cosines, cosines], axis=1),
        jnp.concatenate([-sines, sines], axis=1),
        segment[:, None],
        segment[None, :],
        places[:, None],
        places[None, :],
    )

    normed_group, queries, kv_rot, attended, lse = vmem_call(
        attn_forward_body,
        [
            ((group, width), BF),
            ((group, 384), BF),
            ((group, 256), BF),
            ((group, 384), BF),
            ((group, 128), F32),
        ],
        [*group_inputs, gain_attn, qkv_full, bias, *tables],
        "attention_forward",
        flops=2 * group * (width * 640 + 6 * group * HD),
        moved=2 * group * width * 2 + 2 * width * 768,
    )
    pair = ((2, rows, width), BF)
    keep, give = vmem_call(
        attn_out_body,
        [pair, pair],
        [attended, o_full],
        "attention_out",
        flops=2 * group * width * 384,
        moved=2 * width * 384 + 2 * group * width,
    )
    got = swap(give, "core")
    residual, normed_mlp = vmem_call(
        residual_body,
        [((rows, width), F32), ((rows, width), BF)],
        [layer_input, keep, got, swap(add(keep[1], got[1]), "zl"), gain_mlp],
        "residual_norm",
        moved=10 * rows * width,
    )

    after_rows, before_rows = z_shift(normed_mlp, -1), z_shift(normed_mlp, 1)
    far_rows = z_shift(normed_mlp, 2)
    own = (normed_mlp, swap(normed_mlp, "core"))
    own_out = ff_rows(own, cot_groups[0], mlp, cot_local)
    near = stacked((after_rows, before_rows), own_out[0])
    near = (near, swap(near, "core"))
    near_out = ff_rows(near, cot_groups[1], mlp, own_out[0])
    far_rows = stacked((far_rows,), near_out[0])
    far = (far_rows, swap(far_rows, "core"))
    near_sum = [
        add(mine, swap(others, "core"))
        for mine, others in zip(halves(near_out[3], 0), halves(near_out[4], 0))
    ]
    near_got = (z_shift(near_sum[0], 1), z_shift(near_sum[1], -1))
    far_out = ff_rows(far, cot_groups[2], mlp, near_sum[1])
    far_sum = add(far_out[3], swap(far_out[4], "core"))
    own_got = swap(own_out[4], "core")
    far_got = z_shift(far_sum, 2)
    results = (own_out, near_out, far_out)
    hidden, gate_grads, up_grads = ([r[i] for r in results] for i in range(3))
    flat_normed = [*own, *near, *far]
    flat_cots = [part for pair in cot_groups for part in pair]
    mlp_grads = weight_grads(flat_normed, flat_cots, hidden, gate_grads, up_grads, far_sum)
    residual_grad, branch, gain_mlp_grad = vmem_call(
        ff_back_body,
        [((rows, width), F32), ((rows, width), BF), ((1, width), F32)],
        [own_out[3], own_got, *near_got, far_got, residual, cot_local, gain_mlp],
        "residual_gradient",
        (mlp_grads,),
        moved=24 * rows * width,
    )
    mlp_grads = lax.psum_scatter(
        mlp_grads.reshape(6, width // 2, HALF), PLANE, scatter_dimension=1, tiled=True
    ).reshape(3, 2, 48, HALF)
    own_grads = lax.dynamic_index_in_dim(mlp_grads, zh, 1, keepdims=False)
    other_grads = swap(lax.dynamic_index_in_dim(mlp_grads, 1 - zh, 1, keepdims=False), "zh")
    own_grads, other_grads = own_grads.astype(F32), other_grads.astype(F32)
    mlp_shard = jnp.concatenate(
        [pick(zh, own_grads, other_grads), pick(zh, other_grads, own_grads)], axis=-1
    )[..., : gate_up.shape[2]]
    gate_up_shard = mlp_shard[:2]
    down_shard = mlp_shard[2].T

    layer_output = (residual + token_sums(down_rows(hidden, mlp, branch))).astype(BF)

    across = swap(branch, "zl")
    branch_group = (branch, swap(branch, "core"), across, swap(across, "core"))
    o_terms = rows_product(branch_group, attended, "o_weight_gradient", ())
    o_got = exchange(o_terms, DATA)
    qkv_grad, keep, give, sums = vmem_call(
        attn_backward_body,
        [((group, 640), BF), pair, pair, ((1, 640), F32)],
        [*branch_group, o_full, qkv_full, queries, kv_rot, lse, *tables],
        "attention_backward",
        (o_terms,),
        scratch=[pltpu.VMEM((group, width), BF)],
        flops=2 * group * (width * 1024 + 15 * group * HD) * WEIGHT,
        moved=4 * group * width + 2 * width * 1024,
    )
    got = swap(give, "core")
    other = add(keep[1], got[1])
    qkv_terms = rows_product((normed_group,), qkv_grad, "qkv_weight_gradient", (other, o_got))
    input_grad, gain_attn_grad = vmem_call(
        attn_back_body,
        [((rows, width), F32), ((1, width), F32)],
        [keep, got, swap(other, "zl"), layer_input, residual_grad, gain_attn],
        "input_gradient",
        moved=20 * rows * width,
    )

    o_shard = jnp.sum(o_got.astype(F32), axis=0).T
    attn_shard = jnp.sum(exchange(qkv_terms, DATA).astype(F32), axis=0)
    q_shard = attn_shard[:, :384]
    kv_sum = attn_shard[:, 384:640].reshape(2, 2, 12, 2, HD)
    kv_keep = lax.dynamic_index_in_dim(kv_sum, core, 1, keepdims=False)
    kv_give = lax.dynamic_index_in_dim(kv_sum, 1 - core, 1, keepdims=False)
    kv_sum = kv_keep + swap(kv_give, "core")
    kv_keep = pick(zl, kv_sum[0], kv_sum[1])
    kv_got = swap(pick(zl, kv_sum[1], kv_sum[0]), "zl")
    kv_shard = jnp.concatenate([pick(zl, kv_keep, kv_got), pick(zl, kv_got, kv_keep)], axis=-1)
    kv_shard = kv_shard.transpose(1, 0, 2)

    sums = sums[0]
    ranked = jnp.arange(4, dtype=jnp.int32)[:, None]
    headed = ranked[:2]
    bias_grad = jnp.concatenate(
        [
            jnp.where(ranked == rank, sums[None, :384], 0.0).reshape(1536),
            jnp.where(headed == zl, sums[None, 384:512], 0.0).reshape(256),
        ]
    )
    value_bias_grad = jnp.where(headed == zl, sums[None, 512:], 0.0).reshape(256)
    vectors = jnp.concatenate(
        [
            gain_attn_grad.reshape(128, 12),
            gain_mlp_grad.reshape(128, 12),
            bias_grad.reshape(128, 14),
            value_bias_grad.reshape(128, 2),
            jnp.zeros((128, 88), F32),
        ],
        axis=1,
    )
    vectors = exchange(vectors, AXES)
    vectors = jnp.sum(vectors, axis=0)
    return (
        layer_output,
        input_grad,
        q_shard,
        kv_shard,
        o_shard,
        vectors[:24].reshape(2, 12),
        vectors[24:38],
        vectors[38:40],
        gate_up_shard,
        down_shard,
    )


def solution(mesh):
    fine = Mesh(mesh.devices.reshape(SIZES), AXES)
    dp = ("zh", "y", "x")
    tensor = ("zl", "core")
    every = dp + tensor
    in_specs = (
        P(every, None),
        P(dp, tensor),
        P(None, every, None),
        P(tensor, dp),
        P(None, every),
        P(every),
        P(None, dp, tensor),
        P(tensor, dp),
        P(every, None),
        P(dp, None),
    )
    out_specs = (
        P(every, None),
        P(every, None),
        P(dp, tensor),
        P(None, every, None),
        P(tensor, dp),
        P(None, every),
        P(every),
        P(every),
        P(None, dp, tensor),
        P(tensor, dp),
    )
    return jax.shard_map(shards, mesh=fine, in_specs=in_specs, out_specs=out_specs, check_vma=False)
```

```python
import functools

import jax
import jax.numpy as jnp
from jax import lax
from jax.experimental import pallas as pl
from jax.experimental.pallas import tpu as pltpu
from jax.sharding import Mesh, PartitionSpec as P

HQ = 12
KVH = 2
HD = 128
EPSILON = 1e-06
THETA = 1000000.0

AXES = ("zh", "y", "x", "zl", "core")
SIZES = (2, 4, 4, 2, 2)
ZRING = ("zh", "zl")
PLANE = ("y", "x")
DATA = ("zh", "y", "x")
HALF = 1152
BF = jnp.bfloat16
WEIGHT = 1000
F32 = jnp.float32


def swap(block, axis):
    return lax.ppermute(block, axis, [(0, 1), (1, 0)])


def halves(block, dim):
    middle = block.shape[dim] // 2
    return (
        lax.slice_in_dim(block, 0, middle, axis=dim),
        lax.slice_in_dim(block, middle, block.shape[dim], axis=dim),
    )


def add(*terms):
    total = terms[0].astype(F32)
    for term in terms[1:]:
        total = total + term.astype(F32)
    return total.astype(terms[0].dtype)


def exchange(blocks, axes):
    return lax.all_to_all(blocks, axes, split_axis=0, concat_axis=0, tiled=True)


def spread(block, axes, count):
    return exchange(jnp.broadcast_to(block[None], (count,) + block.shape), axes)


def z_shift(block, by):
    return lax.ppermute(block, ZRING, [(i, (i + by) % 4) for i in range(4)])


def token_groups(block):
    near = jnp.concatenate([z_shift(block, -1), z_shift(block, 1)], axis=0)
    far = z_shift(block, 2)
    return [(part, swap(part, "core")) for part in (block, near, far)]


def token_sums(pairs):
    own, near, far = (add(mine, swap(others, "core")) for mine, others in pairs)
    after_rows, before_rows = halves(near, 0)
    terms = (own, z_shift(after_rows, 1), z_shift(before_rows, -1), z_shift(far, 2))
    return sum(term.astype(F32) for term in terms)


def ff_body(
    na, nb, ca, cb, w, _, m_out, dg_out, du_out, dna_out, dnb_out,
    wbuf, nbuf, cbuf, wsem, nsem, csem, *, tile,
):
    half = na.shape[0]
    weights = [pltpu.make_async_copy(w.at[i], wbuf.at[i], wsem.at[i]) for i in range(3)]
    normed = [
        pltpu.make_async_copy(part, nbuf.at[pl.ds(k * half, half)], nsem.at[k])
        for k, part in enumerate((na, nb))
    ]
    cots = [
        pltpu.make_async_copy(part, cbuf.at[pl.ds(k * half, half)], csem.at[k])
        for k, part in enumerate((ca, cb))
    ]
    for copy in normed + weights[:2] + cots + weights[2:]:
        copy.start()
    for copy in normed + weights[:1]:
        copy.wait()
    tiles = 2 * half // tile
    for i in range(tiles):
        at = pl.ds(i * tile, tile)
        rows = nbuf[at]
        gate = dot(rows, wbuf[0])
        if i == 0:
            weights[1].wait()
        up = dot(rows, wbuf[1])
        if i == 0:
            for copy in cots + weights[2:]:
                copy.wait()
        hidden_grad = dot(cbuf[at], wbuf[2])
        sigma = 1.0 / (1.0 + jnp.exp(-gate))
        act = gate * sigma
        m_out[at] = (act * up).astype(BF)
        up_grad = (hidden_grad * act).astype(BF)
        gate_grad = (hidden_grad * up * sigma * (1.0 + gate * (1.0 - sigma))).astype(BF)
        dg_out[at] = gate_grad
        du_out[at] = up_grad
        back = (dot_t(gate_grad, wbuf[0]) + dot_t(up_grad, wbuf[1])).astype(BF)
        if tiles == 1:
            dna_out[...] = back[:half]
            dnb_out[...] = back[half:]
        else:
            out = dna_out if i < tiles // 2 else dnb_out
            out[pl.ds(i % (tiles // 2) * tile, tile)] = back


def ff_rows(normed, cots, weights, order, tile=256):
    half, width = normed[0].shape
    units = weights.shape[2]
    anywhere = pl.BlockSpec(memory_space=pl.ANY)
    vmem = pl.BlockSpec(memory_space=pltpu.VMEM)
    return pl.pallas_call(
        functools.partial(ff_body, tile=tile),
        out_shape=[jax.ShapeDtypeStruct((2 * half, units), BF)] * 3
        + [jax.ShapeDtypeStruct((half, width), BF)] * 2,
        in_specs=[anywhere] * 6,
        out_specs=[vmem] * 5,
        scratch_shapes=[
            pltpu.VMEM((3, width, units), BF),
            pltpu.VMEM((2 * half, width), BF),
            pltpu.VMEM((2 * half, width), BF),
            pltpu.SemaphoreType.DMA((3,)),
            pltpu.SemaphoreType.DMA((2,)),
            pltpu.SemaphoreType.DMA((2,)),
        ],
        compiler_params=pltpu.CompilerParams(vmem_limit_bytes=60 * 1024 * 1024),
        cost_estimate=pl.CostEstimate(
            flops=20 * half * width * units,
            bytes_accessed=6 * width * units,
            transcendentals=2 * half * units,
        ),
        name="feed_forward_rows",
    )(*normed, *cots, weights, order)


def wg_body(*refs, sizes, tile):
    count = len(sizes)
    groups = count // 2
    normed, cots, refs = refs[:count], refs[count : 2 * count], refs[2 * count :]
    hidden, gates, ups = refs[:groups], refs[groups : 2 * groups], refs[2 * groups : 3 * groups]
    out, nbuf, cbuf, mbuf, gbuf, ubuf, sem = refs[3 * groups + 1 :]
    pair_sizes = [sizes[2 * i] + sizes[2 * i + 1] for i in range(groups)]

    def copies(at, buffer, sources, lengths):
        result, start = [], 0
        for source, length in zip(sources, lengths):
            target = buffer.at[pl.ds(start, length)]
            result.append(pltpu.make_async_copy(source, target, sem.at[at]))
            start += length
        return result

    def normed_copies():
        return copies(0, nbuf, normed, sizes)

    def cot_copies():
        return copies(1, cbuf, cots, sizes)

    def gate_copies():
        return copies(2, gbuf, gates, pair_sizes)

    def up_copies():
        return copies(3, ubuf, ups, pair_sizes)

    def hidden_copies():
        return copies(4, mbuf, hidden, pair_sizes)

    which, step = pl.program_id(0), pl.program_id(1)

    @pl.when((which == 0) & (step == 0))
    def _():
        first = normed_copies() + gate_copies()
        for copy in first + up_copies() + cot_copies() + hidden_copies():
            copy.start()
        for copy in first:
            copy.wait()

    @pl.when((which == 1) & (step == 0))
    def _():
        for copy in up_copies():
            copy.wait()

    @pl.when((which == 2) & (step == 0))
    def _():
        for copy in cot_copies() + hidden_copies():
            copy.wait()

    columns = pl.ds(pl.multiple_of(step * tile, tile), tile)
    for i, (left, right) in enumerate(((nbuf, gbuf), (nbuf, ubuf), (cbuf, mbuf))):

        @pl.when(which == i)
        def _():
            out[...] = t_dot(left[:, columns], right[...]).astype(BF)


def weight_grads(normed, cots, hidden, gates, ups, order, tile=768):
    sizes = tuple(part.shape[0] for part in normed)
    rows, width, units = sum(sizes), normed[0].shape[1], hidden[0].shape[1]
    anywhere = pl.BlockSpec(memory_space=pl.ANY)
    return pl.pallas_call(
        functools.partial(wg_body, sizes=sizes, tile=tile),
        grid=(3, width // tile),
        out_shape=jax.ShapeDtypeStruct((3, width, units), BF),
        in_specs=[anywhere] * (2 * len(normed) + 3 * len(hidden) + 1),
        out_specs=pl.BlockSpec((None, tile, units), lambda i, j: (i, j, 0)),
        scratch_shapes=[pltpu.VMEM((rows, width), BF)] * 2
        + [pltpu.VMEM((rows, units), BF)] * 3
        + [pltpu.SemaphoreType.DMA((5,))],
        compiler_params=pltpu.CompilerParams(vmem_limit_bytes=60 * 1024 * 1024),
        cost_estimate=pl.CostEstimate(
            flops=6 * rows * width * units,
            bytes_accessed=6 * width * units + rows * (4 * width + 6 * units),
            transcendentals=0,
        ),
        name="weight_gradients",
    )(*normed, *cots, *hidden, *gates, *ups, order)


def down_body(ha, hb, hc, w, *outs, tile=256):
    for group, hidden in enumerate((ha, hb, hc)):
        half = hidden.shape[0] // 2
        step = min(tile, 2 * half)
        for start in range(0, 2 * half, step):
            part = dot_t(hidden[pl.ds(start, step)], w[...]).astype(BF)
            if step > half:
                outs[2 * group][...] = part[:half]
                outs[2 * group + 1][...] = part[half:]
            else:
                outs[2 * group + start // half][pl.ds(start % half, step)] = part


def down_rows(hidden, weights, order):
    width, units = weights.shape
    halved = [part.shape[0] // 2 for part in hidden for _ in range(2)]
    outs = vmem_call(
        down_body,
        [((rows, width), BF) for rows in halved],
        [*hidden, weights],
        "down_rows",
        (order,),
        flops=2 * sum(halved) * width * units,
        moved=2 * width * units + 2 * sum(halved) * (width + units),
    )
    return [(outs[0], outs[1]), (outs[2], outs[3]), (outs[4], outs[5])]


def dot(a, b):
    return jnp.dot(a, b, preferred_element_type=F32)


def dot_t(a, b):
    return lax.dot_general(a, b, (((1,), (1,)), ((), ())), preferred_element_type=F32)


def t_dot(a, b):
    return lax.dot_general(a, b, (((0,), (0,)), ((), ())), preferred_element_type=F32)


def pick(index, low, high):
    return jnp.where(index == 0, low, high)


def vmem_call(body, outs, ins, name, order=(), scratch=(), limit=60, flops=0, moved=0):
    count, skipped, results, extra = len(ins), len(order), len(outs), len(scratch)

    def kernel(*refs):
        sources, refs = refs[:count], refs[count + skipped :]
        fixed, buffers, sem = refs[: results + extra], refs[results + extra : -1], refs[-1]
        fetches = [
            pltpu.make_async_copy(source, buffer, sem.at[i])
            for i, (source, buffer) in enumerate(zip(sources, buffers))
        ]
        for fetch in fetches:
            fetch.start()
        for fetch in fetches:
            fetch.wait()
        body(*buffers, *fixed)

    return pl.pallas_call(
        kernel,
        out_shape=[jax.ShapeDtypeStruct(shape, dtype) for shape, dtype in outs],
        in_specs=[pl.BlockSpec(memory_space=pl.ANY)] * (count + skipped),
        out_specs=[pl.BlockSpec(memory_space=pltpu.VMEM)] * results,
        scratch_shapes=[
            *scratch,
            *(pltpu.VMEM(value.shape, value.dtype) for value in ins),
            pltpu.SemaphoreType.DMA((count,)),
        ],
        compiler_params=pltpu.CompilerParams(vmem_limit_bytes=limit * 1024 * 1024),
        cost_estimate=pl.CostEstimate(flops=flops, bytes_accessed=moved, transcendentals=0),
        name=name,
    )(*ins, *order)


def copies_body(block, out):
    for i in range(out.shape[0]):
        out[i] = block[...]


def copies(block, count, *order):
    shape = (count,) + block.shape
    moved = 2 * count * block.size
    return vmem_call(
        copies_body, [(shape, block.dtype)], [block], "copies", order, moved=moved
    )[0]


def arrange_body(own, other, zh, out):
    mine = zh[0:1, 0:1] == 0
    for i in range(3):
        out[2 * i] = jnp.where(mine, own[i], other[i])
        out[2 * i + 1] = jnp.where(mine, other[i], own[i])


def stack_body(*refs):
    *parts, out = refs
    rows = parts[0].shape[0]
    for i, part in enumerate(parts):
        out[i * rows : (i + 1) * rows] = part[...]


def stacked(parts, *order):
    rows, columns = parts[0].shape
    shape = (len(parts) * rows, columns)
    moved = 4 * shape[0] * columns
    return vmem_call(stack_body, [(shape, BF)], list(parts), "stacked", order, moved=moved)[0]


def row_of(blocks, offset, size):
    count, lanes = blocks.shape
    line = (lanes, count * size)
    at = lax.broadcasted_iota(jnp.int32, line, 1)
    from_lane = lax.broadcasted_iota(jnp.int32, line, 0) - offset
    spots = (lax.rem(at, size) == from_lane).astype(BF)
    values = dot(blocks, spots)
    at = lax.broadcasted_iota(jnp.int32, values.shape, 1)
    owner = lax.broadcasted_iota(jnp.int32, values.shape, 0)
    mine = (at >= owner * size) & (at < (owner + 1) * size)
    return jnp.sum(jnp.where(mine, values, 0.0), axis=0, keepdims=True)


def vectors_body(gains, biases, ranks, attn_out, mlp_out, bias_out):
    attn_out[...] = jnp.broadcast_to(row_of(gains[...], 0, 48), attn_out.shape)
    mlp_out[...] = jnp.broadcast_to(row_of(gains[...], 48, 48), mlp_out.shape)
    full = row_of(biases[...], 0, 64)
    rank = ranks[0:1, 0:1]
    query = key = value = 0.0
    for i in range(4):
        query = query + jnp.where(rank == i, full[:, 384 * i : 384 * (i + 1)], 0.0)
    for i in range(2):
        mine = (rank >= 2 * i) & (rank < 2 * i + 2)
        key = key + jnp.where(mine, full[:, 1536 + HD * i : 1536 + HD * (i + 1)], 0.0)
        value = value + jnp.where(mine, full[:, 1792 + HD * i : 1792 + HD * (i + 1)], 0.0)
    line = jnp.concatenate([query, key, value], axis=1)
    bias_out[...] = jnp.broadcast_to(line, bias_out.shape)


def turn(vectors, cos2, sin2):
    return vectors * cos2 + pltpu.roll(vectors, HD // 2, 1) * sin2


def unpack_table(table, places):
    first, last = table[:, 2 * HD : 2 * HD + 1], table[:, 2 * HD + 1 : 2 * HD + 2]
    keys = places[0:1, :]
    return table[:, :HD], table[:, HD : 2 * HD], (keys >= first) & (keys <= last)


def masked_scores(queries, keys, allowed):
    return jnp.where(allowed, dot_t(queries, keys) * HD ** (-0.5), -1e30)


def attn_forward_body(
    x0, x1, x2, x3, gain, w, bias, table, places,
    n_out, q_out, kv_out, o_out, lse_out,
):
    rows = x0.shape[0]
    for i, x in enumerate((x0, x1, x2, x3)):
        part = x[...].astype(F32)
        scale = lax.rsqrt(jnp.mean(part * part, axis=-1, keepdims=True) + EPSILON)
        n_out[i * rows : (i + 1) * rows] = (part * scale * gain[0:1]).astype(BF)
    qkv = dot(n_out[...], w[:, :640]) + bias[0:1]
    cosines, sines, allowed = unpack_table(table, places)
    keys = turn(qkv[:, 384:512], cosines, sines).astype(BF)
    values = qkv[:, 512:].astype(BF)
    kv_out[:, :HD] = keys
    kv_out[:, HD:] = values
    lses = []
    for h in range(3):
        at = slice(h * HD, (h + 1) * HD)
        queries = turn(qkv[:, at], cosines, sines).astype(BF)
        q_out[:, at] = queries
        scores = masked_scores(queries, keys, allowed)
        peak = jnp.max(scores, axis=-1, keepdims=True)
        shifted = jnp.exp(scores - peak)
        total = jnp.sum(shifted, axis=-1, keepdims=True)
        probs = (shifted / total).astype(BF)
        o_out[:, at] = dot(probs, values).astype(BF)
        lses.append(peak + jnp.log(total))
    lse_out[...] = jnp.concatenate(lses + [jnp.zeros((4 * rows, 125), F32)], axis=1)


def parted(partial, keep, give):
    rows = partial.shape[0] // 4
    keep[0] = partial[:rows].astype(BF)
    give[0] = partial[rows : 2 * rows].astype(BF)
    keep[1] = partial[2 * rows : 3 * rows].astype(BF)
    give[1] = partial[3 * rows :].astype(BF)


def attn_out_body(o, w, keep, give):
    parted(dot_t(o[...], w[...]), keep, give)


def residual_body(x, keep, got, across, gain, h_out, n_out):
    h = x[...].astype(F32) + keep[0].astype(F32) + got[0].astype(F32) + across[...].astype(F32)
    h_out[...] = h
    scale = lax.rsqrt(jnp.mean(h * h, axis=-1, keepdims=True) + EPSILON)
    n_out[...] = (h * scale * gain[0:1]).astype(BF)


def norm_backward(grad, rows, gain):
    scale = lax.rsqrt(jnp.mean(rows * rows, axis=-1, keepdims=True) + EPSILON)
    scaled = grad * gain
    back = scale * scaled - rows * scale**3 * jnp.mean(scaled * rows, axis=-1, keepdims=True)
    return back, jnp.sum(grad * rows * scale, axis=0, keepdims=True)


def ff_back_body(own_a, own_b, got_a, got_b, got_c, h, cot, gain, grad_out, branch_out, gain_out):
    grad = sum(part[...].astype(F32) for part in (own_a, own_b, got_a, got_b, got_c))
    back, gain_out[...] = norm_backward(grad, h[...], gain[0:1])
    total = cot[...].astype(F32) + back
    grad_out[...] = total
    branch_out[...] = total.astype(BF)


def attn_back_body(keep, got, across, x, above, gain, grad_out, gain_out):
    grad = keep[0].astype(F32) + got[0].astype(F32) + across[...].astype(F32)
    back, gain_out[...] = norm_backward(grad, x[...].astype(F32), gain[0:1])
    grad_out[...] = above[...] + back


def attn_backward_body(
    b0, b1, b2, b3, wo, w, q, kv, lse, table, places,
    grads_out, keep, give, sums_out, bbuf,
):
    rows = b0.shape[0]
    for i, part in enumerate((b0, b1, b2, b3)):
        bbuf[i * rows : (i + 1) * rows] = part[...]
    attended_grad = dot(bbuf[...], wo[...]).astype(BF)
    keys, values = kv[:, :HD], kv[:, HD:]
    cosines, sines, allowed = unpack_table(table, places)
    sines = -sines
    key_grad = value_grad = 0.0
    for h in range(3):
        at = slice(h * HD, (h + 1) * HD)
        queries, o_grad = q[:, at], attended_grad[:, at]
        probs = jnp.exp(masked_scores(queries, keys, allowed) - lse[:, h : h + 1])
        prob_grad = dot_t(o_grad, values)
        inner = jnp.sum(probs * prob_grad, axis=-1, keepdims=True)
        score_grad = (probs * (prob_grad - inner)).astype(BF)
        query_grad = dot(score_grad, keys) * HD ** (-0.5)
        grads_out[:, at] = turn(query_grad, cosines, sines).astype(BF)
        key_grad = key_grad + t_dot(score_grad, queries)
        value_grad = value_grad + t_dot(probs.astype(BF), o_grad)
    grads_out[:, 384:512] = turn(key_grad * HD ** (-0.5), cosines, sines).astype(BF)
    grads_out[:, 512:] = value_grad.astype(BF)
    grads = grads_out[...]
    sums_out[...] = jnp.sum(grads.astype(F32), axis=0, keepdims=True)
    parted(dot_t(grads, w[:, :640]), keep, give)


def rows_product_body(*refs):
    *rows, right, out, buffer = refs
    size = rows[0].shape[0]
    for i, part in enumerate(rows):
        buffer[i * size : (i + 1) * size] = part[...]
    half = buffer.shape[1] // 2
    for i in range(2):
        grad = t_dot(buffer[:, i * half : (i + 1) * half], right[...]).astype(BF)
        out[16 * i : 16 * (i + 1)] = grad.reshape(16, half // 16, right.shape[1])


def rows_product(rows, right, name, order):
    width, columns = rows[0].shape[1], right.shape[1]
    total = sum(part.shape[0] for part in rows)
    return vmem_call(
        rows_product_body,
        [((32, width // 32, columns), BF)],
        [*rows, right],
        name,
        order,
        [pltpu.VMEM((total, width), BF)],
        flops=2 * total * width * columns,
        moved=2 * (total * width + total * columns + width * columns),
    )[0]


def shards(
    layer_input,
    q_weight,
    kv_weight,
    o_weight,
    norm_gains,
    qkv_bias,
    gate_up,
    down_weight,
    cotangent,
    lengths,
):
    zh, zl, core = (lax.axis_index(a) for a in ("zh", "zl", "core"))
    rank = 2 * zl + core
    width = layer_input.shape[1]
    rows = layer_input.shape[0]

    small = jnp.concatenate([norm_gains.reshape(-1), qkv_bias, jnp.zeros((216,), BF)])
    vectors = jnp.concatenate([kv_weight.reshape(24, 256), small[None], jnp.zeros((7, 256), BF)])
    got = swap(vectors, "core")
    both = jnp.stack([pick(core, vectors, got), pick(core, got, vectors)])
    small_keep = both[:, 24].reshape(2, 2, HD)
    kv_keep = pick(zl, both[:, :24, :HD], both[:, :24, HD:])
    kv_give = pick(zl, both[:, :24, HD:], both[:, :24, :HD])
    got = swap(jnp.concatenate([kv_give, small_keep, jnp.zeros((2, 6, HD), BF)], axis=1), "zl")
    kv_got, small_got = got[:, :24], got[:, 24:26]
    kv_rows = jnp.stack([pick(zl, kv_keep, kv_got), pick(zl, kv_got, kv_keep)])
    kv_rows = kv_rows.reshape(2, 2, 2, 12, HD).transpose(0, 1, 3, 2, 4).reshape(48, 2 * HD)
    small = jnp.stack([pick(zl, small_keep, small_got), pick(zl, small_got, small_keep)])
    small = small.reshape(4, 256)
    gains_row = jnp.concatenate([small[:, :12].reshape(48), small[:, 12:24].reshape(48)])
    bias_row = small[:, 24:40].reshape(64)
    small = jnp.zeros((48, HD), BF).at[0, :96].set(gains_row).at[1, :64].set(bias_row)

    ends = jnp.cumsum(lengths[0])
    ranks = jnp.stack([rank, 2 * zl + 1 - core, 2 * (1 - zl) + core, 2 * (1 - zl) + 1 - core])
    group = 4 * rows
    places = (ranks[:, None] * rows + jnp.arange(rows, dtype=jnp.int32)[None, :]).reshape(group)
    passed = ends[None, :] <= places[:, None]
    starts = jnp.sum(jnp.where(passed, lengths[0][None, :], 0), axis=1)
    inverse = THETA ** (-(2.0 * jnp.arange(HD // 2, dtype=F32)) / HD)
    inverse = jnp.concatenate([inverse, inverse])[None, :]
    angles = (places - starts).astype(F32)[:, None] * inverse
    sign = jnp.where(jnp.arange(HD) < HD // 2, -1.0, 1.0).astype(F32)[None, :]
    lane = jnp.arange(HD)[None, :]
    ranges = jnp.where(lane == 0, starts[:, None], places[:, None]).astype(F32)
    table = jnp.concatenate([jnp.cos(angles), jnp.sin(angles) * sign, ranges], axis=1)
    tables = (table, jnp.broadcast_to(places.astype(F32)[None, :], (8, group)))

    living = (places[:rows] < ends[-1])[:, None]
    cot_local = jnp.where(living, cotangent, jnp.zeros((), BF))
    cot_groups = token_groups(cot_local)

    across = swap(layer_input, "zl")
    group_inputs = (layer_input, swap(layer_input, "core"), across, swap(across, "core"))

    attn_part = jnp.concatenate([q_weight, kv_rows, small], axis=-1)
    qkv_full = exchange(copies(attn_part, 32), DATA)
    waits = (cot_groups[1][1], cot_groups[2][1], group_inputs[3], *tables)
    o_full = exchange(copies(o_weight.T, 32, qkv_full, *waits), DATA).reshape(width, 384)
    small = qkv_full[:, :2, 640:]
    qkv_full = qkv_full.reshape(width, 768)
    gain_attn, gain_mlp, bias = vmem_call(
        vectors_body,
        [((8, width), F32), ((8, width), F32), ((8, 640), F32)],
        [small[:, 0], small[:, 1], jnp.full((8, HD), rank, jnp.int32)],
        "gains_and_biases",
        flops=1,
    )

    mlp = jnp.concatenate([gate_up, down_weight.T[None]], axis=0)
    mlp = jnp.pad(mlp, ((0, 0), (0, 0), (0, 2 * HALF - mlp.shape[2])))
    mlp_own = pick(zh, mlp[..., :HALF], mlp[..., HALF:])
    mlp_other = swap(pick(zh, mlp[..., HALF:], mlp[..., :HALF]), "zh")
    mlp = vmem_call(
        arrange_body,
        [((6, 48, HALF), BF)],
        [mlp_own, mlp_other, jnp.full((8, HD), zh, jnp.int32)],
        "arranged",
        (attn_part,),
        moved=4 * mlp_own.size,
    )[0]
    mlp = lax.all_gather(mlp, PLANE, axis=1, tiled=True)
    mlp = mlp.reshape(3, width, HALF)

    normed_group, queries, kv_rot, attended, lse = vmem_call(
        attn_forward_body,
        [
            ((group, width), BF),
            ((group, 384), BF),
            ((group, 256), BF),
            ((group, 384), BF),
            ((group, 128), F32),
        ],
        [*group_inputs, gain_attn, qkv_full, bias, *tables],
        "attention_forward",
        flops=2 * group * (width * 640 + 6 * group * HD),
        moved=2 * group * width * 2 + 2 * width * 768,
    )
    pair = ((2, rows, width), BF)
    keep, give = vmem_call(
        attn_out_body,
        [pair, pair],
        [attended, o_full],
        "attention_out",
        flops=2 * group * width * 384,
        moved=2 * width * 384 + 2 * group * width,
    )
    got = swap(give, "core")
    residual, normed_mlp = vmem_call(
        residual_body,
        [((rows, width), F32), ((rows, width), BF)],
        [layer_input, keep, got, swap(add(keep[1], got[1]), "zl"), gain_mlp],
        "residual_norm",
        moved=10 * rows * width,
    )

    after_rows, before_rows = z_shift(normed_mlp, -1), z_shift(normed_mlp, 1)
    far_rows = z_shift(normed_mlp, 2)
    own = (normed_mlp, swap(normed_mlp, "core"))
    own_out = ff_rows(own, cot_groups[0], mlp, cot_local)
    near = stacked((after_rows, before_rows), own_out[0])
    near = (near, swap(near, "core"))
    near_out = ff_rows(near, cot_groups[1], mlp, own_out[0])
    far_rows = stacked((far_rows,), near_out[0])
    far = (far_rows, swap(far_rows, "core"))
    near_sum = [
        add(mine, swap(others, "core"))
        for mine, others in zip(halves(near_out[3], 0), halves(near_out[4], 0))
    ]
    near_got = (z_shift(near_sum[0], 1), z_shift(near_sum[1], -1))
    far_out = ff_rows(far, cot_groups[2], mlp, near_sum[1])
    far_sum = add(far_out[3], swap(far_out[4], "core"))
    own_got = swap(own_out[4], "core")
    far_got = z_shift(far_sum, 2)
    results = (own_out, near_out, far_out)
    hidden, gate_grads, up_grads = ([r[i] for r in results] for i in range(3))
    flat_normed = [*own, *near, *far]
    flat_cots = [part for pair in cot_groups for part in pair]
    mlp_grads = weight_grads(flat_normed, flat_cots, hidden, gate_grads, up_grads, far_sum)
    residual_grad, branch, gain_mlp_grad = vmem_call(
        ff_back_body,
        [((rows, width), F32), ((rows, width), BF), ((1, width), F32)],
        [own_out[3], own_got, *near_got, far_got, residual, cot_local, gain_mlp],
        "residual_gradient",
        (mlp_grads,),
        moved=24 * rows * width,
    )
    mlp_grads = lax.psum_scatter(
        mlp_grads.reshape(6, width // 2, HALF), PLANE, scatter_dimension=1, tiled=True
    ).reshape(3, 2, 48, HALF)
    own_grads = lax.dynamic_index_in_dim(mlp_grads, zh, 1, keepdims=False)
    other_grads = swap(lax.dynamic_index_in_dim(mlp_grads, 1 - zh, 1, keepdims=False), "zh")
    own_grads, other_grads = own_grads.astype(F32), other_grads.astype(F32)
    mlp_shard = jnp.concatenate(
        [pick(zh, own_grads, other_grads), pick(zh, other_grads, own_grads)], axis=-1
    )[..., : gate_up.shape[2]]
    gate_up_shard = mlp_shard[:2]
    down_shard = mlp_shard[2].T

    layer_output = (residual + token_sums(down_rows(hidden, mlp[2], branch))).astype(BF)

    across = swap(branch, "zl")
    branch_group = (branch, swap(branch, "core"), across, swap(across, "core"))
    o_terms = rows_product(branch_group, attended, "o_weight_gradient", ())
    o_got = exchange(o_terms, DATA)
    qkv_grad, keep, give, sums = vmem_call(
        attn_backward_body,
        [((group, 640), BF), pair, pair, ((1, 640), F32)],
        [*branch_group, o_full, qkv_full, queries, kv_rot, lse, *tables],
        "attention_backward",
        (o_terms,),
        scratch=[pltpu.VMEM((group, width), BF)],
        flops=2 * group * (width * 1024 + 15 * group * HD) * WEIGHT,
        moved=4 * group * width + 2 * width * 1024,
    )
    got = swap(give, "core")
    other = add(keep[1], got[1])
    qkv_terms = rows_product((normed_group,), qkv_grad, "qkv_weight_gradient", (other, o_got))
    input_grad, gain_attn_grad = vmem_call(
        attn_back_body,
        [((rows, width), F32), ((1, width), F32)],
        [keep, got, swap(other, "zl"), layer_input, residual_grad, gain_attn],
        "input_gradient",
        moved=20 * rows * width,
    )

    o_shard = jnp.sum(o_got.astype(F32), axis=0).T
    attn_shard = jnp.sum(exchange(qkv_terms, DATA).astype(F32), axis=0)
    q_shard = attn_shard[:, :384]
    kv_sum = attn_shard[:, 384:640].reshape(2, 2, 12, 2, HD)
    kv_keep = lax.dynamic_index_in_dim(kv_sum, core, 1, keepdims=False)
    kv_give = lax.dynamic_index_in_dim(kv_sum, 1 - core, 1, keepdims=False)
    kv_sum = kv_keep + swap(kv_give, "core")
    kv_keep = pick(zl, kv_sum[0], kv_sum[1])
    kv_got = swap(pick(zl, kv_sum[1], kv_sum[0]), "zl")
    kv_shard = jnp.concatenate([pick(zl, kv_keep, kv_got), pick(zl, kv_got, kv_keep)], axis=-1)
    kv_shard = kv_shard.transpose(1, 0, 2)

    sums = sums[0]
    ranked = jnp.arange(4, dtype=jnp.int32)[:, None]
    headed = ranked[:2]
    bias_grad = jnp.concatenate(
        [
            jnp.where(ranked == rank, sums[None, :384], 0.0).reshape(1536),
            jnp.where(headed == zl, sums[None, 384:512], 0.0).reshape(256),
        ]
    )
    value_bias_grad = jnp.where(headed == zl, sums[None, 512:], 0.0).reshape(256)
    vectors = jnp.concatenate(
        [
            gain_attn_grad.reshape(128, 12),
            gain_mlp_grad.reshape(128, 12),
            bias_grad.reshape(128, 14),
            value_bias_grad.reshape(128, 2),
            jnp.zeros((128, 88), F32),
        ],
        axis=1,
    )
    vectors = exchange(vectors, AXES)
    vectors = jnp.sum(vectors, axis=0)
    return (
        layer_output,
        input_grad,
        q_shard,
        kv_shard,
        o_shard,
        vectors[:24].reshape(2, 12),
        vectors[24:38],
        vectors[38:40],
        gate_up_shard,
        down_shard,
    )


def solution(mesh):
    fine = Mesh(mesh.devices.reshape(SIZES), AXES)
    dp = ("zh", "y", "x")
    tensor = ("zl", "core")
    every = dp + tensor
    in_specs = (
        P(every, None),
        P(dp, tensor),
        P(None, every, None),
        P(tensor, dp),
        P(None, every),
        P(every),
        P(None, dp, tensor),
        P(tensor, dp),
        P(every, None),
        P(dp, None),
    )
    out_specs = (
        P(every, None),
        P(every, None),
        P(dp, tensor),
        P(None, every, None),
        P(tensor, dp),
        P(None, every),
        P(every),
        P(every),
        P(None, dp, tensor),
        P(tensor, dp),
    )
    return jax.shard_map(shards, mesh=fine, in_specs=in_specs, out_specs=out_specs, check_vma=False)
```

```python
import functools

import jax
import jax.numpy as jnp
from jax import lax
from jax.experimental import pallas as pl
from jax.experimental.pallas import tpu as pltpu
from jax.sharding import Mesh, PartitionSpec as P

HQ = 12
KVH = 2
HD = 128
EPSILON = 1e-06
THETA = 1000000.0

AXES = ("zh", "y", "x", "zl", "core")
SIZES = (2, 4, 4, 2, 2)
ZRING = ("zh", "zl")
PLANE = ("y", "x")
DATA = ("zh", "y", "x")
HALF = 1152
BF = jnp.bfloat16
WEIGHT = 1000
F32 = jnp.float32


def swap(block, axis):
    return lax.ppermute(block, axis, [(0, 1), (1, 0)])


def halves(block, dim):
    middle = block.shape[dim] // 2
    return (
        lax.slice_in_dim(block, 0, middle, axis=dim),
        lax.slice_in_dim(block, middle, block.shape[dim], axis=dim),
    )


def add(*terms):
    total = terms[0].astype(F32)
    for term in terms[1:]:
        total = total + term.astype(F32)
    return total.astype(terms[0].dtype)


def exchange(blocks, axes):
    return lax.all_to_all(blocks, axes, split_axis=0, concat_axis=0, tiled=True)


def spread(block, axes, count):
    return exchange(jnp.broadcast_to(block[None], (count,) + block.shape), axes)


def z_shift(block, by):
    return lax.ppermute(block, ZRING, [(i, (i + by) % 4) for i in range(4)])


def token_groups(block):
    near = jnp.concatenate([z_shift(block, -1), z_shift(block, 1)], axis=0)
    far = z_shift(block, 2)
    return [(part, swap(part, "core")) for part in (block, near, far)]


def token_sums(pairs):
    own, near, far = (add(mine, swap(others, "core")) for mine, others in pairs)
    after_rows, before_rows = halves(near, 0)
    terms = (own, z_shift(after_rows, 1), z_shift(before_rows, -1), z_shift(far, 2))
    return sum(term.astype(F32) for term in terms)


def ff_body(
    na, nb, ca, cb, w, _, m_out, dg_out, du_out, dna_out, dnb_out,
    wbuf, nbuf, cbuf, wsem, nsem, csem, *, tile,
):
    half = na.shape[0]
    weights = [pltpu.make_async_copy(w.at[i], wbuf.at[i], wsem.at[i]) for i in range(3)]
    normed = [
        pltpu.make_async_copy(part, nbuf.at[pl.ds(k * half, half)], nsem.at[k])
        for k, part in enumerate((na, nb))
    ]
    cots = [
        pltpu.make_async_copy(part, cbuf.at[pl.ds(k * half, half)], csem.at[k])
        for k, part in enumerate((ca, cb))
    ]
    for copy in normed + weights[:2] + cots + weights[2:]:
        copy.start()
    for copy in normed + weights[:1]:
        copy.wait()
    tiles = 2 * half // tile
    for i in range(tiles):
        at = pl.ds(i * tile, tile)
        rows = nbuf[at]
        gate = dot(rows, wbuf[0])
        if i == 0:
            weights[1].wait()
        up = dot(rows, wbuf[1])
        if i == 0:
            for copy in cots + weights[2:]:
                copy.wait()
        hidden_grad = dot(cbuf[at], wbuf[2])
        sigma = 1.0 / (1.0 + jnp.exp(-gate))
        act = gate * sigma
        m_out[at] = (act * up).astype(BF)
        up_grad = (hidden_grad * act).astype(BF)
        gate_grad = (hidden_grad * up * sigma * (1.0 + gate * (1.0 - sigma))).astype(BF)
        dg_out[at] = gate_grad
        du_out[at] = up_grad
        back = (dot_t(gate_grad, wbuf[0]) + dot_t(up_grad, wbuf[1])).astype(BF)
        if tiles == 1:
            dna_out[...] = back[:half]
            dnb_out[...] = back[half:]
        else:
            out = dna_out if i < tiles // 2 else dnb_out
            out[pl.ds(i % (tiles // 2) * tile, tile)] = back


def ff_rows(normed, cots, weights, order, tile=256):
    half, width = normed[0].shape
    units = weights.shape[2]
    anywhere = pl.BlockSpec(memory_space=pl.ANY)
    vmem = pl.BlockSpec(memory_space=pltpu.VMEM)
    return pl.pallas_call(
        functools.partial(ff_body, tile=tile),
        out_shape=[jax.ShapeDtypeStruct((2 * half, units), BF)] * 3
        + [jax.ShapeDtypeStruct((half, width), BF)] * 2,
        in_specs=[anywhere] * 6,
        out_specs=[vmem] * 5,
        scratch_shapes=[
            pltpu.VMEM((3, width, units), BF),
            pltpu.VMEM((2 * half, width), BF),
            pltpu.VMEM((2 * half, width), BF),
            pltpu.SemaphoreType.DMA((3,)),
            pltpu.SemaphoreType.DMA((2,)),
            pltpu.SemaphoreType.DMA((2,)),
        ],
        compiler_params=pltpu.CompilerParams(vmem_limit_bytes=60 * 1024 * 1024),
        cost_estimate=pl.CostEstimate(
            flops=20 * half * width * units,
            bytes_accessed=6 * width * units,
            transcendentals=2 * half * units,
        ),
        name="feed_forward_rows",
    )(*normed, *cots, weights, order)


def wg_body(*refs, sizes, tile):
    count = len(sizes)
    groups = count // 2
    normed, cots, refs = refs[:count], refs[count : 2 * count], refs[2 * count :]
    hidden, gates, ups = refs[:groups], refs[groups : 2 * groups], refs[2 * groups : 3 * groups]
    out, nbuf, cbuf, mbuf, gbuf, ubuf, sem = refs[3 * groups + 1 :]
    pair_sizes = [sizes[2 * i] + sizes[2 * i + 1] for i in range(groups)]

    def copies(at, buffer, sources, lengths):
        result, start = [], 0
        for source, length in zip(sources, lengths):
            target = buffer.at[pl.ds(start, length)]
            result.append(pltpu.make_async_copy(source, target, sem.at[at]))
            start += length
        return result

    def normed_copies():
        return copies(0, nbuf, normed, sizes)

    def cot_copies():
        return copies(1, cbuf, cots, sizes)

    def gate_copies():
        return copies(2, gbuf, gates, pair_sizes)

    def up_copies():
        return copies(3, ubuf, ups, pair_sizes)

    def hidden_copies():
        return copies(4, mbuf, hidden, pair_sizes)

    which, step = pl.program_id(0), pl.program_id(1)

    @pl.when((which == 0) & (step == 0))
    def _():
        first = normed_copies() + gate_copies()
        for copy in first + up_copies() + cot_copies() + hidden_copies():
            copy.start()
        for copy in first:
            copy.wait()

    @pl.when((which == 1) & (step == 0))
    def _():
        for copy in up_copies():
            copy.wait()

    @pl.when((which == 2) & (step == 0))
    def _():
        for copy in cot_copies() + hidden_copies():
            copy.wait()

    columns = pl.ds(pl.multiple_of(step * tile, tile), tile)
    for i, (left, right) in enumerate(((nbuf, gbuf), (nbuf, ubuf), (cbuf, mbuf))):

        @pl.when(which == i)
        def _():
            out[...] = t_dot(left[:, columns], right[...]).astype(BF)


def weight_grads(normed, cots, hidden, gates, ups, order, tile=768):
    sizes = tuple(part.shape[0] for part in normed)
    rows, width, units = sum(sizes), normed[0].shape[1], hidden[0].shape[1]
    anywhere = pl.BlockSpec(memory_space=pl.ANY)
    return pl.pallas_call(
        functools.partial(wg_body, sizes=sizes, tile=tile),
        grid=(3, width // tile),
        out_shape=jax.ShapeDtypeStruct((3, width, units), BF),
        in_specs=[anywhere] * (2 * len(normed) + 3 * len(hidden) + 1),
        out_specs=pl.BlockSpec((None, tile, units), lambda i, j: (i, j, 0)),
        scratch_shapes=[pltpu.VMEM((rows, width), BF)] * 2
        + [pltpu.VMEM((rows, units), BF)] * 3
        + [pltpu.SemaphoreType.DMA((5,))],
        compiler_params=pltpu.CompilerParams(vmem_limit_bytes=60 * 1024 * 1024),
        cost_estimate=pl.CostEstimate(
            flops=6 * rows * width * units,
            bytes_accessed=6 * width * units + rows * (4 * width + 6 * units),
            transcendentals=0,
        ),
        name="weight_gradients",
    )(*normed, *cots, *hidden, *gates, *ups, order)


def down_body(ha, hb, hc, w, *outs, tile=256):
    for group, hidden in enumerate((ha, hb, hc)):
        half = hidden.shape[0] // 2
        step = min(tile, 2 * half)
        for start in range(0, 2 * half, step):
            part = dot_t(hidden[pl.ds(start, step)], w[...]).astype(BF)
            if step > half:
                outs[2 * group][...] = part[:half]
                outs[2 * group + 1][...] = part[half:]
            else:
                outs[2 * group + start // half][pl.ds(start % half, step)] = part


def down_rows(hidden, weights, order):
    _, width, units = weights.shape
    halved = [part.shape[0] // 2 for part in hidden for _ in range(2)]
    outs = vmem_call(
        down_body,
        [((rows, width), BF) for rows in halved],
        [*hidden, (weights, 2)],
        "down_rows",
        (order,),
        flops=2 * sum(halved) * width * units,
        moved=2 * width * units + 2 * sum(halved) * (width + units),
    )
    return [(outs[0], outs[1]), (outs[2], outs[3]), (outs[4], outs[5])]


def dot(a, b):
    return jnp.dot(a, b, preferred_element_type=F32)


def dot_t(a, b):
    return lax.dot_general(a, b, (((1,), (1,)), ((), ())), preferred_element_type=F32)


def t_dot(a, b):
    return lax.dot_general(a, b, (((0,), (0,)), ((), ())), preferred_element_type=F32)


def pick(index, low, high):
    return jnp.where(index == 0, low, high)


def vmem_call(body, outs, ins, name, order=(), scratch=(), limit=60, flops=0, moved=0):
    count, skipped, results, extra = len(ins), len(order), len(outs), len(scratch)
    parts = [value[1] if isinstance(value, tuple) else None for value in ins]
    ins = [value[0] if isinstance(value, tuple) else value for value in ins]

    def kernel(*refs):
        sources, refs = refs[:count], refs[count + skipped :]
        fixed, buffers, sem = refs[: results + extra], refs[results + extra : -1], refs[-1]
        fetches = [
            pltpu.make_async_copy(source if at is None else source.at[at], buffer, sem.at[i])
            for i, (source, at, buffer) in enumerate(zip(sources, parts, buffers))
        ]
        for fetch in fetches:
            fetch.start()
        for fetch in fetches:
            fetch.wait()
        body(*buffers, *fixed)

    return pl.pallas_call(
        kernel,
        out_shape=[jax.ShapeDtypeStruct(shape, dtype) for shape, dtype in outs],
        in_specs=[pl.BlockSpec(memory_space=pl.ANY)] * (count + skipped),
        out_specs=[pl.BlockSpec(memory_space=pltpu.VMEM)] * results,
        scratch_shapes=[
            *scratch,
            *(
                pltpu.VMEM(value.shape if at is None else value.shape[1:], value.dtype)
                for value, at in zip(ins, parts)
            ),
            pltpu.SemaphoreType.DMA((count,)),
        ],
        compiler_params=pltpu.CompilerParams(vmem_limit_bytes=limit * 1024 * 1024),
        cost_estimate=pl.CostEstimate(flops=flops, bytes_accessed=moved, transcendentals=0),
        name=name,
    )(*ins, *order)


def copies_body(block, out):
    for i in range(out.shape[0]):
        out[i] = block[...]


def copies(block, count, *order):
    shape = (count,) + block.shape
    moved = 2 * count * block.size
    return vmem_call(
        copies_body, [(shape, block.dtype)], [block], "copies", order, moved=moved
    )[0]


def arrange_body(own, other, zh, out):
    mine = zh[0:1, 0:1] == 0
    for i in range(3):
        out[2 * i] = jnp.where(mine, own[i], other[i])
        out[2 * i + 1] = jnp.where(mine, other[i], own[i])


def ordered_body(own, other, zh, out):
    mine = zh[0:1, 0:1] == 0
    for i in range(own.shape[0]):
        out[0, i] = jnp.where(mine, own[i], other[i])
        out[1, i] = jnp.where(mine, other[i], own[i])


def ordered(own, other, zh, name, order):
    flag = jnp.full((8, HD), zh, jnp.int32)
    shape = (2,) + own.shape
    return vmem_call(
        ordered_body, [(shape, BF)], [own, other, flag], name, order, moved=8 * own.size
    )[0]


def stack_body(*refs):
    *parts, out = refs
    rows = parts[0].shape[0]
    for i, part in enumerate(parts):
        out[i * rows : (i + 1) * rows] = part[...]


def stacked(parts, *order):
    rows, columns = parts[0].shape
    shape = (len(parts) * rows, columns)
    moved = 4 * shape[0] * columns
    return vmem_call(stack_body, [(shape, BF)], list(parts), "stacked", order, moved=moved)[0]


def row_of(blocks, offset, size):
    count, lanes = blocks.shape
    line = (lanes, count * size)
    at = lax.broadcasted_iota(jnp.int32, line, 1)
    from_lane = lax.broadcasted_iota(jnp.int32, line, 0) - offset
    spots = (lax.rem(at, size) == from_lane).astype(BF)
    values = dot(blocks, spots)
    at = lax.broadcasted_iota(jnp.int32, values.shape, 1)
    owner = lax.broadcasted_iota(jnp.int32, values.shape, 0)
    mine = (at >= owner * size) & (at < (owner + 1) * size)
    return jnp.sum(jnp.where(mine, values, 0.0), axis=0, keepdims=True)


def vectors_body(gains, biases, ranks, attn_out, mlp_out, bias_out):
    attn_out[...] = jnp.broadcast_to(row_of(gains[...], 0, 48), attn_out.shape)
    mlp_out[...] = jnp.broadcast_to(row_of(gains[...], 48, 48), mlp_out.shape)
    full = row_of(biases[...], 0, 64)
    rank = ranks[0:1, 0:1]
    query = key = value = 0.0
    for i in range(4):
        query = query + jnp.where(rank == i, full[:, 384 * i : 384 * (i + 1)], 0.0)
    for i in range(2):
        mine = (rank >= 2 * i) & (rank < 2 * i + 2)
        key = key + jnp.where(mine, full[:, 1536 + HD * i : 1536 + HD * (i + 1)], 0.0)
        value = value + jnp.where(mine, full[:, 1792 + HD * i : 1792 + HD * (i + 1)], 0.0)
    line = jnp.concatenate([query, key, value], axis=1)
    bias_out[...] = jnp.broadcast_to(line, bias_out.shape)


def turn(vectors, cos2, sin2):
    return vectors * cos2 + pltpu.roll(vectors, HD // 2, 1) * sin2


def unpack_table(table, places):
    first, last = table[:, 2 * HD : 2 * HD + 1], table[:, 2 * HD + 1 : 2 * HD + 2]
    keys = places[0:1, :]
    return table[:, :HD], table[:, HD : 2 * HD], (keys >= first) & (keys <= last)


def masked_scores(queries, keys, allowed):
    return jnp.where(allowed, dot_t(queries, keys) * HD ** (-0.5), -1e30)


def attn_forward_body(
    x0, x1, x2, x3, gain, w, bias, table, places,
    n_out, q_out, kv_out, o_out, lse_out,
):
    rows = x0.shape[0]
    for i, x in enumerate((x0, x1, x2, x3)):
        part = x[...].astype(F32)
        scale = lax.rsqrt(jnp.mean(part * part, axis=-1, keepdims=True) + EPSILON)
        n_out[i * rows : (i + 1) * rows] = (part * scale * gain[0:1]).astype(BF)
    qkv = dot(n_out[...], w[:, :640]) + bias[0:1]
    cosines, sines, allowed = unpack_table(table, places)
    keys = turn(qkv[:, 384:512], cosines, sines).astype(BF)
    values = qkv[:, 512:].astype(BF)
    kv_out[:, :HD] = keys
    kv_out[:, HD:] = values
    lses = []
    for h in range(3):
        at = slice(h * HD, (h + 1) * HD)
        queries = turn(qkv[:, at], cosines, sines).astype(BF)
        q_out[:, at] = queries
        scores = masked_scores(queries, keys, allowed)
        peak = jnp.max(scores, axis=-1, keepdims=True)
        shifted = jnp.exp(scores - peak)
        total = jnp.sum(shifted, axis=-1, keepdims=True)
        probs = (shifted / total).astype(BF)
        o_out[:, at] = dot(probs, values).astype(BF)
        lses.append(peak + jnp.log(total))
    lse_out[...] = jnp.concatenate(lses + [jnp.zeros((4 * rows, 125), F32)], axis=1)


def parted(partial, keep, give):
    rows = partial.shape[0] // 4
    keep[0] = partial[:rows].astype(BF)
    give[0] = partial[rows : 2 * rows].astype(BF)
    keep[1] = partial[2 * rows : 3 * rows].astype(BF)
    give[1] = partial[3 * rows :].astype(BF)


def attn_out_body(o, w, keep, give):
    parted(dot_t(o[...], w[...]), keep, give)


def residual_body(x, keep, got, across, gain, h_out, n_out):
    h = x[...].astype(F32) + keep[0].astype(F32) + got[0].astype(F32) + across[...].astype(F32)
    h_out[...] = h
    scale = lax.rsqrt(jnp.mean(h * h, axis=-1, keepdims=True) + EPSILON)
    n_out[...] = (h * scale * gain[0:1]).astype(BF)


def norm_backward(grad, rows, gain):
    scale = lax.rsqrt(jnp.mean(rows * rows, axis=-1, keepdims=True) + EPSILON)
    scaled = grad * gain
    back = scale * scaled - rows * scale**3 * jnp.mean(scaled * rows, axis=-1, keepdims=True)
    return back, jnp.sum(grad * rows * scale, axis=0, keepdims=True)


def ff_back_body(own_a, own_b, got_a, got_b, got_c, h, cot, gain, grad_out, branch_out, gain_out):
    grad = sum(part[...].astype(F32) for part in (own_a, own_b, got_a, got_b, got_c))
    back, gain_out[...] = norm_backward(grad, h[...], gain[0:1])
    total = cot[...].astype(F32) + back
    grad_out[...] = total
    branch_out[...] = total.astype(BF)


def attn_back_body(keep, got, across, x, above, gain, grad_out, gain_out):
    grad = keep[0].astype(F32) + got[0].astype(F32) + across[...].astype(F32)
    back, gain_out[...] = norm_backward(grad, x[...].astype(F32), gain[0:1])
    grad_out[...] = above[...] + back


def attn_backward_body(
    b0, b1, b2, b3, wo, w, q, kv, lse, table, places,
    grads_out, keep, give, sums_out, bbuf,
):
    rows = b0.shape[0]
    for i, part in enumerate((b0, b1, b2, b3)):
        bbuf[i * rows : (i + 1) * rows] = part[...]
    attended_grad = dot(bbuf[...], wo[...]).astype(BF)
    keys, values = kv[:, :HD], kv[:, HD:]
    cosines, sines, allowed = unpack_table(table, places)
    sines = -sines
    key_grad = value_grad = 0.0
    for h in range(3):
        at = slice(h * HD, (h + 1) * HD)
        queries, o_grad = q[:, at], attended_grad[:, at]
        probs = jnp.exp(masked_scores(queries, keys, allowed) - lse[:, h : h + 1])
        prob_grad = dot_t(o_grad, values)
        inner = jnp.sum(probs * prob_grad, axis=-1, keepdims=True)
        score_grad = (probs * (prob_grad - inner)).astype(BF)
        query_grad = dot(score_grad, keys) * HD ** (-0.5)
        grads_out[:, at] = turn(query_grad, cosines, sines).astype(BF)
        key_grad = key_grad + t_dot(score_grad, queries)
        value_grad = value_grad + t_dot(probs.astype(BF), o_grad)
    grads_out[:, 384:512] = turn(key_grad * HD ** (-0.5), cosines, sines).astype(BF)
    grads_out[:, 512:] = value_grad.astype(BF)
    grads = grads_out[...]
    sums_out[...] = jnp.sum(grads.astype(F32), axis=0, keepdims=True)
    parted(dot_t(grads, w[:, :640]), keep, give)


def rows_product_body(*refs):
    *rows, right, out, buffer = refs
    size = rows[0].shape[0]
    for i, part in enumerate(rows):
        buffer[i * size : (i + 1) * size] = part[...]
    half = buffer.shape[1] // 2
    for i in range(2):
        grad = t_dot(buffer[:, i * half : (i + 1) * half], right[...]).astype(BF)
        out[16 * i : 16 * (i + 1)] = grad.reshape(16, half // 16, right.shape[1])


def rows_product(rows, right, name, order):
    width, columns = rows[0].shape[1], right.shape[1]
    total = sum(part.shape[0] for part in rows)
    return vmem_call(
        rows_product_body,
        [((32, width // 32, columns), BF)],
        [*rows, right],
        name,
        order,
        [pltpu.VMEM((total, width), BF)],
        flops=2 * total * width * columns,
        moved=2 * (total * width + total * columns + width * columns),
    )[0]


def shards(
    layer_input,
    q_weight,
    kv_weight,
    o_weight,
    norm_gains,
    qkv_bias,
    gate_up,
    down_weight,
    cotangent,
    lengths,
):
    zh, zl, core = (lax.axis_index(a) for a in ("zh", "zl", "core"))
    rank = 2 * zl + core
    width = layer_input.shape[1]
    rows = layer_input.shape[0]

    small = jnp.concatenate([norm_gains.reshape(-1), qkv_bias, jnp.zeros((216,), BF)])
    vectors = jnp.concatenate([kv_weight.reshape(24, 256), small[None], jnp.zeros((7, 256), BF)])
    got = swap(vectors, "core")
    both = jnp.stack([pick(core, vectors, got), pick(core, got, vectors)])
    small_keep = both[:, 24].reshape(2, 2, HD)
    kv_keep = pick(zl, both[:, :24, :HD], both[:, :24, HD:])
    kv_give = pick(zl, both[:, :24, HD:], both[:, :24, :HD])
    got = swap(jnp.concatenate([kv_give, small_keep, jnp.zeros((2, 6, HD), BF)], axis=1), "zl")
    kv_got, small_got = got[:, :24], got[:, 24:26]
    kv_rows = jnp.stack([pick(zl, kv_keep, kv_got), pick(zl, kv_got, kv_keep)])
    kv_rows = kv_rows.reshape(2, 2, 2, 12, HD).transpose(0, 1, 3, 2, 4).reshape(48, 2 * HD)
    small = jnp.stack([pick(zl, small_keep, small_got), pick(zl, small_got, small_keep)])
    small = small.reshape(4, 256)
    gains_row = jnp.concatenate([small[:, :12].reshape(48), small[:, 12:24].reshape(48)])
    bias_row = small[:, 24:40].reshape(64)
    small = jnp.zeros((48, HD), BF).at[0, :96].set(gains_row).at[1, :64].set(bias_row)

    ends = jnp.cumsum(lengths[0])
    ranks = jnp.stack([rank, 2 * zl + 1 - core, 2 * (1 - zl) + core, 2 * (1 - zl) + 1 - core])
    group = 4 * rows
    places = (ranks[:, None] * rows + jnp.arange(rows, dtype=jnp.int32)[None, :]).reshape(group)
    passed = ends[None, :] <= places[:, None]
    starts = jnp.sum(jnp.where(passed, lengths[0][None, :], 0), axis=1)
    inverse = THETA ** (-(2.0 * jnp.arange(HD // 2, dtype=F32)) / HD)
    inverse = jnp.concatenate([inverse, inverse])[None, :]
    angles = (places - starts).astype(F32)[:, None] * inverse
    sign = jnp.where(jnp.arange(HD) < HD // 2, -1.0, 1.0).astype(F32)[None, :]
    lane = jnp.arange(HD)[None, :]
    ranges = jnp.where(lane == 0, starts[:, None], places[:, None]).astype(F32)
    table = jnp.concatenate([jnp.cos(angles), jnp.sin(angles) * sign, ranges], axis=1)
    tables = (table, jnp.broadcast_to(places.astype(F32)[None, :], (8, group)))

    living = (places[:rows] < ends[-1])[:, None]
    cot_local = jnp.where(living, cotangent, jnp.zeros((), BF))
    cot_groups = token_groups(cot_local)

    across = swap(layer_input, "zl")
    group_inputs = (layer_input, swap(layer_input, "core"), across, swap(across, "core"))

    attn_part = jnp.concatenate([q_weight, kv_rows, small, o_weight.T], axis=-1)
    attn_plane = exchange(copies(attn_part, 16, *tables), PLANE)
    qkv_plane, o_plane = attn_plane[..., :768], attn_plane[..., 768:]
    qkv_other = swap(qkv_plane, "zh")
    o_other = swap(o_plane, "zh")
    waits = (cot_groups[1][1], cot_groups[2][1], group_inputs[3])
    qkv_full = ordered(qkv_plane, qkv_other, zh, "qkv_weights", waits)
    o_full = ordered(o_plane, o_other, zh, "o_weights", ()).reshape(width, 384)
    small = qkv_full[:, :, :2, 640:].reshape(32, 2, HD)
    qkv_full = qkv_full.reshape(width, 768)
    gain_attn, gain_mlp, bias = vmem_call(
        vectors_body,
        [((8, width), F32), ((8, width), F32), ((8, 640), F32)],
        [small[:, 0], small[:, 1], jnp.full((8, HD), rank, jnp.int32)],
        "gains_and_biases",
        flops=1,
    )

    mlp = jnp.concatenate([gate_up, down_weight.T[None]], axis=0)
    mlp = jnp.pad(mlp, ((0, 0), (0, 0), (0, 2 * HALF - mlp.shape[2])))
    mlp_own = pick(zh, mlp[..., :HALF], mlp[..., HALF:])
    mlp_other = swap(pick(zh, mlp[..., HALF:], mlp[..., :HALF]), "zh")
    mlp = vmem_call(
        arrange_body,
        [((6, 48, HALF), BF)],
        [mlp_own, mlp_other, jnp.full((8, HD), zh, jnp.int32)],
        "arranged",
        (attn_part,),
        moved=4 * mlp_own.size,
    )[0]
    mlp = lax.all_gather(mlp, PLANE, axis=1, tiled=True)
    mlp = mlp.reshape(3, width, HALF)

    normed_group, queries, kv_rot, attended, lse = vmem_call(
        attn_forward_body,
        [
            ((group, width), BF),
            ((group, 384), BF),
            ((group, 256), BF),
            ((group, 384), BF),
            ((group, 128), F32),
        ],
        [*group_inputs, gain_attn, qkv_full, bias, *tables],
        "attention_forward",
        flops=2 * group * (width * 640 + 6 * group * HD),
        moved=2 * group * width * 2 + 2 * width * 768,
    )
    pair = ((2, rows, width), BF)
    keep, give = vmem_call(
        attn_out_body,
        [pair, pair],
        [attended, o_full],
        "attention_out",
        flops=2 * group * width * 384,
        moved=2 * width * 384 + 2 * group * width,
    )
    got = swap(give, "core")
    residual, normed_mlp = vmem_call(
        residual_body,
        [((rows, width), F32), ((rows, width), BF)],
        [layer_input, keep, got, swap(add(keep[1], got[1]), "zl"), gain_mlp],
        "residual_norm",
        moved=10 * rows * width,
    )

    after_rows, before_rows = z_shift(normed_mlp, -1), z_shift(normed_mlp, 1)
    far_rows = z_shift(normed_mlp, 2)
    own = (normed_mlp, swap(normed_mlp, "core"))
    own_out = ff_rows(own, cot_groups[0], mlp, cot_local)
    near = stacked((after_rows, before_rows), own_out[0])
    near = (near, swap(near, "core"))
    near_out = ff_rows(near, cot_groups[1], mlp, own_out[0])
    far_rows = stacked((far_rows,), near_out[0])
    far = (far_rows, swap(far_rows, "core"))
    near_sum = [
        add(mine, swap(others, "core"))
        for mine, others in zip(halves(near_out[3], 0), halves(near_out[4], 0))
    ]
    near_got = (z_shift(near_sum[0], 1), z_shift(near_sum[1], -1))
    far_out = ff_rows(far, cot_groups[2], mlp, near_sum[1])
    far_sum = add(far_out[3], swap(far_out[4], "core"))
    own_got = swap(own_out[4], "core")
    far_got = z_shift(far_sum, 2)
    results = (own_out, near_out, far_out)
    hidden, gate_grads, up_grads = ([r[i] for r in results] for i in range(3))
    flat_normed = [*own, *near, *far]
    flat_cots = [part for pair in cot_groups for part in pair]
    mlp_grads = weight_grads(flat_normed, flat_cots, hidden, gate_grads, up_grads, far_sum)
    residual_grad, branch, gain_mlp_grad = vmem_call(
        ff_back_body,
        [((rows, width), F32), ((rows, width), BF), ((1, width), F32)],
        [own_out[3], own_got, *near_got, far_got, residual, cot_local, gain_mlp],
        "residual_gradient",
        (mlp_grads,),
        moved=24 * rows * width,
    )
    mlp_grads = lax.psum_scatter(
        mlp_grads.reshape(6, width // 2, HALF), PLANE, scatter_dimension=1, tiled=True
    ).reshape(3, 2, 48, HALF)
    own_grads = lax.dynamic_index_in_dim(mlp_grads, zh, 1, keepdims=False)
    other_grads = swap(lax.dynamic_index_in_dim(mlp_grads, 1 - zh, 1, keepdims=False), "zh")
    own_grads, other_grads = own_grads.astype(F32), other_grads.astype(F32)
    mlp_shard = jnp.concatenate(
        [pick(zh, own_grads, other_grads), pick(zh, other_grads, own_grads)], axis=-1
    )[..., : gate_up.shape[2]]
    gate_up_shard = mlp_shard[:2]
    down_shard = mlp_shard[2].T

    out_pairs = down_rows(hidden, mlp, branch)
    layer_output = (residual + token_sums(out_pairs)).astype(BF)

    across = stacked((swap(branch, "zl"),), out_pairs[0][0])
    branch_group = (branch, swap(branch, "core"), across, swap(across, "core"))
    o_terms = rows_product(branch_group, attended, "o_weight_gradient", ())
    o_got = exchange(o_terms, DATA)
    qkv_grad, keep, give, sums = vmem_call(
        attn_backward_body,
        [((group, 640), BF), pair, pair, ((1, 640), F32)],
        [*branch_group, o_full, qkv_full, queries, kv_rot, lse, *tables],
        "attention_backward",
        (o_terms,),
        scratch=[pltpu.VMEM((group, width), BF)],
        flops=2 * group * (width * 1024 + 15 * group * HD) * WEIGHT,
        moved=4 * group * width + 2 * width * 1024,
    )
    got = swap(give, "core")
    other = add(keep[1], got[1])
    qkv_terms = rows_product((normed_group,), qkv_grad, "qkv_weight_gradient", (other, o_got))
    input_grad, gain_attn_grad = vmem_call(
        attn_back_body,
        [((rows, width), F32), ((1, width), F32)],
        [keep, got, swap(other, "zl"), layer_input, residual_grad, gain_attn],
        "input_gradient",
        moved=20 * rows * width,
    )

    o_shard = jnp.sum(o_got.astype(F32), axis=0).T
    attn_shard = jnp.sum(exchange(qkv_terms, DATA).astype(F32), axis=0)
    q_shard = attn_shard[:, :384]
    kv_sum = attn_shard[:, 384:640].reshape(2, 2, 12, 2, HD)
    kv_keep = lax.dynamic_index_in_dim(kv_sum, core, 1, keepdims=False)
    kv_give = lax.dynamic_index_in_dim(kv_sum, 1 - core, 1, keepdims=False)
    kv_sum = kv_keep + swap(kv_give, "core")
    kv_keep = pick(zl, kv_sum[0], kv_sum[1])
    kv_got = swap(pick(zl, kv_sum[1], kv_sum[0]), "zl")
    kv_shard = jnp.concatenate([pick(zl, kv_keep, kv_got), pick(zl, kv_got, kv_keep)], axis=-1)
    kv_shard = kv_shard.transpose(1, 0, 2)

    sums = sums[0]
    ranked = jnp.arange(4, dtype=jnp.int32)[:, None]
    headed = ranked[:2]
    bias_grad = jnp.concatenate(
        [
            jnp.where(ranked == rank, sums[None, :384], 0.0).reshape(1536),
            jnp.where(headed == zl, sums[None, 384:512], 0.0).reshape(256),
        ]
    )
    value_bias_grad = jnp.where(headed == zl, sums[None, 512:], 0.0).reshape(256)
    vectors = jnp.concatenate(
        [
            gain_attn_grad.reshape(128, 12),
            gain_mlp_grad.reshape(128, 12),
            bias_grad.reshape(128, 14),
            value_bias_grad.reshape(128, 2),
            jnp.zeros((128, 88), F32),
        ],
        axis=1,
    )
    vectors = exchange(vectors, AXES)
    vectors = jnp.sum(vectors, axis=0)
    return (
        layer_output,
        input_grad,
        q_shard,
        kv_shard,
        o_shard,
        vectors[:24].reshape(2, 12),
        vectors[24:38],
        vectors[38:40],
        gate_up_shard,
        down_shard,
    )


def solution(mesh):
    fine = Mesh(mesh.devices.reshape(SIZES), AXES)
    dp = ("zh", "y", "x")
    tensor = ("zl", "core")
    every = dp + tensor
    in_specs = (
        P(every, None),
        P(dp, tensor),
        P(None, every, None),
        P(tensor, dp),
        P(None, every),
        P(every),
        P(None, dp, tensor),
        P(tensor, dp),
        P(every, None),
        P(dp, None),
    )
    out_specs = (
        P(every, None),
        P(every, None),
        P(dp, tensor),
        P(None, every, None),
        P(tensor, dp),
        P(None, every),
        P(every),
        P(every),
        P(None, dp, tensor),
        P(tensor, dp),
    )
    return jax.shard_map(shards, mesh=fine, in_specs=in_specs, out_specs=out_specs, check_vma=False)
```

```python
import functools

import jax
import jax.numpy as jnp
from jax import lax
from jax.experimental import pallas as pl
from jax.experimental.pallas import tpu as pltpu
from jax.sharding import Mesh, PartitionSpec as P

HQ = 12
KVH = 2
HD = 128
EPSILON = 1e-06
THETA = 1000000.0

AXES = ("zh", "y", "x", "zl", "core")
SIZES = (2, 4, 4, 2, 2)
ZRING = ("zh", "zl")
PLANE = ("y", "x")
DATA = ("zh", "y", "x")
HALF = 1152
BF = jnp.bfloat16
WEIGHT = 1000
F32 = jnp.float32


def swap(block, axis):
    return lax.ppermute(block, axis, [(0, 1), (1, 0)])


def halves(block, dim):
    middle = block.shape[dim] // 2
    return (
        lax.slice_in_dim(block, 0, middle, axis=dim),
        lax.slice_in_dim(block, middle, block.shape[dim], axis=dim),
    )


def add(*terms):
    total = terms[0].astype(F32)
    for term in terms[1:]:
        total = total + term.astype(F32)
    return total.astype(terms[0].dtype)


def exchange(blocks, axes):
    return lax.all_to_all(blocks, axes, split_axis=0, concat_axis=0, tiled=True)


def spread(block, axes, count):
    return exchange(jnp.broadcast_to(block[None], (count,) + block.shape), axes)


def z_shift(block, by):
    return lax.ppermute(block, ZRING, [(i, (i + by) % 4) for i in range(4)])


def token_groups(block):
    near = jnp.concatenate([z_shift(block, -1), z_shift(block, 1)], axis=0)
    far = z_shift(block, 2)
    return [(part, swap(part, "core")) for part in (block, near, far)]


def token_sums(pairs):
    own, near, far = (add(mine, swap(others, "core")) for mine, others in pairs)
    after_rows, before_rows = halves(near, 0)
    terms = (own, z_shift(after_rows, 1), z_shift(before_rows, -1), z_shift(far, 2))
    return sum(term.astype(F32) for term in terms)


def ff_body(
    na, nb, ca, cb, w, _, m_out, dg_out, du_out, dna_out, dnb_out,
    wbuf, nbuf, cbuf, wsem, nsem, csem, *, tile,
):
    half = na.shape[0]
    weights = [pltpu.make_async_copy(w.at[i], wbuf.at[i], wsem.at[i]) for i in range(3)]
    normed = [
        pltpu.make_async_copy(part, nbuf.at[pl.ds(k * half, half)], nsem.at[k])
        for k, part in enumerate((na, nb))
    ]
    cots = [
        pltpu.make_async_copy(part, cbuf.at[pl.ds(k * half, half)], csem.at[k])
        for k, part in enumerate((ca, cb))
    ]
    for copy in normed + weights[:2] + cots + weights[2:]:
        copy.start()
    for copy in normed + weights[:1]:
        copy.wait()
    tiles = 2 * half // tile
    for i in range(tiles):
        at = pl.ds(i * tile, tile)
        rows = nbuf[at]
        gate = dot(rows, wbuf[0])
        if i == 0:
            weights[1].wait()
        up = dot(rows, wbuf[1])
        if i == 0:
            for copy in cots + weights[2:]:
                copy.wait()
        hidden_grad = dot(cbuf[at], wbuf[2])
        sigma = 1.0 / (1.0 + jnp.exp(-gate))
        act = gate * sigma
        m_out[at] = (act * up).astype(BF)
        up_grad = (hidden_grad * act).astype(BF)
        gate_grad = (hidden_grad * up * sigma * (1.0 + gate * (1.0 - sigma))).astype(BF)
        dg_out[at] = gate_grad
        du_out[at] = up_grad
        back = (dot_t(gate_grad, wbuf[0]) + dot_t(up_grad, wbuf[1])).astype(BF)
        if tiles == 1:
            dna_out[...] = back[:half]
            dnb_out[...] = back[half:]
        else:
            out = dna_out if i < tiles // 2 else dnb_out
            out[pl.ds(i % (tiles // 2) * tile, tile)] = back


def ff_rows(normed, cots, weights, order, tile=256):
    half, width = normed[0].shape
    units = weights.shape[2]
    anywhere = pl.BlockSpec(memory_space=pl.ANY)
    vmem = pl.BlockSpec(memory_space=pltpu.VMEM)
    return pl.pallas_call(
        functools.partial(ff_body, tile=tile),
        out_shape=[jax.ShapeDtypeStruct((2 * half, units), BF)] * 3
        + [jax.ShapeDtypeStruct((half, width), BF)] * 2,
        in_specs=[anywhere] * 6,
        out_specs=[vmem] * 5,
        scratch_shapes=[
            pltpu.VMEM((3, width, units), BF),
            pltpu.VMEM((2 * half, width), BF),
            pltpu.VMEM((2 * half, width), BF),
            pltpu.SemaphoreType.DMA((3,)),
            pltpu.SemaphoreType.DMA((2,)),
            pltpu.SemaphoreType.DMA((2,)),
        ],
        compiler_params=pltpu.CompilerParams(vmem_limit_bytes=48 * 1024 * 1024),
        cost_estimate=pl.CostEstimate(
            flops=20 * half * width * units,
            bytes_accessed=6 * width * units,
            transcendentals=2 * half * units,
        ),
        name="feed_forward_rows",
    )(*normed, *cots, weights, order)


def wg_body(*refs, sizes, tile):
    count = len(sizes)
    groups = count // 2
    normed, cots, refs = refs[:count], refs[count : 2 * count], refs[2 * count :]
    hidden, gates, ups = refs[:groups], refs[groups : 2 * groups], refs[2 * groups : 3 * groups]
    out, nbuf, cbuf, mbuf, gbuf, ubuf, sem = refs[3 * groups + 1 :]
    pair_sizes = [sizes[2 * i] + sizes[2 * i + 1] for i in range(groups)]

    def copies(at, buffer, sources, lengths):
        result, start = [], 0
        for source, length in zip(sources, lengths):
            target = buffer.at[pl.ds(start, length)]
            result.append(pltpu.make_async_copy(source, target, sem.at[at]))
            start += length
        return result

    def normed_copies():
        return copies(0, nbuf, normed, sizes)

    def cot_copies():
        return copies(1, cbuf, cots, sizes)

    def gate_copies():
        return copies(2, gbuf, gates, pair_sizes)

    def up_copies():
        return copies(3, ubuf, ups, pair_sizes)

    def hidden_copies():
        return copies(4, mbuf, hidden, pair_sizes)

    which, step = pl.program_id(0), pl.program_id(1)

    @pl.when((which == 0) & (step == 0))
    def _():
        first = normed_copies() + gate_copies()
        for copy in first + up_copies() + cot_copies() + hidden_copies():
            copy.start()
        for copy in first:
            copy.wait()

    @pl.when((which == 1) & (step == 0))
    def _():
        for copy in up_copies():
            copy.wait()

    @pl.when((which == 2) & (step == 0))
    def _():
        for copy in cot_copies() + hidden_copies():
            copy.wait()

    columns = pl.ds(pl.multiple_of(step * tile, tile), tile)
    for i, (left, right) in enumerate(((nbuf, gbuf), (nbuf, ubuf), (cbuf, mbuf))):

        @pl.when(which == i)
        def _():
            out[...] = t_dot(left[:, columns], right[...]).astype(BF)


def weight_grads(normed, cots, hidden, gates, ups, order, tile=768):
    sizes = tuple(part.shape[0] for part in normed)
    rows, width, units = sum(sizes), normed[0].shape[1], hidden[0].shape[1]
    anywhere = pl.BlockSpec(memory_space=pl.ANY)
    return pl.pallas_call(
        functools.partial(wg_body, sizes=sizes, tile=tile),
        grid=(3, width // tile),
        out_shape=jax.ShapeDtypeStruct((3, width, units), BF),
        in_specs=[anywhere] * (2 * len(normed) + 3 * len(hidden) + 1),
        out_specs=pl.BlockSpec((None, tile, units), lambda i, j: (i, j, 0)),
        scratch_shapes=[pltpu.VMEM((rows, width), BF)] * 2
        + [pltpu.VMEM((rows, units), BF)] * 3
        + [pltpu.SemaphoreType.DMA((5,))],
        compiler_params=pltpu.CompilerParams(vmem_limit_bytes=48 * 1024 * 1024),
        cost_estimate=pl.CostEstimate(
            flops=6 * rows * width * units,
            bytes_accessed=6 * width * units + rows * (4 * width + 6 * units),
            transcendentals=0,
        ),
        name="weight_gradients",
    )(*normed, *cots, *hidden, *gates, *ups, order)


def down_body(ha, hb, hc, w, *outs, tile=256):
    for group, hidden in enumerate((ha, hb, hc)):
        half = hidden.shape[0] // 2
        step = min(tile, 2 * half)
        for start in range(0, 2 * half, step):
            part = dot_t(hidden[pl.ds(start, step)], w[...]).astype(BF)
            if step > half:
                outs[2 * group][...] = part[:half]
                outs[2 * group + 1][...] = part[half:]
            else:
                outs[2 * group + start // half][pl.ds(start % half, step)] = part


def down_rows(hidden, weights, order):
    _, width, units = weights.shape
    halved = [part.shape[0] // 2 for part in hidden for _ in range(2)]
    outs = vmem_call(
        down_body,
        [((rows, width), BF) for rows in halved],
        [*hidden, (weights, 2)],
        "down_rows",
        (order,),
        limit=32,
        flops=2 * sum(halved) * width * units,
        moved=2 * width * units + 2 * sum(halved) * (width + units),
    )
    return [(outs[0], outs[1]), (outs[2], outs[3]), (outs[4], outs[5])]


def dot(a, b):
    return jnp.dot(a, b, preferred_element_type=F32)


def dot_t(a, b):
    return lax.dot_general(a, b, (((1,), (1,)), ((), ())), preferred_element_type=F32)


def t_dot(a, b):
    return lax.dot_general(a, b, (((0,), (0,)), ((), ())), preferred_element_type=F32)


def pick(index, low, high):
    return jnp.where(index == 0, low, high)


def vmem_call(body, outs, ins, name, order=(), scratch=(), limit=16, flops=0, moved=0):
    count, skipped, results, extra = len(ins), len(order), len(outs), len(scratch)
    parts = [value[1] if isinstance(value, tuple) else None for value in ins]
    ins = [value[0] if isinstance(value, tuple) else value for value in ins]

    def kernel(*refs):
        sources, refs = refs[:count], refs[count + skipped :]
        fixed, buffers, sem = refs[: results + extra], refs[results + extra : -1], refs[-1]
        fetches = [
            pltpu.make_async_copy(source if at is None else source.at[at], buffer, sem.at[i])
            for i, (source, at, buffer) in enumerate(zip(sources, parts, buffers))
        ]
        for fetch in fetches:
            fetch.start()
        for fetch in fetches:
            fetch.wait()
        body(*buffers, *fixed)

    return pl.pallas_call(
        kernel,
        out_shape=[jax.ShapeDtypeStruct(shape, dtype) for shape, dtype in outs],
        in_specs=[pl.BlockSpec(memory_space=pl.ANY)] * (count + skipped),
        out_specs=[pl.BlockSpec(memory_space=pltpu.VMEM)] * results,
        scratch_shapes=[
            *scratch,
            *(
                pltpu.VMEM(value.shape if at is None else value.shape[1:], value.dtype)
                for value, at in zip(ins, parts)
            ),
            pltpu.SemaphoreType.DMA((count,)),
        ],
        compiler_params=pltpu.CompilerParams(vmem_limit_bytes=limit * 1024 * 1024),
        cost_estimate=pl.CostEstimate(flops=flops, bytes_accessed=moved, transcendentals=0),
        name=name,
    )(*ins, *order)


def copies_body(block, out):
    for i in range(out.shape[0]):
        out[i] = block[...]


def copies(block, count, *order):
    shape = (count,) + block.shape
    moved = 2 * count * block.size
    return vmem_call(
        copies_body, [(shape, block.dtype)], [block], "copies", order, moved=moved
    )[0]


def arrange_body(own, other, zh, out):
    mine = zh[0:1, 0:1] == 0
    for i in range(3):
        out[2 * i] = jnp.where(mine, own[i], other[i])
        out[2 * i + 1] = jnp.where(mine, other[i], own[i])


def stack_body(*refs):
    *parts, out = refs
    rows = parts[0].shape[0]
    for i, part in enumerate(parts):
        out[i * rows : (i + 1) * rows] = part[...]


def stacked(parts, *order):
    rows, columns = parts[0].shape
    shape = (len(parts) * rows, columns)
    moved = 4 * shape[0] * columns
    return vmem_call(stack_body, [(shape, BF)], list(parts), "stacked", order, moved=moved)[0]


def row_of(blocks, offset, size):
    count, lanes = blocks.shape
    line = (lanes, count * size)
    at = lax.broadcasted_iota(jnp.int32, line, 1)
    from_lane = lax.broadcasted_iota(jnp.int32, line, 0) - offset
    spots = (lax.rem(at, size) == from_lane).astype(BF)
    values = dot(blocks, spots)
    at = lax.broadcasted_iota(jnp.int32, values.shape, 1)
    owner = lax.broadcasted_iota(jnp.int32, values.shape, 0)
    mine = (at >= owner * size) & (at < (owner + 1) * size)
    return jnp.sum(jnp.where(mine, values, 0.0), axis=0, keepdims=True)


def vectors_body(gains, biases, ranks, attn_out, mlp_out, bias_out):
    attn_out[...] = jnp.broadcast_to(row_of(gains[...], 0, 48), attn_out.shape)
    mlp_out[...] = jnp.broadcast_to(row_of(gains[...], 48, 48), mlp_out.shape)
    full = row_of(biases[...], 0, 64)
    rank = ranks[0:1, 0:1]
    query = key = value = 0.0
    for i in range(4):
        query = query + jnp.where(rank == i, full[:, 384 * i : 384 * (i + 1)], 0.0)
    for i in range(2):
        mine = (rank >= 2 * i) & (rank < 2 * i + 2)
        key = key + jnp.where(mine, full[:, 1536 + HD * i : 1536 + HD * (i + 1)], 0.0)
        value = value + jnp.where(mine, full[:, 1792 + HD * i : 1792 + HD * (i + 1)], 0.0)
    line = jnp.concatenate([query, key, value], axis=1)
    bias_out[...] = jnp.broadcast_to(line, bias_out.shape)


def turn(vectors, cos2, sin2):
    return vectors * cos2 + pltpu.roll(vectors, HD // 2, 1) * sin2


def unpack_table(table, places):
    first, last = table[:, 2 * HD : 2 * HD + 1], table[:, 2 * HD + 1 : 2 * HD + 2]
    keys = places[0:1, :]
    return table[:, :HD], table[:, HD : 2 * HD], (keys >= first) & (keys <= last)


def masked_scores(queries, keys, allowed):
    return jnp.where(allowed, dot_t(queries, keys) * HD ** (-0.5), -1e30)


def attn_forward_body(
    x0, x1, x2, x3, gain, w, bias, table, places,
    n_out, q_out, kv_out, o_out, lse_out,
):
    rows = x0.shape[0]
    for i, x in enumerate((x0, x1, x2, x3)):
        part = x[...].astype(F32)
        scale = lax.rsqrt(jnp.mean(part * part, axis=-1, keepdims=True) + EPSILON)
        n_out[i * rows : (i + 1) * rows] = (part * scale * gain[0:1]).astype(BF)
    qkv = dot(n_out[...], w[:, :640]) + bias[0:1]
    cosines, sines, allowed = unpack_table(table, places)
    keys = turn(qkv[:, 384:512], cosines, sines).astype(BF)
    values = qkv[:, 512:].astype(BF)
    kv_out[:, :HD] = keys
    kv_out[:, HD:] = values
    lses = []
    for h in range(3):
        at = slice(h * HD, (h + 1) * HD)
        queries = turn(qkv[:, at], cosines, sines).astype(BF)
        q_out[:, at] = queries
        scores = masked_scores(queries, keys, allowed)
        peak = jnp.max(scores, axis=-1, keepdims=True)
        shifted = jnp.exp(scores - peak)
        total = jnp.sum(shifted, axis=-1, keepdims=True)
        probs = (shifted / total).astype(BF)
        o_out[:, at] = dot(probs, values).astype(BF)
        lses.append(peak + jnp.log(total))
    lse_out[...] = jnp.concatenate(lses + [jnp.zeros((4 * rows, 125), F32)], axis=1)


def parted(partial, keep, give):
    rows = partial.shape[0] // 4
    keep[0] = partial[:rows].astype(BF)
    give[0] = partial[rows : 2 * rows].astype(BF)
    keep[1] = partial[2 * rows : 3 * rows].astype(BF)
    give[1] = partial[3 * rows :].astype(BF)


def attn_out_body(o, w, keep, give):
    parted(dot_t(o[...], w[:, 768:]), keep, give)


def residual_body(x, keep, got, across, gain, h_out, n_out):
    h = x[...].astype(F32) + keep[0].astype(F32) + got[0].astype(F32) + across[...].astype(F32)
    h_out[...] = h
    scale = lax.rsqrt(jnp.mean(h * h, axis=-1, keepdims=True) + EPSILON)
    n_out[...] = (h * scale * gain[0:1]).astype(BF)


def norm_backward(grad, rows, gain):
    scale = lax.rsqrt(jnp.mean(rows * rows, axis=-1, keepdims=True) + EPSILON)
    scaled = grad * gain
    back = scale * scaled - rows * scale**3 * jnp.mean(scaled * rows, axis=-1, keepdims=True)
    return back, jnp.sum(grad * rows * scale, axis=0, keepdims=True)


def ff_back_body(own_a, own_b, got_a, got_b, got_c, h, cot, gain, grad_out, branch_out, gain_out):
    grad = sum(part[...].astype(F32) for part in (own_a, own_b, got_a, got_b, got_c))
    back, gain_out[...] = norm_backward(grad, h[...], gain[0:1])
    total = cot[...].astype(F32) + back
    grad_out[...] = total
    branch_out[...] = total.astype(BF)


def attn_back_body(keep, got, across, x, above, gain, grad_out, gain_out):
    grad = keep[0].astype(F32) + got[0].astype(F32) + across[...].astype(F32)
    back, gain_out[...] = norm_backward(grad, x[...].astype(F32), gain[0:1])
    grad_out[...] = above[...] + back


def attn_backward_body(
    b0, b1, b2, b3, w, q, kv, lse, table, places,
    grads_out, keep, give, sums_out, bbuf,
):
    rows = b0.shape[0]
    for i, part in enumerate((b0, b1, b2, b3)):
        bbuf[i * rows : (i + 1) * rows] = part[...]
    attended_grad = dot(bbuf[...], w[:, 768:]).astype(BF)
    keys, values = kv[:, :HD], kv[:, HD:]
    cosines, sines, allowed = unpack_table(table, places)
    sines = -sines
    key_grad = value_grad = 0.0
    for h in range(3):
        at = slice(h * HD, (h + 1) * HD)
        queries, o_grad = q[:, at], attended_grad[:, at]
        probs = jnp.exp(masked_scores(queries, keys, allowed) - lse[:, h : h + 1])
        prob_grad = dot_t(o_grad, values)
        inner = jnp.sum(probs * prob_grad, axis=-1, keepdims=True)
        score_grad = (probs * (prob_grad - inner)).astype(BF)
        query_grad = dot(score_grad, keys) * HD ** (-0.5)
        grads_out[:, at] = turn(query_grad, cosines, sines).astype(BF)
        key_grad = key_grad + t_dot(score_grad, queries)
        value_grad = value_grad + t_dot(probs.astype(BF), o_grad)
    grads_out[:, 384:512] = turn(key_grad * HD ** (-0.5), cosines, sines).astype(BF)
    grads_out[:, 512:] = value_grad.astype(BF)
    grads = grads_out[...]
    sums_out[...] = jnp.sum(grads.astype(F32), axis=0, keepdims=True)
    parted(dot_t(grads, w[:, :640]), keep, give)


def blocks_of(row, size):
    count = row.shape[1] // size
    at = lax.broadcasted_iota(jnp.int32, (count, row.shape[1]), 1)
    owner = lax.broadcasted_iota(jnp.int32, (count, row.shape[1]), 0)
    mine = (at >= owner * size) & (at < (owner + 1) * size)
    values = jnp.where(mine, row, 0.0).astype(BF)
    at = lax.broadcasted_iota(jnp.int32, (row.shape[1], HD), 0)
    lane = lax.broadcasted_iota(jnp.int32, (row.shape[1], HD), 1)
    return dot(values, (lax.rem(at, size) == lane).astype(BF))


def gradient_rows(*refs, buffer, right, out):
    rows = refs
    size = rows[0].shape[0]
    for i, part in enumerate(rows):
        buffer[i * size : (i + 1) * size] = part[...]
    half = buffer.shape[1] // 2
    for i in range(2):
        grad = t_dot(buffer[:, i * half : (i + 1) * half], right[...]).astype(BF)
        out[16 * i : 16 * (i + 1), :, : right.shape[1]] = grad.reshape(
            16, half // 16, right.shape[1]
        )


def o_grad_body(*refs):
    *rows, right, out, buffer = refs
    gradient_rows(*rows, buffer=buffer, right=right, out=out)


def qkv_grad_body(rows, right, gain_attn, gain_mlp, sums, ranks, out, buffer):
    gradient_rows(rows, buffer=buffer, right=right, out=out)
    rank = ranks[0:1, 0:1]
    parts = [jnp.where(rank == i, sums[:, :384], 0.0) for i in range(4)]
    for start in (384, 512):
        for i in range(2):
            mine = (rank >= 2 * i) & (rank < 2 * i + 2)
            parts.append(jnp.where(mine, sums[:, start : start + HD], 0.0))
    rows_of = (
        blocks_of(gain_attn[...], 48),
        blocks_of(gain_mlp[...], 48),
        blocks_of(jnp.concatenate(parts[:6], axis=1), 56),
        blocks_of(jnp.concatenate(parts[6:], axis=1), 8),
    )
    at = lax.broadcasted_iota(jnp.int32, (32, out.shape[1], HD), 1)
    tail = jnp.zeros((32, out.shape[1], HD), F32)
    for i, values in enumerate(rows_of):
        tail = jnp.where(at == i, values[:, None, :], tail)
    out[:, :, 640:] = tail.astype(BF)


def rows_product(body, rows, right, extra, columns, name, order):
    width = rows[0].shape[1]
    total = sum(part.shape[0] for part in rows)
    return vmem_call(
        body,
        [((32, width // 32, columns), BF)],
        [*rows, right, *extra],
        name,
        order,
        [pltpu.VMEM((total, width), BF)],
        limit=32,
        flops=2 * total * width * columns,
        moved=2 * (total * width + total * columns + width * columns),
    )[0]


def shards(
    layer_input,
    q_weight,
    kv_weight,
    o_weight,
    norm_gains,
    qkv_bias,
    gate_up,
    down_weight,
    cotangent,
    lengths,
):
    zh, zl, core = (lax.axis_index(a) for a in ("zh", "zl", "core"))
    rank = 2 * zl + core
    width = layer_input.shape[1]
    rows = layer_input.shape[0]

    small = jnp.concatenate([norm_gains.reshape(-1), qkv_bias, jnp.zeros((216,), BF)])
    vectors = jnp.concatenate([kv_weight.reshape(24, 256), small[None], jnp.zeros((7, 256), BF)])
    got = swap(vectors, "core")
    both = jnp.stack([pick(core, vectors, got), pick(core, got, vectors)])
    small_keep = both[:, 24].reshape(2, 2, HD)
    kv_keep = pick(zl, both[:, :24, :HD], both[:, :24, HD:])
    kv_give = pick(zl, both[:, :24, HD:], both[:, :24, :HD])
    got = swap(jnp.concatenate([kv_give, small_keep, jnp.zeros((2, 6, HD), BF)], axis=1), "zl")
    kv_got, small_got = got[:, :24], got[:, 24:26]
    kv_rows = jnp.stack([pick(zl, kv_keep, kv_got), pick(zl, kv_got, kv_keep)])
    kv_rows = kv_rows.reshape(2, 2, 2, 12, HD).transpose(0, 1, 3, 2, 4).reshape(48, 2 * HD)
    small = jnp.stack([pick(zl, small_keep, small_got), pick(zl, small_got, small_keep)])
    small = small.reshape(4, 256)
    gains_row = jnp.concatenate([small[:, :12].reshape(48), small[:, 12:24].reshape(48)])
    bias_row = small[:, 24:40].reshape(64)
    small = jnp.zeros((48, HD), BF).at[0, :96].set(gains_row).at[1, :64].set(bias_row)

    ends = jnp.cumsum(lengths[0])
    ranks = jnp.stack([rank, 2 * zl + 1 - core, 2 * (1 - zl) + core, 2 * (1 - zl) + 1 - core])
    group = 4 * rows
    places = (ranks[:, None] * rows + jnp.arange(rows, dtype=jnp.int32)[None, :]).reshape(group)
    passed = ends[None, :] <= places[:, None]
    starts = jnp.sum(jnp.where(passed, lengths[0][None, :], 0), axis=1)
    inverse = THETA ** (-(2.0 * jnp.arange(HD // 2, dtype=F32)) / HD)
    inverse = jnp.concatenate([inverse, inverse])[None, :]
    angles = (places - starts).astype(F32)[:, None] * inverse
    sign = jnp.where(jnp.arange(HD) < HD // 2, -1.0, 1.0).astype(F32)[None, :]
    lane = jnp.arange(HD)[None, :]
    ranges = jnp.where(lane == 0, starts[:, None], places[:, None]).astype(F32)
    table = jnp.concatenate([jnp.cos(angles), jnp.sin(angles) * sign, ranges], axis=1)
    tables = (table, jnp.broadcast_to(places.astype(F32)[None, :], (8, group)))

    living = (places[:rows] < ends[-1])[:, None]
    cot_local = jnp.where(living, cotangent, jnp.zeros((), BF))
    cot_groups = token_groups(cot_local)

    across = swap(layer_input, "zl")
    group_inputs = (layer_input, swap(layer_input, "core"), across, swap(across, "core"))

    attn_part = jnp.concatenate([q_weight, kv_rows, small, o_weight.T], axis=-1)
    attn_full = exchange(copies(attn_part, 32), DATA)
    small = attn_full[:, :2, 640:768]
    attn_full = attn_full.reshape(width, 1152)
    waits = (cot_groups[1][1], cot_groups[2][1], group_inputs[3], *tables)
    gain_attn, gain_mlp, bias = vmem_call(
        vectors_body,
        [((8, width), F32), ((8, width), F32), ((8, 640), F32)],
        [small[:, 0], small[:, 1], jnp.full((8, HD), rank, jnp.int32)],
        "gains_and_biases",
        waits,
        limit=16,
    )

    mlp = jnp.concatenate([gate_up, down_weight.T[None]], axis=0)
    mlp = jnp.pad(mlp, ((0, 0), (0, 0), (0, 2 * HALF - mlp.shape[2])))
    mlp_own = pick(zh, mlp[..., :HALF], mlp[..., HALF:])
    mlp_other = swap(pick(zh, mlp[..., HALF:], mlp[..., :HALF]), "zh")
    mlp = vmem_call(
        arrange_body,
        [((6, 48, HALF), BF)],
        [mlp_own, mlp_other, jnp.full((8, HD), zh, jnp.int32)],
        "arranged",
        moved=4 * mlp_own.size,
    )[0]
    mlp = lax.all_gather(mlp, PLANE, axis=1, tiled=True)
    mlp = mlp.reshape(3, width, HALF)

    normed_group, queries, kv_rot, attended, lse = vmem_call(
        attn_forward_body,
        [
            ((group, width), BF),
            ((group, 384), BF),
            ((group, 256), BF),
            ((group, 384), BF),
            ((group, 128), F32),
        ],
        [*group_inputs, gain_attn, attn_full, bias, *tables],
        "attention_forward",
        limit=32,
        flops=2 * group * (width * 640 + 6 * group * HD),
        moved=2 * group * width * 2 + 2 * width * 768,
    )
    pair = ((2, rows, width), BF)
    keep, give = vmem_call(
        attn_out_body,
        [pair, pair],
        [attended, attn_full],
        "attention_out",
        flops=2 * group * width * 384,
        moved=2 * width * 384 + 2 * group * width,
    )
    got = swap(give, "core")
    residual, normed_mlp = vmem_call(
        residual_body,
        [((rows, width), F32), ((rows, width), BF)],
        [layer_input, keep, got, swap(add(keep[1], got[1]), "zl"), gain_mlp],
        "residual_norm",
        moved=10 * rows * width,
    )

    after_rows, before_rows = z_shift(normed_mlp, -1), z_shift(normed_mlp, 1)
    far_rows = z_shift(normed_mlp, 2)
    own = (normed_mlp, swap(normed_mlp, "core"))
    own_out = ff_rows(own, cot_groups[0], mlp, cot_local)
    near = stacked((after_rows, before_rows), own_out[0])
    near = (near, swap(near, "core"))
    near_out = ff_rows(near, cot_groups[1], mlp, own_out[0])
    far_rows = stacked((far_rows,), near_out[0])
    far = (far_rows, swap(far_rows, "core"))
    near_sum = [
        add(mine, swap(others, "core"))
        for mine, others in zip(halves(near_out[3], 0), halves(near_out[4], 0))
    ]
    near_got = (z_shift(near_sum[0], 1), z_shift(near_sum[1], -1))
    far_out = ff_rows(far, cot_groups[2], mlp, near_sum[1])
    far_sum = add(far_out[3], swap(far_out[4], "core"))
    own_got = swap(own_out[4], "core")
    far_got = z_shift(far_sum, 2)
    results = (own_out, near_out, far_out)
    hidden, gate_grads, up_grads = ([r[i] for r in results] for i in range(3))
    flat_normed = [*own, *near, *far]
    flat_cots = [part for pair in cot_groups for part in pair]
    mlp_grads = weight_grads(flat_normed, flat_cots, hidden, gate_grads, up_grads, far_sum)
    residual_grad, branch, gain_mlp_grad = vmem_call(
        ff_back_body,
        [((rows, width), F32), ((rows, width), BF), ((1, width), F32)],
        [own_out[3], own_got, *near_got, far_got, residual, cot_local, gain_mlp],
        "residual_gradient",
        (mlp_grads,),
        moved=24 * rows * width,
    )
    mlp_grads = lax.psum_scatter(
        mlp_grads.reshape(6, width // 2, HALF), PLANE, scatter_dimension=1, tiled=True
    ).reshape(3, 2, 48, HALF)
    own_grads = lax.dynamic_index_in_dim(mlp_grads, zh, 1, keepdims=False)
    other_grads = swap(lax.dynamic_index_in_dim(mlp_grads, 1 - zh, 1, keepdims=False), "zh")
    own_grads, other_grads = own_grads.astype(F32), other_grads.astype(F32)
    mlp_shard = jnp.concatenate(
        [pick(zh, own_grads, other_grads), pick(zh, other_grads, own_grads)], axis=-1
    )[..., : gate_up.shape[2]]
    gate_up_shard = mlp_shard[:2]
    down_shard = mlp_shard[2].T

    out_pairs = down_rows(hidden, mlp, branch)
    layer_output = (residual + token_sums(out_pairs)).astype(BF)

    across = stacked((swap(branch, "zl"),), out_pairs[0][0])
    branch_group = (branch, swap(branch, "core"), across, swap(across, "core"))
    o_terms = rows_product(
        o_grad_body, branch_group, attended, (), 384, "o_weight_gradient", ()
    )
    o_got = exchange(o_terms, DATA)
    qkv_grad, keep, give, sums = vmem_call(
        attn_backward_body,
        [((group, 640), BF), pair, pair, ((1, 640), F32)],
        [*branch_group, attn_full, queries, kv_rot, lse, *tables],
        "attention_backward",
        (o_terms,),
        limit=32,
        scratch=[pltpu.VMEM((group, width), BF)],
        flops=2 * group * (width * 1024 + 15 * group * HD) * WEIGHT,
        moved=4 * group * width + 2 * width * 1024,
    )
    got = swap(give, "core")
    other = add(keep[1], got[1])
    input_grad, gain_attn_grad = vmem_call(
        attn_back_body,
        [((rows, width), F32), ((1, width), F32)],
        [keep, got, swap(other, "zl"), layer_input, residual_grad, gain_attn],
        "input_gradient",
        moved=20 * rows * width,
    )

    qkv_terms = rows_product(
        qkv_grad_body,
        (normed_group,),
        qkv_grad,
        (gain_attn_grad, gain_mlp_grad, sums, jnp.full((8, HD), rank, jnp.int32)),
        768,
        "qkv_weight_gradient",
        (o_got,),
    )
    o_shard = jnp.sum(o_got.astype(F32), axis=0).T
    attn_shard = jnp.sum(exchange(qkv_terms, DATA).astype(F32), axis=0)
    q_shard = attn_shard[:, :384]
    kv_sum = attn_shard[:, 384:640].reshape(2, 2, 12, 2, HD)
    kv_keep = lax.dynamic_index_in_dim(kv_sum, core, 1, keepdims=False).reshape(48, HD)
    kv_give = lax.dynamic_index_in_dim(kv_sum, 1 - core, 1, keepdims=False).reshape(48, HD)
    vectors = attn_shard[:8, 640:]
    got = swap(jnp.concatenate([kv_give, vectors]), "core")
    kv_sum = (kv_keep + got[:48]).reshape(2, 24, HD)
    vectors = vectors + got[48:]
    kv_keep = pick(zl, kv_sum[0], kv_sum[1])
    got = swap(jnp.concatenate([pick(zl, kv_sum[1], kv_sum[0]), vectors]), "zl")
    kv_got = got[:24]
    vectors = vectors + got[24:]
    kv_shard = jnp.concatenate([pick(zl, kv_keep, kv_got), pick(zl, kv_got, kv_keep)], axis=-1)
    kv_shard = kv_shard.reshape(12, 2, 2 * HD).transpose(1, 0, 2)

    def own_part(row, size):
        return lax.dynamic_index_in_dim(
            vectors[row, : 4 * size].reshape(4, size), rank, 0, keepdims=False
        )

    return (
        layer_output,
        input_grad,
        q_shard,
        kv_shard,
        o_shard,
        jnp.stack([own_part(0, 12), own_part(1, 12)]),
        own_part(2, 14),
        own_part(3, 2),
        gate_up_shard,
        down_shard,
    )


def solution(mesh):
    fine = Mesh(mesh.devices.reshape(SIZES), AXES)
    dp = ("zh", "y", "x")
    tensor = ("zl", "core")
    every = dp + tensor
    in_specs = (
        P(every, None),
        P(dp, tensor),
        P(None, every, None),
        P(tensor, dp),
        P(None, every),
        P(every),
        P(None, dp, tensor),
        P(tensor, dp),
        P(every, None),
        P(dp, None),
    )
    out_specs = (
        P(every, None),
        P(every, None),
        P(dp, tensor),
        P(None, every, None),
        P(tensor, dp),
        P(None, every),
        P(every),
        P(every),
        P(None, dp, tensor),
        P(tensor, dp),
    )
    return jax.shard_map(shards, mesh=fine, in_specs=in_specs, out_specs=out_specs, check_vma=False)
```

```python
import functools

import jax
import jax.numpy as jnp
from jax import lax
from jax.experimental import pallas as pl
from jax.experimental.pallas import tpu as pltpu
from jax.sharding import Mesh, PartitionSpec as P

HQ = 12
KVH = 2
HD = 128
EPSILON = 1e-06
THETA = 1000000.0

AXES = ("zh", "y", "x", "zl", "core")
SIZES = (2, 4, 4, 2, 2)
ZRING = ("zh", "zl")
PLANE = ("y", "x")
DATA = ("zh", "y", "x")
HALF = 1152
BF = jnp.bfloat16
WEIGHT = 1000
F32 = jnp.float32


def swap(block, axis):
    return lax.ppermute(block, axis, [(0, 1), (1, 0)])


def halves(block, dim):
    middle = block.shape[dim] // 2
    return (
        lax.slice_in_dim(block, 0, middle, axis=dim),
        lax.slice_in_dim(block, middle, block.shape[dim], axis=dim),
    )


def add(*terms):
    total = terms[0].astype(F32)
    for term in terms[1:]:
        total = total + term.astype(F32)
    return total.astype(terms[0].dtype)


def exchange(blocks, axes):
    return lax.all_to_all(blocks, axes, split_axis=0, concat_axis=0, tiled=True)


def spread(block, axes, count):
    return exchange(jnp.broadcast_to(block[None], (count,) + block.shape), axes)


def z_shift(block, by):
    return lax.ppermute(block, ZRING, [(i, (i + by) % 4) for i in range(4)])


def token_groups(block):
    near = jnp.concatenate([z_shift(block, -1), z_shift(block, 1)], axis=0)
    far = z_shift(block, 2)
    return [(part, swap(part, "core")) for part in (block, near, far)]


def token_sums(pairs):
    own, near, far = (add(mine, swap(others, "core")) for mine, others in pairs)
    after_rows, before_rows = halves(near, 0)
    terms = (own, z_shift(after_rows, 1), z_shift(before_rows, -1), z_shift(far, 2))
    return sum(term.astype(F32) for term in terms)


def ff_body(
    na, nb, ca, cb, w, _, m_out, dg_out, du_out, dna_out, dnb_out,
    wbuf, nbuf, cbuf, wsem, nsem, csem, *, tile,
):
    half = na.shape[0]
    weights = [pltpu.make_async_copy(w.at[i], wbuf.at[i], wsem.at[i]) for i in range(3)]
    normed = [
        pltpu.make_async_copy(part, nbuf.at[pl.ds(k * half, half)], nsem.at[k])
        for k, part in enumerate((na, nb))
    ]
    cots = [
        pltpu.make_async_copy(part, cbuf.at[pl.ds(k * half, half)], csem.at[k])
        for k, part in enumerate((ca, cb))
    ]
    for copy in normed + weights[:2] + cots + weights[2:]:
        copy.start()
    for copy in normed + weights[:1]:
        copy.wait()
    tiles = 2 * half // tile
    for i in range(tiles):
        at = pl.ds(i * tile, tile)
        rows = nbuf[at]
        gate = dot(rows, wbuf[0])
        if i == 0:
            weights[1].wait()
        up = dot(rows, wbuf[1])
        if i == 0:
            for copy in cots + weights[2:]:
                copy.wait()
        hidden_grad = dot(cbuf[at], wbuf[2])
        sigma = 1.0 / (1.0 + jnp.exp(-gate))
        act = gate * sigma
        m_out[at] = (act * up).astype(BF)
        up_grad = (hidden_grad * act).astype(BF)
        gate_grad = (hidden_grad * up * sigma * (1.0 + gate * (1.0 - sigma))).astype(BF)
        dg_out[at] = gate_grad
        du_out[at] = up_grad
        back = (dot_t(gate_grad, wbuf[0]) + dot_t(up_grad, wbuf[1])).astype(BF)
        if tiles == 1:
            dna_out[...] = back[:half]
            dnb_out[...] = back[half:]
        else:
            out = dna_out if i < tiles // 2 else dnb_out
            out[pl.ds(i % (tiles // 2) * tile, tile)] = back


def ff_rows(normed, cots, weights, order, tile=256):
    half, width = normed[0].shape
    units = weights.shape[2]
    anywhere = pl.BlockSpec(memory_space=pl.ANY)
    vmem = pl.BlockSpec(memory_space=pltpu.VMEM)
    return pl.pallas_call(
        functools.partial(ff_body, tile=tile),
        out_shape=[jax.ShapeDtypeStruct((2 * half, units), BF)] * 3
        + [jax.ShapeDtypeStruct((half, width), BF)] * 2,
        in_specs=[anywhere] * 6,
        out_specs=[vmem] * 5,
        scratch_shapes=[
            pltpu.VMEM((3, width, units), BF),
            pltpu.VMEM((2 * half, width), BF),
            pltpu.VMEM((2 * half, width), BF),
            pltpu.SemaphoreType.DMA((3,)),
            pltpu.SemaphoreType.DMA((2,)),
            pltpu.SemaphoreType.DMA((2,)),
        ],
        compiler_params=pltpu.CompilerParams(vmem_limit_bytes=48 * 1024 * 1024),
        cost_estimate=pl.CostEstimate(
            flops=20 * half * width * units,
            bytes_accessed=6 * width * units,
            transcendentals=2 * half * units,
        ),
        name="feed_forward_rows",
    )(*normed, *cots, weights, order)


def wg_body(*refs, sizes, tile):
    count = len(sizes)
    groups = count // 2
    normed, cots, refs = refs[:count], refs[count : 2 * count], refs[2 * count :]
    hidden, gates, ups = refs[:groups], refs[groups : 2 * groups], refs[2 * groups : 3 * groups]
    out, nbuf, cbuf, mbuf, gbuf, ubuf, sem = refs[3 * groups + 1 :]
    pair_sizes = [sizes[2 * i] + sizes[2 * i + 1] for i in range(groups)]

    def copies(at, buffer, sources, lengths):
        result, start = [], 0
        for source, length in zip(sources, lengths):
            target = buffer.at[pl.ds(start, length)]
            result.append(pltpu.make_async_copy(source, target, sem.at[at]))
            start += length
        return result

    def normed_copies():
        return copies(0, nbuf, normed, sizes)

    def cot_copies():
        return copies(1, cbuf, cots, sizes)

    def gate_copies():
        return copies(2, gbuf, gates, pair_sizes)

    def up_copies():
        return copies(3, ubuf, ups, pair_sizes)

    def hidden_copies():
        return copies(4, mbuf, hidden, pair_sizes)

    which, step = pl.program_id(0), pl.program_id(1)

    @pl.when((which == 0) & (step == 0))
    def _():
        first = normed_copies() + gate_copies()
        for copy in first + up_copies() + cot_copies() + hidden_copies():
            copy.start()
        for copy in first:
            copy.wait()

    @pl.when((which == 1) & (step == 0))
    def _():
        for copy in up_copies():
            copy.wait()

    @pl.when((which == 2) & (step == 0))
    def _():
        for copy in cot_copies() + hidden_copies():
            copy.wait()

    columns = pl.ds(pl.multiple_of(step * tile, tile), tile)
    for i, (left, right) in enumerate(((nbuf, gbuf), (nbuf, ubuf), (cbuf, mbuf))):

        @pl.when(which == i)
        def _():
            out[...] = t_dot(left[:, columns], right[...]).astype(BF)


def weight_grads(normed, cots, hidden, gates, ups, order, tile=768):
    sizes = tuple(part.shape[0] for part in normed)
    rows, width, units = sum(sizes), normed[0].shape[1], hidden[0].shape[1]
    anywhere = pl.BlockSpec(memory_space=pl.ANY)
    return pl.pallas_call(
        functools.partial(wg_body, sizes=sizes, tile=tile),
        grid=(3, width // tile),
        out_shape=jax.ShapeDtypeStruct((3, width, units), BF),
        in_specs=[anywhere] * (2 * len(normed) + 3 * len(hidden) + 1),
        out_specs=pl.BlockSpec((None, tile, units), lambda i, j: (i, j, 0)),
        scratch_shapes=[pltpu.VMEM((rows, width), BF)] * 2
        + [pltpu.VMEM((rows, units), BF)] * 3
        + [pltpu.SemaphoreType.DMA((5,))],
        compiler_params=pltpu.CompilerParams(vmem_limit_bytes=48 * 1024 * 1024),
        cost_estimate=pl.CostEstimate(
            flops=6 * rows * width * units,
            bytes_accessed=6 * width * units + rows * (4 * width + 6 * units),
            transcendentals=0,
        ),
        name="weight_gradients",
    )(*normed, *cots, *hidden, *gates, *ups, order)


def down_body(ha, hb, hc, w, *outs, tile=256):
    for group, hidden in enumerate((ha, hb, hc)):
        half = hidden.shape[0] // 2
        step = min(tile, 2 * half)
        for start in range(0, 2 * half, step):
            part = dot_t(hidden[pl.ds(start, step)], w[...]).astype(BF)
            if step > half:
                outs[2 * group][...] = part[:half]
                outs[2 * group + 1][...] = part[half:]
            else:
                outs[2 * group + start // half][pl.ds(start % half, step)] = part


def down_rows(hidden, weights, order):
    _, width, units = weights.shape
    halved = [part.shape[0] // 2 for part in hidden for _ in range(2)]
    outs = vmem_call(
        down_body,
        [((rows, width), BF) for rows in halved],
        [*hidden, (weights, 2)],
        "down_rows",
        (order,),
        limit=32,
        flops=2 * sum(halved) * width * units,
        moved=2 * width * units + 2 * sum(halved) * (width + units),
    )
    return [(outs[0], outs[1]), (outs[2], outs[3]), (outs[4], outs[5])]


def dot(a, b):
    return jnp.dot(a, b, preferred_element_type=F32)


def dot_t(a, b):
    return lax.dot_general(a, b, (((1,), (1,)), ((), ())), preferred_element_type=F32)


def t_dot(a, b):
    return lax.dot_general(a, b, (((0,), (0,)), ((), ())), preferred_element_type=F32)


def pick(index, low, high):
    return jnp.where(index == 0, low, high)


def vmem_call(body, outs, ins, name, order=(), scratch=(), limit=16, flops=0, moved=0):
    count, skipped, results, extra = len(ins), len(order), len(outs), len(scratch)
    parts = [value[1] if isinstance(value, tuple) else None for value in ins]
    ins = [value[0] if isinstance(value, tuple) else value for value in ins]

    def kernel(*refs):
        sources, refs = refs[:count], refs[count + skipped :]
        fixed, buffers, sem = refs[: results + extra], refs[results + extra : -1], refs[-1]
        fetches = [
            pltpu.make_async_copy(source if at is None else source.at[at], buffer, sem.at[i])
            for i, (source, at, buffer) in enumerate(zip(sources, parts, buffers))
        ]
        for fetch in fetches:
            fetch.start()
        for fetch in fetches:
            fetch.wait()
        body(*buffers, *fixed)

    return pl.pallas_call(
        kernel,
        out_shape=[jax.ShapeDtypeStruct(shape, dtype) for shape, dtype in outs],
        in_specs=[pl.BlockSpec(memory_space=pl.ANY)] * (count + skipped),
        out_specs=[pl.BlockSpec(memory_space=pltpu.VMEM)] * results,
        scratch_shapes=[
            *scratch,
            *(
                pltpu.VMEM(value.shape if at is None else value.shape[1:], value.dtype)
                for value, at in zip(ins, parts)
            ),
            pltpu.SemaphoreType.DMA((count,)),
        ],
        compiler_params=pltpu.CompilerParams(vmem_limit_bytes=limit * 1024 * 1024),
        cost_estimate=pl.CostEstimate(flops=flops, bytes_accessed=moved, transcendentals=0),
        name=name,
    )(*ins, *order)


def copies_body(block, out):
    for i in range(out.shape[0]):
        out[i] = block[...]


def copies(block, count, *order):
    shape = (count,) + block.shape
    moved = 2 * count * block.size
    return vmem_call(
        copies_body, [(shape, block.dtype)], [block], "copies", order, moved=moved
    )[0]


def arrange_body(own, other, zh, out):
    mine = zh[0:1, 0:1] == 0
    for i in range(3):
        out[2 * i] = jnp.where(mine, own[i], other[i])
        out[2 * i + 1] = jnp.where(mine, other[i], own[i])


def ordered_body(own, other, zh, out):
    mine = zh[0:1, 0:1] == 0
    for i in range(own.shape[0]):
        out[0, i] = jnp.where(mine, own[i], other[i])
        out[1, i] = jnp.where(mine, other[i], own[i])


def ordered(own, other, zh, name, order):
    flag = jnp.full((8, HD), zh, jnp.int32)
    shape = (2,) + own.shape
    return vmem_call(
        ordered_body, [(shape, BF)], [own, other, flag], name, order, moved=8 * own.size
    )[0]


def stack_body(*refs):
    *parts, out = refs
    rows = parts[0].shape[0]
    for i, part in enumerate(parts):
        out[i * rows : (i + 1) * rows] = part[...]


def stacked(parts, *order):
    rows, columns = parts[0].shape
    shape = (len(parts) * rows, columns)
    moved = 4 * shape[0] * columns
    return vmem_call(stack_body, [(shape, BF)], list(parts), "stacked", order, moved=moved)[0]


def row_of(blocks, offset, size):
    count, lanes = blocks.shape
    line = (lanes, count * size)
    at = lax.broadcasted_iota(jnp.int32, line, 1)
    from_lane = lax.broadcasted_iota(jnp.int32, line, 0) - offset
    spots = (lax.rem(at, size) == from_lane).astype(BF)
    values = dot(blocks, spots)
    at = lax.broadcasted_iota(jnp.int32, values.shape, 1)
    owner = lax.broadcasted_iota(jnp.int32, values.shape, 0)
    mine = (at >= owner * size) & (at < (owner + 1) * size)
    return jnp.sum(jnp.where(mine, values, 0.0), axis=0, keepdims=True)


def vectors_body(gains, biases, ranks, attn_out, mlp_out, bias_out):
    attn_out[...] = jnp.broadcast_to(row_of(gains[...], 0, 48), attn_out.shape)
    mlp_out[...] = jnp.broadcast_to(row_of(gains[...], 48, 48), mlp_out.shape)
    full = row_of(biases[...], 0, 64)
    rank = ranks[0:1, 0:1]
    query = key = value = 0.0
    for i in range(4):
        query = query + jnp.where(rank == i, full[:, 384 * i : 384 * (i + 1)], 0.0)
    for i in range(2):
        mine = (rank >= 2 * i) & (rank < 2 * i + 2)
        key = key + jnp.where(mine, full[:, 1536 + HD * i : 1536 + HD * (i + 1)], 0.0)
        value = value + jnp.where(mine, full[:, 1792 + HD * i : 1792 + HD * (i + 1)], 0.0)
    line = jnp.concatenate([query, key, value], axis=1)
    bias_out[...] = jnp.broadcast_to(line, bias_out.shape)


def turn(vectors, cos2, sin2):
    return vectors * cos2 + pltpu.roll(vectors, HD // 2, 1) * sin2


def unpack_table(table, places):
    first, last = table[:, 2 * HD : 2 * HD + 1], table[:, 2 * HD + 1 : 2 * HD + 2]
    keys = places[0:1, :]
    return table[:, :HD], table[:, HD : 2 * HD], (keys >= first) & (keys <= last)


def masked_scores(queries, keys, allowed):
    return jnp.where(allowed, dot_t(queries, keys) * HD ** (-0.5), -1e30)


def attn_forward_body(
    x0, x1, x2, x3, gain, w, bias, table, places,
    n_out, q_out, kv_out, o_out, lse_out,
):
    rows = x0.shape[0]
    for i, x in enumerate((x0, x1, x2, x3)):
        part = x[...].astype(F32)
        scale = lax.rsqrt(jnp.mean(part * part, axis=-1, keepdims=True) + EPSILON)
        n_out[i * rows : (i + 1) * rows] = (part * scale * gain[0:1]).astype(BF)
    qkv = dot(n_out[...], w[:, :640]) + bias[0:1]
    cosines, sines, allowed = unpack_table(table, places)
    keys = turn(qkv[:, 384:512], cosines, sines).astype(BF)
    values = qkv[:, 512:].astype(BF)
    kv_out[:, :HD] = keys
    kv_out[:, HD:] = values
    lses = []
    for h in range(3):
        at = slice(h * HD, (h + 1) * HD)
        queries = turn(qkv[:, at], cosines, sines).astype(BF)
        q_out[:, at] = queries
        scores = masked_scores(queries, keys, allowed)
        peak = jnp.max(scores, axis=-1, keepdims=True)
        shifted = jnp.exp(scores - peak)
        total = jnp.sum(shifted, axis=-1, keepdims=True)
        probs = (shifted / total).astype(BF)
        o_out[:, at] = dot(probs, values).astype(BF)
        lses.append(peak + jnp.log(total))
    lse_out[...] = jnp.concatenate(lses + [jnp.zeros((4 * rows, 125), F32)], axis=1)


def parted(partial, keep, give):
    rows = partial.shape[0] // 4
    keep[0] = partial[:rows].astype(BF)
    give[0] = partial[rows : 2 * rows].astype(BF)
    keep[1] = partial[2 * rows : 3 * rows].astype(BF)
    give[1] = partial[3 * rows :].astype(BF)


def attn_out_body(o, w, keep, give):
    parted(dot_t(o[...], w[...]), keep, give)


def residual_body(x, keep, got, across, gain, h_out, n_out):
    h = x[...].astype(F32) + keep[0].astype(F32) + got[0].astype(F32) + across[...].astype(F32)
    h_out[...] = h
    scale = lax.rsqrt(jnp.mean(h * h, axis=-1, keepdims=True) + EPSILON)
    n_out[...] = (h * scale * gain[0:1]).astype(BF)


def norm_backward(grad, rows, gain):
    scale = lax.rsqrt(jnp.mean(rows * rows, axis=-1, keepdims=True) + EPSILON)
    scaled = grad * gain
    back = scale * scaled - rows * scale**3 * jnp.mean(scaled * rows, axis=-1, keepdims=True)
    return back, jnp.sum(grad * rows * scale, axis=0, keepdims=True)


def ff_back_body(own_a, own_b, got_a, got_b, got_c, h, cot, gain, grad_out, branch_out, gain_out):
    grad = sum(part[...].astype(F32) for part in (own_a, own_b, got_a, got_b, got_c))
    back, gain_out[...] = norm_backward(grad, h[...], gain[0:1])
    total = cot[...].astype(F32) + back
    grad_out[...] = total
    branch_out[...] = total.astype(BF)


def attn_back_body(keep, got, across, x, above, gain, grad_out, gain_out):
    grad = keep[0].astype(F32) + got[...].astype(F32) + across[...].astype(F32)
    back, gain_out[...] = norm_backward(grad, x[...].astype(F32), gain[0:1])
    grad_out[...] = above[...] + back


def attn_backward_body(
    b0, b1, b2, b3, wo, w, q, kv, lse, table, places,
    grads_out, keep, give, sums_out, bbuf,
):
    rows = b0.shape[0]
    for i, part in enumerate((b0, b1, b2, b3)):
        bbuf[i * rows : (i + 1) * rows] = part[...]
    attended_grad = dot(bbuf[...], wo[...]).astype(BF)
    keys, values = kv[:, :HD], kv[:, HD:]
    cosines, sines, allowed = unpack_table(table, places)
    sines = -sines
    key_grad = value_grad = 0.0
    for h in range(3):
        at = slice(h * HD, (h + 1) * HD)
        queries, o_grad = q[:, at], attended_grad[:, at]
        probs = jnp.exp(masked_scores(queries, keys, allowed) - lse[:, h : h + 1])
        prob_grad = dot_t(o_grad, values)
        inner = jnp.sum(probs * prob_grad, axis=-1, keepdims=True)
        score_grad = (probs * (prob_grad - inner)).astype(BF)
        query_grad = dot(score_grad, keys) * HD ** (-0.5)
        grads_out[:, at] = turn(query_grad, cosines, sines).astype(BF)
        key_grad = key_grad + t_dot(score_grad, queries)
        value_grad = value_grad + t_dot(probs.astype(BF), o_grad)
    grads_out[:, 384:512] = turn(key_grad * HD ** (-0.5), cosines, sines).astype(BF)
    grads_out[:, 512:] = value_grad.astype(BF)
    grads = grads_out[...]
    sums_out[...] = jnp.sum(grads.astype(F32), axis=0, keepdims=True)
    parted(dot_t(grads, w[:, :640]), keep, give)


def blocks_of(row, size):
    count = row.shape[1] // size
    at = lax.broadcasted_iota(jnp.int32, (count, row.shape[1]), 1)
    owner = lax.broadcasted_iota(jnp.int32, (count, row.shape[1]), 0)
    mine = (at >= owner * size) & (at < (owner + 1) * size)
    values = jnp.where(mine, row, 0.0).astype(BF)
    at = lax.broadcasted_iota(jnp.int32, (row.shape[1], HD), 0)
    lane = lax.broadcasted_iota(jnp.int32, (row.shape[1], HD), 1)
    return dot(values, (lax.rem(at, size) == lane).astype(BF))


def gradient_rows(*refs, buffer, right, out):
    rows = refs
    size = rows[0].shape[0]
    for i, part in enumerate(rows):
        buffer[i * size : (i + 1) * size] = part[...]
    half = buffer.shape[1] // 2
    for i in range(2):
        grad = t_dot(buffer[:, i * half : (i + 1) * half], right[...]).astype(BF)
        out[16 * i : 16 * (i + 1), :, : right.shape[1]] = grad.reshape(
            16, half // 16, right.shape[1]
        )


def o_grad_body(*refs):
    *rows, right, out, buffer = refs
    gradient_rows(*rows, buffer=buffer, right=right, out=out)


def qkv_grad_body(rows, right, gain_attn, gain_mlp, sums, ranks, out, buffer):
    gradient_rows(rows, buffer=buffer, right=right, out=out)
    rank = ranks[0:1, 0:1]
    parts = [jnp.where(rank == i, sums[:, :384], 0.0) for i in range(4)]
    for start in (384, 512):
        for i in range(2):
            mine = (rank >= 2 * i) & (rank < 2 * i + 2)
            parts.append(jnp.where(mine, sums[:, start : start + HD], 0.0))
    rows_of = (
        blocks_of(gain_attn[...], 48),
        blocks_of(gain_mlp[...], 48),
        blocks_of(jnp.concatenate(parts[:6], axis=1), 56),
        blocks_of(jnp.concatenate(parts[6:], axis=1), 8),
    )
    at = lax.broadcasted_iota(jnp.int32, (32, out.shape[1], HD), 1)
    tail = jnp.zeros((32, out.shape[1], HD), F32)
    for i, values in enumerate(rows_of):
        tail = jnp.where(at == i, values[:, None, :], tail)
    out[:, :, 640:] = tail.astype(BF)


def rows_product(body, rows, right, extra, columns, name, order):
    width = rows[0].shape[1]
    total = sum(part.shape[0] for part in rows)
    return vmem_call(
        body,
        [((32, width // 32, columns), BF)],
        [*rows, right, *extra],
        name,
        order,
        [pltpu.VMEM((total, width), BF)],
        limit=32,
        flops=2 * total * width * columns,
        moved=2 * (total * width + total * columns + width * columns),
    )[0]


def shards(
    layer_input,
    q_weight,
    kv_weight,
    o_weight,
    norm_gains,
    qkv_bias,
    gate_up,
    down_weight,
    cotangent,
    lengths,
):
    zh, zl, core = (lax.axis_index(a) for a in ("zh", "zl", "core"))
    rank = 2 * zl + core
    width = layer_input.shape[1]
    rows = layer_input.shape[0]

    small = jnp.concatenate([norm_gains.reshape(-1), qkv_bias, jnp.zeros((216,), BF)])
    vectors = jnp.concatenate([kv_weight.reshape(24, 256), small[None], jnp.zeros((7, 256), BF)])
    got = swap(vectors, "core")
    both = jnp.stack([pick(core, vectors, got), pick(core, got, vectors)])
    small_keep = both[:, 24].reshape(2, 2, HD)
    kv_keep = pick(zl, both[:, :24, :HD], both[:, :24, HD:])
    kv_give = pick(zl, both[:, :24, HD:], both[:, :24, :HD])
    got = swap(jnp.concatenate([kv_give, small_keep, jnp.zeros((2, 6, HD), BF)], axis=1), "zl")
    kv_got, small_got = got[:, :24], got[:, 24:26]
    kv_rows = jnp.stack([pick(zl, kv_keep, kv_got), pick(zl, kv_got, kv_keep)])
    kv_rows = kv_rows.reshape(2, 2, 2, 12, HD).transpose(0, 1, 3, 2, 4).reshape(48, 2 * HD)
    small = jnp.stack([pick(zl, small_keep, small_got), pick(zl, small_got, small_keep)])
    small = small.reshape(4, 256)
    gains_row = jnp.concatenate([small[:, :12].reshape(48), small[:, 12:24].reshape(48)])
    bias_row = small[:, 24:40].reshape(64)
    small = jnp.zeros((48, HD), BF).at[0, :96].set(gains_row).at[1, :64].set(bias_row)

    ends = jnp.cumsum(lengths[0])
    ranks = jnp.stack([rank, 2 * zl + 1 - core, 2 * (1 - zl) + core, 2 * (1 - zl) + 1 - core])
    group = 4 * rows
    places = (ranks[:, None] * rows + jnp.arange(rows, dtype=jnp.int32)[None, :]).reshape(group)
    passed = ends[None, :] <= places[:, None]
    starts = jnp.sum(jnp.where(passed, lengths[0][None, :], 0), axis=1)
    inverse = THETA ** (-(2.0 * jnp.arange(HD // 2, dtype=F32)) / HD)
    inverse = jnp.concatenate([inverse, inverse])[None, :]
    angles = (places - starts).astype(F32)[:, None] * inverse
    sign = jnp.where(jnp.arange(HD) < HD // 2, -1.0, 1.0).astype(F32)[None, :]
    lane = jnp.arange(HD)[None, :]
    ranges = jnp.where(lane == 0, starts[:, None], places[:, None]).astype(F32)
    table = jnp.concatenate([jnp.cos(angles), jnp.sin(angles) * sign, ranges], axis=1)
    tables = (table, jnp.broadcast_to(places.astype(F32)[None, :], (8, group)))

    living = (places[:rows] < ends[-1])[:, None]
    cot_local = jnp.where(living, cotangent, jnp.zeros((), BF))
    cot_groups = token_groups(cot_local)

    across = swap(layer_input, "zl")
    group_inputs = (layer_input, swap(layer_input, "core"), across, swap(across, "core"))

    attn_part = jnp.concatenate([q_weight, kv_rows, small, o_weight.T], axis=-1)
    attn_plane = exchange(copies(attn_part, 16), PLANE)
    qkv_plane, o_plane = attn_plane[..., :768], attn_plane[..., 768:]
    qkv_other = swap(qkv_plane, "zh")
    o_other = swap(o_plane, "zh")
    waits = (cot_groups[1][1], cot_groups[2][1], group_inputs[3], *tables)
    qkv_full = ordered(qkv_plane, qkv_other, zh, "qkv_weights", waits)
    small = qkv_full[:, :, :2, 640:].reshape(32, 2, HD)
    qkv_full = qkv_full.reshape(width, 768)
    gain_attn, gain_mlp, bias = vmem_call(
        vectors_body,
        [((8, width), F32), ((8, width), F32), ((8, 640), F32)],
        [small[:, 0], small[:, 1], jnp.full((8, HD), rank, jnp.int32)],
        "gains_and_biases",
        limit=16,
    )

    mlp = jnp.concatenate([gate_up, down_weight.T[None]], axis=0)
    mlp = jnp.pad(mlp, ((0, 0), (0, 0), (0, 2 * HALF - mlp.shape[2])))
    mlp_own = pick(zh, mlp[..., :HALF], mlp[..., HALF:])
    mlp_other = swap(pick(zh, mlp[..., HALF:], mlp[..., :HALF]), "zh")
    mlp = vmem_call(
        arrange_body,
        [((6, 48, HALF), BF)],
        [mlp_own, mlp_other, jnp.full((8, HD), zh, jnp.int32)],
        "arranged",
        moved=4 * mlp_own.size,
    )[0]
    mlp = lax.all_gather(mlp, PLANE, axis=1, tiled=True)
    mlp = mlp.reshape(3, width, HALF)

    normed_group, queries, kv_rot, attended, lse = vmem_call(
        attn_forward_body,
        [
            ((group, width), BF),
            ((group, 384), BF),
            ((group, 256), BF),
            ((group, 384), BF),
            ((group, 128), F32),
        ],
        [*group_inputs, gain_attn, qkv_full, bias, *tables],
        "attention_forward",
        limit=32,
        flops=2 * group * (width * 640 + 6 * group * HD),
        moved=2 * group * width * 2 + 2 * width * 768,
    )
    o_full = ordered(o_plane, o_other, zh, "o_weights", (attended,)).reshape(width, 384)
    pair = ((2, rows, width), BF)
    keep, give = vmem_call(
        attn_out_body,
        [pair, pair],
        [attended, o_full],
        "attention_out",
        flops=2 * group * width * 384,
        moved=2 * width * 384 + 2 * group * width,
    )
    got = swap(give, "core")
    residual, normed_mlp = vmem_call(
        residual_body,
        [((rows, width), F32), ((rows, width), BF)],
        [layer_input, keep, got, swap(add(keep[1], got[1]), "zl"), gain_mlp],
        "residual_norm",
        moved=10 * rows * width,
    )

    after_rows, before_rows = z_shift(normed_mlp, -1), z_shift(normed_mlp, 1)
    far_rows = z_shift(normed_mlp, 2)
    own = (normed_mlp, swap(normed_mlp, "core"))
    own_out = ff_rows(own, cot_groups[0], mlp, cot_local)
    near = stacked((after_rows, before_rows), own_out[0])
    near = (near, swap(near, "core"))
    near_out = ff_rows(near, cot_groups[1], mlp, own_out[0])
    far_rows = stacked((far_rows,), near_out[0])
    far = (far_rows, swap(far_rows, "core"))
    near_sum = [
        add(mine, swap(others, "core"))
        for mine, others in zip(halves(near_out[3], 0), halves(near_out[4], 0))
    ]
    near_got = (z_shift(near_sum[0], 1), z_shift(near_sum[1], -1))
    far_out = ff_rows(far, cot_groups[2], mlp, near_sum[1])
    far_sum = add(far_out[3], swap(far_out[4], "core"))
    own_got = swap(own_out[4], "core")
    far_got = z_shift(far_sum, 2)
    results = (own_out, near_out, far_out)
    hidden, gate_grads, up_grads = ([r[i] for r in results] for i in range(3))
    flat_normed = [*own, *near, *far]
    flat_cots = [part for pair in cot_groups for part in pair]
    mlp_grads = weight_grads(flat_normed, flat_cots, hidden, gate_grads, up_grads, far_sum)
    residual_grad, branch, gain_mlp_grad = vmem_call(
        ff_back_body,
        [((rows, width), F32), ((rows, width), BF), ((1, width), F32)],
        [own_out[3], own_got, *near_got, far_got, residual, cot_local, gain_mlp],
        "residual_gradient",
        (mlp_grads,),
        flops=10**9 * WEIGHT,
        moved=24 * rows * width,
    )
    mlp_grads = lax.psum_scatter(
        mlp_grads.reshape(6, width // 2, HALF), PLANE, scatter_dimension=1, tiled=True
    ).reshape(3, 2, 48, HALF)
    own_grads = lax.dynamic_index_in_dim(mlp_grads, zh, 1, keepdims=False)
    other_grads = swap(lax.dynamic_index_in_dim(mlp_grads, 1 - zh, 1, keepdims=False), "zh")
    own_grads, other_grads = own_grads.astype(F32), other_grads.astype(F32)
    mlp_shard = jnp.concatenate(
        [pick(zh, own_grads, other_grads), pick(zh, other_grads, own_grads)], axis=-1
    )[..., : gate_up.shape[2]]
    gate_up_shard = mlp_shard[:2]
    down_shard = mlp_shard[2].T

    out_pairs = down_rows(hidden, mlp, branch)
    layer_output = (residual + token_sums(out_pairs)).astype(BF)

    across = stacked((swap(branch, "zl"),), out_pairs[0][0])
    branch_group = (branch, swap(branch, "core"), across, swap(across, "core"))
    o_terms = rows_product(
        o_grad_body, branch_group, attended, (), 384, "o_weight_gradient", ()
    )
    o_got = exchange(o_terms, DATA)
    qkv_grad, keep, give, sums = vmem_call(
        attn_backward_body,
        [((group, 640), BF), pair, pair, ((1, 640), F32)],
        [*branch_group, o_full, qkv_full, queries, kv_rot, lse, *tables],
        "attention_backward",
        (o_terms,),
        limit=32,
        scratch=[pltpu.VMEM((group, width), BF)],
        flops=2 * group * (width * 1024 + 15 * group * HD),
        moved=4 * group * width + 2 * width * 1024,
    )
    got = [swap(give[i], "core") for i in range(2)]
    other = stacked((add(keep[1], got[1]),), o_got)
    input_grad, gain_attn_grad = vmem_call(
        attn_back_body,
        [((rows, width), F32), ((1, width), F32)],
        [keep, got[0], swap(other, "zl"), layer_input, residual_grad, gain_attn],
        "input_gradient",
        moved=20 * rows * width,
    )

    qkv_terms = rows_product(
        qkv_grad_body,
        (normed_group,),
        qkv_grad,
        (gain_attn_grad, gain_mlp_grad, sums, jnp.full((8, HD), rank, jnp.int32)),
        768,
        "qkv_weight_gradient",
        (o_got,),
    )
    o_shard = jnp.sum(o_got.astype(F32), axis=0).T
    attn_shard = jnp.sum(exchange(qkv_terms, DATA).astype(F32), axis=0)
    q_shard = attn_shard[:, :384]
    kv_sum = attn_shard[:, 384:640].reshape(2, 2, 12, 2, HD)
    kv_keep = lax.dynamic_index_in_dim(kv_sum, core, 1, keepdims=False).reshape(48, HD)
    kv_give = lax.dynamic_index_in_dim(kv_sum, 1 - core, 1, keepdims=False).reshape(48, HD)
    vectors = attn_shard[:8, 640:]
    got = swap(jnp.concatenate([kv_give, vectors]), "core")
    kv_sum = (kv_keep + got[:48]).reshape(2, 24, HD)
    vectors = vectors + got[48:]
    kv_keep = pick(zl, kv_sum[0], kv_sum[1])
    got = swap(jnp.concatenate([pick(zl, kv_sum[1], kv_sum[0]), vectors]), "zl")
    kv_got = got[:24]
    vectors = vectors + got[24:]
    kv_shard = jnp.concatenate([pick(zl, kv_keep, kv_got), pick(zl, kv_got, kv_keep)], axis=-1)
    kv_shard = kv_shard.reshape(12, 2, 2 * HD).transpose(1, 0, 2)

    def own_part(row, size):
        return lax.dynamic_index_in_dim(
            vectors[row, : 4 * size].reshape(4, size), rank, 0, keepdims=False
        )

    return (
        layer_output,
        input_grad,
        q_shard,
        kv_shard,
        o_shard,
        jnp.stack([own_part(0, 12), own_part(1, 12)]),
        own_part(2, 14),
        own_part(3, 2),
        gate_up_shard,
        down_shard,
    )


def solution(mesh):
    fine = Mesh(mesh.devices.reshape(SIZES), AXES)
    dp = ("zh", "y", "x")
    tensor = ("zl", "core")
    every = dp + tensor
    in_specs = (
        P(every, None),
        P(dp, tensor),
        P(None, every, None),
        P(tensor, dp),
        P(None, every),
        P(every),
        P(None, dp, tensor),
        P(tensor, dp),
        P(every, None),
        P(dp, None),
    )
    out_specs = (
        P(every, None),
        P(every, None),
        P(dp, tensor),
        P(None, every, None),
        P(tensor, dp),
        P(None, every),
        P(every),
        P(every),
        P(None, dp, tensor),
        P(tensor, dp),
    )
    return jax.shard_map(shards, mesh=fine, in_specs=in_specs, out_specs=out_specs, check_vma=False)
```

```python
import functools

import jax
import jax.numpy as jnp
from jax import lax
from jax.experimental import pallas as pl
from jax.experimental.pallas import tpu as pltpu
from jax.sharding import Mesh, PartitionSpec as P

HQ = 12
KVH = 2
HD = 128
EPSILON = 1e-06
THETA = 1000000.0

AXES = ("zh", "y", "x", "zl", "core")
SIZES = (2, 4, 4, 2, 2)
ZRING = ("zh", "zl")
PLANE = ("y", "x")
DATA = ("zh", "y", "x")
HALF = 1152
BF = jnp.bfloat16
WEIGHT = 1000
F32 = jnp.float32


def swap(block, axis):
    return lax.ppermute(block, axis, [(0, 1), (1, 0)])


def halves(block, dim):
    middle = block.shape[dim] // 2
    return (
        lax.slice_in_dim(block, 0, middle, axis=dim),
        lax.slice_in_dim(block, middle, block.shape[dim], axis=dim),
    )


def add(*terms):
    total = terms[0].astype(F32)
    for term in terms[1:]:
        total = total + term.astype(F32)
    return total.astype(terms[0].dtype)


def exchange(blocks, axes):
    return lax.all_to_all(blocks, axes, split_axis=0, concat_axis=0, tiled=True)


def spread(block, axes, count):
    return exchange(jnp.broadcast_to(block[None], (count,) + block.shape), axes)


def z_shift(block, by):
    return lax.ppermute(block, ZRING, [(i, (i + by) % 4) for i in range(4)])


def token_groups(block):
    near = jnp.concatenate([z_shift(block, -1), z_shift(block, 1)], axis=0)
    far = z_shift(block, 2)
    return [(part, swap(part, "core")) for part in (block, near, far)]


def token_sums(pairs):
    own, near, far = (add(mine, swap(others, "core")) for mine, others in pairs)
    after_rows, before_rows = halves(near, 0)
    terms = (own, z_shift(after_rows, 1), z_shift(before_rows, -1), z_shift(far, 2))
    return sum(term.astype(F32) for term in terms)


def ff_body(
    na, nb, ca, cb, w, _, m_out, dg_out, du_out, dna_out, dnb_out,
    wbuf, nbuf, cbuf, wsem, nsem, csem, *, tile,
):
    half = na.shape[0]
    weights = [pltpu.make_async_copy(w.at[i], wbuf.at[i], wsem.at[i]) for i in range(3)]
    normed = [
        pltpu.make_async_copy(part, nbuf.at[pl.ds(k * half, half)], nsem.at[k])
        for k, part in enumerate((na, nb))
    ]
    cots = [
        pltpu.make_async_copy(part, cbuf.at[pl.ds(k * half, half)], csem.at[k])
        for k, part in enumerate((ca, cb))
    ]
    for copy in normed + weights[:2] + cots + weights[2:]:
        copy.start()
    for copy in normed + weights[:1]:
        copy.wait()
    tiles = 2 * half // tile
    for i in range(tiles):
        at = pl.ds(i * tile, tile)
        rows = nbuf[at]
        gate = dot(rows, wbuf[0])
        if i == 0:
            weights[1].wait()
        up = dot(rows, wbuf[1])
        if i == 0:
            for copy in cots + weights[2:]:
                copy.wait()
        hidden_grad = dot(cbuf[at], wbuf[2])
        sigma = 1.0 / (1.0 + jnp.exp(-gate))
        act = gate * sigma
        m_out[at] = (act * up).astype(BF)
        up_grad = (hidden_grad * act).astype(BF)
        gate_grad = (hidden_grad * up * sigma * (1.0 + gate * (1.0 - sigma))).astype(BF)
        dg_out[at] = gate_grad
        du_out[at] = up_grad
        back = (dot_t(gate_grad, wbuf[0]) + dot_t(up_grad, wbuf[1])).astype(BF)
        if tiles == 1:
            dna_out[...] = back[:half]
            dnb_out[...] = back[half:]
        else:
            out = dna_out if i < tiles // 2 else dnb_out
            out[pl.ds(i % (tiles // 2) * tile, tile)] = back


def ff_rows(normed, cots, weights, order, tile=256):
    half, width = normed[0].shape
    units = weights.shape[2]
    anywhere = pl.BlockSpec(memory_space=pl.ANY)
    vmem = pl.BlockSpec(memory_space=pltpu.VMEM)
    return pl.pallas_call(
        functools.partial(ff_body, tile=tile),
        out_shape=[jax.ShapeDtypeStruct((2 * half, units), BF)] * 3
        + [jax.ShapeDtypeStruct((half, width), BF)] * 2,
        in_specs=[anywhere] * 6,
        out_specs=[vmem] * 5,
        scratch_shapes=[
            pltpu.VMEM((3, width, units), BF),
            pltpu.VMEM((2 * half, width), BF),
            pltpu.VMEM((2 * half, width), BF),
            pltpu.SemaphoreType.DMA((3,)),
            pltpu.SemaphoreType.DMA((2,)),
            pltpu.SemaphoreType.DMA((2,)),
        ],
        compiler_params=pltpu.CompilerParams(vmem_limit_bytes=48 * 1024 * 1024),
        cost_estimate=pl.CostEstimate(
            flops=20 * half * width * units,
            bytes_accessed=6 * width * units,
            transcendentals=2 * half * units,
        ),
        name="feed_forward_rows",
    )(*normed, *cots, weights, order)


def wg_body(*refs, sizes, tile):
    count = len(sizes)
    groups = count // 2
    normed, cots, refs = refs[:count], refs[count : 2 * count], refs[2 * count :]
    hidden, gates, ups = refs[:groups], refs[groups : 2 * groups], refs[2 * groups : 3 * groups]
    out, nbuf, cbuf, mbuf, gbuf, ubuf, sem = refs[3 * groups + 1 :]
    pair_sizes = [sizes[2 * i] + sizes[2 * i + 1] for i in range(groups)]

    def copies(at, buffer, sources, lengths):
        result, start = [], 0
        for source, length in zip(sources, lengths):
            target = buffer.at[pl.ds(start, length)]
            result.append(pltpu.make_async_copy(source, target, sem.at[at]))
            start += length
        return result

    def normed_copies():
        return copies(0, nbuf, normed, sizes)

    def cot_copies():
        return copies(1, cbuf, cots, sizes)

    def gate_copies():
        return copies(2, gbuf, gates, pair_sizes)

    def up_copies():
        return copies(3, ubuf, ups, pair_sizes)

    def hidden_copies():
        return copies(4, mbuf, hidden, pair_sizes)

    which, step = pl.program_id(0), pl.program_id(1)

    @pl.when((which == 0) & (step == 0))
    def _():
        first = normed_copies() + gate_copies()
        for copy in first + up_copies() + cot_copies() + hidden_copies():
            copy.start()
        for copy in first:
            copy.wait()

    @pl.when((which == 1) & (step == 0))
    def _():
        for copy in up_copies():
            copy.wait()

    @pl.when((which == 2) & (step == 0))
    def _():
        for copy in cot_copies() + hidden_copies():
            copy.wait()

    columns = pl.ds(pl.multiple_of(step * tile, tile), tile)
    for i, (left, right) in enumerate(((nbuf, gbuf), (nbuf, ubuf), (cbuf, mbuf))):

        @pl.when(which == i)
        def _():
            out[...] = t_dot(left[:, columns], right[...]).astype(BF)


def weight_grads(normed, cots, hidden, gates, ups, order, tile=768):
    sizes = tuple(part.shape[0] for part in normed)
    rows, width, units = sum(sizes), normed[0].shape[1], hidden[0].shape[1]
    anywhere = pl.BlockSpec(memory_space=pl.ANY)
    return pl.pallas_call(
        functools.partial(wg_body, sizes=sizes, tile=tile),
        grid=(3, width // tile),
        out_shape=jax.ShapeDtypeStruct((3, width, units), BF),
        in_specs=[anywhere] * (2 * len(normed) + 3 * len(hidden) + 1),
        out_specs=pl.BlockSpec((None, tile, units), lambda i, j: (i, j, 0)),
        scratch_shapes=[pltpu.VMEM((rows, width), BF)] * 2
        + [pltpu.VMEM((rows, units), BF)] * 3
        + [pltpu.SemaphoreType.DMA((5,))],
        compiler_params=pltpu.CompilerParams(vmem_limit_bytes=48 * 1024 * 1024),
        cost_estimate=pl.CostEstimate(
            flops=6 * rows * width * units,
            bytes_accessed=6 * width * units + rows * (4 * width + 6 * units),
            transcendentals=0,
        ),
        name="weight_gradients",
    )(*normed, *cots, *hidden, *gates, *ups, order)


def down_body(ha, hb, hc, w, *outs, tile=256):
    for group, hidden in enumerate((ha, hb, hc)):
        half = hidden.shape[0] // 2
        step = min(tile, 2 * half)
        for start in range(0, 2 * half, step):
            part = dot_t(hidden[pl.ds(start, step)], w[...]).astype(BF)
            if step > half:
                outs[2 * group][...] = part[:half]
                outs[2 * group + 1][...] = part[half:]
            else:
                outs[2 * group + start // half][pl.ds(start % half, step)] = part


def down_rows(hidden, weights, order):
    _, width, units = weights.shape
    halved = [part.shape[0] // 2 for part in hidden for _ in range(2)]
    outs = vmem_call(
        down_body,
        [((rows, width), BF) for rows in halved],
        [*hidden, (weights, 2)],
        "down_rows",
        (order,),
        limit=32,
        flops=2 * sum(halved) * width * units,
        moved=2 * width * units + 2 * sum(halved) * (width + units),
    )
    return [(outs[0], outs[1]), (outs[2], outs[3]), (outs[4], outs[5])]


def dot(a, b):
    return jnp.dot(a, b, preferred_element_type=F32)


def dot_t(a, b):
    return lax.dot_general(a, b, (((1,), (1,)), ((), ())), preferred_element_type=F32)


def t_dot(a, b):
    return lax.dot_general(a, b, (((0,), (0,)), ((), ())), preferred_element_type=F32)


def pick(index, low, high):
    return jnp.where(index == 0, low, high)


def vmem_call(body, outs, ins, name, order=(), scratch=(), limit=16, flops=0, moved=0):
    count, skipped, results, extra = len(ins), len(order), len(outs), len(scratch)
    parts = [value[1] if isinstance(value, tuple) else None for value in ins]
    ins = [value[0] if isinstance(value, tuple) else value for value in ins]

    def kernel(*refs):
        sources, refs = refs[:count], refs[count + skipped :]
        fixed, buffers, sem = refs[: results + extra], refs[results + extra : -1], refs[-1]
        fetches = [
            pltpu.make_async_copy(source if at is None else source.at[at], buffer, sem.at[i])
            for i, (source, at, buffer) in enumerate(zip(sources, parts, buffers))
        ]
        for fetch in fetches:
            fetch.start()
        for fetch in fetches:
            fetch.wait()
        body(*buffers, *fixed)

    return pl.pallas_call(
        kernel,
        out_shape=[jax.ShapeDtypeStruct(shape, dtype) for shape, dtype in outs],
        in_specs=[pl.BlockSpec(memory_space=pl.ANY)] * (count + skipped),
        out_specs=[pl.BlockSpec(memory_space=pltpu.VMEM)] * results,
        scratch_shapes=[
            *scratch,
            *(
                pltpu.VMEM(value.shape if at is None else value.shape[1:], value.dtype)
                for value, at in zip(ins, parts)
            ),
            pltpu.SemaphoreType.DMA((count,)),
        ],
        compiler_params=pltpu.CompilerParams(vmem_limit_bytes=limit * 1024 * 1024),
        cost_estimate=pl.CostEstimate(flops=flops, bytes_accessed=moved, transcendentals=0),
        name=name,
    )(*ins, *order)


def copies_body(block, out):
    for i in range(out.shape[0]):
        out[i] = block[...]


def copies(block, count, *order):
    shape = (count,) + block.shape
    moved = 2 * count * block.size
    return vmem_call(
        copies_body, [(shape, block.dtype)], [block], "copies", order, moved=moved
    )[0]


def arrange_body(own, other, zh, out):
    mine = zh[0:1, 0:1] == 0
    for i in range(3):
        out[2 * i] = jnp.where(mine, own[i], other[i])
        out[2 * i + 1] = jnp.where(mine, other[i], own[i])


def ordered_body(own, other, zh, out):
    mine = zh[0:1, 0:1] == 0
    for i in range(own.shape[0]):
        out[0, i] = jnp.where(mine, own[i], other[i])
        out[1, i] = jnp.where(mine, other[i], own[i])


def ordered(own, other, zh, name, order):
    flag = jnp.full((8, HD), zh, jnp.int32)
    shape = (2,) + own.shape
    return vmem_call(
        ordered_body, [(shape, BF)], [own, other, flag], name, order, moved=8 * own.size
    )[0]


def sum_body(terms, out):
    total = terms[0].astype(F32)
    for i in range(1, terms.shape[0]):
        total = total + terms[i].astype(F32)
    out[...] = total


def summed(terms, order):
    return vmem_call(
        sum_body, [(terms.shape[1:], F32)], [terms], "summed", order, moved=2 * terms.size
    )[0]


def stack_body(*refs):
    *parts, out = refs
    rows = parts[0].shape[0]
    for i, part in enumerate(parts):
        out[i * rows : (i + 1) * rows] = part[...]


def stacked(parts, *order):
    rows, columns = parts[0].shape
    shape = (len(parts) * rows, columns)
    moved = 4 * shape[0] * columns
    return vmem_call(stack_body, [(shape, BF)], list(parts), "stacked", order, moved=moved)[0]


def row_of(blocks, offset, size):
    count, lanes = blocks.shape
    line = (lanes, count * size)
    at = lax.broadcasted_iota(jnp.int32, line, 1)
    from_lane = lax.broadcasted_iota(jnp.int32, line, 0) - offset
    spots = (lax.rem(at, size) == from_lane).astype(BF)
    values = dot(blocks, spots)
    at = lax.broadcasted_iota(jnp.int32, values.shape, 1)
    owner = lax.broadcasted_iota(jnp.int32, values.shape, 0)
    mine = (at >= owner * size) & (at < (owner + 1) * size)
    return jnp.sum(jnp.where(mine, values, 0.0), axis=0, keepdims=True)


def vectors_body(gains, biases, ranks, attn_out, mlp_out, bias_out):
    attn_out[...] = jnp.broadcast_to(row_of(gains[...], 0, 48), attn_out.shape)
    mlp_out[...] = jnp.broadcast_to(row_of(gains[...], 48, 48), mlp_out.shape)
    full = row_of(biases[...], 0, 64)
    rank = ranks[0:1, 0:1]
    query = key = value = 0.0
    for i in range(4):
        query = query + jnp.where(rank == i, full[:, 384 * i : 384 * (i + 1)], 0.0)
    for i in range(2):
        mine = (rank >= 2 * i) & (rank < 2 * i + 2)
        key = key + jnp.where(mine, full[:, 1536 + HD * i : 1536 + HD * (i + 1)], 0.0)
        value = value + jnp.where(mine, full[:, 1792 + HD * i : 1792 + HD * (i + 1)], 0.0)
    line = jnp.concatenate([query, key, value], axis=1)
    bias_out[...] = jnp.broadcast_to(line, bias_out.shape)


def turn(vectors, cos2, sin2):
    return vectors * cos2 + pltpu.roll(vectors, HD // 2, 1) * sin2


def unpack_table(table, places):
    first, last = table[:, 2 * HD : 2 * HD + 1], table[:, 2 * HD + 1 : 2 * HD + 2]
    keys = places[0:1, :]
    return table[:, :HD], table[:, HD : 2 * HD], (keys >= first) & (keys <= last)


def masked_scores(queries, keys, allowed):
    return jnp.where(allowed, dot_t(queries, keys) * HD ** (-0.5), -1e30)


def attn_forward_body(
    x0, x1, x2, x3, gain, w, bias, table, places,
    n_out, q_out, kv_out, o_out, lse_out,
):
    rows = x0.shape[0]
    for i, x in enumerate((x0, x1, x2, x3)):
        part = x[...].astype(F32)
        scale = lax.rsqrt(jnp.mean(part * part, axis=-1, keepdims=True) + EPSILON)
        n_out[i * rows : (i + 1) * rows] = (part * scale * gain[0:1]).astype(BF)
    qkv = dot(n_out[...], w[:, :640]) + bias[0:1]
    cosines, sines, allowed = unpack_table(table, places)
    keys = turn(qkv[:, 384:512], cosines, sines).astype(BF)
    values = qkv[:, 512:].astype(BF)
    kv_out[:, :HD] = keys
    kv_out[:, HD:] = values
    lses = []
    for h in range(3):
        at = slice(h * HD, (h + 1) * HD)
        queries = turn(qkv[:, at], cosines, sines).astype(BF)
        q_out[:, at] = queries
        scores = masked_scores(queries, keys, allowed)
        peak = jnp.max(scores, axis=-1, keepdims=True)
        shifted = jnp.exp(scores - peak)
        total = jnp.sum(shifted, axis=-1, keepdims=True)
        probs = (shifted / total).astype(BF)
        o_out[:, at] = dot(probs, values).astype(BF)
        lses.append(peak + jnp.log(total))
    lse_out[...] = jnp.concatenate(lses + [jnp.zeros((4 * rows, 125), F32)], axis=1)


def parted(partial, keep, give):
    rows = partial.shape[0] // 4
    keep[0] = partial[:rows].astype(BF)
    give[0] = partial[rows : 2 * rows].astype(BF)
    keep[1] = partial[2 * rows : 3 * rows].astype(BF)
    give[1] = partial[3 * rows :].astype(BF)


def attn_out_body(o, w, keep, give):
    parted(dot_t(o[...], w[...]), keep, give)


def residual_body(x, keep, got, across, gain, h_out, n_out):
    h = x[...].astype(F32) + keep[0].astype(F32) + got[0].astype(F32) + across[...].astype(F32)
    h_out[...] = h
    scale = lax.rsqrt(jnp.mean(h * h, axis=-1, keepdims=True) + EPSILON)
    n_out[...] = (h * scale * gain[0:1]).astype(BF)


def norm_backward(grad, rows, gain):
    scale = lax.rsqrt(jnp.mean(rows * rows, axis=-1, keepdims=True) + EPSILON)
    scaled = grad * gain
    back = scale * scaled - rows * scale**3 * jnp.mean(scaled * rows, axis=-1, keepdims=True)
    return back, jnp.sum(grad * rows * scale, axis=0, keepdims=True)


def ff_back_body(own_a, own_b, got_a, got_b, got_c, h, cot, gain, grad_out, branch_out, gain_out):
    grad = sum(part[...].astype(F32) for part in (own_a, own_b, got_a, got_b, got_c))
    back, gain_out[...] = norm_backward(grad, h[...], gain[0:1])
    total = cot[...].astype(F32) + back
    grad_out[...] = total
    branch_out[...] = total.astype(BF)


def attn_back_body(keep, got, across, x, above, gain, grad_out):
    grad = keep[0].astype(F32) + got[0].astype(F32) + across[...].astype(F32)
    back, _ = norm_backward(grad, x[...].astype(F32), gain[0:1])
    grad_out[...] = above[...] + back


def attn_backward_body(
    b0, b1, b2, b3, x0, x1, x2, x3, wo, w, q, kv, lse, table, places,
    grads_out, keep, give, sums_out, gain_out, bbuf,
):
    rows = b0.shape[0]
    for i, part in enumerate((b0, b1, b2, b3)):
        bbuf[i * rows : (i + 1) * rows] = part[...]
    attended_grad = dot(bbuf[...], wo[...]).astype(BF)
    keys, values = kv[:, :HD], kv[:, HD:]
    cosines, sines, allowed = unpack_table(table, places)
    sines = -sines
    key_grad = value_grad = 0.0
    for h in range(3):
        at = slice(h * HD, (h + 1) * HD)
        queries, o_grad = q[:, at], attended_grad[:, at]
        probs = jnp.exp(masked_scores(queries, keys, allowed) - lse[:, h : h + 1])
        prob_grad = dot_t(o_grad, values)
        inner = jnp.sum(probs * prob_grad, axis=-1, keepdims=True)
        score_grad = (probs * (prob_grad - inner)).astype(BF)
        query_grad = dot(score_grad, keys) * HD ** (-0.5)
        grads_out[:, at] = turn(query_grad, cosines, sines).astype(BF)
        key_grad = key_grad + t_dot(score_grad, queries)
        value_grad = value_grad + t_dot(probs.astype(BF), o_grad)
    grads_out[:, 384:512] = turn(key_grad * HD ** (-0.5), cosines, sines).astype(BF)
    grads_out[:, 512:] = value_grad.astype(BF)
    grads = grads_out[...]
    sums_out[...] = jnp.sum(grads.astype(F32), axis=0, keepdims=True)
    partial = dot_t(grads, w[:, :640])
    parted(partial, keep, give)
    gain_grad = 0.0
    for i, x in enumerate((x0, x1, x2, x3)):
        part = x[...].astype(F32)
        scale = lax.rsqrt(jnp.mean(part * part, axis=-1, keepdims=True) + EPSILON)
        terms = partial[i * rows : (i + 1) * rows] * part * scale
        gain_grad = gain_grad + jnp.sum(terms, axis=0, keepdims=True)
    gain_out[...] = gain_grad


def blocks_of(row, size):
    count = row.shape[1] // size
    at = lax.broadcasted_iota(jnp.int32, (count, row.shape[1]), 1)
    owner = lax.broadcasted_iota(jnp.int32, (count, row.shape[1]), 0)
    mine = (at >= owner * size) & (at < (owner + 1) * size)
    values = jnp.where(mine, row, 0.0).astype(BF)
    at = lax.broadcasted_iota(jnp.int32, (row.shape[1], HD), 0)
    lane = lax.broadcasted_iota(jnp.int32, (row.shape[1], HD), 1)
    return dot(values, (lax.rem(at, size) == lane).astype(BF))


def attn_grads_body(
    normed, b0, b1, b2, b3, qkv_grad, attended, gain_attn, gain_mlp, sums, ranks, out, bbuf
):
    size = b0.shape[0]
    for i, part in enumerate((b0, b1, b2, b3)):
        bbuf[i * size : (i + 1) * size] = part[...]
    half = bbuf.shape[1] // 2
    for i in range(2):
        at, blocks = slice(i * half, (i + 1) * half), slice(16 * i, 16 * (i + 1))
        grad = t_dot(normed[:, at], qkv_grad[...]).astype(BF)
        out[blocks, :, :640] = grad.reshape(16, half // 16, 640)
        grad = t_dot(bbuf[:, at], attended[...]).astype(BF)
        out[blocks, :, 768:] = grad.reshape(16, half // 16, 384)
    rank = ranks[0:1, 0:1]
    parts = [jnp.where(rank == i, sums[:, :384], 0.0) for i in range(4)]
    for start in (384, 512):
        for i in range(2):
            mine = (rank >= 2 * i) & (rank < 2 * i + 2)
            parts.append(jnp.where(mine, sums[:, start : start + HD], 0.0))
    rows_of = (
        blocks_of(gain_attn[...], 48),
        blocks_of(gain_mlp[...], 48),
        blocks_of(jnp.concatenate(parts[:6], axis=1), 56),
        blocks_of(jnp.concatenate(parts[6:], axis=1), 8),
    )
    at = lax.broadcasted_iota(jnp.int32, (32, out.shape[1], HD), 1)
    tail = jnp.zeros((32, out.shape[1], HD), F32)
    for i, values in enumerate(rows_of):
        tail = jnp.where(at == i, values[:, None, :], tail)
    out[:, :, 640:768] = tail.astype(BF)


def shards(
    layer_input,
    q_weight,
    kv_weight,
    o_weight,
    norm_gains,
    qkv_bias,
    gate_up,
    down_weight,
    cotangent,
    lengths,
):
    zh, zl, core = (lax.axis_index(a) for a in ("zh", "zl", "core"))
    rank = 2 * zl + core
    width = layer_input.shape[1]
    rows = layer_input.shape[0]

    small = jnp.concatenate([norm_gains.reshape(-1), qkv_bias, jnp.zeros((216,), BF)])
    vectors = jnp.concatenate([kv_weight.reshape(24, 256), small[None], jnp.zeros((7, 256), BF)])
    got = swap(vectors, "core")
    both = jnp.stack([pick(core, vectors, got), pick(core, got, vectors)])
    small_keep = both[:, 24].reshape(2, 2, HD)
    kv_keep = pick(zl, both[:, :24, :HD], both[:, :24, HD:])
    kv_give = pick(zl, both[:, :24, HD:], both[:, :24, :HD])
    kv_crossed = swap(
        jnp.concatenate([kv_give, small_keep, jnp.zeros((2, 6, HD), BF)], axis=1), "zl"
    )
    kv_got, small_got = kv_crossed[:, :24], kv_crossed[:, 24:26]
    kv_rows = jnp.stack([pick(zl, kv_keep, kv_got), pick(zl, kv_got, kv_keep)])
    kv_rows = kv_rows.reshape(2, 2, 2, 12, HD).transpose(0, 1, 3, 2, 4).reshape(48, 2 * HD)
    small = jnp.stack([pick(zl, small_keep, small_got), pick(zl, small_got, small_keep)])
    small = small.reshape(4, 256)
    gains_row = jnp.concatenate([small[:, :12].reshape(48), small[:, 12:24].reshape(48)])
    bias_row = small[:, 24:40].reshape(64)
    small = jnp.zeros((48, HD), BF).at[0, :96].set(gains_row).at[1, :64].set(bias_row)

    ends = jnp.cumsum(lengths[0])
    ranks = jnp.stack([rank, 2 * zl + 1 - core, 2 * (1 - zl) + core, 2 * (1 - zl) + 1 - core])
    group = 4 * rows
    places = (ranks[:, None] * rows + jnp.arange(rows, dtype=jnp.int32)[None, :]).reshape(group)
    passed = ends[None, :] <= places[:, None]
    starts = jnp.sum(jnp.where(passed, lengths[0][None, :], 0), axis=1)
    inverse = THETA ** (-(2.0 * jnp.arange(HD // 2, dtype=F32)) / HD)
    inverse = jnp.concatenate([inverse, inverse])[None, :]
    angles = (places - starts).astype(F32)[:, None] * inverse
    sign = jnp.where(jnp.arange(HD) < HD // 2, -1.0, 1.0).astype(F32)[None, :]
    lane = jnp.arange(HD)[None, :]
    ranges = jnp.where(lane == 0, starts[:, None], places[:, None]).astype(F32)
    table = jnp.concatenate([jnp.cos(angles), jnp.sin(angles) * sign, ranges], axis=1)
    tables = (table, jnp.broadcast_to(places.astype(F32)[None, :], (8, group)))

    living = (places[:rows] < ends[-1])[:, None]
    cot_local = jnp.where(living, cotangent, jnp.zeros((), BF))
    cot_groups = token_groups(cot_local)

    across = swap(layer_input, "zl")
    group_inputs = (layer_input, swap(layer_input, "core"), across, swap(across, "core"))

    attn_part = jnp.concatenate([q_weight, kv_rows, small, o_weight.T], axis=-1)
    attn_plane = exchange(copies(attn_part, 16), PLANE)
    qkv_plane, o_plane = attn_plane[..., :768], attn_plane[..., 768:]
    qkv_other = swap(qkv_plane, "zh")
    o_other = swap(o_plane, "zh")
    waits = (cot_groups[1][1], cot_groups[2][1], group_inputs[3], *tables)
    qkv_full = ordered(qkv_plane, qkv_other, zh, "qkv_weights", waits)
    small = qkv_full[:, :, :2, 640:].reshape(32, 2, HD)
    qkv_full = qkv_full.reshape(width, 768)
    gain_attn, gain_mlp, bias = vmem_call(
        vectors_body,
        [((8, width), F32), ((8, width), F32), ((8, 640), F32)],
        [small[:, 0], small[:, 1], jnp.full((8, HD), rank, jnp.int32)],
        "gains_and_biases",
        limit=16,
    )

    mlp = jnp.concatenate([gate_up, down_weight.T[None]], axis=0)
    mlp = jnp.pad(mlp, ((0, 0), (0, 0), (0, 2 * HALF - mlp.shape[2])))
    mlp_own = pick(zh, mlp[..., :HALF], mlp[..., HALF:])
    mlp_other = swap(pick(zh, mlp[..., HALF:], mlp[..., :HALF]), "zh")
    mlp = vmem_call(
        arrange_body,
        [((6, 48, HALF), BF)],
        [mlp_own, mlp_other, jnp.full((8, HD), zh, jnp.int32)],
        "arranged",
        (kv_crossed,),
        moved=4 * mlp_own.size,
    )[0]
    mlp = lax.all_gather(mlp, PLANE, axis=1, tiled=True)
    mlp = mlp.reshape(3, width, HALF)

    normed_group, queries, kv_rot, attended, lse = vmem_call(
        attn_forward_body,
        [
            ((group, width), BF),
            ((group, 384), BF),
            ((group, 256), BF),
            ((group, 384), BF),
            ((group, 128), F32),
        ],
        [*group_inputs, gain_attn, qkv_full, bias, *tables],
        "attention_forward",
        limit=32,
        flops=2 * group * (width * 640 + 6 * group * HD),
        moved=2 * group * width * 2 + 2 * width * 768,
    )
    o_full = ordered(o_plane, o_other, zh, "o_weights", (attended,)).reshape(width, 384)
    pair = ((2, rows, width), BF)
    keep, give = vmem_call(
        attn_out_body,
        [pair, pair],
        [attended, o_full],
        "attention_out",
        flops=2 * group * width * 384,
        moved=2 * width * 384 + 2 * group * width,
    )
    got = swap(give, "core")
    residual, normed_mlp = vmem_call(
        residual_body,
        [((rows, width), F32), ((rows, width), BF)],
        [layer_input, keep, got, swap(add(keep[1], got[1]), "zl"), gain_mlp],
        "residual_norm",
        moved=10 * rows * width,
    )

    after_rows, before_rows = z_shift(normed_mlp, -1), z_shift(normed_mlp, 1)
    far_rows = z_shift(normed_mlp, 2)
    own = (normed_mlp, swap(normed_mlp, "core"))
    own_out = ff_rows(own, cot_groups[0], mlp, cot_local)
    near = stacked((after_rows, before_rows), own_out[0])
    near = (near, swap(near, "core"))
    near_out = ff_rows(near, cot_groups[1], mlp, own_out[0])
    far_rows = stacked((far_rows,), near_out[0])
    far = (far_rows, swap(far_rows, "core"))
    near_sum = [
        add(mine, swap(others, "core"))
        for mine, others in zip(halves(near_out[3], 0), halves(near_out[4], 0))
    ]
    near_got = (z_shift(near_sum[0], 1), z_shift(near_sum[1], -1))
    far_out = ff_rows(far, cot_groups[2], mlp, near_sum[1])
    far_sum = add(far_out[3], swap(far_out[4], "core"))
    own_got = swap(own_out[4], "core")
    far_got = z_shift(far_sum, 2)
    results = (own_out, near_out, far_out)
    hidden, gate_grads, up_grads = ([r[i] for r in results] for i in range(3))
    flat_normed = [*own, *near, *far]
    flat_cots = [part for pair in cot_groups for part in pair]
    grad_terms = weight_grads(flat_normed, flat_cots, hidden, gate_grads, up_grads, far_sum)
    residual_grad, branch, gain_mlp_grad = vmem_call(
        ff_back_body,
        [((rows, width), F32), ((rows, width), BF), ((1, width), F32)],
        [own_out[3], own_got, *near_got, far_got, residual, cot_local, gain_mlp],
        "residual_gradient",
        (grad_terms,),
        limit=60,
        flops=10**9 * WEIGHT,
        moved=24 * rows * width,
    )
    mlp_grads = lax.psum_scatter(
        grad_terms.reshape(6, width // 2, HALF), PLANE, scatter_dimension=1, tiled=True
    ).reshape(3, 2, 48, HALF)
    own_grads = lax.dynamic_index_in_dim(mlp_grads, zh, 1, keepdims=False)
    other_grads = swap(lax.dynamic_index_in_dim(mlp_grads, 1 - zh, 1, keepdims=False), "zh")
    own_grads, other_grads = own_grads.astype(F32), other_grads.astype(F32)
    mlp_shard = jnp.concatenate(
        [pick(zh, own_grads, other_grads), pick(zh, other_grads, own_grads)], axis=-1
    )[..., : gate_up.shape[2]]
    gate_up_shard = mlp_shard[:2]
    down_shard = mlp_shard[2].T

    out_pairs = down_rows(hidden, mlp, branch)
    layer_output = (residual + token_sums(out_pairs)).astype(BF)

    across = stacked((swap(branch, "zl"),), out_pairs[0][0])
    branch_group = (branch, swap(branch, "core"), across, swap(across, "core"))
    qkv_grad, keep, give, sums, gain_attn_grad = vmem_call(
        attn_backward_body,
        [((group, 640), BF), pair, pair, ((1, 640), F32), ((1, width), F32)],
        [*branch_group, *group_inputs, o_full, qkv_full, queries, kv_rot, lse, *tables],
        "attention_backward",
        limit=60,
        scratch=[pltpu.VMEM((group, width), BF)],
        flops=2 * group * (width * 1024 + 15 * group * HD),
        moved=4 * group * width + 2 * width * 1024,
    )
    terms = vmem_call(
        attn_grads_body,
        [((32, width // 32, 1152), BF)],
        [
            normed_group,
            *branch_group,
            qkv_grad,
            attended,
            gain_attn_grad,
            gain_mlp_grad,
            sums,
            jnp.full((8, HD), rank, jnp.int32),
        ],
        "attention_weight_gradients",
        scratch=[pltpu.VMEM((group, width), BF)],
        limit=60,
        flops=2 * group * width * 1024,
        moved=4 * group * width + 2 * width * 1152,
    )[0]
    attn_shard = summed(exchange(terms, DATA), (mlp_grads,))

    got = swap(give, "core")
    across = swap(add(keep[1], got[1]), "zl")
    input_grad = vmem_call(
        attn_back_body,
        [((rows, width), F32)],
        [keep, got, across, layer_input, residual_grad, gain_attn],
        "input_gradient",
        moved=20 * rows * width,
    )[0]

    q_shard = attn_shard[:, :384]
    o_shard = attn_shard[:, 768:].T
    kv_sum = attn_shard[:, 384:640].reshape(2, 2, 12, 2, HD)
    kv_keep = lax.dynamic_index_in_dim(kv_sum, core, 1, keepdims=False).reshape(48, HD)
    kv_give = lax.dynamic_index_in_dim(kv_sum, 1 - core, 1, keepdims=False).reshape(48, HD)
    vectors = attn_shard[:8, 640:768]
    got = swap(jnp.concatenate([kv_give, vectors]), "core")
    kv_sum = (kv_keep + got[:48]).reshape(2, 24, HD)
    vectors = vectors + got[48:]
    kv_keep = pick(zl, kv_sum[0], kv_sum[1])
    got = swap(jnp.concatenate([pick(zl, kv_sum[1], kv_sum[0]), vectors]), "zl")
    kv_got = got[:24]
    vectors = vectors + got[24:]
    kv_shard = jnp.concatenate([pick(zl, kv_keep, kv_got), pick(zl, kv_got, kv_keep)], axis=-1)
    kv_shard = kv_shard.reshape(12, 2, 2 * HD).transpose(1, 0, 2)

    def own_part(row, size):
        return lax.dynamic_index_in_dim(
            vectors[row, : 4 * size].reshape(4, size), rank, 0, keepdims=False
        )

    return (
        layer_output,
        input_grad,
        q_shard,
        kv_shard,
        o_shard,
        jnp.stack([own_part(0, 12), own_part(1, 12)]),
        own_part(2, 14),
        own_part(3, 2),
        gate_up_shard,
        down_shard,
    )


def solution(mesh):
    fine = Mesh(mesh.devices.reshape(SIZES), AXES)
    dp = ("zh", "y", "x")
    tensor = ("zl", "core")
    every = dp + tensor
    in_specs = (
        P(every, None),
        P(dp, tensor),
        P(None, every, None),
        P(tensor, dp),
        P(None, every),
        P(every),
        P(None, dp, tensor),
        P(tensor, dp),
        P(every, None),
        P(dp, None),
    )
    out_specs = (
        P(every, None),
        P(every, None),
        P(dp, tensor),
        P(None, every, None),
        P(tensor, dp),
        P(None, every),
        P(every),
        P(every),
        P(None, dp, tensor),
        P(tensor, dp),
    )
    return jax.shard_map(shards, mesh=fine, in_specs=in_specs, out_specs=out_specs, check_vma=False)
```

```python
import functools

import jax
import jax.numpy as jnp
from jax import lax
from jax.experimental import pallas as pl
from jax.experimental.pallas import tpu as pltpu
from jax.sharding import Mesh, PartitionSpec as P

HQ = 12
KVH = 2
HD = 128
EPSILON = 1e-06
THETA = 1000000.0

AXES = ("zh", "y", "x", "zl", "core")
SIZES = (2, 4, 4, 2, 2)
ZRING = ("zh", "zl")
PLANE = ("y", "x")
DATA = ("zh", "y", "x")
HALF = 1152
BF = jnp.bfloat16
WEIGHT = 1000
F32 = jnp.float32


def swap(block, axis):
    return lax.ppermute(block, axis, [(0, 1), (1, 0)])


def halves(block, dim):
    middle = block.shape[dim] // 2
    return (
        lax.slice_in_dim(block, 0, middle, axis=dim),
        lax.slice_in_dim(block, middle, block.shape[dim], axis=dim),
    )


def add(*terms):
    total = terms[0].astype(F32)
    for term in terms[1:]:
        total = total + term.astype(F32)
    return total.astype(terms[0].dtype)


def exchange(blocks, axes):
    return lax.all_to_all(blocks, axes, split_axis=0, concat_axis=0, tiled=True)


def spread(block, axes, count):
    return exchange(jnp.broadcast_to(block[None], (count,) + block.shape), axes)


def z_shift(block, by):
    return lax.ppermute(block, ZRING, [(i, (i + by) % 4) for i in range(4)])


def token_groups(block):
    near = jnp.concatenate([z_shift(block, -1), z_shift(block, 1)], axis=0)
    far = z_shift(block, 2)
    return [(part, swap(part, "core")) for part in (block, near, far)]


def token_sums(pairs):
    own, near, far = (add(mine, swap(others, "core")) for mine, others in pairs)
    after_rows, before_rows = halves(near, 0)
    terms = (own, z_shift(after_rows, 1), z_shift(before_rows, -1), z_shift(far, 2))
    return sum(term.astype(F32) for term in terms)


def ff_body(
    na, nb, ca, cb, w, _, m_out, dg_out, du_out, dna_out, dnb_out,
    wbuf, nbuf, cbuf, wsem, nsem, csem, *, tile,
):
    half = na.shape[0]
    weights = [pltpu.make_async_copy(w.at[i], wbuf.at[i], wsem.at[i]) for i in range(3)]
    normed = [
        pltpu.make_async_copy(part, nbuf.at[pl.ds(k * half, half)], nsem.at[k])
        for k, part in enumerate((na, nb))
    ]
    cots = [
        pltpu.make_async_copy(part, cbuf.at[pl.ds(k * half, half)], csem.at[k])
        for k, part in enumerate((ca, cb))
    ]
    for copy in normed + weights[:2] + cots + weights[2:]:
        copy.start()
    for copy in normed + weights[:1]:
        copy.wait()
    tiles = 2 * half // tile
    for i in range(tiles):
        at = pl.ds(i * tile, tile)
        rows = nbuf[at]
        gate = dot(rows, wbuf[0])
        if i == 0:
            weights[1].wait()
        up = dot(rows, wbuf[1])
        if i == 0:
            for copy in cots + weights[2:]:
                copy.wait()
        hidden_grad = dot(cbuf[at], wbuf[2])
        sigma = 1.0 / (1.0 + jnp.exp(-gate))
        act = gate * sigma
        m_out[at] = (act * up).astype(BF)
        up_grad = (hidden_grad * act).astype(BF)
        gate_grad = (hidden_grad * up * sigma * (1.0 + gate * (1.0 - sigma))).astype(BF)
        dg_out[at] = gate_grad
        du_out[at] = up_grad
        back = (dot_t(gate_grad, wbuf[0]) + dot_t(up_grad, wbuf[1])).astype(BF)
        if tiles == 1:
            dna_out[...] = back[:half]
            dnb_out[...] = back[half:]
        else:
            out = dna_out if i < tiles // 2 else dnb_out
            out[pl.ds(i % (tiles // 2) * tile, tile)] = back


def ff_rows(normed, cots, weights, order, tile=256):
    half, width = normed[0].shape
    units = weights.shape[2]
    anywhere = pl.BlockSpec(memory_space=pl.ANY)
    vmem = pl.BlockSpec(memory_space=pltpu.VMEM)
    return pl.pallas_call(
        functools.partial(ff_body, tile=tile),
        out_shape=[jax.ShapeDtypeStruct((2 * half, units), BF)] * 3
        + [jax.ShapeDtypeStruct((half, width), BF)] * 2,
        in_specs=[anywhere] * 6,
        out_specs=[vmem] * 5,
        scratch_shapes=[
            pltpu.VMEM((3, width, units), BF),
            pltpu.VMEM((2 * half, width), BF),
            pltpu.VMEM((2 * half, width), BF),
            pltpu.SemaphoreType.DMA((3,)),
            pltpu.SemaphoreType.DMA((2,)),
            pltpu.SemaphoreType.DMA((2,)),
        ],
        compiler_params=pltpu.CompilerParams(vmem_limit_bytes=48 * 1024 * 1024),
        cost_estimate=pl.CostEstimate(
            flops=20 * half * width * units,
            bytes_accessed=6 * width * units,
            transcendentals=2 * half * units,
        ),
        name="feed_forward_rows",
    )(*normed, *cots, weights, order)


def wg_body(*refs, sizes, tile):
    count = len(sizes)
    groups = count // 2
    normed, cots, refs = refs[:count], refs[count : 2 * count], refs[2 * count :]
    hidden, gates, ups = refs[:groups], refs[groups : 2 * groups], refs[2 * groups : 3 * groups]
    out, down_out, nbuf, cbuf, mbuf, gbuf, ubuf, sem = refs[3 * groups + 1 :]
    pair_sizes = [sizes[2 * i] + sizes[2 * i + 1] for i in range(groups)]

    def copies(at, buffer, sources, lengths):
        result, start = [], 0
        for source, length in zip(sources, lengths):
            target = buffer.at[pl.ds(start, length)]
            result.append(pltpu.make_async_copy(source, target, sem.at[at]))
            start += length
        return result

    def normed_copies():
        return copies(0, nbuf, normed, sizes)

    def cot_copies():
        return copies(1, cbuf, cots, sizes)

    def gate_copies():
        return copies(2, gbuf, gates, pair_sizes)

    def up_copies():
        return copies(3, ubuf, ups, pair_sizes)

    def hidden_copies():
        return copies(4, mbuf, hidden, pair_sizes)

    which, step = pl.program_id(0), pl.program_id(1)

    @pl.when((which == 0) & (step == 0))
    def _():
        first = normed_copies() + gate_copies()
        for copy in first + up_copies() + cot_copies() + hidden_copies():
            copy.start()
        for copy in first:
            copy.wait()

    @pl.when((which == 1) & (step == 0))
    def _():
        for copy in up_copies():
            copy.wait()

    @pl.when((which == 2) & (step == 0))
    def _():
        for copy in cot_copies() + hidden_copies():
            copy.wait()

    columns = pl.ds(pl.multiple_of(step * tile, tile), tile)
    for i, right in enumerate((gbuf, ubuf)):

        @pl.when(which == i)
        def _():
            out[...] = t_dot(nbuf[:, columns], right[...]).astype(BF)

    @pl.when(which == 2)
    def _():
        grad = t_dot(cbuf[:, columns], mbuf[...]).astype(BF)
        down_out[:, step] = grad.reshape(down_out.shape[0], *down_out.shape[2:])


def weight_grads(normed, cots, hidden, gates, ups, order):
    sizes = tuple(part.shape[0] for part in normed)
    rows, width, units = sum(sizes), normed[0].shape[1], hidden[0].shape[1]
    tile = width // 2
    down = (16, 2, width // 32, units)
    anywhere = pl.BlockSpec(memory_space=pl.ANY)
    return pl.pallas_call(
        functools.partial(wg_body, sizes=sizes, tile=tile),
        grid=(3, 2),
        out_shape=[
            jax.ShapeDtypeStruct((2, width, units), BF),
            jax.ShapeDtypeStruct(down, BF),
        ],
        in_specs=[anywhere] * (2 * len(normed) + 3 * len(hidden) + 1),
        out_specs=[
            pl.BlockSpec(
                (None, tile, units), lambda i, j: (jnp.minimum(i, 1), jnp.where(i == 2, 1, j), 0)
            ),
            pl.BlockSpec(down, lambda i, j: (0, 0, 0, 0)),
        ],
        scratch_shapes=[pltpu.VMEM((rows, width), BF)] * 2
        + [pltpu.VMEM((rows, units), BF)] * 3
        + [pltpu.SemaphoreType.DMA((5,))],
        compiler_params=pltpu.CompilerParams(vmem_limit_bytes=48 * 1024 * 1024),
        cost_estimate=pl.CostEstimate(
            flops=6 * rows * width * units,
            bytes_accessed=6 * width * units + rows * (4 * width + 6 * units),
            transcendentals=0,
        ),
        name="weight_gradients",
    )(*normed, *cots, *hidden, *gates, *ups, order)


def down_body(ha, hb, hc, w, *outs, tile=256):
    for group, hidden in enumerate((ha, hb, hc)):
        half = hidden.shape[0] // 2
        step = min(tile, 2 * half)
        for start in range(0, 2 * half, step):
            part = dot_t(hidden[pl.ds(start, step)], w[...]).astype(BF)
            if step > half:
                outs[2 * group][...] = part[:half]
                outs[2 * group + 1][...] = part[half:]
            else:
                outs[2 * group + start // half][pl.ds(start % half, step)] = part


def down_rows(hidden, weights, order):
    _, width, units = weights.shape
    halved = [part.shape[0] // 2 for part in hidden for _ in range(2)]
    outs = vmem_call(
        down_body,
        [((rows, width), BF) for rows in halved],
        [*hidden, (weights, 2)],
        "down_rows",
        (order,),
        limit=32,
        flops=2 * sum(halved) * width * units,
        moved=2 * width * units + 2 * sum(halved) * (width + units),
    )
    return [(outs[0], outs[1]), (outs[2], outs[3]), (outs[4], outs[5])]


def dot(a, b):
    return jnp.dot(a, b, preferred_element_type=F32)


def dot_t(a, b):
    return lax.dot_general(a, b, (((1,), (1,)), ((), ())), preferred_element_type=F32)


def t_dot(a, b):
    return lax.dot_general(a, b, (((0,), (0,)), ((), ())), preferred_element_type=F32)


def pick(index, low, high):
    return jnp.where(index == 0, low, high)


def vmem_call(body, outs, ins, name, order=(), scratch=(), limit=16, flops=0, moved=0):
    count, skipped, results, extra = len(ins), len(order), len(outs), len(scratch)
    parts = [value[1] if isinstance(value, tuple) else None for value in ins]
    ins = [value[0] if isinstance(value, tuple) else value for value in ins]

    def kernel(*refs):
        sources, refs = refs[:count], refs[count + skipped :]
        fixed, buffers, sem = refs[: results + extra], refs[results + extra : -1], refs[-1]
        fetches = [
            pltpu.make_async_copy(source if at is None else source.at[at], buffer, sem.at[i])
            for i, (source, at, buffer) in enumerate(zip(sources, parts, buffers))
        ]
        for fetch in fetches:
            fetch.start()
        for fetch in fetches:
            fetch.wait()
        body(*buffers, *fixed)

    return pl.pallas_call(
        kernel,
        out_shape=[jax.ShapeDtypeStruct(shape, dtype) for shape, dtype in outs],
        in_specs=[pl.BlockSpec(memory_space=pl.ANY)] * (count + skipped),
        out_specs=[pl.BlockSpec(memory_space=pltpu.VMEM)] * results,
        scratch_shapes=[
            *scratch,
            *(
                pltpu.VMEM(value.shape if at is None else value.shape[1:], value.dtype)
                for value, at in zip(ins, parts)
            ),
            pltpu.SemaphoreType.DMA((count,)),
        ],
        compiler_params=pltpu.CompilerParams(vmem_limit_bytes=limit * 1024 * 1024),
        cost_estimate=pl.CostEstimate(flops=flops, bytes_accessed=moved, transcendentals=0),
        name=name,
    )(*ins, *order)


def copies_body(block, out):
    for i in range(out.shape[0]):
        out[i] = block[...]


def copies(block, count, *order):
    shape = (count,) + block.shape
    moved = 2 * count * block.size
    return vmem_call(
        copies_body, [(shape, block.dtype)], [block], "copies", order, moved=moved
    )[0]


def arrange_body(own, other, zh, out):
    mine = zh[0:1, 0:1] == 0
    for i in range(3):
        out[2 * i] = jnp.where(mine, own[i], other[i])
        out[2 * i + 1] = jnp.where(mine, other[i], own[i])


def ordered_body(own, other, zh, out):
    mine = zh[0:1, 0:1] == 0
    for i in range(own.shape[0]):
        out[0, i] = jnp.where(mine, own[i], other[i])
        out[1, i] = jnp.where(mine, other[i], own[i])


def ordered(own, other, zh, name, order):
    flag = jnp.full((8, HD), zh, jnp.int32)
    shape = (2,) + own.shape
    return vmem_call(
        ordered_body, [(shape, BF)], [own, other, flag], name, order, moved=8 * own.size
    )[0]


def sum_body(terms, out):
    total = terms[0].astype(F32)
    for i in range(1, terms.shape[0]):
        total = total + terms[i].astype(F32)
    out[...] = total


def summed(terms, *order):
    return vmem_call(
        sum_body, [(terms.shape[1:], F32)], [terms], "summed", order, moved=2 * terms.size
    )[0]


def stack_body(*refs):
    *parts, out = refs
    rows = parts[0].shape[0]
    for i, part in enumerate(parts):
        out[i * rows : (i + 1) * rows] = part[...]


def stacked(parts, *order):
    rows, columns = parts[0].shape
    shape = (len(parts) * rows, columns)
    moved = 4 * shape[0] * columns
    return vmem_call(stack_body, [(shape, BF)], list(parts), "stacked", order, moved=moved)[0]


def row_of(blocks, offset, size):
    count, lanes = blocks.shape
    line = (lanes, count * size)
    at = lax.broadcasted_iota(jnp.int32, line, 1)
    from_lane = lax.broadcasted_iota(jnp.int32, line, 0) - offset
    spots = (lax.rem(at, size) == from_lane).astype(BF)
    values = dot(blocks, spots)
    at = lax.broadcasted_iota(jnp.int32, values.shape, 1)
    owner = lax.broadcasted_iota(jnp.int32, values.shape, 0)
    mine = (at >= owner * size) & (at < (owner + 1) * size)
    return jnp.sum(jnp.where(mine, values, 0.0), axis=0, keepdims=True)


def vectors_body(gains, biases, ranks, attn_out, mlp_out, bias_out):
    attn_out[...] = jnp.broadcast_to(row_of(gains[...], 0, 48), attn_out.shape)
    mlp_out[...] = jnp.broadcast_to(row_of(gains[...], 48, 48), mlp_out.shape)
    full = row_of(biases[...], 0, 64)
    rank = ranks[0:1, 0:1]
    query = key = value = 0.0
    for i in range(4):
        query = query + jnp.where(rank == i, full[:, 384 * i : 384 * (i + 1)], 0.0)
    for i in range(2):
        mine = (rank >= 2 * i) & (rank < 2 * i + 2)
        key = key + jnp.where(mine, full[:, 1536 + HD * i : 1536 + HD * (i + 1)], 0.0)
        value = value + jnp.where(mine, full[:, 1792 + HD * i : 1792 + HD * (i + 1)], 0.0)
    line = jnp.concatenate([query, key, value], axis=1)
    bias_out[...] = jnp.broadcast_to(line, bias_out.shape)


def turn(vectors, cos2, sin2):
    return vectors * cos2 + pltpu.roll(vectors, HD // 2, 1) * sin2


def unpack_table(table, places):
    first, last = table[:, 2 * HD : 2 * HD + 1], table[:, 2 * HD + 1 : 2 * HD + 2]
    keys = places[0:1, :]
    return table[:, :HD], table[:, HD : 2 * HD], (keys >= first) & (keys <= last)


def masked_scores(queries, keys, allowed):
    return jnp.where(allowed, dot_t(queries, keys) * HD ** (-0.5), -1e30)


def attn_forward_body(
    x0, x1, x2, x3, gain, w, bias, table, places,
    n_out, q_out, kv_out, o_out, lse_out,
):
    rows = x0.shape[0]
    for i, x in enumerate((x0, x1, x2, x3)):
        part = x[...].astype(F32)
        scale = lax.rsqrt(jnp.mean(part * part, axis=-1, keepdims=True) + EPSILON)
        n_out[i * rows : (i + 1) * rows] = (part * scale * gain[0:1]).astype(BF)
    qkv = dot(n_out[...], w[:, :640]) + bias[0:1]
    cosines, sines, allowed = unpack_table(table, places)
    keys = turn(qkv[:, 384:512], cosines, sines).astype(BF)
    values = qkv[:, 512:].astype(BF)
    kv_out[:, :HD] = keys
    kv_out[:, HD:] = values
    lses = []
    for h in range(3):
        at = slice(h * HD, (h + 1) * HD)
        queries = turn(qkv[:, at], cosines, sines).astype(BF)
        q_out[:, at] = queries
        scores = masked_scores(queries, keys, allowed)
        peak = jnp.max(scores, axis=-1, keepdims=True)
        shifted = jnp.exp(scores - peak)
        total = jnp.sum(shifted, axis=-1, keepdims=True)
        probs = (shifted / total).astype(BF)
        o_out[:, at] = dot(probs, values).astype(BF)
        lses.append(peak + jnp.log(total))
    lse_out[...] = jnp.concatenate(lses + [jnp.zeros((4 * rows, 125), F32)], axis=1)


def parted(partial, keep, give):
    rows = partial.shape[0] // 4
    keep[0] = partial[:rows].astype(BF)
    give[0] = partial[rows : 2 * rows].astype(BF)
    keep[1] = partial[2 * rows : 3 * rows].astype(BF)
    give[1] = partial[3 * rows :].astype(BF)


def attn_out_body(o, w, keep, give):
    parted(dot_t(o[...], w[...]), keep, give)


def residual_body(x, keep, got, across, gain, h_out, n_out):
    h = x[...].astype(F32) + keep[0].astype(F32) + got[0].astype(F32) + across[...].astype(F32)
    h_out[...] = h
    scale = lax.rsqrt(jnp.mean(h * h, axis=-1, keepdims=True) + EPSILON)
    n_out[...] = (h * scale * gain[0:1]).astype(BF)


def norm_backward(grad, rows, gain):
    scale = lax.rsqrt(jnp.mean(rows * rows, axis=-1, keepdims=True) + EPSILON)
    scaled = grad * gain
    back = scale * scaled - rows * scale**3 * jnp.mean(scaled * rows, axis=-1, keepdims=True)
    return back, jnp.sum(grad * rows * scale, axis=0, keepdims=True)


def ff_back_body(own_a, own_b, got_a, got_b, got_c, h, cot, gain, grad_out, branch_out, gain_out):
    grad = sum(part[...].astype(F32) for part in (own_a, own_b, got_a, got_b, got_c))
    back, gain_out[...] = norm_backward(grad, h[...], gain[0:1])
    total = cot[...].astype(F32) + back
    grad_out[...] = total
    branch_out[...] = total.astype(BF)


def attn_back_body(keep, got, across, x, above, gain, grad_out):
    grad = keep[0].astype(F32) + got[0].astype(F32) + across[...].astype(F32)
    back, _ = norm_backward(grad, x[...].astype(F32), gain[0:1])
    grad_out[...] = above[...] + back


def attn_backward_body(
    b0, b1, b2, b3, x0, x1, x2, x3, wo, w, q, kv, lse, table, places,
    grads_out, keep, give, sums_out, gain_out, bbuf,
):
    rows = b0.shape[0]
    for i, part in enumerate((b0, b1, b2, b3)):
        bbuf[i * rows : (i + 1) * rows] = part[...]
    attended_grad = dot(bbuf[...], wo[...]).astype(BF)
    keys, values = kv[:, :HD], kv[:, HD:]
    cosines, sines, allowed = unpack_table(table, places)
    sines = -sines
    key_grad = value_grad = 0.0
    for h in range(3):
        at = slice(h * HD, (h + 1) * HD)
        queries, o_grad = q[:, at], attended_grad[:, at]
        probs = jnp.exp(masked_scores(queries, keys, allowed) - lse[:, h : h + 1])
        prob_grad = dot_t(o_grad, values)
        inner = jnp.sum(probs * prob_grad, axis=-1, keepdims=True)
        score_grad = (probs * (prob_grad - inner)).astype(BF)
        query_grad = dot(score_grad, keys) * HD ** (-0.5)
        grads_out[:, at] = turn(query_grad, cosines, sines).astype(BF)
        key_grad = key_grad + t_dot(score_grad, queries)
        value_grad = value_grad + t_dot(probs.astype(BF), o_grad)
    grads_out[:, 384:512] = turn(key_grad * HD ** (-0.5), cosines, sines).astype(BF)
    grads_out[:, 512:] = value_grad.astype(BF)
    grads = grads_out[...]
    sums_out[...] = jnp.sum(grads.astype(F32), axis=0, keepdims=True)
    partial = dot_t(grads, w[:, :640])
    parted(partial, keep, give)
    gain_grad = 0.0
    for i, x in enumerate((x0, x1, x2, x3)):
        part = x[...].astype(F32)
        scale = lax.rsqrt(jnp.mean(part * part, axis=-1, keepdims=True) + EPSILON)
        terms = partial[i * rows : (i + 1) * rows] * part * scale
        gain_grad = gain_grad + jnp.sum(terms, axis=0, keepdims=True)
    gain_out[...] = gain_grad


def blocks_of(row, size):
    count = row.shape[1] // size
    at = lax.broadcasted_iota(jnp.int32, (count, row.shape[1]), 1)
    owner = lax.broadcasted_iota(jnp.int32, (count, row.shape[1]), 0)
    mine = (at >= owner * size) & (at < (owner + 1) * size)
    values = jnp.where(mine, row, 0.0).astype(BF)
    at = lax.broadcasted_iota(jnp.int32, (row.shape[1], HD), 0)
    lane = lax.broadcasted_iota(jnp.int32, (row.shape[1], HD), 1)
    return dot(values, (lax.rem(at, size) == lane).astype(BF))


def attn_grads_body(
    normed, b0, b1, b2, b3, qkv_grad, attended, gain_attn, gain_mlp, sums, ranks, out, bbuf
):
    size = b0.shape[0]
    for i, part in enumerate((b0, b1, b2, b3)):
        bbuf[i * size : (i + 1) * size] = part[...]
    half = bbuf.shape[1] // 2
    for i in range(2):
        at, blocks = slice(i * half, (i + 1) * half), slice(16 * i, 16 * (i + 1))
        grad = t_dot(normed[:, at], qkv_grad[...]).astype(BF)
        out[blocks, :, :640] = grad.reshape(16, half // 16, 640)
        grad = t_dot(bbuf[:, at], attended[...]).astype(BF)
        out[blocks, :, 768:] = grad.reshape(16, half // 16, 384)
    rank = ranks[0:1, 0:1]
    parts = [jnp.where(rank == i, sums[:, :384], 0.0) for i in range(4)]
    for start in (384, 512):
        for i in range(2):
            mine = (rank >= 2 * i) & (rank < 2 * i + 2)
            parts.append(jnp.where(mine, sums[:, start : start + HD], 0.0))
    rows_of = (
        blocks_of(gain_attn[...], 48),
        blocks_of(gain_mlp[...], 48),
        blocks_of(jnp.concatenate(parts[:6], axis=1), 56),
        blocks_of(jnp.concatenate(parts[6:], axis=1), 8),
    )
    at = lax.broadcasted_iota(jnp.int32, (32, out.shape[1], HD), 1)
    tail = jnp.zeros((32, out.shape[1], HD), F32)
    for i, values in enumerate(rows_of):
        tail = jnp.where(at == i, values[:, None, :], tail)
    out[:, :, 640:768] = tail.astype(BF)


def shards(
    layer_input,
    q_weight,
    kv_weight,
    o_weight,
    norm_gains,
    qkv_bias,
    gate_up,
    down_weight,
    cotangent,
    lengths,
):
    zh, zl, core = (lax.axis_index(a) for a in ("zh", "zl", "core"))
    rank = 2 * zl + core
    width = layer_input.shape[1]
    rows = layer_input.shape[0]

    small = jnp.concatenate([norm_gains.reshape(-1), qkv_bias, jnp.zeros((216,), BF)])
    vectors = jnp.concatenate([kv_weight.reshape(24, 256), small[None], jnp.zeros((7, 256), BF)])
    got = swap(vectors, "core")
    both = jnp.stack([pick(core, vectors, got), pick(core, got, vectors)])
    small_keep = both[:, 24].reshape(2, 2, HD)
    kv_keep = pick(zl, both[:, :24, :HD], both[:, :24, HD:])
    kv_give = pick(zl, both[:, :24, HD:], both[:, :24, :HD])
    kv_crossed = swap(
        jnp.concatenate([kv_give, small_keep, jnp.zeros((2, 6, HD), BF)], axis=1), "zl"
    )
    kv_got, small_got = kv_crossed[:, :24], kv_crossed[:, 24:26]
    kv_rows = jnp.stack([pick(zl, kv_keep, kv_got), pick(zl, kv_got, kv_keep)])
    kv_rows = kv_rows.reshape(2, 2, 2, 12, HD).transpose(0, 1, 3, 2, 4).reshape(48, 2 * HD)
    small = jnp.stack([pick(zl, small_keep, small_got), pick(zl, small_got, small_keep)])
    small = small.reshape(4, 256)
    gains_row = jnp.concatenate([small[:, :12].reshape(48), small[:, 12:24].reshape(48)])
    bias_row = small[:, 24:40].reshape(64)
    small = jnp.zeros((48, HD), BF).at[0, :96].set(gains_row).at[1, :64].set(bias_row)

    ends = jnp.cumsum(lengths[0])
    ranks = jnp.stack([rank, 2 * zl + 1 - core, 2 * (1 - zl) + core, 2 * (1 - zl) + 1 - core])
    group = 4 * rows
    places = (ranks[:, None] * rows + jnp.arange(rows, dtype=jnp.int32)[None, :]).reshape(group)
    passed = ends[None, :] <= places[:, None]
    starts = jnp.sum(jnp.where(passed, lengths[0][None, :], 0), axis=1)
    inverse = THETA ** (-(2.0 * jnp.arange(HD // 2, dtype=F32)) / HD)
    inverse = jnp.concatenate([inverse, inverse])[None, :]
    angles = (places - starts).astype(F32)[:, None] * inverse
    sign = jnp.where(jnp.arange(HD) < HD // 2, -1.0, 1.0).astype(F32)[None, :]
    lane = jnp.arange(HD)[None, :]
    ranges = jnp.where(lane == 0, starts[:, None], places[:, None]).astype(F32)
    table = jnp.concatenate([jnp.cos(angles), jnp.sin(angles) * sign, ranges], axis=1)
    tables = (table, jnp.broadcast_to(places.astype(F32)[None, :], (8, group)))

    living = (places[:rows] < ends[-1])[:, None]
    cot_local = jnp.where(living, cotangent, jnp.zeros((), BF))
    cot_groups = token_groups(cot_local)

    across = swap(layer_input, "zl")
    group_inputs = (layer_input, swap(layer_input, "core"), across, swap(across, "core"))

    attn_part = jnp.concatenate([q_weight, kv_rows, small, o_weight.T], axis=-1)
    attn_plane = exchange(copies(attn_part, 16), PLANE)
    qkv_plane, o_plane = attn_plane[..., :768], attn_plane[..., 768:]
    qkv_other = swap(qkv_plane, "zh")
    o_other = swap(o_plane, "zh")
    waits = (cot_groups[1][1], cot_groups[2][1], group_inputs[3], *tables)
    qkv_full = ordered(qkv_plane, qkv_other, zh, "qkv_weights", waits)
    small = qkv_full[:, :, :2, 640:].reshape(32, 2, HD)
    qkv_full = qkv_full.reshape(width, 768)
    gain_attn, gain_mlp, bias = vmem_call(
        vectors_body,
        [((8, width), F32), ((8, width), F32), ((8, 640), F32)],
        [small[:, 0], small[:, 1], jnp.full((8, HD), rank, jnp.int32)],
        "gains_and_biases",
        limit=16,
    )

    mlp = jnp.concatenate([gate_up, down_weight.T[None]], axis=0)
    mlp = jnp.pad(mlp, ((0, 0), (0, 0), (0, 2 * HALF - mlp.shape[2])))
    mlp_own = pick(zh, mlp[..., :HALF], mlp[..., HALF:])
    mlp_other = swap(pick(zh, mlp[..., HALF:], mlp[..., :HALF]), "zh")
    mlp = vmem_call(
        arrange_body,
        [((6, 48, HALF), BF)],
        [mlp_own, mlp_other, jnp.full((8, HD), zh, jnp.int32)],
        "arranged",
        (kv_crossed,),
        moved=4 * mlp_own.size,
    )[0]
    mlp = lax.all_gather(mlp, PLANE, axis=1, tiled=True)
    mlp = mlp.reshape(3, width, HALF)

    normed_group, queries, kv_rot, attended, lse = vmem_call(
        attn_forward_body,
        [
            ((group, width), BF),
            ((group, 384), BF),
            ((group, 256), BF),
            ((group, 384), BF),
            ((group, 128), F32),
        ],
        [*group_inputs, gain_attn, qkv_full, bias, *tables],
        "attention_forward",
        limit=32,
        flops=2 * group * (width * 640 + 6 * group * HD),
        moved=2 * group * width * 2 + 2 * width * 768,
    )
    o_full = ordered(o_plane, o_other, zh, "o_weights", (attended,)).reshape(width, 384)
    pair = ((2, rows, width), BF)
    keep, give = vmem_call(
        attn_out_body,
        [pair, pair],
        [attended, o_full],
        "attention_out",
        flops=2 * group * width * 384,
        moved=2 * width * 384 + 2 * group * width,
    )
    got = swap(give, "core")
    residual, normed_mlp = vmem_call(
        residual_body,
        [((rows, width), F32), ((rows, width), BF)],
        [layer_input, keep, got, swap(add(keep[1], got[1]), "zl"), gain_mlp],
        "residual_norm",
        moved=10 * rows * width,
    )

    after_rows, before_rows = z_shift(normed_mlp, -1), z_shift(normed_mlp, 1)
    far_rows = z_shift(normed_mlp, 2)
    own = (normed_mlp, swap(normed_mlp, "core"))
    own_out = ff_rows(own, cot_groups[0], mlp, cot_local)
    near = stacked((after_rows, before_rows), own_out[0])
    near = (near, swap(near, "core"))
    near_out = ff_rows(near, cot_groups[1], mlp, own_out[0])
    far_rows = stacked((far_rows,), near_out[0])
    far = (far_rows, swap(far_rows, "core"))
    near_sum = [
        add(mine, swap(others, "core"))
        for mine, others in zip(halves(near_out[3], 0), halves(near_out[4], 0))
    ]
    near_got = (z_shift(near_sum[0], 1), z_shift(near_sum[1], -1))
    far_out = ff_rows(far, cot_groups[2], mlp, near_sum[1])
    far_sum = add(far_out[3], swap(far_out[4], "core"))
    own_got = swap(own_out[4], "core")
    far_got = z_shift(far_sum, 2)
    results = (own_out, near_out, far_out)
    hidden, gate_grads, up_grads = ([r[i] for r in results] for i in range(3))
    flat_normed = [*own, *near, *far]
    flat_cots = [part for pair in cot_groups for part in pair]
    grad_terms, down_terms = weight_grads(
        flat_normed, flat_cots, hidden, gate_grads, up_grads, far_sum
    )
    residual_grad, branch, gain_mlp_grad = vmem_call(
        ff_back_body,
        [((rows, width), F32), ((rows, width), BF), ((1, width), F32)],
        [own_out[3], own_got, *near_got, far_got, residual, cot_local, gain_mlp],
        "residual_gradient",
        (grad_terms, down_terms),
        limit=60,
        flops=10**9 * WEIGHT,
        moved=24 * rows * width,
    )
    mlp_grads = lax.psum_scatter(
        grad_terms.reshape(4, width // 2, HALF), PLANE, scatter_dimension=1, tiled=True
    ).reshape(2, 2, 48, HALF)
    down_grads = summed(exchange(down_terms, PLANE))

    def joined(grads, dim):
        own = lax.dynamic_index_in_dim(grads, zh, dim, keepdims=False)
        other = lax.dynamic_index_in_dim(grads, 1 - zh, dim, keepdims=False)
        other = swap(other.astype(BF), "zh").astype(F32)
        own = own.astype(F32)
        both = jnp.concatenate([pick(zh, own, other), pick(zh, other, own)], axis=-1)
        return both[..., : gate_up.shape[2]]

    gate_up_shard = joined(mlp_grads, 1)
    down_shard = joined(down_grads, 0).T

    out_pairs = down_rows(hidden, mlp, branch)
    layer_output = (residual + token_sums(out_pairs)).astype(BF)

    across = stacked((swap(branch, "zl"),), out_pairs[0][0])
    branch_group = (branch, swap(branch, "core"), across, swap(across, "core"))
    qkv_grad, keep, give, sums, gain_attn_grad = vmem_call(
        attn_backward_body,
        [((group, 640), BF), pair, pair, ((1, 640), F32), ((1, width), F32)],
        [*branch_group, *group_inputs, o_full, qkv_full, queries, kv_rot, lse, *tables],
        "attention_backward",
        limit=60,
        scratch=[pltpu.VMEM((group, width), BF)],
        flops=2 * group * (width * 1024 + 15 * group * HD),
        moved=4 * group * width + 2 * width * 1024,
    )
    terms = vmem_call(
        attn_grads_body,
        [((32, width // 32, 1152), BF)],
        [
            normed_group,
            *branch_group,
            qkv_grad,
            attended,
            gain_attn_grad,
            gain_mlp_grad,
            sums,
            jnp.full((8, HD), rank, jnp.int32),
        ],
        "attention_weight_gradients",
        scratch=[pltpu.VMEM((group, width), BF)],
        limit=60,
        flops=2 * group * width * 1024,
        moved=4 * group * width + 2 * width * 1152,
    )[0]
    attn_shard = summed(exchange(terms, DATA))

    got = swap(give, "core")
    across = swap(add(keep[1], got[1]), "zl")
    input_grad = vmem_call(
        attn_back_body,
        [((rows, width), F32)],
        [keep, got, across, layer_input, residual_grad, gain_attn],
        "input_gradient",
        moved=20 * rows * width,
    )[0]

    q_shard = attn_shard[:, :384]
    o_shard = attn_shard[:, 768:].T
    kv_sum = attn_shard[:, 384:640].reshape(2, 2, 12, 2, HD)
    kv_keep = lax.dynamic_index_in_dim(kv_sum, core, 1, keepdims=False).reshape(48, HD)
    kv_give = lax.dynamic_index_in_dim(kv_sum, 1 - core, 1, keepdims=False).reshape(48, HD)
    vectors = attn_shard[:8, 640:768]
    got = swap(jnp.concatenate([kv_give, vectors]), "core")
    kv_sum = (kv_keep + got[:48]).reshape(2, 24, HD)
    vectors = vectors + got[48:]
    kv_keep = pick(zl, kv_sum[0], kv_sum[1])
    got = swap(jnp.concatenate([pick(zl, kv_sum[1], kv_sum[0]), vectors]), "zl")
    kv_got = got[:24]
    vectors = vectors + got[24:]
    kv_shard = jnp.concatenate([pick(zl, kv_keep, kv_got), pick(zl, kv_got, kv_keep)], axis=-1)
    kv_shard = kv_shard.reshape(12, 2, 2 * HD).transpose(1, 0, 2)

    def own_part(row, size):
        return lax.dynamic_index_in_dim(
            vectors[row, : 4 * size].reshape(4, size), rank, 0, keepdims=False
        )

    return (
        layer_output,
        input_grad,
        q_shard,
        kv_shard,
        o_shard,
        jnp.stack([own_part(0, 12), own_part(1, 12)]),
        own_part(2, 14),
        own_part(3, 2),
        gate_up_shard,
        down_shard,
    )


def solution(mesh):
    fine = Mesh(mesh.devices.reshape(SIZES), AXES)
    dp = ("zh", "y", "x")
    tensor = ("zl", "core")
    every = dp + tensor
    in_specs = (
        P(every, None),
        P(dp, tensor),
        P(None, every, None),
        P(tensor, dp),
        P(None, every),
        P(every),
        P(None, dp, tensor),
        P(tensor, dp),
        P(every, None),
        P(dp, None),
    )
    out_specs = (
        P(every, None),
        P(every, None),
        P(dp, tensor),
        P(None, every, None),
        P(tensor, dp),
        P(None, every),
        P(every),
        P(every),
        P(None, dp, tensor),
        P(tensor, dp),
    )
    return jax.shard_map(shards, mesh=fine, in_specs=in_specs, out_specs=out_specs, check_vma=False)
```

```python
import functools

import jax
import jax.numpy as jnp
from jax import lax
from jax.experimental import pallas as pl
from jax.experimental.pallas import tpu as pltpu
from jax.sharding import Mesh, PartitionSpec as P

HQ = 12
KVH = 2
HD = 128
EPSILON = 1e-06
THETA = 1000000.0

AXES = ("zh", "y", "x", "zl", "core")
SIZES = (2, 4, 4, 2, 2)
ZRING = ("zh", "zl")
PLANE = ("y", "x")
DATA = ("zh", "y", "x")
HALF = 1152
BF = jnp.bfloat16
WEIGHT = 1000
F32 = jnp.float32


def swap(block, axis):
    return lax.ppermute(block, axis, [(0, 1), (1, 0)])


def halves(block, dim):
    middle = block.shape[dim] // 2
    return (
        lax.slice_in_dim(block, 0, middle, axis=dim),
        lax.slice_in_dim(block, middle, block.shape[dim], axis=dim),
    )


def add(*terms):
    total = terms[0].astype(F32)
    for term in terms[1:]:
        total = total + term.astype(F32)
    return total.astype(terms[0].dtype)


def exchange(blocks, axes):
    return lax.all_to_all(blocks, axes, split_axis=0, concat_axis=0, tiled=True)


def spread(block, axes, count):
    return exchange(jnp.broadcast_to(block[None], (count,) + block.shape), axes)


def z_shift(block, by):
    return lax.ppermute(block, ZRING, [(i, (i + by) % 4) for i in range(4)])


def token_groups(block):
    near = jnp.concatenate([z_shift(block, -1), z_shift(block, 1)], axis=0)
    far = z_shift(block, 2)
    return [(part, swap(part, "core")) for part in (block, near, far)]


def token_sums(pairs):
    own, near, far = (add(mine, swap(others, "core")) for mine, others in pairs)
    after_rows, before_rows = halves(near, 0)
    terms = (own, z_shift(after_rows, 1), z_shift(before_rows, -1), z_shift(far, 2))
    return sum(term.astype(F32) for term in terms)


def ff_body(
    na, nb, ca, cb, w, _, m_out, dg_out, du_out, dna_out, dnb_out,
    wbuf, nbuf, cbuf, wsem, nsem, csem, *, tile,
):
    half = na.shape[0]
    weights = [pltpu.make_async_copy(w.at[i], wbuf.at[i], wsem.at[i]) for i in range(3)]
    normed = [
        pltpu.make_async_copy(part, nbuf.at[pl.ds(k * half, half)], nsem.at[k])
        for k, part in enumerate((na, nb))
    ]
    cots = [
        pltpu.make_async_copy(part, cbuf.at[pl.ds(k * half, half)], csem.at[k])
        for k, part in enumerate((ca, cb))
    ]
    for copy in normed + weights[:2] + cots + weights[2:]:
        copy.start()
    for copy in normed + weights[:1]:
        copy.wait()
    tiles = 2 * half // tile
    for i in range(tiles):
        at = pl.ds(i * tile, tile)
        rows = nbuf[at]
        gate = dot(rows, wbuf[0])
        if i == 0:
            weights[1].wait()
        up = dot(rows, wbuf[1])
        if i == 0:
            for copy in cots + weights[2:]:
                copy.wait()
        hidden_grad = dot(cbuf[at], wbuf[2])
        sigma = 1.0 / (1.0 + jnp.exp(-gate))
        act = gate * sigma
        m_out[at] = (act * up).astype(BF)
        up_grad = (hidden_grad * act).astype(BF)
        gate_grad = (hidden_grad * up * sigma * (1.0 + gate * (1.0 - sigma))).astype(BF)
        dg_out[at] = gate_grad
        du_out[at] = up_grad
        back = (dot_t(gate_grad, wbuf[0]) + dot_t(up_grad, wbuf[1])).astype(BF)
        if tiles == 1:
            dna_out[...] = back[:half]
            dnb_out[...] = back[half:]
        else:
            out = dna_out if i < tiles // 2 else dnb_out
            out[pl.ds(i % (tiles // 2) * tile, tile)] = back


def ff_rows(normed, cots, weights, order, tile=256):
    half, width = normed[0].shape
    units = weights.shape[2]
    anywhere = pl.BlockSpec(memory_space=pl.ANY)
    vmem = pl.BlockSpec(memory_space=pltpu.VMEM)
    return pl.pallas_call(
        functools.partial(ff_body, tile=tile),
        out_shape=[jax.ShapeDtypeStruct((2 * half, units), BF)] * 3
        + [jax.ShapeDtypeStruct((half, width), BF)] * 2,
        in_specs=[anywhere] * 6,
        out_specs=[vmem] * 5,
        scratch_shapes=[
            pltpu.VMEM((3, width, units), BF),
            pltpu.VMEM((2 * half, width), BF),
            pltpu.VMEM((2 * half, width), BF),
            pltpu.SemaphoreType.DMA((3,)),
            pltpu.SemaphoreType.DMA((2,)),
            pltpu.SemaphoreType.DMA((2,)),
        ],
        compiler_params=pltpu.CompilerParams(vmem_limit_bytes=48 * 1024 * 1024),
        cost_estimate=pl.CostEstimate(
            flops=20 * half * width * units,
            bytes_accessed=6 * width * units,
            transcendentals=2 * half * units,
        ),
        name="feed_forward_rows",
    )(*normed, *cots, weights, order)


def wg_body(*refs, sizes, tile):
    count = len(sizes)
    groups = count // 2
    normed, cots, refs = refs[:count], refs[count : 2 * count], refs[2 * count :]
    hidden, gates, ups = refs[:groups], refs[groups : 2 * groups], refs[2 * groups : 3 * groups]
    out, nbuf, cbuf, mbuf, gbuf, ubuf, sem = refs[3 * groups + 1 :]
    pair_sizes = [sizes[2 * i] + sizes[2 * i + 1] for i in range(groups)]

    def copies(at, buffer, sources, lengths):
        result, start = [], 0
        for source, length in zip(sources, lengths):
            target = buffer.at[pl.ds(start, length)]
            result.append(pltpu.make_async_copy(source, target, sem.at[at]))
            start += length
        return result

    def normed_copies():
        return copies(0, nbuf, normed, sizes)

    def cot_copies():
        return copies(1, cbuf, cots, sizes)

    def gate_copies():
        return copies(2, gbuf, gates, pair_sizes)

    def up_copies():
        return copies(3, ubuf, ups, pair_sizes)

    def hidden_copies():
        return copies(4, mbuf, hidden, pair_sizes)

    which, step = pl.program_id(0), pl.program_id(1)

    @pl.when((which == 0) & (step == 0))
    def _():
        first = normed_copies() + gate_copies()
        for copy in first + up_copies() + cot_copies() + hidden_copies():
            copy.start()
        for copy in first:
            copy.wait()

    @pl.when((which == 1) & (step == 0))
    def _():
        for copy in up_copies():
            copy.wait()

    @pl.when((which == 2) & (step == 0))
    def _():
        for copy in cot_copies() + hidden_copies():
            copy.wait()

    columns = pl.ds(pl.multiple_of(step * tile, tile), tile)
    for i, (left, right) in enumerate(((nbuf, gbuf), (nbuf, ubuf), (cbuf, mbuf))):

        @pl.when(which == i)
        def _():
            out[...] = t_dot(left[:, columns], right[...]).astype(BF)


def weight_grads(normed, cots, hidden, gates, ups, order, tile=768):
    sizes = tuple(part.shape[0] for part in normed)
    rows, width, units = sum(sizes), normed[0].shape[1], hidden[0].shape[1]
    anywhere = pl.BlockSpec(memory_space=pl.ANY)
    return pl.pallas_call(
        functools.partial(wg_body, sizes=sizes, tile=tile),
        grid=(3, width // tile),
        out_shape=jax.ShapeDtypeStruct((3, width, units), BF),
        in_specs=[anywhere] * (2 * len(normed) + 3 * len(hidden) + 1),
        out_specs=pl.BlockSpec((None, tile, units), lambda i, j: (i, j, 0)),
        scratch_shapes=[pltpu.VMEM((rows, width), BF)] * 2
        + [pltpu.VMEM((rows, units), BF)] * 3
        + [pltpu.SemaphoreType.DMA((5,))],
        compiler_params=pltpu.CompilerParams(vmem_limit_bytes=48 * 1024 * 1024),
        cost_estimate=pl.CostEstimate(
            flops=6 * rows * width * units,
            bytes_accessed=6 * width * units + rows * (4 * width + 6 * units),
            transcendentals=0,
        ),
        name="weight_gradients",
    )(*normed, *cots, *hidden, *gates, *ups, order)


def down_body(ha, hb, hc, w, *outs, tile=256):
    for group, hidden in enumerate((ha, hb, hc)):
        half = hidden.shape[0] // 2
        step = min(tile, 2 * half)
        for start in range(0, 2 * half, step):
            part = dot_t(hidden[pl.ds(start, step)], w[...]).astype(BF)
            if step > half:
                outs[2 * group][...] = part[:half]
                outs[2 * group + 1][...] = part[half:]
            else:
                outs[2 * group + start // half][pl.ds(start % half, step)] = part


def down_rows(hidden, weights, order):
    _, width, units = weights.shape
    halved = [part.shape[0] // 2 for part in hidden for _ in range(2)]
    outs = vmem_call(
        down_body,
        [((rows, width), BF) for rows in halved],
        [*hidden, (weights, 2)],
        "down_rows",
        (order,),
        limit=60,
        flops=2 * sum(halved) * width * units,
        moved=2 * width * units + 2 * sum(halved) * (width + units),
    )
    return [(outs[0], outs[1]), (outs[2], outs[3]), (outs[4], outs[5])]


def dot(a, b):
    return jnp.dot(a, b, preferred_element_type=F32)


def dot_t(a, b):
    return lax.dot_general(a, b, (((1,), (1,)), ((), ())), preferred_element_type=F32)


def t_dot(a, b):
    return lax.dot_general(a, b, (((0,), (0,)), ((), ())), preferred_element_type=F32)


def pick(index, low, high):
    return jnp.where(index == 0, low, high)


def vmem_call(body, outs, ins, name, order=(), scratch=(), limit=16, flops=0, moved=0):
    count, skipped, results, extra = len(ins), len(order), len(outs), len(scratch)
    parts = [value[1] if isinstance(value, tuple) else None for value in ins]
    ins = [value[0] if isinstance(value, tuple) else value for value in ins]

    def kernel(*refs):
        sources, refs = refs[:count], refs[count + skipped :]
        fixed, buffers, sem = refs[: results + extra], refs[results + extra : -1], refs[-1]
        fetches = [
            pltpu.make_async_copy(source if at is None else source.at[at], buffer, sem.at[i])
            for i, (source, at, buffer) in enumerate(zip(sources, parts, buffers))
        ]
        for fetch in fetches:
            fetch.start()
        for fetch in fetches:
            fetch.wait()
        body(*buffers, *fixed)

    return pl.pallas_call(
        kernel,
        out_shape=[jax.ShapeDtypeStruct(shape, dtype) for shape, dtype in outs],
        in_specs=[pl.BlockSpec(memory_space=pl.ANY)] * (count + skipped),
        out_specs=[pl.BlockSpec(memory_space=pltpu.VMEM)] * results,
        scratch_shapes=[
            *scratch,
            *(
                pltpu.VMEM(value.shape if at is None else value.shape[1:], value.dtype)
                for value, at in zip(ins, parts)
            ),
            pltpu.SemaphoreType.DMA((count,)),
        ],
        compiler_params=pltpu.CompilerParams(vmem_limit_bytes=limit * 1024 * 1024),
        cost_estimate=pl.CostEstimate(flops=flops, bytes_accessed=moved, transcendentals=0),
        name=name,
    )(*ins, *order)


def copies_body(block, out):
    for i in range(out.shape[0]):
        out[i] = block[...]


def copies(block, count, *order):
    shape = (count,) + block.shape
    moved = 2 * count * block.size
    return vmem_call(
        copies_body, [(shape, block.dtype)], [block], "copies", order, moved=moved
    )[0]


def arrange_body(own, other, zh, out):
    mine = zh[0:1, 0:1] == 0
    for i in range(3):
        out[2 * i] = jnp.where(mine, own[i], other[i])
        out[2 * i + 1] = jnp.where(mine, other[i], own[i])


def ordered_body(own, other, zh, out):
    mine = zh[0:1, 0:1] == 0
    for i in range(own.shape[0]):
        out[0, i] = jnp.where(mine, own[i], other[i])
        out[1, i] = jnp.where(mine, other[i], own[i])


def ordered(own, other, zh, name, order):
    flag = jnp.full((8, HD), zh, jnp.int32)
    shape = (2,) + own.shape
    return vmem_call(
        ordered_body, [(shape, BF)], [own, other, flag], name, order, moved=8 * own.size
    )[0]


def sum_body(terms, out):
    total = terms[0].astype(F32)
    for i in range(1, terms.shape[0]):
        total = total + terms[i].astype(F32)
    out[...] = total


def summed(terms, *order):
    return vmem_call(
        sum_body, [(terms.shape[1:], F32)], [terms], "summed", order, moved=2 * terms.size
    )[0]


def stack_body(*refs):
    *parts, out = refs
    rows = parts[0].shape[0]
    for i, part in enumerate(parts):
        out[i * rows : (i + 1) * rows] = part[...]


def stacked(parts, *order):
    rows, columns = parts[0].shape
    shape = (len(parts) * rows, columns)
    moved = 4 * shape[0] * columns
    return vmem_call(stack_body, [(shape, BF)], list(parts), "stacked", order, moved=moved)[0]


def row_of(blocks, offset, size):
    count, lanes = blocks.shape
    line = (lanes, count * size)
    at = lax.broadcasted_iota(jnp.int32, line, 1)
    from_lane = lax.broadcasted_iota(jnp.int32, line, 0) - offset
    spots = (lax.rem(at, size) == from_lane).astype(BF)
    values = dot(blocks, spots)
    at = lax.broadcasted_iota(jnp.int32, values.shape, 1)
    owner = lax.broadcasted_iota(jnp.int32, values.shape, 0)
    mine = (at >= owner * size) & (at < (owner + 1) * size)
    return jnp.sum(jnp.where(mine, values, 0.0), axis=0, keepdims=True)


def vectors_body(gains, biases, ranks, attn_out, mlp_out, bias_out):
    attn_out[...] = jnp.broadcast_to(row_of(gains[...], 0, 48), attn_out.shape)
    mlp_out[...] = jnp.broadcast_to(row_of(gains[...], 48, 48), mlp_out.shape)
    full = row_of(biases[...], 0, 64)
    rank = ranks[0:1, 0:1]
    query = key = value = 0.0
    for i in range(4):
        query = query + jnp.where(rank == i, full[:, 384 * i : 384 * (i + 1)], 0.0)
    for i in range(2):
        mine = (rank >= 2 * i) & (rank < 2 * i + 2)
        key = key + jnp.where(mine, full[:, 1536 + HD * i : 1536 + HD * (i + 1)], 0.0)
        value = value + jnp.where(mine, full[:, 1792 + HD * i : 1792 + HD * (i + 1)], 0.0)
    line = jnp.concatenate([query, key, value], axis=1)
    bias_out[...] = jnp.broadcast_to(line, bias_out.shape)


def turn(vectors, cos2, sin2):
    return vectors * cos2 + pltpu.roll(vectors, HD // 2, 1) * sin2


def unpack_table(table, places):
    first, last = table[:, 2 * HD : 2 * HD + 1], table[:, 2 * HD + 1 : 2 * HD + 2]
    keys = places[0:1, :]
    return table[:, :HD], table[:, HD : 2 * HD], (keys >= first) & (keys <= last)


def masked_scores(queries, keys, allowed):
    return jnp.where(allowed, dot_t(queries, keys) * HD ** (-0.5), -1e30)


def attn_forward_body(
    x0, x1, x2, x3, gain, w, bias, table, places,
    n_out, q_out, kv_out, o_out, lse_out,
):
    rows = x0.shape[0]
    for i, x in enumerate((x0, x1, x2, x3)):
        part = x[...].astype(F32)
        scale = lax.rsqrt(jnp.mean(part * part, axis=-1, keepdims=True) + EPSILON)
        n_out[i * rows : (i + 1) * rows] = (part * scale * gain[0:1]).astype(BF)
    qkv = dot(n_out[...], w[...]) + bias[0:1]
    cosines, sines, allowed = unpack_table(table, places)
    keys = turn(qkv[:, 384:512], cosines, sines).astype(BF)
    values = qkv[:, 512:].astype(BF)
    kv_out[:, :HD] = keys
    kv_out[:, HD:] = values
    lses = []
    for h in range(3):
        at = slice(h * HD, (h + 1) * HD)
        queries = turn(qkv[:, at], cosines, sines).astype(BF)
        q_out[:, at] = queries
        scores = masked_scores(queries, keys, allowed)
        peak = jnp.max(scores, axis=-1, keepdims=True)
        shifted = jnp.exp(scores - peak)
        total = jnp.sum(shifted, axis=-1, keepdims=True)
        probs = (shifted / total).astype(BF)
        o_out[:, at] = dot(probs, values).astype(BF)
        lses.append(peak + jnp.log(total))
    lse_out[...] = jnp.concatenate(lses + [jnp.zeros((4 * rows, 125), F32)], axis=1)


def parted(partial, keep, give):
    rows = partial.shape[0] // 4
    keep[0] = partial[:rows].astype(BF)
    give[0] = partial[rows : 2 * rows].astype(BF)
    keep[1] = partial[2 * rows : 3 * rows].astype(BF)
    give[1] = partial[3 * rows :].astype(BF)


def attn_out_body(o, w, keep, give):
    parted(dot_t(o[...], w[...]), keep, give)


def residual_body(x, keep, got, across, gain, h_out, n_out):
    h = x[...].astype(F32) + keep[0].astype(F32) + got[0].astype(F32) + across[...].astype(F32)
    h_out[...] = h
    scale = lax.rsqrt(jnp.mean(h * h, axis=-1, keepdims=True) + EPSILON)
    n_out[...] = (h * scale * gain[0:1]).astype(BF)


def norm_backward(grad, rows, gain):
    scale = lax.rsqrt(jnp.mean(rows * rows, axis=-1, keepdims=True) + EPSILON)
    scaled = grad * gain
    back = scale * scaled - rows * scale**3 * jnp.mean(scaled * rows, axis=-1, keepdims=True)
    return back, jnp.sum(grad * rows * scale, axis=0, keepdims=True)


def ff_back_body(own_a, own_b, got_a, got_b, got_c, h, cot, gain, grad_out, branch_out, gain_out):
    grad = sum(part[...].astype(F32) for part in (own_a, own_b, got_a, got_b, got_c))
    back, gain_out[...] = norm_backward(grad, h[...], gain[0:1])
    total = cot[...].astype(F32) + back
    grad_out[...] = total
    branch_out[...] = total.astype(BF)


def attn_back_body(keep, got, across, x, above, gain, grad_out):
    grad = keep[0].astype(F32) + got[0].astype(F32) + across[...].astype(F32)
    back, _ = norm_backward(grad, x[...].astype(F32), gain[0:1])
    grad_out[...] = above[...] + back


def attn_backward_body(
    b0, b1, b2, b3, x0, x1, x2, x3, wo, w, q, kv, lse, table, places,
    grads_out, keep, give, sums_out, gain_out, bbuf,
):
    rows = b0.shape[0]
    for i, part in enumerate((b0, b1, b2, b3)):
        bbuf[i * rows : (i + 1) * rows] = part[...]
    attended_grad = dot(bbuf[...], wo[...]).astype(BF)
    keys, values = kv[:, :HD], kv[:, HD:]
    cosines, sines, allowed = unpack_table(table, places)
    sines = -sines
    key_grad = value_grad = 0.0
    for h in range(3):
        at = slice(h * HD, (h + 1) * HD)
        queries, o_grad = q[:, at], attended_grad[:, at]
        probs = jnp.exp(masked_scores(queries, keys, allowed) - lse[:, h : h + 1])
        prob_grad = dot_t(o_grad, values)
        inner = jnp.sum(probs * prob_grad, axis=-1, keepdims=True)
        score_grad = (probs * (prob_grad - inner)).astype(BF)
        query_grad = dot(score_grad, keys) * HD ** (-0.5)
        grads_out[:, at] = turn(query_grad, cosines, sines).astype(BF)
        key_grad = key_grad + t_dot(score_grad, queries)
        value_grad = value_grad + t_dot(probs.astype(BF), o_grad)
    grads_out[:, 384:512] = turn(key_grad * HD ** (-0.5), cosines, sines).astype(BF)
    grads_out[:, 512:] = value_grad.astype(BF)
    grads = grads_out[...]
    sums_out[...] = jnp.sum(grads.astype(F32), axis=0, keepdims=True)
    partial = dot_t(grads, w[...])
    parted(partial, keep, give)
    gain_grad = 0.0
    for i, x in enumerate((x0, x1, x2, x3)):
        part = x[...].astype(F32)
        scale = lax.rsqrt(jnp.mean(part * part, axis=-1, keepdims=True) + EPSILON)
        terms = partial[i * rows : (i + 1) * rows] * part * scale
        gain_grad = gain_grad + jnp.sum(terms, axis=0, keepdims=True)
    gain_out[...] = gain_grad


def blocks_of(row, size):
    count = row.shape[1] // size
    at = lax.broadcasted_iota(jnp.int32, (count, row.shape[1]), 1)
    owner = lax.broadcasted_iota(jnp.int32, (count, row.shape[1]), 0)
    mine = (at >= owner * size) & (at < (owner + 1) * size)
    values = jnp.where(mine, row, 0.0).astype(BF)
    at = lax.broadcasted_iota(jnp.int32, (row.shape[1], HD), 0)
    lane = lax.broadcasted_iota(jnp.int32, (row.shape[1], HD), 1)
    return dot(values, (lax.rem(at, size) == lane).astype(BF))


def attn_grads_body(
    normed, b0, b1, b2, b3, qkv_grad, attended, gain_attn, gain_mlp, sums, ranks, out, bbuf
):
    size = b0.shape[0]
    for i, part in enumerate((b0, b1, b2, b3)):
        bbuf[i * size : (i + 1) * size] = part[...]
    half = bbuf.shape[1] // 2
    for i in range(2):
        at, blocks = slice(i * half, (i + 1) * half), slice(16 * i, 16 * (i + 1))
        grad = t_dot(normed[:, at], qkv_grad[...]).astype(BF)
        out[blocks, :, :640] = grad.reshape(16, half // 16, 640)
        grad = t_dot(bbuf[:, at], attended[...]).astype(BF)
        out[blocks, :, 768:] = grad.reshape(16, half // 16, 384)
    rank = ranks[0:1, 0:1]
    parts = [jnp.where(rank == i, sums[:, :384], 0.0) for i in range(4)]
    for start in (384, 512):
        for i in range(2):
            mine = (rank >= 2 * i) & (rank < 2 * i + 2)
            parts.append(jnp.where(mine, sums[:, start : start + HD], 0.0))
    rows_of = (
        blocks_of(gain_attn[...], 48),
        blocks_of(gain_mlp[...], 48),
        blocks_of(jnp.concatenate(parts[:6], axis=1), 56),
        blocks_of(jnp.concatenate(parts[6:], axis=1), 8),
    )
    at = lax.broadcasted_iota(jnp.int32, (32, out.shape[1], HD), 1)
    tail = jnp.zeros((32, out.shape[1], HD), F32)
    for i, values in enumerate(rows_of):
        tail = jnp.where(at == i, values[:, None, :], tail)
    out[:, :, 640:768] = tail.astype(BF)


def shards(
    layer_input,
    q_weight,
    kv_weight,
    o_weight,
    norm_gains,
    qkv_bias,
    gate_up,
    down_weight,
    cotangent,
    lengths,
):
    zh, zl, core = (lax.axis_index(a) for a in ("zh", "zl", "core"))
    rank = 2 * zl + core
    width = layer_input.shape[1]
    rows = layer_input.shape[0]

    small = jnp.concatenate([norm_gains.reshape(-1), qkv_bias, jnp.zeros((216,), BF)])
    vectors = jnp.concatenate([kv_weight.reshape(24, 256), small[None], jnp.zeros((7, 256), BF)])
    got = swap(vectors, "core")
    both = jnp.stack([pick(core, vectors, got), pick(core, got, vectors)])
    small_keep = both[:, 24].reshape(2, 2, HD)
    kv_keep = pick(zl, both[:, :24, :HD], both[:, :24, HD:])
    kv_give = pick(zl, both[:, :24, HD:], both[:, :24, :HD])
    kv_crossed = swap(
        jnp.concatenate([kv_give, small_keep, jnp.zeros((2, 6, HD), BF)], axis=1), "zl"
    )
    kv_got, small_got = kv_crossed[:, :24], kv_crossed[:, 24:26]
    kv_rows = jnp.stack([pick(zl, kv_keep, kv_got), pick(zl, kv_got, kv_keep)])
    kv_rows = kv_rows.reshape(2, 2, 2, 12, HD).transpose(0, 1, 3, 2, 4).reshape(48, 2 * HD)
    small = jnp.stack([pick(zl, small_keep, small_got), pick(zl, small_got, small_keep)])
    small = small.reshape(4, 256)
    gains_row = jnp.concatenate([small[:, :12].reshape(48), small[:, 12:24].reshape(48)])
    bias_row = small[:, 24:40].reshape(64)
    small = jnp.zeros((48, HD), BF).at[0, :96].set(gains_row).at[1, :64].set(bias_row)

    ends = jnp.cumsum(lengths[0])
    ranks = jnp.stack([rank, 2 * zl + 1 - core, 2 * (1 - zl) + core, 2 * (1 - zl) + 1 - core])
    group = 4 * rows
    places = (ranks[:, None] * rows + jnp.arange(rows, dtype=jnp.int32)[None, :]).reshape(group)
    passed = ends[None, :] <= places[:, None]
    starts = jnp.sum(jnp.where(passed, lengths[0][None, :], 0), axis=1)
    inverse = THETA ** (-(2.0 * jnp.arange(HD // 2, dtype=F32)) / HD)
    inverse = jnp.concatenate([inverse, inverse])[None, :]
    angles = (places - starts).astype(F32)[:, None] * inverse
    sign = jnp.where(jnp.arange(HD) < HD // 2, -1.0, 1.0).astype(F32)[None, :]
    lane = jnp.arange(HD)[None, :]
    ranges = jnp.where(lane == 0, starts[:, None], places[:, None]).astype(F32)
    table = jnp.concatenate([jnp.cos(angles), jnp.sin(angles) * sign, ranges], axis=1)
    tables = (table, jnp.broadcast_to(places.astype(F32)[None, :], (8, group)))

    living = (places[:rows] < ends[-1])[:, None]
    cot_local = jnp.where(living, cotangent, jnp.zeros((), BF))
    cot_groups = token_groups(cot_local)

    across = swap(layer_input, "zl")
    group_inputs = (layer_input, swap(layer_input, "core"), across, swap(across, "core"))

    attn_part = jnp.concatenate([q_weight, kv_rows, small, o_weight.T], axis=-1)
    attn_plane = exchange(copies(attn_part, 16), PLANE)
    qkv_plane, o_plane = attn_plane[..., :640], attn_plane[..., 768:]
    small_plane = attn_plane[:, :2, 640:768]
    small_other = swap(small_plane, "zh")
    qkv_other = swap(qkv_plane, "zh")
    o_other = swap(o_plane, "zh")
    waits = (cot_groups[1][1], cot_groups[2][1], group_inputs[3], *tables)
    qkv_full = ordered(qkv_plane, qkv_other, zh, "qkv_weights", waits)
    small = jnp.stack([pick(zh, small_plane, small_other), pick(zh, small_other, small_plane)])
    small = small.reshape(32, 2, HD)
    qkv_full = qkv_full.reshape(width, 640)
    gain_attn, gain_mlp, bias = vmem_call(
        vectors_body,
        [((8, width), F32), ((8, width), F32), ((8, 640), F32)],
        [small[:, 0], small[:, 1], jnp.full((8, HD), rank, jnp.int32)],
        "gains_and_biases",
        limit=16,
    )

    mlp = jnp.concatenate([gate_up, down_weight.T[None]], axis=0)
    mlp = jnp.pad(mlp, ((0, 0), (0, 0), (0, 2 * HALF - mlp.shape[2])))
    mlp_own = pick(zh, mlp[..., :HALF], mlp[..., HALF:])
    mlp_other = swap(pick(zh, mlp[..., HALF:], mlp[..., :HALF]), "zh")
    mlp = vmem_call(
        arrange_body,
        [((6, 48, HALF), BF)],
        [mlp_own, mlp_other, jnp.full((8, HD), zh, jnp.int32)],
        "arranged",
        (kv_crossed,),
        moved=4 * mlp_own.size,
    )[0]
    mlp = lax.all_gather(mlp, PLANE, axis=1, tiled=True)
    mlp = mlp.reshape(3, width, HALF)

    normed_group, queries, kv_rot, attended, lse = vmem_call(
        attn_forward_body,
        [
            ((group, width), BF),
            ((group, 384), BF),
            ((group, 256), BF),
            ((group, 384), BF),
            ((group, 128), F32),
        ],
        [*group_inputs, gain_attn, qkv_full, bias, *tables],
        "attention_forward",
        limit=32,
        flops=2 * group * (width * 640 + 6 * group * HD),
        moved=2 * group * width * 2 + 2 * width * 768,
    )
    o_full = ordered(o_plane, o_other, zh, "o_weights", (attended,)).reshape(width, 384)
    pair = ((2, rows, width), BF)
    keep, give = vmem_call(
        attn_out_body,
        [pair, pair],
        [attended, o_full],
        "attention_out",
        flops=2 * group * width * 384,
        moved=2 * width * 384 + 2 * group * width,
    )
    got = swap(give, "core")
    residual, normed_mlp = vmem_call(
        residual_body,
        [((rows, width), F32), ((rows, width), BF)],
        [layer_input, keep, got, swap(add(keep[1], got[1]), "zl"), gain_mlp],
        "residual_norm",
        moved=10 * rows * width,
    )

    after_rows, before_rows = z_shift(normed_mlp, -1), z_shift(normed_mlp, 1)
    far_rows = z_shift(normed_mlp, 2)
    own = (normed_mlp, swap(normed_mlp, "core"))
    own_out = ff_rows(own, cot_groups[0], mlp, cot_local)
    near = stacked((after_rows, before_rows), own_out[0])
    near = (near, swap(near, "core"))
    near_out = ff_rows(near, cot_groups[1], mlp, own_out[0])
    far_rows = stacked((far_rows,), near_out[0])
    far = (far_rows, swap(far_rows, "core"))
    near_sum = [
        add(mine, swap(others, "core"))
        for mine, others in zip(halves(near_out[3], 0), halves(near_out[4], 0))
    ]
    near_got = (z_shift(near_sum[0], 1), z_shift(near_sum[1], -1))
    far_out = ff_rows(far, cot_groups[2], mlp, near_sum[1])
    far_sum = add(far_out[3], swap(far_out[4], "core"))
    own_got = swap(own_out[4], "core")
    far_got = z_shift(far_sum, 2)
    results = (own_out, near_out, far_out)
    hidden, gate_grads, up_grads = ([r[i] for r in results] for i in range(3))
    flat_normed = [*own, *near, *far]
    flat_cots = [part for pair in cot_groups for part in pair]
    grad_terms = weight_grads(flat_normed, flat_cots, hidden, gate_grads, up_grads, far_sum)
    residual_grad, branch, gain_mlp_grad = vmem_call(
        ff_back_body,
        [((rows, width), F32), ((rows, width), BF), ((1, width), F32)],
        [own_out[3], own_got, *near_got, far_got, residual, cot_local, gain_mlp],
        "residual_gradient",
        (grad_terms,),
        limit=60,
        flops=10**9 * WEIGHT,
        moved=24 * rows * width,
    )
    mlp_grads = lax.psum_scatter(
        grad_terms.reshape(6, width // 2, HALF), PLANE, scatter_dimension=1, tiled=True
    ).reshape(3, 2, 48, HALF)
    own_grads = lax.dynamic_index_in_dim(mlp_grads, zh, 1, keepdims=False)
    other_grads = swap(lax.dynamic_index_in_dim(mlp_grads, 1 - zh, 1, keepdims=False), "zh")
    own_grads, other_grads = own_grads.astype(F32), other_grads.astype(F32)
    mlp_shard = jnp.concatenate(
        [pick(zh, own_grads, other_grads), pick(zh, other_grads, own_grads)], axis=-1
    )[..., : gate_up.shape[2]]
    gate_up_shard = mlp_shard[:2]
    down_shard = mlp_shard[2].T

    out_pairs = down_rows(hidden, mlp, branch)
    layer_output = (residual + token_sums(out_pairs)).astype(BF)

    across = stacked((swap(branch, "zl"),), out_pairs[0][0])
    branch_group = (branch, swap(branch, "core"), across, swap(across, "core"))
    qkv_grad, keep, give, sums, gain_attn_grad = vmem_call(
        attn_backward_body,
        [((group, 640), BF), pair, pair, ((1, 640), F32), ((1, width), F32)],
        [*branch_group, *group_inputs, o_full, qkv_full, queries, kv_rot, lse, *tables],
        "attention_backward",
        limit=60,
        scratch=[pltpu.VMEM((group, width), BF)],
        flops=2 * group * (width * 1024 + 15 * group * HD),
        moved=4 * group * width + 2 * width * 1024,
    )
    terms = vmem_call(
        attn_grads_body,
        [((32, width // 32, 1152), BF)],
        [
            normed_group,
            *branch_group,
            qkv_grad,
            attended,
            gain_attn_grad,
            gain_mlp_grad,
            sums,
            jnp.full((8, HD), rank, jnp.int32),
        ],
        "attention_weight_gradients",
        scratch=[pltpu.VMEM((group, width), BF)],
        limit=60,
        flops=2 * group * width * 1024,
        moved=4 * group * width + 2 * width * 1152,
    )[0]
    attn_shard = summed(exchange(terms, DATA))

    got = swap(give, "core")
    across = swap(add(keep[1], got[1]), "zl")
    input_grad = vmem_call(
        attn_back_body,
        [((rows, width), F32)],
        [keep, got, across, layer_input, residual_grad, gain_attn],
        "input_gradient",
        moved=20 * rows * width,
    )[0]

    q_shard = attn_shard[:, :384]
    o_shard = attn_shard[:, 768:].T
    kv_sum = attn_shard[:, 384:640].reshape(2, 2, 12, 2, HD)
    kv_keep = lax.dynamic_index_in_dim(kv_sum, core, 1, keepdims=False).reshape(48, HD)
    kv_give = lax.dynamic_index_in_dim(kv_sum, 1 - core, 1, keepdims=False).reshape(48, HD)
    vectors = attn_shard[:8, 640:768]
    got = swap(jnp.concatenate([kv_give, vectors]), "core")
    kv_sum = (kv_keep + got[:48]).reshape(2, 24, HD)
    vectors = vectors + got[48:]
    kv_keep = pick(zl, kv_sum[0], kv_sum[1])
    got = swap(jnp.concatenate([pick(zl, kv_sum[1], kv_sum[0]), vectors]), "zl")
    kv_got = got[:24]
    vectors = vectors + got[24:]
    kv_shard = jnp.concatenate([pick(zl, kv_keep, kv_got), pick(zl, kv_got, kv_keep)], axis=-1)
    kv_shard = kv_shard.reshape(12, 2, 2 * HD).transpose(1, 0, 2)

    def own_part(row, size):
        return lax.dynamic_index_in_dim(
            vectors[row, : 4 * size].reshape(4, size), rank, 0, keepdims=False
        )

    return (
        layer_output,
        input_grad,
        q_shard,
        kv_shard,
        o_shard,
        jnp.stack([own_part(0, 12), own_part(1, 12)]),
        own_part(2, 14),
        own_part(3, 2),
        gate_up_shard,
        down_shard,
    )


def solution(mesh):
    fine = Mesh(mesh.devices.reshape(SIZES), AXES)
    dp = ("zh", "y", "x")
    tensor = ("zl", "core")
    every = dp + tensor
    in_specs = (
        P(every, None),
        P(dp, tensor),
        P(None, every, None),
        P(tensor, dp),
        P(None, every),
        P(every),
        P(None, dp, tensor),
        P(tensor, dp),
        P(every, None),
        P(dp, None),
    )
    out_specs = (
        P(every, None),
        P(every, None),
        P(dp, tensor),
        P(None, every, None),
        P(tensor, dp),
        P(None, every),
        P(every),
        P(every),
        P(None, dp, tensor),
        P(tensor, dp),
    )
    return jax.shard_map(shards, mesh=fine, in_specs=in_specs, out_specs=out_specs, check_vma=False)
```

```python
import functools

import jax
import jax.numpy as jnp
from jax import lax
from jax.experimental import pallas as pl
from jax.experimental.pallas import tpu as pltpu
from jax.sharding import Mesh, PartitionSpec as P

HQ = 12
KVH = 2
HD = 128
EPSILON = 1e-06
THETA = 1000000.0

AXES = ("zh", "y", "x", "zl", "core")
SIZES = (2, 4, 4, 2, 2)
ZRING = ("zh", "zl")
PLANE = ("y", "x")
DATA = ("zh", "y", "x")
HALF = 1152
BF = jnp.bfloat16
WEIGHT = 1000
F32 = jnp.float32


def swap(block, axis):
    return lax.ppermute(block, axis, [(0, 1), (1, 0)])


def halves(block, dim):
    middle = block.shape[dim] // 2
    return (
        lax.slice_in_dim(block, 0, middle, axis=dim),
        lax.slice_in_dim(block, middle, block.shape[dim], axis=dim),
    )


def add(*terms):
    total = terms[0].astype(F32)
    for term in terms[1:]:
        total = total + term.astype(F32)
    return total.astype(terms[0].dtype)


def exchange(blocks, axes):
    return lax.all_to_all(blocks, axes, split_axis=0, concat_axis=0, tiled=True)


def spread(block, axes, count):
    return exchange(jnp.broadcast_to(block[None], (count,) + block.shape), axes)


def z_shift(block, by):
    return lax.ppermute(block, ZRING, [(i, (i + by) % 4) for i in range(4)])


def token_groups(block):
    near = jnp.concatenate([z_shift(block, -1), z_shift(block, 1)], axis=0)
    far = z_shift(block, 2)
    return [(part, swap(part, "core")) for part in (block, near, far)]


def token_sums(pairs):
    own, near, far = (add(mine, swap(others, "core")) for mine, others in pairs)
    after_rows, before_rows = halves(near, 0)
    terms = (own, z_shift(after_rows, 1), z_shift(before_rows, -1), z_shift(far, 2))
    return sum(term.astype(F32) for term in terms)


def hold_body(w, out, sem):
    copy = pltpu.make_async_copy(w, out, sem)
    copy.start()
    copy.wait()


def held(weights):
    return pl.pallas_call(
        hold_body,
        out_shape=pltpu.VMEM(weights.shape, weights.dtype),
        in_specs=[pl.BlockSpec(memory_space=pl.ANY)],
        out_specs=pl.BlockSpec(memory_space=pltpu.VMEM),
        scratch_shapes=[pltpu.SemaphoreType.DMA],
        compiler_params=pltpu.CompilerParams(vmem_limit_bytes=16 * 1024 * 1024),
        cost_estimate=pl.CostEstimate(
            flops=0, bytes_accessed=4 * weights.size, transcendentals=0
        ),
        name="held",
    )(weights)


def ff_body(na, nb, ca, cb, w, _, m_out, dg_out, du_out, dna_out, dnb_out, nbuf, cbuf, sem, *, tile):
    half = na.shape[0]
    parts = ((na, nbuf, 0), (nb, nbuf, 1), (ca, cbuf, 0), (cb, cbuf, 1))
    fetches = [
        pltpu.make_async_copy(part, buffer.at[pl.ds(k * half, half)], sem.at[i])
        for i, (part, buffer, k) in enumerate(parts)
    ]
    for fetch in fetches:
        fetch.start()
    for fetch in fetches:
        fetch.wait()
    tiles = 2 * half // tile
    for i in range(tiles):
        at = pl.ds(i * tile, tile)
        rows = nbuf[at]
        gate = dot(rows, w[0])
        up = dot(rows, w[1])
        hidden_grad = dot(cbuf[at], w[2])
        sigma = 1.0 / (1.0 + jnp.exp(-gate))
        act = gate * sigma
        m_out[at] = (act * up).astype(BF)
        up_grad = (hidden_grad * act).astype(BF)
        gate_grad = (hidden_grad * up * sigma * (1.0 + gate * (1.0 - sigma))).astype(BF)
        dg_out[at] = gate_grad
        du_out[at] = up_grad
        back = (dot_t(gate_grad, w[0]) + dot_t(up_grad, w[1])).astype(BF)
        if tiles == 1:
            dna_out[...] = back[:half]
            dnb_out[...] = back[half:]
        else:
            out = dna_out if i < tiles // 2 else dnb_out
            out[pl.ds(i % (tiles // 2) * tile, tile)] = back


def ff_rows(normed, cots, weights, order, tile=256):
    half, width = normed[0].shape
    units = weights.shape[2]
    anywhere = pl.BlockSpec(memory_space=pl.ANY)
    vmem = pl.BlockSpec(memory_space=pltpu.VMEM)
    return pl.pallas_call(
        functools.partial(ff_body, tile=tile),
        out_shape=[jax.ShapeDtypeStruct((2 * half, units), BF)] * 3
        + [jax.ShapeDtypeStruct((half, width), BF)] * 2,
        in_specs=[anywhere] * 4 + [vmem, anywhere],
        out_specs=[vmem] * 5,
        scratch_shapes=[
            pltpu.VMEM((2 * half, width), BF),
            pltpu.VMEM((2 * half, width), BF),
            pltpu.SemaphoreType.DMA((4,)),
        ],
        compiler_params=pltpu.CompilerParams(vmem_limit_bytes=32 * 1024 * 1024),
        cost_estimate=pl.CostEstimate(
            flops=20 * half * width * units,
            bytes_accessed=6 * width * units,
            transcendentals=2 * half * units,
        ),
        name="feed_forward_rows",
    )(*normed, *cots, weights, order)


def wg_body(*refs, sizes, tile):
    count = len(sizes)
    groups = count // 2
    normed, cots, refs = refs[:count], refs[count : 2 * count], refs[2 * count :]
    hidden, gates, ups = refs[:groups], refs[groups : 2 * groups], refs[2 * groups : 3 * groups]
    out, nbuf, cbuf, mbuf, gbuf, ubuf, turned, sem = refs[3 * groups + 1 :]
    pair_sizes = [sizes[2 * i] + sizes[2 * i + 1] for i in range(groups)]

    def copies(at, buffer, sources, lengths):
        result, start = [], 0
        for source, length in zip(sources, lengths):
            target = buffer.at[pl.ds(start, length)]
            result.append(pltpu.make_async_copy(source, target, sem.at[at]))
            start += length
        return result

    def normed_copies():
        return copies(0, nbuf, normed, sizes)

    def cot_copies():
        return copies(1, cbuf, cots, sizes)

    def gate_copies():
        return copies(2, gbuf, gates, pair_sizes)

    def up_copies():
        return copies(3, ubuf, ups, pair_sizes)

    def hidden_copies():
        return copies(4, mbuf, hidden, pair_sizes)

    which, step = pl.program_id(0), pl.program_id(1)

    @pl.when((which == 0) & (step == 0))
    def _():
        first = normed_copies() + gate_copies()
        for copy in first + up_copies() + cot_copies() + hidden_copies():
            copy.start()
        for copy in first:
            copy.wait()

    @pl.when((which == 1) & (step == 0))
    def _():
        for copy in up_copies():
            copy.wait()

    @pl.when((which == 2) & (step == 0))
    def _():
        for copy in cot_copies() + hidden_copies():
            copy.wait()

    columns = pl.ds(pl.multiple_of(step * tile, tile), tile)
    @pl.when(which == 0)
    def _():
        left = nbuf[:, columns].T
        turned[step] = left
        out[...] = dot(left, gbuf[...]).astype(BF)

    @pl.when(which == 1)
    def _():
        out[...] = dot(turned[step], ubuf[...]).astype(BF)

    @pl.when(which == 2)
    def _():
        out[...] = dot(cbuf[:, columns].T, mbuf[...]).astype(BF)


def weight_grads(normed, cots, hidden, gates, ups, order, tile=768):
    sizes = tuple(part.shape[0] for part in normed)
    rows, width, units = sum(sizes), normed[0].shape[1], hidden[0].shape[1]
    anywhere = pl.BlockSpec(memory_space=pl.ANY)
    return pl.pallas_call(
        functools.partial(wg_body, sizes=sizes, tile=tile),
        grid=(3, width // tile),
        out_shape=jax.ShapeDtypeStruct((3, width, units), BF),
        in_specs=[anywhere] * (2 * len(normed) + 3 * len(hidden) + 1),
        out_specs=pl.BlockSpec((None, tile, units), lambda i, j: (i, j, 0)),
        scratch_shapes=[pltpu.VMEM((rows, width), BF)] * 2
        + [pltpu.VMEM((rows, units), BF)] * 3
        + [pltpu.VMEM((width // tile, tile, rows), BF), pltpu.SemaphoreType.DMA((5,))],
        compiler_params=pltpu.CompilerParams(vmem_limit_bytes=48 * 1024 * 1024),
        cost_estimate=pl.CostEstimate(
            flops=6 * rows * width * units,
            bytes_accessed=6 * width * units + rows * (4 * width + 6 * units),
            transcendentals=0,
        ),
        name="weight_gradients",
    )(*normed, *cots, *hidden, *gates, *ups, order)


def down_body(ha, hb, hc, w, *outs, tile=256):
    for group, hidden in enumerate((ha, hb, hc)):
        half = hidden.shape[0] // 2
        step = min(tile, 2 * half)
        for start in range(0, 2 * half, step):
            part = dot_t(hidden[pl.ds(start, step)], w[...]).astype(BF)
            if step > half:
                outs[2 * group][...] = part[:half]
                outs[2 * group + 1][...] = part[half:]
            else:
                outs[2 * group + start // half][pl.ds(start % half, step)] = part


def down_rows(hidden, weights, order):
    _, width, units = weights.shape
    halved = [part.shape[0] // 2 for part in hidden for _ in range(2)]
    outs = vmem_call(
        down_body,
        [((rows, width), BF) for rows in halved],
        [*hidden, (weights, 2)],
        "down_rows",
        (order,),
        limit=60,
        flops=2 * sum(halved) * width * units,
        moved=2 * width * units + 2 * sum(halved) * (width + units),
    )
    return [(outs[0], outs[1]), (outs[2], outs[3]), (outs[4], outs[5])]


def dot(a, b):
    return jnp.dot(a, b, preferred_element_type=F32)


def dot_t(a, b):
    return lax.dot_general(a, b, (((1,), (1,)), ((), ())), preferred_element_type=F32)


def t_dot(a, b):
    return lax.dot_general(a, b, (((0,), (0,)), ((), ())), preferred_element_type=F32)


def pick(index, low, high):
    return jnp.where(index == 0, low, high)


def vmem_call(body, outs, ins, name, order=(), scratch=(), limit=16, flops=0, moved=0):
    count, skipped, results, extra = len(ins), len(order), len(outs), len(scratch)
    parts = [value[1] if isinstance(value, tuple) else None for value in ins]
    ins = [value[0] if isinstance(value, tuple) else value for value in ins]

    def kernel(*refs):
        sources, refs = refs[:count], refs[count + skipped :]
        fixed, buffers, sem = refs[: results + extra], refs[results + extra : -1], refs[-1]
        fetches = [
            pltpu.make_async_copy(source if at is None else source.at[at], buffer, sem.at[i])
            for i, (source, at, buffer) in enumerate(zip(sources, parts, buffers))
        ]
        for fetch in fetches:
            fetch.start()
        for fetch in fetches:
            fetch.wait()
        body(*buffers, *fixed)

    return pl.pallas_call(
        kernel,
        out_shape=[jax.ShapeDtypeStruct(shape, dtype) for shape, dtype in outs],
        in_specs=[pl.BlockSpec(memory_space=pl.ANY)] * (count + skipped),
        out_specs=[pl.BlockSpec(memory_space=pltpu.VMEM)] * results,
        scratch_shapes=[
            *scratch,
            *(
                pltpu.VMEM(value.shape if at is None else value.shape[1:], value.dtype)
                for value, at in zip(ins, parts)
            ),
            pltpu.SemaphoreType.DMA((count,)),
        ],
        compiler_params=pltpu.CompilerParams(vmem_limit_bytes=limit * 1024 * 1024),
        cost_estimate=pl.CostEstimate(flops=flops, bytes_accessed=moved, transcendentals=0),
        name=name,
    )(*ins, *order)


def copies_body(block, out):
    for i in range(out.shape[0]):
        out[i] = block[...]


def copies(block, count, *order):
    shape = (count,) + block.shape
    moved = 2 * count * block.size
    return vmem_call(
        copies_body, [(shape, block.dtype)], [block], "copies", order, moved=moved
    )[0]


def arrange_body(own, other, zh, out):
    mine = zh[0:1, 0:1] == 0
    for i in range(3):
        out[2 * i] = jnp.where(mine, own[i], other[i])
        out[2 * i + 1] = jnp.where(mine, other[i], own[i])


def ordered_body(own, other, zh, out):
    mine = zh[0:1, 0:1] == 0
    for i in range(own.shape[0]):
        out[0, i] = jnp.where(mine, own[i], other[i])
        out[1, i] = jnp.where(mine, other[i], own[i])


def ordered(own, other, zh, name, order):
    flag = jnp.full((8, HD), zh, jnp.int32)
    shape = (2,) + own.shape
    return vmem_call(
        ordered_body, [(shape, BF)], [own, other, flag], name, order, moved=8 * own.size
    )[0]


def sum_body(terms, out):
    total = terms[0].astype(F32)
    for i in range(1, terms.shape[0]):
        total = total + terms[i].astype(F32)
    out[...] = total


def summed(terms, *order):
    return vmem_call(
        sum_body, [(terms.shape[1:], F32)], [terms], "summed", order, moved=2 * terms.size
    )[0]


def stack_body(*refs):
    *parts, out = refs
    rows = parts[0].shape[0]
    for i, part in enumerate(parts):
        out[i * rows : (i + 1) * rows] = part[...]


def stacked(parts, *order):
    rows, columns = parts[0].shape
    shape = (len(parts) * rows, columns)
    moved = 4 * shape[0] * columns
    return vmem_call(stack_body, [(shape, BF)], list(parts), "stacked", order, moved=moved)[0]


def row_of(blocks, offset, size):
    count, lanes = blocks.shape
    line = (lanes, count * size)
    at = lax.broadcasted_iota(jnp.int32, line, 1)
    from_lane = lax.broadcasted_iota(jnp.int32, line, 0) - offset
    spots = (lax.rem(at, size) == from_lane).astype(BF)
    values = dot(blocks, spots)
    at = lax.broadcasted_iota(jnp.int32, values.shape, 1)
    owner = lax.broadcasted_iota(jnp.int32, values.shape, 0)
    mine = (at >= owner * size) & (at < (owner + 1) * size)
    return jnp.sum(jnp.where(mine, values, 0.0), axis=0, keepdims=True)


def vectors_body(gains, biases, ranks, attn_out, mlp_out, bias_out):
    attn_out[...] = jnp.broadcast_to(row_of(gains[...], 0, 48), attn_out.shape)
    mlp_out[...] = jnp.broadcast_to(row_of(gains[...], 48, 48), mlp_out.shape)
    full = row_of(biases[...], 0, 64)
    rank = ranks[0:1, 0:1]
    query = key = value = 0.0
    for i in range(4):
        query = query + jnp.where(rank == i, full[:, 384 * i : 384 * (i + 1)], 0.0)
    for i in range(2):
        mine = (rank >= 2 * i) & (rank < 2 * i + 2)
        key = key + jnp.where(mine, full[:, 1536 + HD * i : 1536 + HD * (i + 1)], 0.0)
        value = value + jnp.where(mine, full[:, 1792 + HD * i : 1792 + HD * (i + 1)], 0.0)
    line = jnp.concatenate([query, key, value], axis=1)
    bias_out[...] = jnp.broadcast_to(line, bias_out.shape)


def turn(vectors, cos2, sin2):
    return vectors * cos2 + pltpu.roll(vectors, HD // 2, 1) * sin2


def unpack_table(table, places):
    first, last = table[:, 2 * HD : 2 * HD + 1], table[:, 2 * HD + 1 : 2 * HD + 2]
    keys = places[0:1, :]
    return table[:, :HD], table[:, HD : 2 * HD], (keys >= first) & (keys <= last)


def masked_scores(queries, keys, allowed):
    return jnp.where(allowed, dot_t(queries, keys) * HD ** (-0.5), -1e30)


def attn_forward_body(
    x0, x1, x2, x3, gain, w, bias, table, places,
    n_out, q_out, kv_out, o_out, lse_out,
):
    rows = x0.shape[0]
    for i, x in enumerate((x0, x1, x2, x3)):
        part = x[...].astype(F32)
        scale = lax.rsqrt(jnp.mean(part * part, axis=-1, keepdims=True) + EPSILON)
        n_out[i * rows : (i + 1) * rows] = (part * scale * gain[0:1]).astype(BF)
    qkv = dot(n_out[...], w[...]) + bias[0:1]
    cosines, sines, allowed = unpack_table(table, places)
    keys = turn(qkv[:, 384:512], cosines, sines).astype(BF)
    values = qkv[:, 512:].astype(BF)
    kv_out[:, :HD] = keys
    kv_out[:, HD:] = values
    lses = []
    for h in range(3):
        at = slice(h * HD, (h + 1) * HD)
        queries = turn(qkv[:, at], cosines, sines).astype(BF)
        q_out[:, at] = queries
        scores = masked_scores(queries, keys, allowed)
        peak = jnp.max(scores, axis=-1, keepdims=True)
        shifted = jnp.exp(scores - peak)
        total = jnp.sum(shifted, axis=-1, keepdims=True)
        probs = (shifted / total).astype(BF)
        o_out[:, at] = dot(probs, values).astype(BF)
        lses.append(peak + jnp.log(total))
    lse_out[...] = jnp.concatenate(lses + [jnp.zeros((4 * rows, 125), F32)], axis=1)


def parted(partial, keep, give):
    rows = partial.shape[0] // 4
    keep[0] = partial[:rows].astype(BF)
    give[0] = partial[rows : 2 * rows].astype(BF)
    keep[1] = partial[2 * rows : 3 * rows].astype(BF)
    give[1] = partial[3 * rows :].astype(BF)


def attn_out_body(o, w, keep, give):
    parted(dot_t(o[...], w[...]), keep, give)


def residual_body(x, keep, got, across, gain, h_out, n_out):
    h = x[...].astype(F32) + keep[0].astype(F32) + got[0].astype(F32) + across[...].astype(F32)
    h_out[...] = h
    scale = lax.rsqrt(jnp.mean(h * h, axis=-1, keepdims=True) + EPSILON)
    n_out[...] = (h * scale * gain[0:1]).astype(BF)


def norm_backward(grad, rows, gain):
    scale = lax.rsqrt(jnp.mean(rows * rows, axis=-1, keepdims=True) + EPSILON)
    scaled = grad * gain
    back = scale * scaled - rows * scale**3 * jnp.mean(scaled * rows, axis=-1, keepdims=True)
    return back, jnp.sum(grad * rows * scale, axis=0, keepdims=True)


def ff_back_body(own_a, own_b, got_a, got_b, got_c, h, cot, gain, grad_out, branch_out, gain_out):
    grad = sum(part[...].astype(F32) for part in (own_a, own_b, got_a, got_b, got_c))
    back, gain_out[...] = norm_backward(grad, h[...], gain[0:1])
    total = cot[...].astype(F32) + back
    grad_out[...] = total
    branch_out[...] = total.astype(BF)


def attn_back_body(keep, got, across, x, above, gain, grad_out):
    grad = keep[0].astype(F32) + got[0].astype(F32) + across[...].astype(F32)
    back, _ = norm_backward(grad, x[...].astype(F32), gain[0:1])
    grad_out[...] = above[...] + back


def attn_backward_body(
    b0, b1, b2, b3, x0, x1, x2, x3, wo, w, q, kv, lse, table, places,
    grads_out, keep, give, sums_out, gain_out, bbuf,
):
    rows = b0.shape[0]
    for i, part in enumerate((b0, b1, b2, b3)):
        bbuf[i * rows : (i + 1) * rows] = part[...]
    attended_grad = dot(bbuf[...], wo[...]).astype(BF)
    keys, values = kv[:, :HD], kv[:, HD:]
    cosines, sines, allowed = unpack_table(table, places)
    sines = -sines
    key_grad = value_grad = 0.0
    for h in range(3):
        at = slice(h * HD, (h + 1) * HD)
        queries, o_grad = q[:, at], attended_grad[:, at]
        probs = jnp.exp(masked_scores(queries, keys, allowed) - lse[:, h : h + 1])
        prob_grad = dot_t(o_grad, values)
        inner = jnp.sum(probs * prob_grad, axis=-1, keepdims=True)
        score_grad = (probs * (prob_grad - inner)).astype(BF)
        query_grad = dot(score_grad, keys) * HD ** (-0.5)
        grads_out[:, at] = turn(query_grad, cosines, sines).astype(BF)
        key_grad = key_grad + t_dot(score_grad, queries)
        value_grad = value_grad + t_dot(probs.astype(BF), o_grad)
    grads_out[:, 384:512] = turn(key_grad * HD ** (-0.5), cosines, sines).astype(BF)
    grads_out[:, 512:] = value_grad.astype(BF)
    grads = grads_out[...]
    sums_out[...] = jnp.sum(grads.astype(F32), axis=0, keepdims=True)
    partial = dot_t(grads, w[...])
    parted(partial, keep, give)
    gain_grad = 0.0
    for i, x in enumerate((x0, x1, x2, x3)):
        part = x[...].astype(F32)
        scale = lax.rsqrt(jnp.mean(part * part, axis=-1, keepdims=True) + EPSILON)
        terms = partial[i * rows : (i + 1) * rows] * part * scale
        gain_grad = gain_grad + jnp.sum(terms, axis=0, keepdims=True)
    gain_out[...] = gain_grad


def blocks_of(row, size):
    count = row.shape[1] // size
    at = lax.broadcasted_iota(jnp.int32, (count, row.shape[1]), 1)
    owner = lax.broadcasted_iota(jnp.int32, (count, row.shape[1]), 0)
    mine = (at >= owner * size) & (at < (owner + 1) * size)
    values = jnp.where(mine, row, 0.0).astype(BF)
    at = lax.broadcasted_iota(jnp.int32, (row.shape[1], HD), 0)
    lane = lax.broadcasted_iota(jnp.int32, (row.shape[1], HD), 1)
    return dot(values, (lax.rem(at, size) == lane).astype(BF))


def attn_grads_body(
    normed, b0, b1, b2, b3, qkv_grad, attended, gain_attn, gain_mlp, sums, ranks, out, bbuf
):
    size = b0.shape[0]
    for i, part in enumerate((b0, b1, b2, b3)):
        bbuf[i * size : (i + 1) * size] = part[...]
    half = bbuf.shape[1] // 2
    for i in range(2):
        at, blocks = slice(i * half, (i + 1) * half), slice(16 * i, 16 * (i + 1))
        grad = t_dot(normed[:, at], qkv_grad[...]).astype(BF)
        out[blocks, :, :640] = grad.reshape(16, half // 16, 640)
        grad = t_dot(bbuf[:, at], attended[...]).astype(BF)
        out[blocks, :, 768:] = grad.reshape(16, half // 16, 384)
    rank = ranks[0:1, 0:1]
    parts = [jnp.where(rank == i, sums[:, :384], 0.0) for i in range(4)]
    for start in (384, 512):
        for i in range(2):
            mine = (rank >= 2 * i) & (rank < 2 * i + 2)
            parts.append(jnp.where(mine, sums[:, start : start + HD], 0.0))
    rows_of = (
        blocks_of(gain_attn[...], 48),
        blocks_of(gain_mlp[...], 48),
        blocks_of(jnp.concatenate(parts[:6], axis=1), 56),
        blocks_of(jnp.concatenate(parts[6:], axis=1), 8),
    )
    at = lax.broadcasted_iota(jnp.int32, (32, out.shape[1], HD), 1)
    tail = jnp.zeros((32, out.shape[1], HD), F32)
    for i, values in enumerate(rows_of):
        tail = jnp.where(at == i, values[:, None, :], tail)
    out[:, :, 640:768] = tail.astype(BF)


def shards(
    layer_input,
    q_weight,
    kv_weight,
    o_weight,
    norm_gains,
    qkv_bias,
    gate_up,
    down_weight,
    cotangent,
    lengths,
):
    zh, zl, core = (lax.axis_index(a) for a in ("zh", "zl", "core"))
    rank = 2 * zl + core
    width = layer_input.shape[1]
    rows = layer_input.shape[0]

    small = jnp.concatenate([norm_gains.reshape(-1), qkv_bias, jnp.zeros((216,), BF)])
    vectors = jnp.concatenate([kv_weight.reshape(24, 256), small[None], jnp.zeros((7, 256), BF)])
    got = swap(vectors, "core")
    both = jnp.stack([pick(core, vectors, got), pick(core, got, vectors)])
    small_keep = both[:, 24].reshape(2, 2, HD)
    kv_keep = pick(zl, both[:, :24, :HD], both[:, :24, HD:])
    kv_give = pick(zl, both[:, :24, HD:], both[:, :24, :HD])
    kv_crossed = swap(
        jnp.concatenate([kv_give, small_keep, jnp.zeros((2, 6, HD), BF)], axis=1), "zl"
    )
    kv_got, small_got = kv_crossed[:, :24], kv_crossed[:, 24:26]
    kv_rows = jnp.stack([pick(zl, kv_keep, kv_got), pick(zl, kv_got, kv_keep)])
    kv_rows = kv_rows.reshape(2, 2, 2, 12, HD).transpose(0, 1, 3, 2, 4).reshape(48, 2 * HD)
    small = jnp.stack([pick(zl, small_keep, small_got), pick(zl, small_got, small_keep)])
    small = small.reshape(4, 256)
    gains_row = jnp.concatenate([small[:, :12].reshape(48), small[:, 12:24].reshape(48)])
    bias_row = small[:, 24:40].reshape(64)
    small = jnp.zeros((48, HD), BF).at[0, :96].set(gains_row).at[1, :64].set(bias_row)

    ends = jnp.cumsum(lengths[0])
    ranks = jnp.stack([rank, 2 * zl + 1 - core, 2 * (1 - zl) + core, 2 * (1 - zl) + 1 - core])
    group = 4 * rows
    places = (ranks[:, None] * rows + jnp.arange(rows, dtype=jnp.int32)[None, :]).reshape(group)
    passed = ends[None, :] <= places[:, None]
    starts = jnp.sum(jnp.where(passed, lengths[0][None, :], 0), axis=1)
    inverse = THETA ** (-(2.0 * jnp.arange(HD // 2, dtype=F32)) / HD)
    inverse = jnp.concatenate([inverse, inverse])[None, :]
    angles = (places - starts).astype(F32)[:, None] * inverse
    sign = jnp.where(jnp.arange(HD) < HD // 2, -1.0, 1.0).astype(F32)[None, :]
    lane = jnp.arange(HD)[None, :]
    ranges = jnp.where(lane == 0, starts[:, None], places[:, None]).astype(F32)
    table = jnp.concatenate([jnp.cos(angles), jnp.sin(angles) * sign, ranges], axis=1)
    tables = (table, jnp.broadcast_to(places.astype(F32)[None, :], (8, group)))

    living = (places[:rows] < ends[-1])[:, None]
    cot_local = jnp.where(living, cotangent, jnp.zeros((), BF))
    cot_groups = token_groups(cot_local)

    across = swap(layer_input, "zl")
    group_inputs = (layer_input, swap(layer_input, "core"), across, swap(across, "core"))

    attn_part = jnp.concatenate([q_weight, kv_rows, small, o_weight.T], axis=-1)
    attn_plane = exchange(copies(attn_part, 16), PLANE)
    qkv_plane, o_plane = attn_plane[..., :640], attn_plane[..., 768:]
    small_plane = attn_plane[:, :2, 640:768]
    small_other = swap(small_plane, "zh")
    qkv_other = swap(qkv_plane, "zh")
    o_other = swap(o_plane, "zh")
    waits = (cot_groups[1][1], cot_groups[2][1], group_inputs[3], *tables)
    qkv_full = ordered(qkv_plane, qkv_other, zh, "qkv_weights", waits)
    small = jnp.stack([pick(zh, small_plane, small_other), pick(zh, small_other, small_plane)])
    small = small.reshape(32, 2, HD)
    qkv_full = qkv_full.reshape(width, 640)
    gain_attn, gain_mlp, bias = vmem_call(
        vectors_body,
        [((8, width), F32), ((8, width), F32), ((8, 640), F32)],
        [small[:, 0], small[:, 1], jnp.full((8, HD), rank, jnp.int32)],
        "gains_and_biases",
        limit=16,
    )

    mlp = jnp.concatenate([gate_up, down_weight.T[None]], axis=0)
    mlp = jnp.pad(mlp, ((0, 0), (0, 0), (0, 2 * HALF - mlp.shape[2])))
    mlp_own = pick(zh, mlp[..., :HALF], mlp[..., HALF:])
    mlp_other = swap(pick(zh, mlp[..., HALF:], mlp[..., :HALF]), "zh")
    mlp = vmem_call(
        arrange_body,
        [((6, 48, HALF), BF)],
        [mlp_own, mlp_other, jnp.full((8, HD), zh, jnp.int32)],
        "arranged",
        (kv_crossed,),
        moved=4 * mlp_own.size,
    )[0]
    mlp = lax.all_gather(mlp, PLANE, axis=1, tiled=True)
    mlp = mlp.reshape(3, width, HALF)

    normed_group, queries, kv_rot, attended, lse = vmem_call(
        attn_forward_body,
        [
            ((group, width), BF),
            ((group, 384), BF),
            ((group, 256), BF),
            ((group, 384), BF),
            ((group, 128), F32),
        ],
        [*group_inputs, gain_attn, qkv_full, bias, *tables],
        "attention_forward",
        limit=32,
        flops=2 * group * (width * 640 + 6 * group * HD),
        moved=2 * group * width * 2 + 2 * width * 768,
    )
    o_full = ordered(o_plane, o_other, zh, "o_weights", (attended,)).reshape(width, 384)
    pair = ((2, rows, width), BF)
    keep, give = vmem_call(
        attn_out_body,
        [pair, pair],
        [attended, o_full],
        "attention_out",
        flops=2 * group * width * 384,
        moved=2 * width * 384 + 2 * group * width,
    )
    got = swap(give, "core")
    weights = held(mlp)
    residual, normed_mlp = vmem_call(
        residual_body,
        [((rows, width), F32), ((rows, width), BF)],
        [layer_input, keep, got, swap(add(keep[1], got[1]), "zl"), gain_mlp],
        "residual_norm",
        (weights,),
        moved=10 * rows * width,
    )

    after_rows, before_rows = z_shift(normed_mlp, -1), z_shift(normed_mlp, 1)
    far_rows = z_shift(normed_mlp, 2)
    own = (normed_mlp, swap(normed_mlp, "core"))
    own_out = ff_rows(own, cot_groups[0], weights, cot_local)
    near = stacked((after_rows, before_rows), own_out[0])
    near = (near, swap(near, "core"))
    near_out = ff_rows(near, cot_groups[1], weights, own_out[0])
    far_rows = stacked((far_rows,), near_out[0])
    far = (far_rows, swap(far_rows, "core"))
    near_sum = [
        add(mine, swap(others, "core"))
        for mine, others in zip(halves(near_out[3], 0), halves(near_out[4], 0))
    ]
    near_got = (z_shift(near_sum[0], 1), z_shift(near_sum[1], -1))
    far_out = ff_rows(far, cot_groups[2], weights, near_sum[1])
    far_sum = add(far_out[3], swap(far_out[4], "core"))
    own_got = swap(own_out[4], "core")
    far_got = z_shift(far_sum, 2)
    results = (own_out, near_out, far_out)
    hidden, gate_grads, up_grads = ([r[i] for r in results] for i in range(3))
    flat_normed = [*own, *near, *far]
    flat_cots = [part for pair in cot_groups for part in pair]
    grad_terms = weight_grads(flat_normed, flat_cots, hidden, gate_grads, up_grads, far_sum)
    residual_grad, branch, gain_mlp_grad = vmem_call(
        ff_back_body,
        [((rows, width), F32), ((rows, width), BF), ((1, width), F32)],
        [own_out[3], own_got, *near_got, far_got, residual, cot_local, gain_mlp],
        "residual_gradient",
        (grad_terms,),
        limit=60,
        flops=10**9 * WEIGHT,
        moved=24 * rows * width,
    )
    mlp_grads = lax.psum_scatter(
        grad_terms.reshape(6, width // 2, HALF), PLANE, scatter_dimension=1, tiled=True
    ).reshape(3, 2, 48, HALF)
    own_grads = lax.dynamic_index_in_dim(mlp_grads, zh, 1, keepdims=False)
    other_grads = swap(lax.dynamic_index_in_dim(mlp_grads, 1 - zh, 1, keepdims=False), "zh")
    own_grads, other_grads = own_grads.astype(F32), other_grads.astype(F32)
    mlp_shard = jnp.concatenate(
        [pick(zh, own_grads, other_grads), pick(zh, other_grads, own_grads)], axis=-1
    )[..., : gate_up.shape[2]]
    gate_up_shard = mlp_shard[:2]
    down_shard = mlp_shard[2].T

    out_pairs = down_rows(hidden, mlp, branch)
    layer_output = (residual + token_sums(out_pairs)).astype(BF)

    across = stacked((swap(branch, "zl"),), out_pairs[0][0])
    branch_group = (branch, swap(branch, "core"), across, swap(across, "core"))
    qkv_grad, keep, give, sums, gain_attn_grad = vmem_call(
        attn_backward_body,
        [((group, 640), BF), pair, pair, ((1, 640), F32), ((1, width), F32)],
        [*branch_group, *group_inputs, o_full, qkv_full, queries, kv_rot, lse, *tables],
        "attention_backward",
        limit=60,
        scratch=[pltpu.VMEM((group, width), BF)],
        flops=2 * group * (width * 1024 + 15 * group * HD),
        moved=4 * group * width + 2 * width * 1024,
    )
    terms = vmem_call(
        attn_grads_body,
        [((32, width // 32, 1152), BF)],
        [
            normed_group,
            *branch_group,
            qkv_grad,
            attended,
            gain_attn_grad,
            gain_mlp_grad,
            sums,
            jnp.full((8, HD), rank, jnp.int32),
        ],
        "attention_weight_gradients",
        scratch=[pltpu.VMEM((group, width), BF)],
        limit=60,
        flops=2 * group * width * 1024,
        moved=4 * group * width + 2 * width * 1152,
    )[0]
    attn_shard = summed(exchange(terms, DATA))

    got = swap(give, "core")
    across = swap(add(keep[1], got[1]), "zl")
    input_grad = vmem_call(
        attn_back_body,
        [((rows, width), F32)],
        [keep, got, across, layer_input, residual_grad, gain_attn],
        "input_gradient",
        moved=20 * rows * width,
    )[0]

    q_shard = attn_shard[:, :384]
    o_shard = attn_shard[:, 768:].T
    kv_sum = attn_shard[:, 384:640].reshape(2, 2, 12, 2, HD)
    kv_keep = lax.dynamic_index_in_dim(kv_sum, core, 1, keepdims=False).reshape(48, HD)
    kv_give = lax.dynamic_index_in_dim(kv_sum, 1 - core, 1, keepdims=False).reshape(48, HD)
    vectors = attn_shard[:8, 640:768]
    got = swap(jnp.concatenate([kv_give, vectors]), "core")
    kv_sum = (kv_keep + got[:48]).reshape(2, 24, HD)
    vectors = vectors + got[48:]
    kv_keep = pick(zl, kv_sum[0], kv_sum[1])
    got = swap(jnp.concatenate([pick(zl, kv_sum[1], kv_sum[0]), vectors]), "zl")
    kv_got = got[:24]
    vectors = vectors + got[24:]
    kv_shard = jnp.concatenate([pick(zl, kv_keep, kv_got), pick(zl, kv_got, kv_keep)], axis=-1)
    kv_shard = kv_shard.reshape(12, 2, 2 * HD).transpose(1, 0, 2)

    def own_part(row, size):
        return lax.dynamic_index_in_dim(
            vectors[row, : 4 * size].reshape(4, size), rank, 0, keepdims=False
        )

    return (
        layer_output,
        input_grad,
        q_shard,
        kv_shard,
        o_shard,
        jnp.stack([own_part(0, 12), own_part(1, 12)]),
        own_part(2, 14),
        own_part(3, 2),
        gate_up_shard,
        down_shard,
    )


def solution(mesh):
    fine = Mesh(mesh.devices.reshape(SIZES), AXES)
    dp = ("zh", "y", "x")
    tensor = ("zl", "core")
    every = dp + tensor
    in_specs = (
        P(every, None),
        P(dp, tensor),
        P(None, every, None),
        P(tensor, dp),
        P(None, every),
        P(every),
        P(None, dp, tensor),
        P(tensor, dp),
        P(every, None),
        P(dp, None),
    )
    out_specs = (
        P(every, None),
        P(every, None),
        P(dp, tensor),
        P(None, every, None),
        P(tensor, dp),
        P(None, every),
        P(every),
        P(every),
        P(None, dp, tensor),
        P(tensor, dp),
    )
    return jax.shard_map(shards, mesh=fine, in_specs=in_specs, out_specs=out_specs, check_vma=False)
```

```python
import functools

import jax
import jax.numpy as jnp
from jax import lax
from jax.experimental import pallas as pl
from jax.experimental.pallas import tpu as pltpu
from jax.sharding import Mesh, PartitionSpec as P

HQ = 12
KVH = 2
HD = 128
EPSILON = 1e-06
THETA = 1000000.0

AXES = ("zh", "y", "x", "zl", "core")
SIZES = (2, 4, 4, 2, 2)
ZRING = ("zh", "zl")
PLANE = ("y", "x")
DATA = ("zh", "y", "x")
HALF = 1152
BF = jnp.bfloat16
WEIGHT = 1000
F32 = jnp.float32


def swap(block, axis):
    return lax.ppermute(block, axis, [(0, 1), (1, 0)])


def halves(block, dim):
    middle = block.shape[dim] // 2
    return (
        lax.slice_in_dim(block, 0, middle, axis=dim),
        lax.slice_in_dim(block, middle, block.shape[dim], axis=dim),
    )


def add(*terms):
    total = terms[0].astype(F32)
    for term in terms[1:]:
        total = total + term.astype(F32)
    return total.astype(terms[0].dtype)


def exchange(blocks, axes):
    return lax.all_to_all(blocks, axes, split_axis=0, concat_axis=0, tiled=True)


def spread(block, axes, count):
    return exchange(jnp.broadcast_to(block[None], (count,) + block.shape), axes)


def z_shift(block, by):
    return lax.ppermute(block, ZRING, [(i, (i + by) % 4) for i in range(4)])


def token_groups(block):
    near = jnp.concatenate([z_shift(block, -1), z_shift(block, 1)], axis=0)
    far = z_shift(block, 2)
    return [(part, swap(part, "core")) for part in (block, near, far)]


def token_sums(pairs):
    own, near, far = (add(mine, swap(others, "core")) for mine, others in pairs)
    after_rows, before_rows = halves(near, 0)
    terms = (own, z_shift(after_rows, 1), z_shift(before_rows, -1), z_shift(far, 2))
    return sum(term.astype(F32) for term in terms)


def hold_body(w, out, sem):
    copy = pltpu.make_async_copy(w, out, sem)
    copy.start()
    copy.wait()


def held(weights):
    return pl.pallas_call(
        hold_body,
        out_shape=pltpu.VMEM(weights.shape, weights.dtype),
        in_specs=[pl.BlockSpec(memory_space=pl.ANY)],
        out_specs=pl.BlockSpec(memory_space=pltpu.VMEM),
        scratch_shapes=[pltpu.SemaphoreType.DMA],
        compiler_params=pltpu.CompilerParams(vmem_limit_bytes=16 * 1024 * 1024),
        cost_estimate=pl.CostEstimate(
            flops=0, bytes_accessed=4 * weights.size, transcendentals=0
        ),
        name="held",
    )(weights)


def cot_products_body(ca, cb, da, db, w, near_out, far_out):
    half = ca.shape[0]
    for i, part in enumerate((ca, cb)):
        near_out[i * half : (i + 1) * half] = dot(part[...], w[...])
    half = da.shape[0]
    for i, part in enumerate((da, db)):
        far_out[i * half : (i + 1) * half] = dot(part[...], w[...])


def ff_body(*refs, tile, given):
    (na, nb), cots, refs = refs[:2], refs[2 : 3 if given else 4], refs[3 if given else 4 :]
    w, _, m_out, dg_out, du_out, dna_out, dnb_out, nbuf, cbuf, sem = refs
    half = na.shape[0]
    parts = [(na, nbuf, 0), (nb, nbuf, 1)]
    if not given:
        parts += [(cots[0], cbuf, 0), (cots[1], cbuf, 1)]
    fetches = [
        pltpu.make_async_copy(part, buffer.at[pl.ds(k * half, half)], sem.at[i])
        for i, (part, buffer, k) in enumerate(parts)
    ]
    if given:
        fetches.append(pltpu.make_async_copy(cots[0], cbuf, sem.at[2]))
    for fetch in fetches:
        fetch.start()
    for fetch in fetches:
        fetch.wait()
    tiles = 2 * half // tile
    for i in range(tiles):
        at = pl.ds(i * tile, tile)
        rows = nbuf[at]
        gate = dot(rows, w[0])
        up = dot(rows, w[1])
        hidden_grad = cbuf[at] if given else dot(cbuf[at], w[2])
        sigma = 1.0 / (1.0 + jnp.exp(-gate))
        act = gate * sigma
        m_out[at] = (act * up).astype(BF)
        up_grad = (hidden_grad * act).astype(BF)
        gate_grad = (hidden_grad * up * sigma * (1.0 + gate * (1.0 - sigma))).astype(BF)
        dg_out[at] = gate_grad
        du_out[at] = up_grad
        back = (dot_t(gate_grad, w[0]) + dot_t(up_grad, w[1])).astype(BF)
        if tiles == 1:
            dna_out[...] = back[:half]
            dnb_out[...] = back[half:]
        else:
            out = dna_out if i < tiles // 2 else dnb_out
            out[pl.ds(i % (tiles // 2) * tile, tile)] = back


def ff_rows(normed, cots, weights, order, tile=256):
    given = len(cots) == 1
    half, width = normed[0].shape
    units = weights.shape[2]
    anywhere = pl.BlockSpec(memory_space=pl.ANY)
    vmem = pl.BlockSpec(memory_space=pltpu.VMEM)
    return pl.pallas_call(
        functools.partial(ff_body, tile=tile, given=given),
        out_shape=[jax.ShapeDtypeStruct((2 * half, units), BF)] * 3
        + [jax.ShapeDtypeStruct((half, width), BF)] * 2,
        in_specs=[anywhere] * (2 + len(cots)) + [vmem, anywhere],
        out_specs=[vmem] * 5,
        scratch_shapes=[
            pltpu.VMEM((2 * half, width), BF),
            pltpu.VMEM((2 * half, units), F32) if given else pltpu.VMEM((2 * half, width), BF),
            pltpu.SemaphoreType.DMA((4,)),
        ],
        compiler_params=pltpu.CompilerParams(vmem_limit_bytes=32 * 1024 * 1024),
        cost_estimate=pl.CostEstimate(
            flops=20 * half * width * units,
            bytes_accessed=6 * width * units,
            transcendentals=2 * half * units,
        ),
        name="feed_forward_rows",
    )(*normed, *cots, weights, order)


def wg_body(*refs, sizes, tile):
    count = len(sizes)
    groups = count // 2
    normed, cots, refs = refs[:count], refs[count : 2 * count], refs[2 * count :]
    hidden, gates, ups = refs[:groups], refs[groups : 2 * groups], refs[2 * groups : 3 * groups]
    out, nbuf, cbuf, mbuf, gbuf, ubuf, turned, sem = refs[3 * groups + 1 :]
    pair_sizes = [sizes[2 * i] + sizes[2 * i + 1] for i in range(groups)]

    def copies(at, buffer, sources, lengths):
        result, start = [], 0
        for source, length in zip(sources, lengths):
            target = buffer.at[pl.ds(start, length)]
            result.append(pltpu.make_async_copy(source, target, sem.at[at]))
            start += length
        return result

    def normed_copies():
        return copies(0, nbuf, normed, sizes)

    def cot_copies():
        return copies(1, cbuf, cots, sizes)

    def gate_copies():
        return copies(2, gbuf, gates, pair_sizes)

    def up_copies():
        return copies(3, ubuf, ups, pair_sizes)

    def hidden_copies():
        return copies(4, mbuf, hidden, pair_sizes)

    which, step = pl.program_id(0), pl.program_id(1)

    @pl.when((which == 0) & (step == 0))
    def _():
        first = normed_copies() + gate_copies()
        for copy in first + up_copies() + cot_copies() + hidden_copies():
            copy.start()
        for copy in first:
            copy.wait()

    @pl.when((which == 1) & (step == 0))
    def _():
        for copy in up_copies():
            copy.wait()

    @pl.when((which == 2) & (step == 0))
    def _():
        for copy in cot_copies() + hidden_copies():
            copy.wait()

    columns = pl.ds(pl.multiple_of(step * tile, tile), tile)
    @pl.when(which == 0)
    def _():
        left = nbuf[:, columns].T
        turned[step] = left
        out[...] = dot(left, gbuf[...]).astype(BF)

    @pl.when(which == 1)
    def _():
        out[...] = dot(turned[step], ubuf[...]).astype(BF)

    @pl.when(which == 2)
    def _():
        out[...] = dot(cbuf[:, columns].T, mbuf[...]).astype(BF)


def weight_grads(normed, cots, hidden, gates, ups, order, tile=768):
    sizes = tuple(part.shape[0] for part in normed)
    rows, width, units = sum(sizes), normed[0].shape[1], hidden[0].shape[1]
    anywhere = pl.BlockSpec(memory_space=pl.ANY)
    return pl.pallas_call(
        functools.partial(wg_body, sizes=sizes, tile=tile),
        grid=(3, width // tile),
        out_shape=jax.ShapeDtypeStruct((3, width, units), BF),
        in_specs=[anywhere] * (2 * len(normed) + 3 * len(hidden) + 1),
        out_specs=pl.BlockSpec((None, tile, units), lambda i, j: (i, j, 0)),
        scratch_shapes=[pltpu.VMEM((rows, width), BF)] * 2
        + [pltpu.VMEM((rows, units), BF)] * 3
        + [pltpu.VMEM((width // tile, tile, rows), BF), pltpu.SemaphoreType.DMA((5,))],
        compiler_params=pltpu.CompilerParams(vmem_limit_bytes=48 * 1024 * 1024),
        cost_estimate=pl.CostEstimate(
            flops=6 * rows * width * units,
            bytes_accessed=6 * width * units + rows * (4 * width + 6 * units),
            transcendentals=0,
        ),
        name="weight_gradients",
    )(*normed, *cots, *hidden, *gates, *ups, order)


def down_body(ha, hb, hc, w, *outs, tile=256):
    for group, hidden in enumerate((ha, hb, hc)):
        half = hidden.shape[0] // 2
        step = min(tile, 2 * half)
        for start in range(0, 2 * half, step):
            part = dot_t(hidden[pl.ds(start, step)], w[...]).astype(BF)
            if step > half:
                outs[2 * group][...] = part[:half]
                outs[2 * group + 1][...] = part[half:]
            else:
                outs[2 * group + start // half][pl.ds(start % half, step)] = part


def down_rows(hidden, weights, order):
    _, width, units = weights.shape
    halved = [part.shape[0] // 2 for part in hidden for _ in range(2)]
    outs = vmem_call(
        down_body,
        [((rows, width), BF) for rows in halved],
        [*hidden, (weights, 2)],
        "down_rows",
        (order,),
        limit=60,
        flops=2 * sum(halved) * width * units,
        moved=2 * width * units + 2 * sum(halved) * (width + units),
    )
    return [(outs[0], outs[1]), (outs[2], outs[3]), (outs[4], outs[5])]


def dot(a, b):
    return jnp.dot(a, b, preferred_element_type=F32)


def dot_t(a, b):
    return lax.dot_general(a, b, (((1,), (1,)), ((), ())), preferred_element_type=F32)


def t_dot(a, b):
    return lax.dot_general(a, b, (((0,), (0,)), ((), ())), preferred_element_type=F32)


def pick(index, low, high):
    return jnp.where(index == 0, low, high)


def vmem_call(
    body, outs, ins, name, order=(), scratch=(), limit=16, flops=0, moved=0, first=None
):
    count, skipped, results, extra = len(ins), len(order), len(outs), len(scratch)
    parts = [value[1] if isinstance(value, tuple) else None for value in ins]
    ins = [value[0] if isinstance(value, tuple) else value for value in ins]

    def kernel(*refs):
        sources, refs = refs[:count], refs[count + skipped :]
        fixed, buffers, sem = refs[: results + extra], refs[results + extra : -1], refs[-1]
        fetches = [
            pltpu.make_async_copy(source if at is None else source.at[at], buffer, sem.at[i])
            for i, (source, at, buffer) in enumerate(zip(sources, parts, buffers))
        ]
        for fetch in fetches:
            fetch.start()
        for fetch in fetches[:first]:
            fetch.wait()

        def rest():
            for fetch in fetches[first:]:
                fetch.wait()

        body(*(() if first is None else (rest,)), *buffers, *fixed)

    return pl.pallas_call(
        kernel,
        out_shape=[jax.ShapeDtypeStruct(shape, dtype) for shape, dtype in outs],
        in_specs=[pl.BlockSpec(memory_space=pl.ANY)] * (count + skipped),
        out_specs=[pl.BlockSpec(memory_space=pltpu.VMEM)] * results,
        scratch_shapes=[
            *scratch,
            *(
                pltpu.VMEM(value.shape if at is None else value.shape[1:], value.dtype)
                for value, at in zip(ins, parts)
            ),
            pltpu.SemaphoreType.DMA((count,)),
        ],
        compiler_params=pltpu.CompilerParams(vmem_limit_bytes=limit * 1024 * 1024),
        cost_estimate=pl.CostEstimate(flops=flops, bytes_accessed=moved, transcendentals=0),
        name=name,
    )(*ins, *order)


def copies_body(block, out):
    for i in range(out.shape[0]):
        out[i] = block[...]


def copies(block, count, *order):
    shape = (count,) + block.shape
    moved = 2 * count * block.size
    return vmem_call(
        copies_body, [(shape, block.dtype)], [block], "copies", order, moved=moved
    )[0]


def arrange_body(own, other, zh, out):
    mine = zh[0:1, 0:1] == 0
    for i in range(3):
        out[2 * i] = jnp.where(mine, own[i], other[i])
        out[2 * i + 1] = jnp.where(mine, other[i], own[i])


def ordered_body(own, other, zh, out):
    mine = zh[0:1, 0:1] == 0
    for i in range(own.shape[0]):
        out[0, i] = jnp.where(mine, own[i], other[i])
        out[1, i] = jnp.where(mine, other[i], own[i])


def ordered(own, other, zh, name, order):
    flag = jnp.full((8, HD), zh, jnp.int32)
    shape = (2,) + own.shape
    return vmem_call(
        ordered_body, [(shape, BF)], [own, other, flag], name, order, moved=8 * own.size
    )[0]


def sum_body(terms, out):
    total = terms[0].astype(F32)
    for i in range(1, terms.shape[0]):
        total = total + terms[i].astype(F32)
    out[...] = total


def summed(terms, *order):
    return vmem_call(
        sum_body, [(terms.shape[1:], F32)], [terms], "summed", order, moved=2 * terms.size
    )[0]


def stack_body(*refs):
    *parts, out = refs
    rows = parts[0].shape[0]
    for i, part in enumerate(parts):
        out[i * rows : (i + 1) * rows] = part[...]


def stacked(parts, *order):
    rows, columns = parts[0].shape
    shape = (len(parts) * rows, columns)
    moved = 4 * shape[0] * columns
    return vmem_call(stack_body, [(shape, BF)], list(parts), "stacked", order, moved=moved)[0]


def row_of(blocks, offset, size):
    count, lanes = blocks.shape
    line = (lanes, count * size)
    at = lax.broadcasted_iota(jnp.int32, line, 1)
    from_lane = lax.broadcasted_iota(jnp.int32, line, 0) - offset
    spots = (lax.rem(at, size) == from_lane).astype(BF)
    values = dot(blocks, spots)
    at = lax.broadcasted_iota(jnp.int32, values.shape, 1)
    owner = lax.broadcasted_iota(jnp.int32, values.shape, 0)
    mine = (at >= owner * size) & (at < (owner + 1) * size)
    return jnp.sum(jnp.where(mine, values, 0.0), axis=0, keepdims=True)


def vectors_body(gains, biases, ranks, attn_out, mlp_out, bias_out):
    attn_out[...] = jnp.broadcast_to(row_of(gains[...], 0, 48), attn_out.shape)
    mlp_out[...] = jnp.broadcast_to(row_of(gains[...], 48, 48), mlp_out.shape)
    full = row_of(biases[...], 0, 64)
    rank = ranks[0:1, 0:1]
    query = key = value = 0.0
    for i in range(4):
        query = query + jnp.where(rank == i, full[:, 384 * i : 384 * (i + 1)], 0.0)
    for i in range(2):
        mine = (rank >= 2 * i) & (rank < 2 * i + 2)
        key = key + jnp.where(mine, full[:, 1536 + HD * i : 1536 + HD * (i + 1)], 0.0)
        value = value + jnp.where(mine, full[:, 1792 + HD * i : 1792 + HD * (i + 1)], 0.0)
    line = jnp.concatenate([query, key, value], axis=1)
    bias_out[...] = jnp.broadcast_to(line, bias_out.shape)


def turn(vectors, cos2, sin2):
    return vectors * cos2 + pltpu.roll(vectors, HD // 2, 1) * sin2


def unpack_table(table, places):
    first, last = table[:, 2 * HD : 2 * HD + 1], table[:, 2 * HD + 1 : 2 * HD + 2]
    keys = places[0:1, :]
    return table[:, :HD], table[:, HD : 2 * HD], (keys >= first) & (keys <= last)


def masked_scores(queries, keys, allowed):
    return jnp.where(allowed, dot_t(queries, keys) * HD ** (-0.5), -1e30)


def attn_forward_body(
    x0, x1, x2, x3, gain, w, bias, table, places,
    n_out, q_out, kv_out, o_out, lse_out,
):
    rows = x0.shape[0]
    for i, x in enumerate((x0, x1, x2, x3)):
        part = x[...].astype(F32)
        scale = lax.rsqrt(jnp.mean(part * part, axis=-1, keepdims=True) + EPSILON)
        n_out[i * rows : (i + 1) * rows] = (part * scale * gain[0:1]).astype(BF)
    qkv = dot(n_out[...], w[...]) + bias[0:1]
    cosines, sines, allowed = unpack_table(table, places)
    keys = turn(qkv[:, 384:512], cosines, sines).astype(BF)
    values = qkv[:, 512:].astype(BF)
    kv_out[:, :HD] = keys
    kv_out[:, HD:] = values
    lses = []
    for h in range(3):
        at = slice(h * HD, (h + 1) * HD)
        queries = turn(qkv[:, at], cosines, sines).astype(BF)
        q_out[:, at] = queries
        scores = masked_scores(queries, keys, allowed)
        peak = jnp.max(scores, axis=-1, keepdims=True)
        shifted = jnp.exp(scores - peak)
        total = jnp.sum(shifted, axis=-1, keepdims=True)
        probs = (shifted / total).astype(BF)
        o_out[:, at] = dot(probs, values).astype(BF)
        lses.append(peak + jnp.log(total))
    lse_out[...] = jnp.concatenate(lses + [jnp.zeros((4 * rows, 125), F32)], axis=1)


def parted(partial, keep, give):
    rows = partial.shape[0] // 4
    keep[0] = partial[:rows].astype(BF)
    give[0] = partial[rows : 2 * rows].astype(BF)
    keep[1] = partial[2 * rows : 3 * rows].astype(BF)
    give[1] = partial[3 * rows :].astype(BF)


def attn_out_body(o, w, keep, give):
    parted(dot_t(o[...], w[...]), keep, give)


def residual_body(x, keep, got, across, gain, h_out, n_out):
    h = x[...].astype(F32) + keep[0].astype(F32) + got[0].astype(F32) + across[...].astype(F32)
    h_out[...] = h
    scale = lax.rsqrt(jnp.mean(h * h, axis=-1, keepdims=True) + EPSILON)
    n_out[...] = (h * scale * gain[0:1]).astype(BF)


def norm_backward(grad, rows, gain):
    scale = lax.rsqrt(jnp.mean(rows * rows, axis=-1, keepdims=True) + EPSILON)
    scaled = grad * gain
    back = scale * scaled - rows * scale**3 * jnp.mean(scaled * rows, axis=-1, keepdims=True)
    return back, jnp.sum(grad * rows * scale, axis=0, keepdims=True)


def ff_back_body(own_a, own_b, got_a, got_b, got_c, h, cot, gain, grad_out, branch_out, gain_out):
    grad = sum(part[...].astype(F32) for part in (own_a, own_b, got_a, got_b, got_c))
    back, gain_out[...] = norm_backward(grad, h[...], gain[0:1])
    total = cot[...].astype(F32) + back
    grad_out[...] = total
    branch_out[...] = total.astype(BF)


def attn_back_body(keep, got, across, x, above, gain, grad_out):
    grad = keep[0].astype(F32) + got[0].astype(F32) + across[...].astype(F32)
    back, _ = norm_backward(grad, x[...].astype(F32), gain[0:1])
    grad_out[...] = above[...] + back


def attn_backward_body(
    rest, b0, b1, b2, b3, wo, x0, x1, x2, x3, w, q, kv, lse, table, places,
    grads_out, keep, give, sums_out, gain_out, bbuf,
):
    rows = b0.shape[0]
    for i, part in enumerate((b0, b1, b2, b3)):
        bbuf[i * rows : (i + 1) * rows] = part[...]
    attended_grad = dot(bbuf[...], wo[...]).astype(BF)
    rest()
    keys, values = kv[:, :HD], kv[:, HD:]
    cosines, sines, allowed = unpack_table(table, places)
    sines = -sines
    key_grad = value_grad = 0.0
    for h in range(3):
        at = slice(h * HD, (h + 1) * HD)
        queries, o_grad = q[:, at], attended_grad[:, at]
        probs = jnp.exp(masked_scores(queries, keys, allowed) - lse[:, h : h + 1])
        prob_grad = dot_t(o_grad, values)
        inner = jnp.sum(probs * prob_grad, axis=-1, keepdims=True)
        score_grad = (probs * (prob_grad - inner)).astype(BF)
        query_grad = dot(score_grad, keys) * HD ** (-0.5)
        grads_out[:, at] = turn(query_grad, cosines, sines).astype(BF)
        key_grad = key_grad + t_dot(score_grad, queries)
        value_grad = value_grad + t_dot(probs.astype(BF), o_grad)
    grads_out[:, 384:512] = turn(key_grad * HD ** (-0.5), cosines, sines).astype(BF)
    grads_out[:, 512:] = value_grad.astype(BF)
    grads = grads_out[...]
    sums_out[...] = jnp.sum(grads.astype(F32), axis=0, keepdims=True)
    partial = dot_t(grads, w[...])
    parted(partial, keep, give)
    gain_grad = 0.0
    for i, x in enumerate((x0, x1, x2, x3)):
        part = x[...].astype(F32)
        scale = lax.rsqrt(jnp.mean(part * part, axis=-1, keepdims=True) + EPSILON)
        terms = partial[i * rows : (i + 1) * rows] * part * scale
        gain_grad = gain_grad + jnp.sum(terms, axis=0, keepdims=True)
    gain_out[...] = gain_grad


def blocks_of(row, size):
    count = row.shape[1] // size
    at = lax.broadcasted_iota(jnp.int32, (count, row.shape[1]), 1)
    owner = lax.broadcasted_iota(jnp.int32, (count, row.shape[1]), 0)
    mine = (at >= owner * size) & (at < (owner + 1) * size)
    values = jnp.where(mine, row, 0.0).astype(BF)
    at = lax.broadcasted_iota(jnp.int32, (row.shape[1], HD), 0)
    lane = lax.broadcasted_iota(jnp.int32, (row.shape[1], HD), 1)
    return dot(values, (lax.rem(at, size) == lane).astype(BF))


def attn_grads_body(
    rest, b0, b1, b2, b3, attended, normed, qkv_grad, gain_attn, gain_mlp, sums, ranks, out, bbuf
):
    size = b0.shape[0]
    for i, part in enumerate((b0, b1, b2, b3)):
        bbuf[i * size : (i + 1) * size] = part[...]
    half = bbuf.shape[1] // 2
    spans = [(slice(i * half, (i + 1) * half), slice(16 * i, 16 * (i + 1))) for i in range(2)]
    for at, blocks in spans:
        grad = t_dot(bbuf[:, at], attended[...]).astype(BF)
        out[blocks, :, 768:] = grad.reshape(16, half // 16, 384)
    rest()
    for at, blocks in spans:
        grad = t_dot(normed[:, at], qkv_grad[...]).astype(BF)
        out[blocks, :, :640] = grad.reshape(16, half // 16, 640)
    rank = ranks[0:1, 0:1]
    parts = [jnp.where(rank == i, sums[:, :384], 0.0) for i in range(4)]
    for start in (384, 512):
        for i in range(2):
            mine = (rank >= 2 * i) & (rank < 2 * i + 2)
            parts.append(jnp.where(mine, sums[:, start : start + HD], 0.0))
    rows_of = (
        blocks_of(gain_attn[...], 48),
        blocks_of(gain_mlp[...], 48),
        blocks_of(jnp.concatenate(parts[:6], axis=1), 56),
        blocks_of(jnp.concatenate(parts[6:], axis=1), 8),
    )
    at = lax.broadcasted_iota(jnp.int32, (32, out.shape[1], HD), 1)
    tail = jnp.zeros((32, out.shape[1], HD), F32)
    for i, values in enumerate(rows_of):
        tail = jnp.where(at == i, values[:, None, :], tail)
    out[:, :, 640:768] = tail.astype(BF)


def shards(
    layer_input,
    q_weight,
    kv_weight,
    o_weight,
    norm_gains,
    qkv_bias,
    gate_up,
    down_weight,
    cotangent,
    lengths,
):
    zh, zl, core = (lax.axis_index(a) for a in ("zh", "zl", "core"))
    rank = 2 * zl + core
    width = layer_input.shape[1]
    rows = layer_input.shape[0]

    small = jnp.concatenate([norm_gains.reshape(-1), qkv_bias, jnp.zeros((216,), BF)])
    vectors = jnp.concatenate([kv_weight.reshape(24, 256), small[None], jnp.zeros((7, 256), BF)])
    got = swap(vectors, "core")
    both = jnp.stack([pick(core, vectors, got), pick(core, got, vectors)])
    small_keep = both[:, 24].reshape(2, 2, HD)
    kv_keep = pick(zl, both[:, :24, :HD], both[:, :24, HD:])
    kv_give = pick(zl, both[:, :24, HD:], both[:, :24, :HD])
    kv_crossed = swap(
        jnp.concatenate([kv_give, small_keep, jnp.zeros((2, 6, HD), BF)], axis=1), "zl"
    )
    kv_got, small_got = kv_crossed[:, :24], kv_crossed[:, 24:26]
    kv_rows = jnp.stack([pick(zl, kv_keep, kv_got), pick(zl, kv_got, kv_keep)])
    kv_rows = kv_rows.reshape(2, 2, 2, 12, HD).transpose(0, 1, 3, 2, 4).reshape(48, 2 * HD)
    small = jnp.stack([pick(zl, small_keep, small_got), pick(zl, small_got, small_keep)])
    small = small.reshape(4, 256)
    gains_row = jnp.concatenate([small[:, :12].reshape(48), small[:, 12:24].reshape(48)])
    bias_row = small[:, 24:40].reshape(64)
    small = jnp.zeros((48, HD), BF).at[0, :96].set(gains_row).at[1, :64].set(bias_row)

    ends = jnp.cumsum(lengths[0])
    ranks = jnp.stack([rank, 2 * zl + 1 - core, 2 * (1 - zl) + core, 2 * (1 - zl) + 1 - core])
    group = 4 * rows
    places = (ranks[:, None] * rows + jnp.arange(rows, dtype=jnp.int32)[None, :]).reshape(group)
    passed = ends[None, :] <= places[:, None]
    starts = jnp.sum(jnp.where(passed, lengths[0][None, :], 0), axis=1)
    inverse = THETA ** (-(2.0 * jnp.arange(HD // 2, dtype=F32)) / HD)
    inverse = jnp.concatenate([inverse, inverse])[None, :]
    angles = (places - starts).astype(F32)[:, None] * inverse
    sign = jnp.where(jnp.arange(HD) < HD // 2, -1.0, 1.0).astype(F32)[None, :]
    lane = jnp.arange(HD)[None, :]
    ranges = jnp.where(lane == 0, starts[:, None], places[:, None]).astype(F32)
    table = jnp.concatenate([jnp.cos(angles), jnp.sin(angles) * sign, ranges], axis=1)
    tables = (table, jnp.broadcast_to(places.astype(F32)[None, :], (8, group)))

    living = (places[:rows] < ends[-1])[:, None]
    cot_local = jnp.where(living, cotangent, jnp.zeros((), BF))
    cot_groups = token_groups(cot_local)

    across = swap(layer_input, "zl")
    group_inputs = (layer_input, swap(layer_input, "core"), across, swap(across, "core"))

    attn_part = jnp.concatenate([q_weight, kv_rows, small, o_weight.T], axis=-1)
    attn_plane = exchange(copies(attn_part, 16), PLANE)
    qkv_plane, o_plane = attn_plane[..., :640], attn_plane[..., 768:]
    small_plane = attn_plane[:, :2, 640:768]
    small_other = swap(small_plane, "zh")
    qkv_other = swap(qkv_plane, "zh")
    o_other = swap(o_plane, "zh")
    waits = (cot_groups[1][1], cot_groups[2][1], group_inputs[3], *tables)
    qkv_full = ordered(qkv_plane, qkv_other, zh, "qkv_weights", waits)
    small = jnp.stack([pick(zh, small_plane, small_other), pick(zh, small_other, small_plane)])
    small = small.reshape(32, 2, HD)
    qkv_full = qkv_full.reshape(width, 640)
    gain_attn, gain_mlp, bias = vmem_call(
        vectors_body,
        [((8, width), F32), ((8, width), F32), ((8, 640), F32)],
        [small[:, 0], small[:, 1], jnp.full((8, HD), rank, jnp.int32)],
        "gains_and_biases",
        limit=16,
    )

    mlp = jnp.concatenate([gate_up, down_weight.T[None]], axis=0)
    mlp = jnp.pad(mlp, ((0, 0), (0, 0), (0, 2 * HALF - mlp.shape[2])))
    mlp_own = pick(zh, mlp[..., :HALF], mlp[..., HALF:])
    mlp_other = swap(pick(zh, mlp[..., HALF:], mlp[..., :HALF]), "zh")
    mlp = vmem_call(
        arrange_body,
        [((6, 48, HALF), BF)],
        [mlp_own, mlp_other, jnp.full((8, HD), zh, jnp.int32)],
        "arranged",
        (kv_crossed,),
        moved=4 * mlp_own.size,
    )[0]
    mlp = lax.all_gather(mlp, PLANE, axis=1, tiled=True)
    mlp = mlp.reshape(3, width, HALF)

    normed_group, queries, kv_rot, attended, lse = vmem_call(
        attn_forward_body,
        [
            ((group, width), BF),
            ((group, 384), BF),
            ((group, 256), BF),
            ((group, 384), BF),
            ((group, 128), F32),
        ],
        [*group_inputs, gain_attn, qkv_full, bias, *tables],
        "attention_forward",
        limit=32,
        flops=2 * group * (width * 640 + 6 * group * HD),
        moved=2 * group * width * 2 + 2 * width * 768,
    )
    o_full = ordered(o_plane, o_other, zh, "o_weights", (attended,)).reshape(width, 384)
    pair = ((2, rows, width), BF)
    keep, give = vmem_call(
        attn_out_body,
        [pair, pair],
        [attended, o_full],
        "attention_out",
        flops=2 * group * width * 384,
        moved=2 * width * 384 + 2 * group * width,
    )
    got = swap(give, "core")
    weights = held(mlp)
    residual, normed_mlp = vmem_call(
        residual_body,
        [((rows, width), F32), ((rows, width), BF)],
        [layer_input, keep, got, swap(add(keep[1], got[1]), "zl"), gain_mlp],
        "residual_norm",
        (weights,),
        moved=10 * rows * width,
    )

    after_rows, before_rows = z_shift(normed_mlp, -1), z_shift(normed_mlp, 1)
    far_rows = z_shift(normed_mlp, 2)
    own = (normed_mlp, swap(normed_mlp, "core"))
    own_out = ff_rows(own, cot_groups[0], weights, cot_local)
    cot_near, cot_far = vmem_call(
        cot_products_body,
        [((4 * rows, HALF), F32), ((2 * rows, HALF), F32)],
        [*cot_groups[1], *cot_groups[2], (mlp, 2)],
        "cotangent_products",
        (own_out[0],),
        limit=32,
        flops=12 * rows * width * HALF,
    )
    near = stacked((after_rows, before_rows), cot_near)
    near = (near, swap(near, "core"))
    near_out = ff_rows(near, (cot_near,), weights, own_out[0])
    far_rows = stacked((far_rows,), near_out[0])
    far = (far_rows, swap(far_rows, "core"))
    near_sum = [
        add(mine, swap(others, "core"))
        for mine, others in zip(halves(near_out[3], 0), halves(near_out[4], 0))
    ]
    near_got = (z_shift(near_sum[0], 1), z_shift(near_sum[1], -1))
    far_out = ff_rows(far, (cot_far,), weights, near_sum[1])
    far_sum = add(far_out[3], swap(far_out[4], "core"))
    own_got = swap(own_out[4], "core")
    far_got = z_shift(far_sum, 2)
    results = (own_out, near_out, far_out)
    hidden, gate_grads, up_grads = ([r[i] for r in results] for i in range(3))
    flat_normed = [*own, *near, *far]
    flat_cots = [part for pair in cot_groups for part in pair]
    grad_terms = weight_grads(flat_normed, flat_cots, hidden, gate_grads, up_grads, far_sum)
    residual_grad, branch, gain_mlp_grad = vmem_call(
        ff_back_body,
        [((rows, width), F32), ((rows, width), BF), ((1, width), F32)],
        [own_out[3], own_got, *near_got, far_got, residual, cot_local, gain_mlp],
        "residual_gradient",
        (grad_terms,),
        limit=60,
        flops=10**9 * WEIGHT,
        moved=24 * rows * width,
    )
    mlp_grads = lax.psum_scatter(
        grad_terms.reshape(6, width // 2, HALF), PLANE, scatter_dimension=1, tiled=True
    ).reshape(3, 2, 48, HALF)
    own_grads = lax.dynamic_index_in_dim(mlp_grads, zh, 1, keepdims=False)
    other_grads = swap(lax.dynamic_index_in_dim(mlp_grads, 1 - zh, 1, keepdims=False), "zh")
    own_grads, other_grads = own_grads.astype(F32), other_grads.astype(F32)
    mlp_shard = jnp.concatenate(
        [pick(zh, own_grads, other_grads), pick(zh, other_grads, own_grads)], axis=-1
    )[..., : gate_up.shape[2]]
    gate_up_shard = mlp_shard[:2]
    down_shard = mlp_shard[2].T

    out_pairs = down_rows(hidden, mlp, branch)
    layer_output = (residual + token_sums(out_pairs)).astype(BF)

    across = stacked((swap(branch, "zl"),), out_pairs[0][0])
    branch_group = (branch, swap(branch, "core"), across, swap(across, "core"))
    qkv_grad, keep, give, sums, gain_attn_grad = vmem_call(
        attn_backward_body,
        [((group, 640), BF), pair, pair, ((1, 640), F32), ((1, width), F32)],
        [*branch_group, o_full, *group_inputs, qkv_full, queries, kv_rot, lse, *tables],
        "attention_backward",
        limit=60,
        first=5,
        scratch=[pltpu.VMEM((group, width), BF)],
        flops=2 * group * (width * 1024 + 15 * group * HD),
        moved=4 * group * width + 2 * width * 1024,
    )
    terms = vmem_call(
        attn_grads_body,
        [((32, width // 32, 1152), BF)],
        [
            *branch_group,
            attended,
            normed_group,
            qkv_grad,
            gain_attn_grad,
            gain_mlp_grad,
            sums,
            jnp.full((8, HD), rank, jnp.int32),
        ],
        "attention_weight_gradients",
        scratch=[pltpu.VMEM((group, width), BF)],
        limit=60,
        first=5,
        flops=2 * group * width * 1024,
        moved=4 * group * width + 2 * width * 1152,
    )[0]
    attn_shard = summed(exchange(terms, DATA))

    got = swap(give, "core")
    across = swap(add(keep[1], got[1]), "zl")
    input_grad = vmem_call(
        attn_back_body,
        [((rows, width), F32)],
        [keep, got, across, layer_input, residual_grad, gain_attn],
        "input_gradient",
        moved=20 * rows * width,
    )[0]

    q_shard = attn_shard[:, :384]
    o_shard = attn_shard[:, 768:].T
    kv_sum = attn_shard[:, 384:640].reshape(2, 2, 12, 2, HD)
    kv_keep = lax.dynamic_index_in_dim(kv_sum, core, 1, keepdims=False).reshape(48, HD)
    kv_give = lax.dynamic_index_in_dim(kv_sum, 1 - core, 1, keepdims=False).reshape(48, HD)
    vectors = attn_shard[:8, 640:768]
    got = swap(jnp.concatenate([kv_give, vectors]), "core")
    kv_sum = (kv_keep + got[:48]).reshape(2, 24, HD)
    vectors = vectors + got[48:]
    kv_keep = pick(zl, kv_sum[0], kv_sum[1])
    got = swap(jnp.concatenate([pick(zl, kv_sum[1], kv_sum[0]), vectors]), "zl")
    kv_got = got[:24]
    vectors = vectors + got[24:]
    kv_shard = jnp.concatenate([pick(zl, kv_keep, kv_got), pick(zl, kv_got, kv_keep)], axis=-1)
    kv_shard = kv_shard.reshape(12, 2, 2 * HD).transpose(1, 0, 2)

    def own_part(row, size):
        return lax.dynamic_index_in_dim(
            vectors[row, : 4 * size].reshape(4, size), rank, 0, keepdims=False
        )

    return (
        layer_output,
        input_grad,
        q_shard,
        kv_shard,
        o_shard,
        jnp.stack([own_part(0, 12), own_part(1, 12)]),
        own_part(2, 14),
        own_part(3, 2),
        gate_up_shard,
        down_shard,
    )


def solution(mesh):
    fine = Mesh(mesh.devices.reshape(SIZES), AXES)
    dp = ("zh", "y", "x")
    tensor = ("zl", "core")
    every = dp + tensor
    in_specs = (
        P(every, None),
        P(dp, tensor),
        P(None, every, None),
        P(tensor, dp),
        P(None, every),
        P(every),
        P(None, dp, tensor),
        P(tensor, dp),
        P(every, None),
        P(dp, None),
    )
    out_specs = (
        P(every, None),
        P(every, None),
        P(dp, tensor),
        P(None, every, None),
        P(tensor, dp),
        P(None, every),
        P(every),
        P(every),
        P(None, dp, tensor),
        P(tensor, dp),
    )
    return jax.shard_map(shards, mesh=fine, in_specs=in_specs, out_specs=out_specs, check_vma=False)
```

```python
import functools

import jax
import jax.numpy as jnp
from jax import lax
from jax.experimental import pallas as pl
from jax.experimental.pallas import tpu as pltpu
from jax.sharding import Mesh, PartitionSpec as P

HQ = 12
KVH = 2
HD = 128
EPSILON = 1e-06
THETA = 1000000.0

AXES = ("zh", "y", "x", "zl", "core")
SIZES = (2, 4, 4, 2, 2)
ZRING = ("zh", "zl")
PLANE = ("y", "x")
DATA = ("zh", "y", "x")
HALF = 1152
BF = jnp.bfloat16
WEIGHT = 1000
F32 = jnp.float32


def swap(block, axis):
    return lax.ppermute(block, axis, [(0, 1), (1, 0)])


def halves(block, dim):
    middle = block.shape[dim] // 2
    return (
        lax.slice_in_dim(block, 0, middle, axis=dim),
        lax.slice_in_dim(block, middle, block.shape[dim], axis=dim),
    )


def add(*terms):
    total = terms[0].astype(F32)
    for term in terms[1:]:
        total = total + term.astype(F32)
    return total.astype(terms[0].dtype)


def exchange(blocks, axes):
    return lax.all_to_all(blocks, axes, split_axis=0, concat_axis=0, tiled=True)


def spread(block, axes, count):
    return exchange(jnp.broadcast_to(block[None], (count,) + block.shape), axes)


def z_shift(block, by):
    return lax.ppermute(block, ZRING, [(i, (i + by) % 4) for i in range(4)])


def token_groups(block):
    near = jnp.concatenate([z_shift(block, -1), z_shift(block, 1)], axis=0)
    far = z_shift(block, 2)
    return [(part, swap(part, "core")) for part in (block, near, far)]


def token_sums(pairs):
    own, near, far = (add(mine, swap(others, "core")) for mine, others in pairs)
    after_rows, before_rows = halves(near, 0)
    terms = (own, z_shift(after_rows, 1), z_shift(before_rows, -1), z_shift(far, 2))
    return sum(term.astype(F32) for term in terms)


def hold_body(w, out, sem):
    copy = pltpu.make_async_copy(w, out, sem)
    copy.start()
    copy.wait()


def held(weights):
    return pl.pallas_call(
        hold_body,
        out_shape=pltpu.VMEM(weights.shape, weights.dtype),
        in_specs=[pl.BlockSpec(memory_space=pl.ANY)],
        out_specs=pl.BlockSpec(memory_space=pltpu.VMEM),
        scratch_shapes=[pltpu.SemaphoreType.DMA],
        compiler_params=pltpu.CompilerParams(vmem_limit_bytes=16 * 1024 * 1024),
        cost_estimate=pl.CostEstimate(
            flops=0, bytes_accessed=4 * weights.size, transcendentals=0
        ),
        name="held",
    )(weights)


def cot_products_body(ca, cb, da, db, w, near_out, far_out):
    half = ca.shape[0]
    for i, part in enumerate((ca, cb)):
        near_out[i * half : (i + 1) * half] = dot(part[...], w[...])
    half = da.shape[0]
    for i, part in enumerate((da, db)):
        far_out[i * half : (i + 1) * half] = dot(part[...], w[...])


def ff_body(*refs, tile, given):
    (na, nb), cots, refs = refs[:2], refs[2 : 3 if given else 4], refs[3 if given else 4 :]
    w, _, m_out, dg_out, du_out, dna_out, dnb_out, nbuf, cbuf, sem = refs
    half = na.shape[0]
    parts = [(na, nbuf, 0), (nb, nbuf, 1)]
    if not given:
        parts += [(cots[0], cbuf, 0), (cots[1], cbuf, 1)]
    fetches = [
        pltpu.make_async_copy(part, buffer.at[pl.ds(k * half, half)], sem.at[i])
        for i, (part, buffer, k) in enumerate(parts)
    ]
    if given:
        fetches.append(pltpu.make_async_copy(cots[0], cbuf, sem.at[2]))
    for fetch in fetches:
        fetch.start()
    for fetch in fetches:
        fetch.wait()
    tiles = 2 * half // tile
    for i in range(tiles):
        at = pl.ds(i * tile, tile)
        rows = nbuf[at]
        gate = dot(rows, w[0])
        up = dot(rows, w[1])
        hidden_grad = cbuf[at] if given else dot(cbuf[at], w[2])
        sigma = 1.0 / (1.0 + jnp.exp(-gate))
        act = gate * sigma
        m_out[at] = (act * up).astype(BF)
        up_grad = (hidden_grad * act).astype(BF)
        gate_grad = (hidden_grad * up * sigma * (1.0 + gate * (1.0 - sigma))).astype(BF)
        dg_out[at] = gate_grad
        du_out[at] = up_grad
        back = (dot_t(gate_grad, w[0]) + dot_t(up_grad, w[1])).astype(BF)
        if tiles == 1:
            dna_out[...] = back[:half]
            dnb_out[...] = back[half:]
        else:
            out = dna_out if i < tiles // 2 else dnb_out
            out[pl.ds(i % (tiles // 2) * tile, tile)] = back


def ff_rows(normed, cots, weights, order, tile=256):
    given = len(cots) == 1
    half, width = normed[0].shape
    units = weights.shape[2]
    anywhere = pl.BlockSpec(memory_space=pl.ANY)
    vmem = pl.BlockSpec(memory_space=pltpu.VMEM)
    return pl.pallas_call(
        functools.partial(ff_body, tile=tile, given=given),
        out_shape=[jax.ShapeDtypeStruct((2 * half, units), BF)] * 3
        + [jax.ShapeDtypeStruct((half, width), BF)] * 2,
        in_specs=[anywhere] * (2 + len(cots)) + [vmem, anywhere],
        out_specs=[vmem] * 5,
        scratch_shapes=[
            pltpu.VMEM((2 * half, width), BF),
            pltpu.VMEM((2 * half, units), F32) if given else pltpu.VMEM((2 * half, width), BF),
            pltpu.SemaphoreType.DMA((4,)),
        ],
        compiler_params=pltpu.CompilerParams(vmem_limit_bytes=24 * 1024 * 1024),
        cost_estimate=pl.CostEstimate(
            flops=20 * half * width * units,
            bytes_accessed=6 * width * units,
            transcendentals=2 * half * units,
        ),
        name="feed_forward_rows",
    )(*normed, *cots, weights, order)


def wg_body(*refs, sizes, tile):
    count = len(sizes)
    groups = count // 2
    normed, cots, refs = refs[:count], refs[count : 2 * count], refs[2 * count :]
    hidden, gates, ups = refs[:groups], refs[groups : 2 * groups], refs[2 * groups : 3 * groups]
    out, nbuf, cbuf, mbuf, gbuf, ubuf, turned, sem = refs[3 * groups + 1 :]
    pair_sizes = [sizes[2 * i] + sizes[2 * i + 1] for i in range(groups)]

    def copies(at, buffer, sources, lengths):
        result, start = [], 0
        for source, length in zip(sources, lengths):
            target = buffer.at[pl.ds(start, length)]
            result.append(pltpu.make_async_copy(source, target, sem.at[at]))
            start += length
        return result

    def normed_copies():
        return copies(0, nbuf, normed, sizes)

    def cot_copies():
        return copies(1, cbuf, cots, sizes)

    def gate_copies():
        return copies(2, gbuf, gates, pair_sizes)

    def up_copies():
        return copies(3, ubuf, ups, pair_sizes)

    def hidden_copies():
        return copies(4, mbuf, hidden, pair_sizes)

    which, step = pl.program_id(0), pl.program_id(1)

    @pl.when((which == 0) & (step == 0))
    def _():
        first = normed_copies() + gate_copies()
        for copy in first + up_copies() + cot_copies() + hidden_copies():
            copy.start()
        for copy in first:
            copy.wait()

    @pl.when((which == 1) & (step == 0))
    def _():
        for copy in up_copies():
            copy.wait()

    @pl.when((which == 2) & (step == 0))
    def _():
        for copy in cot_copies() + hidden_copies():
            copy.wait()

    columns = pl.ds(pl.multiple_of(step * tile, tile), tile)
    @pl.when(which == 0)
    def _():
        left = nbuf[:, columns].T
        turned[step] = left
        out[...] = dot(left, gbuf[...]).astype(BF)

    @pl.when(which == 1)
    def _():
        out[...] = dot(turned[step], ubuf[...]).astype(BF)

    @pl.when(which == 2)
    def _():
        out[...] = dot(cbuf[:, columns].T, mbuf[...]).astype(BF)


def weight_grads(normed, cots, hidden, gates, ups, order, tile=768):
    sizes = tuple(part.shape[0] for part in normed)
    rows, width, units = sum(sizes), normed[0].shape[1], hidden[0].shape[1]
    anywhere = pl.BlockSpec(memory_space=pl.ANY)
    return pl.pallas_call(
        functools.partial(wg_body, sizes=sizes, tile=tile),
        grid=(3, width // tile),
        out_shape=jax.ShapeDtypeStruct((3, width, units), BF),
        in_specs=[anywhere] * (2 * len(normed) + 3 * len(hidden) + 1),
        out_specs=pl.BlockSpec((None, tile, units), lambda i, j: (i, j, 0)),
        scratch_shapes=[pltpu.VMEM((rows, width), BF)] * 2
        + [pltpu.VMEM((rows, units), BF)] * 3
        + [pltpu.VMEM((width // tile, tile, rows), BF), pltpu.SemaphoreType.DMA((5,))],
        compiler_params=pltpu.CompilerParams(vmem_limit_bytes=48 * 1024 * 1024),
        cost_estimate=pl.CostEstimate(
            flops=6 * rows * width * units,
            bytes_accessed=6 * width * units + rows * (4 * width + 6 * units),
            transcendentals=0,
        ),
        name="weight_gradients",
    )(*normed, *cots, *hidden, *gates, *ups, order)


def down_body(ha, hb, hc, w, *outs, tile=256):
    for group, hidden in enumerate((ha, hb, hc)):
        half = hidden.shape[0] // 2
        step = min(tile, 2 * half)
        for start in range(0, 2 * half, step):
            part = dot_t(hidden[pl.ds(start, step)], w[...]).astype(BF)
            if step > half:
                outs[2 * group][...] = part[:half]
                outs[2 * group + 1][...] = part[half:]
            else:
                outs[2 * group + start // half][pl.ds(start % half, step)] = part


def down_rows(hidden, weights, order):
    _, width, units = weights.shape
    halved = [part.shape[0] // 2 for part in hidden for _ in range(2)]
    outs = vmem_call(
        down_body,
        [((rows, width), BF) for rows in halved],
        [*hidden, (weights, 2)],
        "down_rows",
        (order,),
        limit=60,
        flops=2 * sum(halved) * width * units,
        moved=2 * width * units + 2 * sum(halved) * (width + units),
    )
    return [(outs[0], outs[1]), (outs[2], outs[3]), (outs[4], outs[5])]


def dot(a, b):
    return jnp.dot(a, b, preferred_element_type=F32)


def dot_t(a, b):
    return lax.dot_general(a, b, (((1,), (1,)), ((), ())), preferred_element_type=F32)


def t_dot(a, b):
    return lax.dot_general(a, b, (((0,), (0,)), ((), ())), preferred_element_type=F32)


def pick(index, low, high):
    return jnp.where(index == 0, low, high)


def vmem_call(
    body, outs, ins, name, order=(), scratch=(), limit=16, flops=0, moved=0, first=None
):
    count, skipped, results, extra = len(ins), len(order), len(outs), len(scratch)
    parts = [value[1] if isinstance(value, tuple) else None for value in ins]
    ins = [value[0] if isinstance(value, tuple) else value for value in ins]

    def kernel(*refs):
        sources, refs = refs[:count], refs[count + skipped :]
        fixed, buffers, sem = refs[: results + extra], refs[results + extra : -1], refs[-1]
        fetches = [
            pltpu.make_async_copy(source if at is None else source.at[at], buffer, sem.at[i])
            for i, (source, at, buffer) in enumerate(zip(sources, parts, buffers))
        ]
        for fetch in fetches:
            fetch.start()
        for fetch in fetches[:first]:
            fetch.wait()

        def rest():
            for fetch in fetches[first:]:
                fetch.wait()

        body(*(() if first is None else (rest,)), *buffers, *fixed)

    return pl.pallas_call(
        kernel,
        out_shape=[jax.ShapeDtypeStruct(shape, dtype) for shape, dtype in outs],
        in_specs=[pl.BlockSpec(memory_space=pl.ANY)] * (count + skipped),
        out_specs=[pl.BlockSpec(memory_space=pltpu.VMEM)] * results,
        scratch_shapes=[
            *scratch,
            *(
                pltpu.VMEM(value.shape if at is None else value.shape[1:], value.dtype)
                for value, at in zip(ins, parts)
            ),
            pltpu.SemaphoreType.DMA((count,)),
        ],
        compiler_params=pltpu.CompilerParams(vmem_limit_bytes=limit * 1024 * 1024),
        cost_estimate=pl.CostEstimate(flops=flops, bytes_accessed=moved, transcendentals=0),
        name=name,
    )(*ins, *order)


def copies_body(block, out):
    for i in range(out.shape[0]):
        out[i] = block[...]


def copies(block, count, *order):
    shape = (count,) + block.shape
    moved = 2 * count * block.size
    return vmem_call(
        copies_body, [(shape, block.dtype)], [block], "copies", order, moved=moved
    )[0]


def arrange_body(own, other, zh, out):
    mine = zh[0:1, 0:1] == 0
    for i in range(3):
        out[2 * i] = jnp.where(mine, own[i], other[i])
        out[2 * i + 1] = jnp.where(mine, other[i], own[i])


def ordered_body(own, other, zh, out):
    mine = zh[0:1, 0:1] == 0
    for i in range(own.shape[0]):
        out[0, i] = jnp.where(mine, own[i], other[i])
        out[1, i] = jnp.where(mine, other[i], own[i])


def ordered(own, other, zh, name, order):
    flag = jnp.full((8, HD), zh, jnp.int32)
    shape = (2,) + own.shape
    return vmem_call(
        ordered_body, [(shape, BF)], [own, other, flag], name, order, moved=8 * own.size
    )[0]


def sum_body(terms, out):
    total = terms[0].astype(F32)
    for i in range(1, terms.shape[0]):
        total = total + terms[i].astype(F32)
    out[...] = total


def summed(terms, *order):
    return vmem_call(
        sum_body, [(terms.shape[1:], F32)], [terms], "summed", order, moved=2 * terms.size
    )[0]


def stack_body(*refs):
    *parts, out = refs
    rows = parts[0].shape[0]
    for i, part in enumerate(parts):
        out[i * rows : (i + 1) * rows] = part[...]


def stacked(parts, *order):
    rows, columns = parts[0].shape
    shape = (len(parts) * rows, columns)
    moved = 4 * shape[0] * columns
    return vmem_call(stack_body, [(shape, BF)], list(parts), "stacked", order, moved=moved)[0]


def row_of(blocks, offset, size):
    count, lanes = blocks.shape
    line = (lanes, count * size)
    at = lax.broadcasted_iota(jnp.int32, line, 1)
    from_lane = lax.broadcasted_iota(jnp.int32, line, 0) - offset
    spots = (lax.rem(at, size) == from_lane).astype(BF)
    values = dot(blocks, spots)
    at = lax.broadcasted_iota(jnp.int32, values.shape, 1)
    owner = lax.broadcasted_iota(jnp.int32, values.shape, 0)
    mine = (at >= owner * size) & (at < (owner + 1) * size)
    return jnp.sum(jnp.where(mine, values, 0.0), axis=0, keepdims=True)


def vectors_body(gains, biases, ranks, attn_out, mlp_out, bias_out):
    attn_out[...] = jnp.broadcast_to(row_of(gains[...], 0, 48), attn_out.shape)
    mlp_out[...] = jnp.broadcast_to(row_of(gains[...], 48, 48), mlp_out.shape)
    full = row_of(biases[...], 0, 64)
    rank = ranks[0:1, 0:1]
    query = key = value = 0.0
    for i in range(4):
        query = query + jnp.where(rank == i, full[:, 384 * i : 384 * (i + 1)], 0.0)
    for i in range(2):
        mine = (rank >= 2 * i) & (rank < 2 * i + 2)
        key = key + jnp.where(mine, full[:, 1536 + HD * i : 1536 + HD * (i + 1)], 0.0)
        value = value + jnp.where(mine, full[:, 1792 + HD * i : 1792 + HD * (i + 1)], 0.0)
    line = jnp.concatenate([query, key, value], axis=1)
    bias_out[...] = jnp.broadcast_to(line, bias_out.shape)


def turn(vectors, cos2, sin2):
    return vectors * cos2 + pltpu.roll(vectors, HD // 2, 1) * sin2


def unpack_table(table, places):
    first, last = table[:, 2 * HD : 2 * HD + 1], table[:, 2 * HD + 1 : 2 * HD + 2]
    keys = places[0:1, :]
    return table[:, :HD], table[:, HD : 2 * HD], (keys >= first) & (keys <= last)


def masked_scores(queries, keys, allowed):
    return jnp.where(allowed, dot_t(queries, keys) * HD ** (-0.5), -1e30)


def attn_forward_body(
    x0, x1, x2, x3, gain, w, bias, table, places,
    n_out, q_out, kv_out, o_out, lse_out,
):
    rows = x0.shape[0]
    for i, x in enumerate((x0, x1, x2, x3)):
        part = x[...].astype(F32)
        scale = lax.rsqrt(jnp.mean(part * part, axis=-1, keepdims=True) + EPSILON)
        n_out[i * rows : (i + 1) * rows] = (part * scale * gain[0:1]).astype(BF)
    qkv = dot(n_out[...], w[...]) + bias[0:1]
    cosines, sines, allowed = unpack_table(table, places)
    keys = turn(qkv[:, 384:512], cosines, sines).astype(BF)
    values = qkv[:, 512:].astype(BF)
    kv_out[:, :HD] = keys
    kv_out[:, HD:] = values
    lses = []
    for h in range(3):
        at = slice(h * HD, (h + 1) * HD)
        queries = turn(qkv[:, at], cosines, sines).astype(BF)
        q_out[:, at] = queries
        scores = masked_scores(queries, keys, allowed)
        peak = jnp.max(scores, axis=-1, keepdims=True)
        shifted = jnp.exp(scores - peak)
        total = jnp.sum(shifted, axis=-1, keepdims=True)
        probs = (shifted / total).astype(BF)
        o_out[:, at] = dot(probs, values).astype(BF)
        lses.append(peak + jnp.log(total))
    lse_out[...] = jnp.concatenate(lses + [jnp.zeros((4 * rows, 125), F32)], axis=1)


def parted(partial, keep, give):
    rows = partial.shape[0] // 4
    keep[0] = partial[:rows].astype(BF)
    give[0] = partial[rows : 2 * rows].astype(BF)
    keep[1] = partial[2 * rows : 3 * rows].astype(BF)
    give[1] = partial[3 * rows :].astype(BF)


def attn_out_body(o, w, keep, give):
    parted(dot_t(o[...], w[...]), keep, give)


def residual_body(x, keep, got, across, gain, h_out, n_out):
    h = x[...].astype(F32) + keep[0].astype(F32) + got[0].astype(F32) + across[...].astype(F32)
    h_out[...] = h
    scale = lax.rsqrt(jnp.mean(h * h, axis=-1, keepdims=True) + EPSILON)
    n_out[...] = (h * scale * gain[0:1]).astype(BF)


def norm_backward(grad, rows, gain):
    scale = lax.rsqrt(jnp.mean(rows * rows, axis=-1, keepdims=True) + EPSILON)
    scaled = grad * gain
    back = scale * scaled - rows * scale**3 * jnp.mean(scaled * rows, axis=-1, keepdims=True)
    return back, jnp.sum(grad * rows * scale, axis=0, keepdims=True)


def ff_back_body(own_a, own_b, got_a, got_b, got_c, h, cot, gain, grad_out, branch_out, gain_out):
    grad = sum(part[...].astype(F32) for part in (own_a, own_b, got_a, got_b, got_c))
    back, gain_out[...] = norm_backward(grad, h[...], gain[0:1])
    total = cot[...].astype(F32) + back
    grad_out[...] = total
    branch_out[...] = total.astype(BF)


def attn_back_body(keep, got, across, x, above, gain, grad_out):
    grad = keep[0].astype(F32) + got[0].astype(F32) + across[...].astype(F32)
    back, _ = norm_backward(grad, x[...].astype(F32), gain[0:1])
    grad_out[...] = above[...] + back


def attn_backward_body(
    rest, b0, b1, b2, b3, wo, x0, x1, x2, x3, w, q, kv, lse, table, places,
    grads_out, keep, give, sums_out, gain_out, bbuf,
):
    rows = b0.shape[0]
    for i, part in enumerate((b0, b1, b2, b3)):
        bbuf[i * rows : (i + 1) * rows] = part[...]
    attended_grad = dot(bbuf[...], wo[...]).astype(BF)
    rest()
    keys, values = kv[:, :HD], kv[:, HD:]
    cosines, sines, allowed = unpack_table(table, places)
    sines = -sines
    key_grad = value_grad = 0.0
    for h in range(3):
        at = slice(h * HD, (h + 1) * HD)
        queries, o_grad = q[:, at], attended_grad[:, at]
        probs = jnp.exp(masked_scores(queries, keys, allowed) - lse[:, h : h + 1])
        prob_grad = dot_t(o_grad, values)
        inner = jnp.sum(probs * prob_grad, axis=-1, keepdims=True)
        score_grad = (probs * (prob_grad - inner)).astype(BF)
        query_grad = dot(score_grad, keys) * HD ** (-0.5)
        grads_out[:, at] = turn(query_grad, cosines, sines).astype(BF)
        key_grad = key_grad + t_dot(score_grad, queries)
        value_grad = value_grad + t_dot(probs.astype(BF), o_grad)
    grads_out[:, 384:512] = turn(key_grad * HD ** (-0.5), cosines, sines).astype(BF)
    grads_out[:, 512:] = value_grad.astype(BF)
    grads = grads_out[...]
    sums_out[...] = jnp.sum(grads.astype(F32), axis=0, keepdims=True)
    partial = dot_t(grads, w[...])
    parted(partial, keep, give)
    gain_grad = 0.0
    for i, x in enumerate((x0, x1, x2, x3)):
        part = x[...].astype(F32)
        scale = lax.rsqrt(jnp.mean(part * part, axis=-1, keepdims=True) + EPSILON)
        terms = partial[i * rows : (i + 1) * rows] * part * scale
        gain_grad = gain_grad + jnp.sum(terms, axis=0, keepdims=True)
    gain_out[...] = gain_grad


def blocks_of(row, size):
    count = row.shape[1] // size
    at = lax.broadcasted_iota(jnp.int32, (count, row.shape[1]), 1)
    owner = lax.broadcasted_iota(jnp.int32, (count, row.shape[1]), 0)
    mine = (at >= owner * size) & (at < (owner + 1) * size)
    values = jnp.where(mine, row, 0.0).astype(BF)
    at = lax.broadcasted_iota(jnp.int32, (row.shape[1], HD), 0)
    lane = lax.broadcasted_iota(jnp.int32, (row.shape[1], HD), 1)
    return dot(values, (lax.rem(at, size) == lane).astype(BF))


def attn_grads_body(
    rest, b0, b1, b2, b3, attended, normed, qkv_grad, gain_attn, gain_mlp, sums, ranks, out, bbuf
):
    size = b0.shape[0]
    for i, part in enumerate((b0, b1, b2, b3)):
        bbuf[i * size : (i + 1) * size] = part[...]
    half = bbuf.shape[1] // 2
    spans = [(slice(i * half, (i + 1) * half), slice(16 * i, 16 * (i + 1))) for i in range(2)]
    for at, blocks in spans:
        grad = t_dot(bbuf[:, at], attended[...]).astype(BF)
        out[blocks, :, 768:] = grad.reshape(16, half // 16, 384)
    rest()
    for at, blocks in spans:
        grad = t_dot(normed[:, at], qkv_grad[...]).astype(BF)
        out[blocks, :, :640] = grad.reshape(16, half // 16, 640)
    rank = ranks[0:1, 0:1]
    parts = [jnp.where(rank == i, sums[:, :384], 0.0) for i in range(4)]
    for start in (384, 512):
        for i in range(2):
            mine = (rank >= 2 * i) & (rank < 2 * i + 2)
            parts.append(jnp.where(mine, sums[:, start : start + HD], 0.0))
    rows_of = (
        blocks_of(gain_attn[...], 48),
        blocks_of(gain_mlp[...], 48),
        blocks_of(jnp.concatenate(parts[:6], axis=1), 56),
        blocks_of(jnp.concatenate(parts[6:], axis=1), 8),
    )
    at = lax.broadcasted_iota(jnp.int32, (32, out.shape[1], HD), 1)
    tail = jnp.zeros((32, out.shape[1], HD), F32)
    for i, values in enumerate(rows_of):
        tail = jnp.where(at == i, values[:, None, :], tail)
    out[:, :, 640:768] = tail.astype(BF)


def shards(
    layer_input,
    q_weight,
    kv_weight,
    o_weight,
    norm_gains,
    qkv_bias,
    gate_up,
    down_weight,
    cotangent,
    lengths,
):
    zh, zl, core = (lax.axis_index(a) for a in ("zh", "zl", "core"))
    rank = 2 * zl + core
    width = layer_input.shape[1]
    rows = layer_input.shape[0]

    small = jnp.concatenate([norm_gains.reshape(-1), qkv_bias, jnp.zeros((216,), BF)])
    vectors = jnp.concatenate([kv_weight.reshape(24, 256), small[None], jnp.zeros((7, 256), BF)])
    got = swap(vectors, "core")
    both = jnp.stack([pick(core, vectors, got), pick(core, got, vectors)])
    small_keep = both[:, 24].reshape(2, 2, HD)
    kv_keep = pick(zl, both[:, :24, :HD], both[:, :24, HD:])
    kv_give = pick(zl, both[:, :24, HD:], both[:, :24, :HD])
    kv_crossed = swap(
        jnp.concatenate([kv_give, small_keep, jnp.zeros((2, 6, HD), BF)], axis=1), "zl"
    )
    kv_got, small_got = kv_crossed[:, :24], kv_crossed[:, 24:26]
    kv_rows = jnp.stack([pick(zl, kv_keep, kv_got), pick(zl, kv_got, kv_keep)])
    kv_rows = kv_rows.reshape(2, 2, 2, 12, HD).transpose(0, 1, 3, 2, 4).reshape(48, 2 * HD)
    small = jnp.stack([pick(zl, small_keep, small_got), pick(zl, small_got, small_keep)])
    small = small.reshape(4, 256)
    gains_row = jnp.concatenate([small[:, :12].reshape(48), small[:, 12:24].reshape(48)])
    bias_row = small[:, 24:40].reshape(64)
    small = jnp.zeros((48, HD), BF).at[0, :96].set(gains_row).at[1, :64].set(bias_row)

    ends = jnp.cumsum(lengths[0])
    ranks = jnp.stack([rank, 2 * zl + 1 - core, 2 * (1 - zl) + core, 2 * (1 - zl) + 1 - core])
    group = 4 * rows
    places = (ranks[:, None] * rows + jnp.arange(rows, dtype=jnp.int32)[None, :]).reshape(group)
    passed = ends[None, :] <= places[:, None]
    starts = jnp.sum(jnp.where(passed, lengths[0][None, :], 0), axis=1)
    inverse = THETA ** (-(2.0 * jnp.arange(HD // 2, dtype=F32)) / HD)
    inverse = jnp.concatenate([inverse, inverse])[None, :]
    angles = (places - starts).astype(F32)[:, None] * inverse
    sign = jnp.where(jnp.arange(HD) < HD // 2, -1.0, 1.0).astype(F32)[None, :]
    lane = jnp.arange(HD)[None, :]
    ranges = jnp.where(lane == 0, starts[:, None], places[:, None]).astype(F32)
    table = jnp.concatenate([jnp.cos(angles), jnp.sin(angles) * sign, ranges], axis=1)
    tables = (table, jnp.broadcast_to(places.astype(F32)[None, :], (8, group)))

    living = (places[:rows] < ends[-1])[:, None]
    cot_local = jnp.where(living, cotangent, jnp.zeros((), BF))
    cot_groups = token_groups(cot_local)

    across = swap(layer_input, "zl")
    group_inputs = (layer_input, swap(layer_input, "core"), across, swap(across, "core"))

    attn_part = jnp.concatenate([q_weight, kv_rows, small, o_weight.T], axis=-1)
    attn_plane = exchange(copies(attn_part, 16), PLANE)
    qkv_plane, o_plane = attn_plane[..., :640], attn_plane[..., 768:]
    small_plane = attn_plane[:, :2, 640:768]
    small_other = swap(small_plane, "zh")
    qkv_other = swap(qkv_plane, "zh")
    o_other = swap(o_plane, "zh")
    waits = (cot_groups[1][1], cot_groups[2][1], group_inputs[3], *tables)
    qkv_full = ordered(qkv_plane, qkv_other, zh, "qkv_weights", waits)
    small = jnp.stack([pick(zh, small_plane, small_other), pick(zh, small_other, small_plane)])
    small = small.reshape(32, 2, HD)
    qkv_full = qkv_full.reshape(width, 640)
    gain_attn, gain_mlp, bias = vmem_call(
        vectors_body,
        [((8, width), F32), ((8, width), F32), ((8, 640), F32)],
        [small[:, 0], small[:, 1], jnp.full((8, HD), rank, jnp.int32)],
        "gains_and_biases",
        limit=16,
    )

    mlp = jnp.concatenate([gate_up, down_weight.T[None]], axis=0)
    mlp = jnp.pad(mlp, ((0, 0), (0, 0), (0, 2 * HALF - mlp.shape[2])))
    mlp_own = pick(zh, mlp[..., :HALF], mlp[..., HALF:])
    mlp_other = swap(pick(zh, mlp[..., HALF:], mlp[..., :HALF]), "zh")
    mlp = vmem_call(
        arrange_body,
        [((6, 48, HALF), BF)],
        [mlp_own, mlp_other, jnp.full((8, HD), zh, jnp.int32)],
        "arranged",
        (kv_crossed,),
        moved=4 * mlp_own.size,
    )[0]
    mlp = lax.all_gather(mlp, PLANE, axis=1, tiled=True)
    mlp = mlp.reshape(3, width, HALF)

    normed_group, queries, kv_rot, attended, lse = vmem_call(
        attn_forward_body,
        [
            ((group, width), BF),
            ((group, 384), BF),
            ((group, 256), BF),
            ((group, 384), BF),
            ((group, 128), F32),
        ],
        [*group_inputs, gain_attn, qkv_full, bias, *tables],
        "attention_forward",
        limit=32,
        flops=2 * group * (width * 640 + 6 * group * HD),
        moved=2 * group * width * 2 + 2 * width * 768,
    )
    o_full = ordered(o_plane, o_other, zh, "o_weights", (attended,)).reshape(width, 384)
    pair = ((2, rows, width), BF)
    keep, give = vmem_call(
        attn_out_body,
        [pair, pair],
        [attended, o_full],
        "attention_out",
        flops=2 * group * width * 384,
        moved=2 * width * 384 + 2 * group * width,
    )
    got = swap(give, "core")
    weights = held(mlp)
    residual, normed_mlp = vmem_call(
        residual_body,
        [((rows, width), F32), ((rows, width), BF)],
        [layer_input, keep, got, swap(add(keep[1], got[1]), "zl"), gain_mlp],
        "residual_norm",
        (weights,),
        moved=10 * rows * width,
    )

    after_rows, before_rows = z_shift(normed_mlp, -1), z_shift(normed_mlp, 1)
    far_rows = z_shift(normed_mlp, 2)
    own = (normed_mlp, swap(normed_mlp, "core"))
    own_out = ff_rows(own, cot_groups[0], weights, cot_local)
    cot_near, cot_far = vmem_call(
        cot_products_body,
        [((4 * rows, HALF), F32), ((2 * rows, HALF), F32)],
        [*cot_groups[1], *cot_groups[2], (mlp, 2)],
        "cotangent_products",
        (own_out[0],),
        flops=12 * rows * width * HALF,
    )
    near = stacked((after_rows, before_rows), cot_near)
    near = (near, swap(near, "core"))
    near_out = ff_rows(near, (cot_near,), weights, own_out[0])
    far_rows = stacked((far_rows,), near_out[0])
    far = (far_rows, swap(far_rows, "core"))
    near_sum = [
        add(mine, swap(others, "core"))
        for mine, others in zip(halves(near_out[3], 0), halves(near_out[4], 0))
    ]
    near_got = (z_shift(near_sum[0], 1), z_shift(near_sum[1], -1))
    far_out = ff_rows(far, (cot_far,), weights, near_sum[1])
    far_sum = add(far_out[3], swap(far_out[4], "core"))
    own_got = swap(own_out[4], "core")
    far_got = z_shift(far_sum, 2)
    results = (own_out, near_out, far_out)
    hidden, gate_grads, up_grads = ([r[i] for r in results] for i in range(3))
    flat_normed = [*own, *near, *far]
    flat_cots = [part for pair in cot_groups for part in pair]
    grad_terms = weight_grads(flat_normed, flat_cots, hidden, gate_grads, up_grads, far_sum)
    residual_grad, branch, gain_mlp_grad = vmem_call(
        ff_back_body,
        [((rows, width), F32), ((rows, width), BF), ((1, width), F32)],
        [own_out[3], own_got, *near_got, far_got, residual, cot_local, gain_mlp],
        "residual_gradient",
        (grad_terms,),
        limit=60,
        flops=10**9 * WEIGHT,
        moved=24 * rows * width,
    )
    mlp_grads = lax.psum_scatter(
        grad_terms.reshape(6, width // 2, HALF), PLANE, scatter_dimension=1, tiled=True
    ).reshape(3, 2, 48, HALF)
    own_grads = lax.dynamic_index_in_dim(mlp_grads, zh, 1, keepdims=False)
    other_grads = swap(lax.dynamic_index_in_dim(mlp_grads, 1 - zh, 1, keepdims=False), "zh")
    own_grads, other_grads = own_grads.astype(F32), other_grads.astype(F32)
    mlp_shard = jnp.concatenate(
        [pick(zh, own_grads, other_grads), pick(zh, other_grads, own_grads)], axis=-1
    )[..., : gate_up.shape[2]]
    gate_up_shard = mlp_shard[:2]
    down_shard = mlp_shard[2].T

    out_pairs = down_rows(hidden, mlp, branch)
    layer_output = (residual + token_sums(out_pairs)).astype(BF)

    across = stacked((swap(branch, "zl"),), out_pairs[0][0])
    branch_group = (branch, swap(branch, "core"), across, swap(across, "core"))
    qkv_grad, keep, give, sums, gain_attn_grad = vmem_call(
        attn_backward_body,
        [((group, 640), BF), pair, pair, ((1, 640), F32), ((1, width), F32)],
        [*branch_group, o_full, *group_inputs, qkv_full, queries, kv_rot, lse, *tables],
        "attention_backward",
        limit=60,
        first=5,
        scratch=[pltpu.VMEM((group, width), BF)],
        flops=2 * group * (width * 1024 + 15 * group * HD),
        moved=4 * group * width + 2 * width * 1024,
    )
    terms = vmem_call(
        attn_grads_body,
        [((32, width // 32, 1152), BF)],
        [
            *branch_group,
            attended,
            normed_group,
            qkv_grad,
            gain_attn_grad,
            gain_mlp_grad,
            sums,
            jnp.full((8, HD), rank, jnp.int32),
        ],
        "attention_weight_gradients",
        scratch=[pltpu.VMEM((group, width), BF)],
        limit=60,
        first=5,
        flops=2 * group * width * 1024,
        moved=4 * group * width + 2 * width * 1152,
    )[0]
    attn_shard = summed(exchange(terms, DATA))

    got = swap(give, "core")
    across = swap(add(keep[1], got[1]), "zl")
    input_grad = vmem_call(
        attn_back_body,
        [((rows, width), F32)],
        [keep, got, across, layer_input, residual_grad, gain_attn],
        "input_gradient",
        moved=20 * rows * width,
    )[0]

    q_shard = attn_shard[:, :384]
    o_shard = attn_shard[:, 768:].T
    kv_sum = attn_shard[:, 384:640].reshape(2, 2, 12, 2, HD)
    kv_keep = lax.dynamic_index_in_dim(kv_sum, core, 1, keepdims=False).reshape(48, HD)
    kv_give = lax.dynamic_index_in_dim(kv_sum, 1 - core, 1, keepdims=False).reshape(48, HD)
    vectors = attn_shard[:8, 640:768]
    got = swap(jnp.concatenate([kv_give, vectors]), "core")
    kv_sum = (kv_keep + got[:48]).reshape(2, 24, HD)
    vectors = vectors + got[48:]
    kv_keep = pick(zl, kv_sum[0], kv_sum[1])
    got = swap(jnp.concatenate([pick(zl, kv_sum[1], kv_sum[0]), vectors]), "zl")
    kv_got = got[:24]
    vectors = vectors + got[24:]
    kv_shard = jnp.concatenate([pick(zl, kv_keep, kv_got), pick(zl, kv_got, kv_keep)], axis=-1)
    kv_shard = kv_shard.reshape(12, 2, 2 * HD).transpose(1, 0, 2)

    def own_part(row, size):
        return lax.dynamic_index_in_dim(
            vectors[row, : 4 * size].reshape(4, size), rank, 0, keepdims=False
        )

    return (
        layer_output,
        input_grad,
        q_shard,
        kv_shard,
        o_shard,
        jnp.stack([own_part(0, 12), own_part(1, 12)]),
        own_part(2, 14),
        own_part(3, 2),
        gate_up_shard,
        down_shard,
    )


def solution(mesh):
    fine = Mesh(mesh.devices.reshape(SIZES), AXES)
    dp = ("zh", "y", "x")
    tensor = ("zl", "core")
    every = dp + tensor
    in_specs = (
        P(every, None),
        P(dp, tensor),
        P(None, every, None),
        P(tensor, dp),
        P(None, every),
        P(every),
        P(None, dp, tensor),
        P(tensor, dp),
        P(every, None),
        P(dp, None),
    )
    out_specs = (
        P(every, None),
        P(every, None),
        P(dp, tensor),
        P(None, every, None),
        P(tensor, dp),
        P(None, every),
        P(every),
        P(every),
        P(None, dp, tensor),
        P(tensor, dp),
    )
    return jax.shard_map(shards, mesh=fine, in_specs=in_specs, out_specs=out_specs, check_vma=False)
```

```python
import functools

import jax
import jax.numpy as jnp
from jax import lax
from jax.experimental import pallas as pl
from jax.experimental.pallas import tpu as pltpu
from jax.sharding import Mesh, PartitionSpec as P

HQ = 12
KVH = 2
HD = 128
EPSILON = 1e-06
THETA = 1000000.0

AXES = ("zh", "y", "x", "zl", "core")
SIZES = (2, 4, 4, 2, 2)
ZRING = ("zh", "zl")
PLANE = ("y", "x")
DATA = ("zh", "y", "x")
HALF = 1152
BF = jnp.bfloat16
WEIGHT = 1000
F32 = jnp.float32


def swap(block, axis):
    return lax.ppermute(block, axis, [(0, 1), (1, 0)])


def halves(block, dim):
    middle = block.shape[dim] // 2
    return (
        lax.slice_in_dim(block, 0, middle, axis=dim),
        lax.slice_in_dim(block, middle, block.shape[dim], axis=dim),
    )


def add(*terms):
    total = terms[0].astype(F32)
    for term in terms[1:]:
        total = total + term.astype(F32)
    return total.astype(terms[0].dtype)


def exchange(blocks, axes):
    return lax.all_to_all(blocks, axes, split_axis=0, concat_axis=0, tiled=True)


def spread(block, axes, count):
    return exchange(jnp.broadcast_to(block[None], (count,) + block.shape), axes)


def z_shift(block, by):
    return lax.ppermute(block, ZRING, [(i, (i + by) % 4) for i in range(4)])


def token_groups(block):
    near = jnp.concatenate([z_shift(block, -1), z_shift(block, 1)], axis=0)
    far = z_shift(block, 2)
    return [(part, swap(part, "core")) for part in (block, near, far)]


def token_sums(pairs):
    own, near, far = (add(mine, swap(others, "core")) for mine, others in pairs)
    after_rows, before_rows = halves(near, 0)
    terms = (own, z_shift(after_rows, 1), z_shift(before_rows, -1), z_shift(far, 2))
    return sum(term.astype(F32) for term in terms)


def hold_body(w, out, sem):
    copy = pltpu.make_async_copy(w, out, sem)
    copy.start()
    copy.wait()


def held(weights):
    return pl.pallas_call(
        hold_body,
        out_shape=pltpu.VMEM(weights.shape, weights.dtype),
        in_specs=[pl.BlockSpec(memory_space=pl.ANY)],
        out_specs=pl.BlockSpec(memory_space=pltpu.VMEM),
        scratch_shapes=[pltpu.SemaphoreType.DMA],
        compiler_params=pltpu.CompilerParams(vmem_limit_bytes=44 * 1024 * 1024),
        cost_estimate=pl.CostEstimate(
            flops=0, bytes_accessed=4 * weights.size, transcendentals=0
        ),
        name="held",
    )(weights)


def cot_products_body(ca, cb, da, db, w, near_out, far_out):
    half = ca.shape[0]
    for i, part in enumerate((ca, cb)):
        near_out[i * half : (i + 1) * half] = dot(part[...], w[...])
    half = da.shape[0]
    for i, part in enumerate((da, db)):
        far_out[i * half : (i + 1) * half] = dot(part[...], w[...])


def ff_body(*refs, tile, given):
    (na, nb), cots, refs = refs[:2], refs[2 : 3 if given else 4], refs[3 if given else 4 :]
    w, _, m_out, dg_out, du_out, dna_out, dnb_out, nbuf, cbuf, sem = refs
    half = na.shape[0]
    parts = [(na, nbuf, 0), (nb, nbuf, 1)]
    if not given:
        parts += [(cots[0], cbuf, 0), (cots[1], cbuf, 1)]
    fetches = [
        pltpu.make_async_copy(part, buffer.at[pl.ds(k * half, half)], sem.at[i])
        for i, (part, buffer, k) in enumerate(parts)
    ]
    if given:
        fetches.append(pltpu.make_async_copy(cots[0], cbuf, sem.at[2]))
    for fetch in fetches:
        fetch.start()
    for fetch in fetches:
        fetch.wait()
    tiles = 2 * half // tile
    for i in range(tiles):
        at = pl.ds(i * tile, tile)
        rows = nbuf[at]
        gate = dot(rows, w[0])
        up = dot(rows, w[1])
        hidden_grad = cbuf[at] if given else dot(cbuf[at], w[2])
        sigma = 1.0 / (1.0 + jnp.exp(-gate))
        act = gate * sigma
        m_out[at] = (act * up).astype(BF)
        up_grad = (hidden_grad * act).astype(BF)
        gate_grad = (hidden_grad * up * sigma * (1.0 + gate * (1.0 - sigma))).astype(BF)
        dg_out[at] = gate_grad
        du_out[at] = up_grad
        back = (dot_t(gate_grad, w[0]) + dot_t(up_grad, w[1])).astype(BF)
        if tiles == 1:
            dna_out[...] = back[:half]
            dnb_out[...] = back[half:]
        else:
            out = dna_out if i < tiles // 2 else dnb_out
            out[pl.ds(i % (tiles // 2) * tile, tile)] = back


def ff_rows(normed, cots, weights, order, tile=256):
    given = len(cots) == 1
    half, width = normed[0].shape
    units = weights.shape[2]
    anywhere = pl.BlockSpec(memory_space=pl.ANY)
    vmem = pl.BlockSpec(memory_space=pltpu.VMEM)
    return pl.pallas_call(
        functools.partial(ff_body, tile=tile, given=given),
        out_shape=[jax.ShapeDtypeStruct((2 * half, units), BF)] * 3
        + [jax.ShapeDtypeStruct((half, width), BF)] * 2,
        in_specs=[anywhere] * (2 + len(cots)) + [vmem, anywhere],
        out_specs=[vmem] * 5,
        scratch_shapes=[
            pltpu.VMEM((2 * half, width), BF),
            pltpu.VMEM((2 * half, units), F32) if given else pltpu.VMEM((2 * half, width), BF),
            pltpu.SemaphoreType.DMA((4,)),
        ],
        compiler_params=pltpu.CompilerParams(vmem_limit_bytes=24 * 1024 * 1024),
        cost_estimate=pl.CostEstimate(
            flops=20 * half * width * units,
            bytes_accessed=6 * width * units,
            transcendentals=2 * half * units,
        ),
        name="feed_forward_rows",
    )(*normed, *cots, weights, order)


def wg_body(*refs, sizes, tile):
    count = len(sizes)
    groups = count // 2
    normed, cots, refs = refs[:count], refs[count : 2 * count], refs[2 * count :]
    hidden, gates, ups = refs[:groups], refs[groups : 2 * groups], refs[2 * groups : 3 * groups]
    out, nbuf, cbuf, mbuf, gbuf, ubuf, turned, sem = refs[3 * groups + 1 :]
    pair_sizes = [sizes[2 * i] + sizes[2 * i + 1] for i in range(groups)]

    def copies(at, buffer, sources, lengths):
        result, start = [], 0
        for source, length in zip(sources, lengths):
            target = buffer.at[pl.ds(start, length)]
            result.append(pltpu.make_async_copy(source, target, sem.at[at]))
            start += length
        return result

    def normed_copies():
        return copies(0, nbuf, normed, sizes)

    def cot_copies():
        return copies(1, cbuf, cots, sizes)

    def gate_copies():
        return copies(2, gbuf, gates, pair_sizes)

    def up_copies():
        return copies(3, ubuf, ups, pair_sizes)

    def hidden_copies():
        return copies(4, mbuf, hidden, pair_sizes)

    which, step = pl.program_id(0), pl.program_id(1)

    @pl.when((which == 0) & (step == 0))
    def _():
        first = normed_copies() + gate_copies()
        for copy in first + up_copies() + cot_copies() + hidden_copies():
            copy.start()
        for copy in first:
            copy.wait()

    @pl.when((which == 1) & (step == 0))
    def _():
        for copy in up_copies():
            copy.wait()

    @pl.when((which == 2) & (step == 0))
    def _():
        for copy in cot_copies() + hidden_copies():
            copy.wait()

    columns = pl.ds(pl.multiple_of(step * tile, tile), tile)
    @pl.when(which == 0)
    def _():
        left = nbuf[:, columns].T
        turned[step] = left
        out[...] = dot(left, gbuf[...]).astype(BF)

    @pl.when(which == 1)
    def _():
        out[...] = dot(turned[step], ubuf[...]).astype(BF)

    @pl.when(which == 2)
    def _():
        out[...] = dot(cbuf[:, columns].T, mbuf[...]).astype(BF)


def weight_grads(normed, cots, hidden, gates, ups, order, tile=768):
    sizes = tuple(part.shape[0] for part in normed)
    rows, width, units = sum(sizes), normed[0].shape[1], hidden[0].shape[1]
    anywhere = pl.BlockSpec(memory_space=pl.ANY)
    return pl.pallas_call(
        functools.partial(wg_body, sizes=sizes, tile=tile),
        grid=(3, width // tile),
        out_shape=jax.ShapeDtypeStruct((3, width, units), BF),
        in_specs=[anywhere] * (2 * len(normed) + 3 * len(hidden) + 1),
        out_specs=pl.BlockSpec((None, tile, units), lambda i, j: (i, j, 0)),
        scratch_shapes=[pltpu.VMEM((rows, width), BF)] * 2
        + [pltpu.VMEM((rows, units), BF)] * 3
        + [pltpu.VMEM((width // tile, tile, rows), BF), pltpu.SemaphoreType.DMA((5,))],
        compiler_params=pltpu.CompilerParams(vmem_limit_bytes=48 * 1024 * 1024),
        cost_estimate=pl.CostEstimate(
            flops=6 * rows * width * units,
            bytes_accessed=6 * width * units + rows * (4 * width + 6 * units),
            transcendentals=0,
        ),
        name="weight_gradients",
    )(*normed, *cots, *hidden, *gates, *ups, order)


def down_body(ha, hb, hc, w, *outs, tile=256):
    for group, hidden in enumerate((ha, hb, hc)):
        half = hidden.shape[0] // 2
        step = min(tile, 2 * half)
        for start in range(0, 2 * half, step):
            part = dot_t(hidden[pl.ds(start, step)], w[...]).astype(BF)
            if step > half:
                outs[2 * group][...] = part[:half]
                outs[2 * group + 1][...] = part[half:]
            else:
                outs[2 * group + start // half][pl.ds(start % half, step)] = part


def down_rows(hidden, weights, order):
    _, width, units = weights.shape
    halved = [part.shape[0] // 2 for part in hidden for _ in range(2)]
    outs = vmem_call(
        down_body,
        [((rows, width), BF) for rows in halved],
        [*hidden, (weights, 2)],
        "down_rows",
        (order,),
        limit=60,
        flops=2 * sum(halved) * width * units,
        moved=2 * width * units + 2 * sum(halved) * (width + units),
    )
    return [(outs[0], outs[1]), (outs[2], outs[3]), (outs[4], outs[5])]


def dot(a, b):
    return jnp.dot(a, b, preferred_element_type=F32)


def dot_t(a, b):
    return lax.dot_general(a, b, (((1,), (1,)), ((), ())), preferred_element_type=F32)


def t_dot(a, b):
    return lax.dot_general(a, b, (((0,), (0,)), ((), ())), preferred_element_type=F32)


def pick(index, low, high):
    return jnp.where(index == 0, low, high)


def vmem_call(
    body, outs, ins, name, order=(), scratch=(), limit=16, flops=0, moved=0, first=None
):
    count, skipped, results, extra = len(ins), len(order), len(outs), len(scratch)
    parts = [value[1] if isinstance(value, tuple) else None for value in ins]
    ins = [value[0] if isinstance(value, tuple) else value for value in ins]

    def kernel(*refs):
        sources, refs = refs[:count], refs[count + skipped :]
        fixed, buffers, sem = refs[: results + extra], refs[results + extra : -1], refs[-1]
        fetches = [
            pltpu.make_async_copy(source if at is None else source.at[at], buffer, sem.at[i])
            for i, (source, at, buffer) in enumerate(zip(sources, parts, buffers))
        ]
        for fetch in fetches:
            fetch.start()
        for fetch in fetches[:first]:
            fetch.wait()

        def rest():
            for fetch in fetches[first:]:
                fetch.wait()

        body(*(() if first is None else (rest,)), *buffers, *fixed)

    return pl.pallas_call(
        kernel,
        out_shape=[jax.ShapeDtypeStruct(shape, dtype) for shape, dtype in outs],
        in_specs=[pl.BlockSpec(memory_space=pl.ANY)] * (count + skipped),
        out_specs=[pl.BlockSpec(memory_space=pltpu.VMEM)] * results,
        scratch_shapes=[
            *scratch,
            *(
                pltpu.VMEM(value.shape if at is None else value.shape[1:], value.dtype)
                for value, at in zip(ins, parts)
            ),
            pltpu.SemaphoreType.DMA((count,)),
        ],
        compiler_params=pltpu.CompilerParams(vmem_limit_bytes=limit * 1024 * 1024),
        cost_estimate=pl.CostEstimate(flops=flops, bytes_accessed=moved, transcendentals=0),
        name=name,
    )(*ins, *order)


def copies_body(block, out):
    for i in range(out.shape[0]):
        out[i] = block[...]


def copies(block, count, *order):
    shape = (count,) + block.shape
    moved = 2 * count * block.size
    return vmem_call(
        copies_body, [(shape, block.dtype)], [block], "copies", order, moved=moved
    )[0]


def arrange_body(own, other, zh, out):
    mine = zh[0:1, 0:1] == 0
    for i in range(3):
        out[2 * i] = jnp.where(mine, own[i], other[i])
        out[2 * i + 1] = jnp.where(mine, other[i], own[i])


def ordered_body(own, other, zh, out):
    mine = zh[0:1, 0:1] == 0
    for i in range(own.shape[0]):
        out[0, i] = jnp.where(mine, own[i], other[i])
        out[1, i] = jnp.where(mine, other[i], own[i])


def ordered(own, other, zh, name, order):
    flag = jnp.full((8, HD), zh, jnp.int32)
    shape = (2,) + own.shape
    return vmem_call(
        ordered_body, [(shape, BF)], [own, other, flag], name, order, moved=8 * own.size
    )[0]


def sum_body(terms, out):
    total = terms[0].astype(F32)
    for i in range(1, terms.shape[0]):
        total = total + terms[i].astype(F32)
    out[...] = total


def summed(terms, *order):
    return vmem_call(
        sum_body, [(terms.shape[1:], F32)], [terms], "summed", order, moved=2 * terms.size
    )[0]


def stack_body(*refs):
    *parts, out = refs
    rows = parts[0].shape[0]
    for i, part in enumerate(parts):
        out[i * rows : (i + 1) * rows] = part[...]


def stacked(parts, *order):
    rows, columns = parts[0].shape
    shape = (len(parts) * rows, columns)
    moved = 4 * shape[0] * columns
    return vmem_call(stack_body, [(shape, BF)], list(parts), "stacked", order, moved=moved)[0]


def row_of(blocks, offset, size):
    count, lanes = blocks.shape
    line = (lanes, count * size)
    at = lax.broadcasted_iota(jnp.int32, line, 1)
    from_lane = lax.broadcasted_iota(jnp.int32, line, 0) - offset
    spots = (lax.rem(at, size) == from_lane).astype(BF)
    values = dot(blocks, spots)
    at = lax.broadcasted_iota(jnp.int32, values.shape, 1)
    owner = lax.broadcasted_iota(jnp.int32, values.shape, 0)
    mine = (at >= owner * size) & (at < (owner + 1) * size)
    return jnp.sum(jnp.where(mine, values, 0.0), axis=0, keepdims=True)


def vectors_body(gains, biases, ranks, attn_out, mlp_out, bias_out):
    attn_out[...] = jnp.broadcast_to(row_of(gains[...], 0, 48), attn_out.shape)
    mlp_out[...] = jnp.broadcast_to(row_of(gains[...], 48, 48), mlp_out.shape)
    full = row_of(biases[...], 0, 64)
    rank = ranks[0:1, 0:1]
    query = key = value = 0.0
    for i in range(4):
        query = query + jnp.where(rank == i, full[:, 384 * i : 384 * (i + 1)], 0.0)
    for i in range(2):
        mine = (rank >= 2 * i) & (rank < 2 * i + 2)
        key = key + jnp.where(mine, full[:, 1536 + HD * i : 1536 + HD * (i + 1)], 0.0)
        value = value + jnp.where(mine, full[:, 1792 + HD * i : 1792 + HD * (i + 1)], 0.0)
    line = jnp.concatenate([query, key, value], axis=1)
    bias_out[...] = jnp.broadcast_to(line, bias_out.shape)


def turn(vectors, cos2, sin2):
    return vectors * cos2 + pltpu.roll(vectors, HD // 2, 1) * sin2


def unpack_table(table, places):
    first, last = table[:, 2 * HD : 2 * HD + 1], table[:, 2 * HD + 1 : 2 * HD + 2]
    keys = places[0:1, :]
    return table[:, :HD], table[:, HD : 2 * HD], (keys >= first) & (keys <= last)


def masked_scores(queries, keys, allowed):
    return jnp.where(allowed, dot_t(queries, keys) * HD ** (-0.5), -1e30)


def attn_forward_body(
    x0, x1, x2, x3, gain, w, bias, table, places,
    n_out, q_out, kv_out, o_out, lse_out,
):
    rows = x0.shape[0]
    for i, x in enumerate((x0, x1, x2, x3)):
        part = x[...].astype(F32)
        scale = lax.rsqrt(jnp.mean(part * part, axis=-1, keepdims=True) + EPSILON)
        n_out[i * rows : (i + 1) * rows] = (part * scale * gain[0:1]).astype(BF)
    qkv = dot(n_out[...], w[...]) + bias[0:1]
    cosines, sines, allowed = unpack_table(table, places)
    keys = turn(qkv[:, 384:512], cosines, sines).astype(BF)
    values = qkv[:, 512:].astype(BF)
    kv_out[:, :HD] = keys
    kv_out[:, HD:] = values
    lses = []
    for h in range(3):
        at = slice(h * HD, (h + 1) * HD)
        queries = turn(qkv[:, at], cosines, sines).astype(BF)
        q_out[:, at] = queries
        scores = masked_scores(queries, keys, allowed)
        peak = jnp.max(scores, axis=-1, keepdims=True)
        shifted = jnp.exp(scores - peak)
        total = jnp.sum(shifted, axis=-1, keepdims=True)
        probs = (shifted / total).astype(BF)
        o_out[:, at] = dot(probs, values).astype(BF)
        lses.append(peak + jnp.log(total))
    lse_out[...] = jnp.concatenate(lses + [jnp.zeros((4 * rows, 125), F32)], axis=1)


def parted(partial, keep, give):
    rows = partial.shape[0] // 4
    keep[0] = partial[:rows].astype(BF)
    give[0] = partial[rows : 2 * rows].astype(BF)
    keep[1] = partial[2 * rows : 3 * rows].astype(BF)
    give[1] = partial[3 * rows :].astype(BF)


def attn_out_body(o, w, keep, give):
    parted(dot_t(o[...], w[...]), keep, give)


def residual_body(x, keep, got, across, gain, h_out, n_out):
    h = x[...].astype(F32) + keep[0].astype(F32) + got[0].astype(F32) + across[...].astype(F32)
    h_out[...] = h
    scale = lax.rsqrt(jnp.mean(h * h, axis=-1, keepdims=True) + EPSILON)
    n_out[...] = (h * scale * gain[0:1]).astype(BF)


def norm_backward(grad, rows, gain):
    scale = lax.rsqrt(jnp.mean(rows * rows, axis=-1, keepdims=True) + EPSILON)
    scaled = grad * gain
    back = scale * scaled - rows * scale**3 * jnp.mean(scaled * rows, axis=-1, keepdims=True)
    return back, jnp.sum(grad * rows * scale, axis=0, keepdims=True)


def ff_back_body(own_a, own_b, got_a, got_b, got_c, h, cot, gain, grad_out, branch_out, gain_out):
    grad = sum(part[...].astype(F32) for part in (own_a, own_b, got_a, got_b, got_c))
    back, gain_out[...] = norm_backward(grad, h[...], gain[0:1])
    total = cot[...].astype(F32) + back
    grad_out[...] = total
    branch_out[...] = total.astype(BF)


def attn_back_body(keep, got, across, x, above, gain, grad_out):
    grad = keep[0].astype(F32) + got[0].astype(F32) + across[...].astype(F32)
    back, _ = norm_backward(grad, x[...].astype(F32), gain[0:1])
    grad_out[...] = above[...] + back


def attn_backward_body(
    rest, b0, b1, b2, b3, wo, x0, x1, x2, x3, w, q, kv, lse, table, places,
    grads_out, keep, give, sums_out, gain_out, bbuf,
):
    rows = b0.shape[0]
    for i, part in enumerate((b0, b1, b2, b3)):
        bbuf[i * rows : (i + 1) * rows] = part[...]
    attended_grad = dot(bbuf[...], wo[...]).astype(BF)
    rest()
    keys, values = kv[:, :HD], kv[:, HD:]
    cosines, sines, allowed = unpack_table(table, places)
    sines = -sines
    key_grad = value_grad = 0.0
    for h in range(3):
        at = slice(h * HD, (h + 1) * HD)
        queries, o_grad = q[:, at], attended_grad[:, at]
        probs = jnp.exp(masked_scores(queries, keys, allowed) - lse[:, h : h + 1])
        prob_grad = dot_t(o_grad, values)
        inner = jnp.sum(probs * prob_grad, axis=-1, keepdims=True)
        score_grad = (probs * (prob_grad - inner)).astype(BF)
        query_grad = dot(score_grad, keys) * HD ** (-0.5)
        grads_out[:, at] = turn(query_grad, cosines, sines).astype(BF)
        key_grad = key_grad + t_dot(score_grad, queries)
        value_grad = value_grad + t_dot(probs.astype(BF), o_grad)
    grads_out[:, 384:512] = turn(key_grad * HD ** (-0.5), cosines, sines).astype(BF)
    grads_out[:, 512:] = value_grad.astype(BF)
    grads = grads_out[...]
    sums_out[...] = jnp.sum(grads.astype(F32), axis=0, keepdims=True)
    partial = dot_t(grads, w[...])
    parted(partial, keep, give)
    gain_grad = 0.0
    for i, x in enumerate((x0, x1, x2, x3)):
        part = x[...].astype(F32)
        scale = lax.rsqrt(jnp.mean(part * part, axis=-1, keepdims=True) + EPSILON)
        terms = partial[i * rows : (i + 1) * rows] * part * scale
        gain_grad = gain_grad + jnp.sum(terms, axis=0, keepdims=True)
    gain_out[...] = gain_grad


def blocks_of(row, size):
    count = row.shape[1] // size
    at = lax.broadcasted_iota(jnp.int32, (count, row.shape[1]), 1)
    owner = lax.broadcasted_iota(jnp.int32, (count, row.shape[1]), 0)
    mine = (at >= owner * size) & (at < (owner + 1) * size)
    values = jnp.where(mine, row, 0.0).astype(BF)
    at = lax.broadcasted_iota(jnp.int32, (row.shape[1], HD), 0)
    lane = lax.broadcasted_iota(jnp.int32, (row.shape[1], HD), 1)
    return dot(values, (lax.rem(at, size) == lane).astype(BF))


def attn_grads_body(
    rest, b0, b1, b2, b3, attended, normed, qkv_grad, gain_attn, gain_mlp, sums, ranks, out, bbuf
):
    size = b0.shape[0]
    for i, part in enumerate((b0, b1, b2, b3)):
        bbuf[i * size : (i + 1) * size] = part[...]
    half = bbuf.shape[1] // 2
    spans = [(slice(i * half, (i + 1) * half), slice(16 * i, 16 * (i + 1))) for i in range(2)]
    for at, blocks in spans:
        grad = t_dot(bbuf[:, at], attended[...]).astype(BF)
        out[blocks, :, 640:] = grad.reshape(16, half // 16, 384)
    rest()
    for at, blocks in spans:
        grad = t_dot(normed[:, at], qkv_grad[...]).astype(BF)
        out[blocks, :, :512] = grad.reshape(16, half // 16, 512)
    rank = ranks[0:1, 0:1]
    parts = [jnp.where(rank == i, sums[:, :384], 0.0) for i in range(4)]
    for start in (384, 512):
        for i in range(2):
            mine = (rank >= 2 * i) & (rank < 2 * i + 2)
            parts.append(jnp.where(mine, sums[:, start : start + HD], 0.0))
    rows_of = (
        blocks_of(gain_attn[...], 48),
        blocks_of(gain_mlp[...], 48),
        blocks_of(jnp.concatenate(parts[:6], axis=1), 56),
        blocks_of(jnp.concatenate(parts[6:], axis=1), 8),
    )
    at = lax.broadcasted_iota(jnp.int32, (32, out.shape[1], HD), 1)
    tail = jnp.zeros((32, out.shape[1], HD), F32)
    for i, values in enumerate(rows_of):
        tail = jnp.where(at == i, values[:, None, :], tail)
    out[:, :, 512:640] = tail.astype(BF)


def shards(
    layer_input,
    q_weight,
    kv_weight,
    o_weight,
    norm_gains,
    qkv_bias,
    gate_up,
    down_weight,
    cotangent,
    lengths,
):
    zh, zl, core = (lax.axis_index(a) for a in ("zh", "zl", "core"))
    rank = 2 * zl + core
    width = layer_input.shape[1]
    rows = layer_input.shape[0]

    small = jnp.concatenate([norm_gains.reshape(-1), qkv_bias, jnp.zeros((216,), BF)])
    vectors = jnp.concatenate([kv_weight.reshape(24, 256), small[None], jnp.zeros((7, 256), BF)])
    got = swap(vectors, "core")
    both = jnp.stack([pick(core, vectors, got), pick(core, got, vectors)])
    small_keep = both[:, 24].reshape(2, 2, HD)
    kv_keep = pick(zl, both[:, :24, :HD], both[:, :24, HD:])
    kv_give = pick(zl, both[:, :24, HD:], both[:, :24, :HD])
    kv_crossed = swap(
        jnp.concatenate([kv_give, small_keep, jnp.zeros((2, 6, HD), BF)], axis=1), "zl"
    )
    kv_got, small_got = kv_crossed[:, :24], kv_crossed[:, 24:26]
    kv_rows = jnp.stack([pick(zl, kv_keep, kv_got), pick(zl, kv_got, kv_keep)])
    kv_rows = kv_rows.reshape(2, 2, 2, 12, HD).transpose(0, 1, 3, 2, 4).reshape(48, 2 * HD)
    small = jnp.stack([pick(zl, small_keep, small_got), pick(zl, small_got, small_keep)])
    small = small.reshape(4, 256)
    gains_row = jnp.concatenate([small[:, :12].reshape(48), small[:, 12:24].reshape(48)])
    bias_row = small[:, 24:40].reshape(64)
    small = jnp.zeros((48, HD), BF).at[0, :96].set(gains_row).at[1, :64].set(bias_row)

    ends = jnp.cumsum(lengths[0])
    ranks = jnp.stack([rank, 2 * zl + 1 - core, 2 * (1 - zl) + core, 2 * (1 - zl) + 1 - core])
    group = 4 * rows
    places = (ranks[:, None] * rows + jnp.arange(rows, dtype=jnp.int32)[None, :]).reshape(group)
    passed = ends[None, :] <= places[:, None]
    starts = jnp.sum(jnp.where(passed, lengths[0][None, :], 0), axis=1)
    inverse = THETA ** (-(2.0 * jnp.arange(HD // 2, dtype=F32)) / HD)
    inverse = jnp.concatenate([inverse, inverse])[None, :]
    angles = (places - starts).astype(F32)[:, None] * inverse
    sign = jnp.where(jnp.arange(HD) < HD // 2, -1.0, 1.0).astype(F32)[None, :]
    lane = jnp.arange(HD)[None, :]
    ranges = jnp.where(lane == 0, starts[:, None], places[:, None]).astype(F32)
    table = jnp.concatenate([jnp.cos(angles), jnp.sin(angles) * sign, ranges], axis=1)
    tables = (table, jnp.broadcast_to(places.astype(F32)[None, :], (8, group)))

    living = (places[:rows] < ends[-1])[:, None]
    cot_local = jnp.where(living, cotangent, jnp.zeros((), BF))
    cot_groups = token_groups(cot_local)

    across = swap(layer_input, "zl")
    group_inputs = (layer_input, swap(layer_input, "core"), across, swap(across, "core"))

    attn_part = jnp.concatenate([q_weight, kv_rows, small, o_weight.T], axis=-1)
    attn_plane = exchange(copies(attn_part, 16), PLANE)
    qkv_plane, o_plane = attn_plane[..., :640], attn_plane[..., 768:]
    small_plane = attn_plane[:, :2, 640:768]
    small_other = swap(small_plane, "zh")
    qkv_other = swap(qkv_plane, "zh")
    o_other = swap(o_plane, "zh")
    waits = (cot_groups[1][1], cot_groups[2][1], group_inputs[3], *tables)
    qkv_full = ordered(qkv_plane, qkv_other, zh, "qkv_weights", waits)
    small = jnp.stack([pick(zh, small_plane, small_other), pick(zh, small_other, small_plane)])
    small = small.reshape(32, 2, HD)
    qkv_full = qkv_full.reshape(width, 640)
    gain_attn, gain_mlp, bias = vmem_call(
        vectors_body,
        [((8, width), F32), ((8, width), F32), ((8, 640), F32)],
        [small[:, 0], small[:, 1], jnp.full((8, HD), rank, jnp.int32)],
        "gains_and_biases",
        limit=16,
    )

    mlp = jnp.concatenate([gate_up, down_weight.T[None]], axis=0)
    mlp = jnp.pad(mlp, ((0, 0), (0, 0), (0, 2 * HALF - mlp.shape[2])))
    mlp_own = pick(zh, mlp[..., :HALF], mlp[..., HALF:])
    mlp_other = swap(pick(zh, mlp[..., HALF:], mlp[..., :HALF]), "zh")
    mlp = vmem_call(
        arrange_body,
        [((6, 48, HALF), BF)],
        [mlp_own, mlp_other, jnp.full((8, HD), zh, jnp.int32)],
        "arranged",
        (kv_crossed,),
        moved=4 * mlp_own.size,
    )[0]
    mlp = lax.all_gather(mlp, PLANE, axis=1, tiled=True)
    mlp = mlp.reshape(3, width, HALF)

    normed_group, queries, kv_rot, attended, lse = vmem_call(
        attn_forward_body,
        [
            ((group, width), BF),
            ((group, 384), BF),
            ((group, 256), BF),
            ((group, 384), BF),
            ((group, 128), F32),
        ],
        [*group_inputs, gain_attn, qkv_full, bias, *tables],
        "attention_forward",
        limit=32,
        flops=2 * group * (width * 640 + 6 * group * HD),
        moved=2 * group * width * 2 + 2 * width * 768,
    )
    o_full = ordered(o_plane, o_other, zh, "o_weights", (attended,)).reshape(width, 384)
    pair = ((2, rows, width), BF)
    keep, give = vmem_call(
        attn_out_body,
        [pair, pair],
        [attended, o_full],
        "attention_out",
        flops=2 * group * width * 384,
        moved=2 * width * 384 + 2 * group * width,
    )
    got = swap(give, "core")
    weights = held(mlp)
    residual, normed_mlp = vmem_call(
        residual_body,
        [((rows, width), F32), ((rows, width), BF)],
        [layer_input, keep, got, swap(add(keep[1], got[1]), "zl"), gain_mlp],
        "residual_norm",
        (weights,),
        moved=10 * rows * width,
    )

    after_rows, before_rows = z_shift(normed_mlp, -1), z_shift(normed_mlp, 1)
    far_rows = z_shift(normed_mlp, 2)
    own = (normed_mlp, swap(normed_mlp, "core"))
    own_out = ff_rows(own, cot_groups[0], weights, cot_local)
    cot_near, cot_far = vmem_call(
        cot_products_body,
        [((4 * rows, HALF), F32), ((2 * rows, HALF), F32)],
        [*cot_groups[1], *cot_groups[2], (mlp, 2)],
        "cotangent_products",
        (own_out[0],),
        flops=12 * rows * width * HALF,
    )
    near = stacked((after_rows, before_rows), cot_near)
    near = (near, swap(near, "core"))
    near_out = ff_rows(near, (cot_near,), weights, own_out[0])
    far_rows = stacked((far_rows,), near_out[0])
    far = (far_rows, swap(far_rows, "core"))
    near_sum = [
        add(mine, swap(others, "core"))
        for mine, others in zip(halves(near_out[3], 0), halves(near_out[4], 0))
    ]
    near_got = (z_shift(near_sum[0], 1), z_shift(near_sum[1], -1))
    far_out = ff_rows(far, (cot_far,), weights, near_sum[1])
    far_sum = add(far_out[3], swap(far_out[4], "core"))
    own_got = swap(own_out[4], "core")
    far_got = z_shift(far_sum, 2)
    results = (own_out, near_out, far_out)
    hidden, gate_grads, up_grads = ([r[i] for r in results] for i in range(3))
    flat_normed = [*own, *near, *far]
    flat_cots = [part for pair in cot_groups for part in pair]
    grad_terms = weight_grads(flat_normed, flat_cots, hidden, gate_grads, up_grads, far_sum)
    residual_grad, branch, gain_mlp_grad = vmem_call(
        ff_back_body,
        [((rows, width), F32), ((rows, width), BF), ((1, width), F32)],
        [own_out[3], own_got, *near_got, far_got, residual, cot_local, gain_mlp],
        "residual_gradient",
        (grad_terms,),
        limit=60,
        flops=10**9 * WEIGHT,
        moved=24 * rows * width,
    )
    mlp_grads = lax.psum_scatter(
        grad_terms.reshape(6, width // 2, HALF), PLANE, scatter_dimension=1, tiled=True
    ).reshape(3, 2, 48, HALF)
    own_grads = lax.dynamic_index_in_dim(mlp_grads, zh, 1, keepdims=False)
    other_grads = swap(lax.dynamic_index_in_dim(mlp_grads, 1 - zh, 1, keepdims=False), "zh")
    own_grads, other_grads = own_grads.astype(F32), other_grads.astype(F32)
    mlp_shard = jnp.concatenate(
        [pick(zh, own_grads, other_grads), pick(zh, other_grads, own_grads)], axis=-1
    )[..., : gate_up.shape[2]]
    gate_up_shard = mlp_shard[:2]
    down_shard = mlp_shard[2].T

    out_pairs = down_rows(hidden, mlp, branch)
    layer_output = (residual + token_sums(out_pairs)).astype(BF)

    across = stacked((swap(branch, "zl"),), out_pairs[0][0])
    branch_group = (branch, swap(branch, "core"), across, swap(across, "core"))
    qkv_grad, keep, give, sums, gain_attn_grad = vmem_call(
        attn_backward_body,
        [((group, 640), BF), pair, pair, ((1, 640), F32), ((1, width), F32)],
        [*branch_group, o_full, *group_inputs, qkv_full, queries, kv_rot, lse, *tables],
        "attention_backward",
        limit=60,
        first=5,
        scratch=[pltpu.VMEM((group, width), BF)],
        flops=2 * group * (width * 1024 + 15 * group * HD),
        moved=4 * group * width + 2 * width * 1024,
    )
    key_grad, value_grad = qkv_grad[:, 384:512], qkv_grad[:, 512:]
    got = swap(pick(core, value_grad, key_grad), "core").reshape(2, 2, rows, HD)[:, ::-1]
    own = pick(core, key_grad, value_grad).astype(F32) + got.reshape(group, HD).astype(F32)
    right = jnp.concatenate([qkv_grad[:, :384], own.astype(BF)], axis=1)

    terms = vmem_call(
        attn_grads_body,
        [((32, width // 32, 1024), BF)],
        [
            *branch_group,
            attended,
            normed_group,
            right,
            gain_attn_grad,
            gain_mlp_grad,
            sums,
            jnp.full((8, HD), rank, jnp.int32),
        ],
        "attention_weight_gradients",
        scratch=[pltpu.VMEM((group, width), BF)],
        limit=60,
        first=5,
        flops=2 * group * width * 1024,
        moved=4 * group * width + 2 * width * 1152,
    )[0]
    attn_shard = summed(exchange(terms, DATA))

    got = swap(give, "core")
    across = swap(add(keep[1], got[1]), "zl")
    input_grad = vmem_call(
        attn_back_body,
        [((rows, width), F32)],
        [keep, got, across, layer_input, residual_grad, gain_attn],
        "input_gradient",
        moved=20 * rows * width,
    )[0]

    q_shard = attn_shard[:, :384]
    o_shard = attn_shard[:, 640:].T
    kv_sum = attn_shard[:, 384:512].reshape(2, 2, 12, HD)
    kv_keep = lax.dynamic_index_in_dim(kv_sum, core, 1, keepdims=False)
    kv_give = lax.dynamic_index_in_dim(kv_sum, 1 - core, 1, keepdims=False)
    vectors = attn_shard[:8, 512:640]
    got = swap(jnp.concatenate([kv_give.reshape(24, HD), vectors]), "core")
    kv_got = got[:24].reshape(2, 12, HD)
    vectors = vectors + got[24:]
    kv_sum = jnp.stack([pick(core, kv_keep, kv_got), pick(core, kv_got, kv_keep)], axis=2)
    kv_sum = kv_sum.reshape(2, 24, HD)
    kv_keep = pick(zl, kv_sum[0], kv_sum[1])
    got = swap(jnp.concatenate([pick(zl, kv_sum[1], kv_sum[0]), vectors]), "zl")
    kv_got = got[:24]
    vectors = vectors + got[24:]
    kv_shard = jnp.concatenate([pick(zl, kv_keep, kv_got), pick(zl, kv_got, kv_keep)], axis=-1)
    kv_shard = kv_shard.reshape(12, 2, 2 * HD).transpose(1, 0, 2)

    def own_part(row, size):
        return lax.dynamic_index_in_dim(
            vectors[row, : 4 * size].reshape(4, size), rank, 0, keepdims=False
        )

    return (
        layer_output,
        input_grad,
        q_shard,
        kv_shard,
        o_shard,
        jnp.stack([own_part(0, 12), own_part(1, 12)]),
        own_part(2, 14),
        own_part(3, 2),
        gate_up_shard,
        down_shard,
    )


def solution(mesh):
    fine = Mesh(mesh.devices.reshape(SIZES), AXES)
    dp = ("zh", "y", "x")
    tensor = ("zl", "core")
    every = dp + tensor
    in_specs = (
        P(every, None),
        P(dp, tensor),
        P(None, every, None),
        P(tensor, dp),
        P(None, every),
        P(every),
        P(None, dp, tensor),
        P(tensor, dp),
        P(every, None),
        P(dp, None),
    )
    out_specs = (
        P(every, None),
        P(every, None),
        P(dp, tensor),
        P(None, every, None),
        P(tensor, dp),
        P(None, every),
        P(every),
        P(every),
        P(None, dp, tensor),
        P(tensor, dp),
    )
    return jax.shard_map(shards, mesh=fine, in_specs=in_specs, out_specs=out_specs, check_vma=False)
```

```python
import functools

import jax
import jax.numpy as jnp
from jax import lax
from jax.experimental import pallas as pl
from jax.experimental.pallas import tpu as pltpu
from jax.sharding import Mesh, PartitionSpec as P

HQ = 12
KVH = 2
HD = 128
EPSILON = 1e-06
THETA = 1000000.0

AXES = ("zh", "y", "x", "zl", "core")
SIZES = (2, 4, 4, 2, 2)
ZRING = ("zh", "zl")
PLANE = ("y", "x")
DATA = ("zh", "y", "x")
HALF = 1152
BF = jnp.bfloat16
WEIGHT = 1000
F32 = jnp.float32


def swap(block, axis):
    return lax.ppermute(block, axis, [(0, 1), (1, 0)])


def halves(block, dim):
    middle = block.shape[dim] // 2
    return (
        lax.slice_in_dim(block, 0, middle, axis=dim),
        lax.slice_in_dim(block, middle, block.shape[dim], axis=dim),
    )


def add(*terms):
    total = terms[0].astype(F32)
    for term in terms[1:]:
        total = total + term.astype(F32)
    return total.astype(terms[0].dtype)


def exchange(blocks, axes):
    return lax.all_to_all(blocks, axes, split_axis=0, concat_axis=0, tiled=True)


def spread(block, axes, count):
    return exchange(jnp.broadcast_to(block[None], (count,) + block.shape), axes)


def z_shift(block, by):
    return lax.ppermute(block, ZRING, [(i, (i + by) % 4) for i in range(4)])


def token_groups(block):
    near = jnp.concatenate([z_shift(block, -1), z_shift(block, 1)], axis=0)
    far = z_shift(block, 2)
    return [(part, swap(part, "core")) for part in (block, near, far)]


def token_sums(pairs):
    own, near, far = (add(mine, swap(others, "core")) for mine, others in pairs)
    after_rows, before_rows = halves(near, 0)
    terms = (own, z_shift(after_rows, 1), z_shift(before_rows, -1), z_shift(far, 2))
    return sum(term.astype(F32) for term in terms)


def hold_body(w, out, sem):
    copy = pltpu.make_async_copy(w, out, sem)
    copy.start()
    copy.wait()


def held(weights):
    return pl.pallas_call(
        hold_body,
        out_shape=pltpu.VMEM(weights.shape, weights.dtype),
        in_specs=[pl.BlockSpec(memory_space=pl.ANY)],
        out_specs=pl.BlockSpec(memory_space=pltpu.VMEM),
        scratch_shapes=[pltpu.SemaphoreType.DMA],
        compiler_params=pltpu.CompilerParams(vmem_limit_bytes=44 * 1024 * 1024),
        cost_estimate=pl.CostEstimate(
            flops=0, bytes_accessed=4 * weights.size, transcendentals=0
        ),
        name="held",
    )(weights)


def cot_products_body(ca, cb, da, db, w, near_out, far_out):
    half = ca.shape[0]
    for i, part in enumerate((ca, cb)):
        near_out[i * half : (i + 1) * half] = dot(part[...], w[...])
    half = da.shape[0]
    for i, part in enumerate((da, db)):
        far_out[i * half : (i + 1) * half] = dot(part[...], w[...])


def ff_body(*refs, tile, given):
    (na, nb), cots, refs = refs[:2], refs[2 : 3 if given else 4], refs[3 if given else 4 :]
    w, _, m_out, dg_out, du_out, dna_out, dnb_out, nbuf, cbuf, sem = refs
    half = na.shape[0]
    parts = [(na, nbuf, 0), (nb, nbuf, 1)]
    if not given:
        parts += [(cots[0], cbuf, 0), (cots[1], cbuf, 1)]
    fetches = [
        pltpu.make_async_copy(part, buffer.at[pl.ds(k * half, half)], sem.at[i])
        for i, (part, buffer, k) in enumerate(parts)
    ]
    if given:
        fetches.append(pltpu.make_async_copy(cots[0], cbuf, sem.at[2]))
    for fetch in fetches:
        fetch.start()
    for fetch in fetches:
        fetch.wait()
    tiles = 2 * half // tile
    for i in range(tiles):
        at = pl.ds(i * tile, tile)
        rows = nbuf[at]
        gate = dot(rows, w[0])
        up = dot(rows, w[1])
        hidden_grad = cbuf[at] if given else dot(cbuf[at], w[2])
        sigma = 1.0 / (1.0 + jnp.exp(-gate))
        act = gate * sigma
        m_out[at] = (act * up).astype(BF)
        up_grad = (hidden_grad * act).astype(BF)
        gate_grad = (hidden_grad * up * sigma * (1.0 + gate * (1.0 - sigma))).astype(BF)
        dg_out[at] = gate_grad
        du_out[at] = up_grad
        back = (dot_t(gate_grad, w[0]) + dot_t(up_grad, w[1])).astype(BF)
        if tiles == 1:
            dna_out[...] = back[:half]
            dnb_out[...] = back[half:]
        else:
            out = dna_out if i < tiles // 2 else dnb_out
            out[pl.ds(i % (tiles // 2) * tile, tile)] = back


def ff_rows(normed, cots, weights, order, tile=256):
    given = len(cots) == 1
    half, width = normed[0].shape
    units = weights.shape[2]
    anywhere = pl.BlockSpec(memory_space=pl.ANY)
    vmem = pl.BlockSpec(memory_space=pltpu.VMEM)
    return pl.pallas_call(
        functools.partial(ff_body, tile=tile, given=given),
        out_shape=[jax.ShapeDtypeStruct((2 * half, units), BF)] * 3
        + [jax.ShapeDtypeStruct((half, width), BF)] * 2,
        in_specs=[anywhere] * (2 + len(cots)) + [vmem, anywhere],
        out_specs=[vmem] * 5,
        scratch_shapes=[
            pltpu.VMEM((2 * half, width), BF),
            pltpu.VMEM((2 * half, units), F32) if given else pltpu.VMEM((2 * half, width), BF),
            pltpu.SemaphoreType.DMA((4,)),
        ],
        compiler_params=pltpu.CompilerParams(vmem_limit_bytes=24 * 1024 * 1024),
        cost_estimate=pl.CostEstimate(
            flops=20 * half * width * units,
            bytes_accessed=6 * width * units,
            transcendentals=2 * half * units,
        ),
        name="feed_forward_rows",
    )(*normed, *cots, weights, order)


def wg_body(*refs, sizes, tile):
    count = len(sizes)
    groups = count // 2
    normed, cots, refs = refs[:count], refs[count : 2 * count], refs[2 * count :]
    hidden, gates, ups = refs[:groups], refs[groups : 2 * groups], refs[2 * groups : 3 * groups]
    out, nbuf, cbuf, mbuf, gbuf, ubuf, turned, sem = refs[3 * groups + 1 :]
    pair_sizes = [sizes[2 * i] + sizes[2 * i + 1] for i in range(groups)]

    def copies(at, buffer, sources, lengths):
        result, start = [], 0
        for source, length in zip(sources, lengths):
            target = buffer.at[pl.ds(start, length)]
            result.append(pltpu.make_async_copy(source, target, sem.at[at]))
            start += length
        return result

    def normed_copies():
        return copies(0, nbuf, normed, sizes)

    def cot_copies():
        return copies(1, cbuf, cots, sizes)

    def gate_copies():
        return copies(2, gbuf, gates, pair_sizes)

    def up_copies():
        return copies(3, ubuf, ups, pair_sizes)

    def hidden_copies():
        return copies(4, mbuf, hidden, pair_sizes)

    which, step = pl.program_id(0), pl.program_id(1)

    @pl.when((which == 0) & (step == 0))
    def _():
        first = normed_copies() + gate_copies()
        for copy in first + up_copies() + cot_copies() + hidden_copies():
            copy.start()
        for copy in first:
            copy.wait()

    @pl.when((which == 1) & (step == 0))
    def _():
        for copy in up_copies():
            copy.wait()

    @pl.when((which == 2) & (step == 0))
    def _():
        for copy in cot_copies() + hidden_copies():
            copy.wait()

    columns = pl.ds(pl.multiple_of(step * tile, tile), tile)
    @pl.when(which == 0)
    def _():
        left = nbuf[:, columns].T
        turned[step] = left
        out[...] = dot(left, gbuf[...]).astype(BF)

    @pl.when(which == 1)
    def _():
        out[...] = dot(turned[step], ubuf[...]).astype(BF)

    @pl.when(which == 2)
    def _():
        out[...] = dot(cbuf[:, columns].T, mbuf[...]).astype(BF)


def weight_grads(normed, cots, hidden, gates, ups, order, tile=768):
    sizes = tuple(part.shape[0] for part in normed)
    rows, width, units = sum(sizes), normed[0].shape[1], hidden[0].shape[1]
    anywhere = pl.BlockSpec(memory_space=pl.ANY)
    return pl.pallas_call(
        functools.partial(wg_body, sizes=sizes, tile=tile),
        grid=(3, width // tile),
        out_shape=jax.ShapeDtypeStruct((3, width, units), BF),
        in_specs=[anywhere] * (2 * len(normed) + 3 * len(hidden) + 1),
        out_specs=pl.BlockSpec((None, tile, units), lambda i, j: (i, j, 0)),
        scratch_shapes=[pltpu.VMEM((rows, width), BF)] * 2
        + [pltpu.VMEM((rows, units), BF)] * 3
        + [pltpu.VMEM((width // tile, tile, rows), BF), pltpu.SemaphoreType.DMA((5,))],
        compiler_params=pltpu.CompilerParams(vmem_limit_bytes=60 * 1024 * 1024),
        cost_estimate=pl.CostEstimate(
            flops=6 * rows * width * units,
            bytes_accessed=6 * width * units + rows * (4 * width + 6 * units),
            transcendentals=0,
        ),
        name="weight_gradients",
    )(*normed, *cots, *hidden, *gates, *ups, order)


def down_body(ha, hb, hc, w, *outs, tile=256):
    for group, hidden in enumerate((ha, hb, hc)):
        half = hidden.shape[0] // 2
        step = min(tile, 2 * half)
        for start in range(0, 2 * half, step):
            part = dot_t(hidden[pl.ds(start, step)], w[...]).astype(BF)
            if step > half:
                outs[2 * group][...] = part[:half]
                outs[2 * group + 1][...] = part[half:]
            else:
                outs[2 * group + start // half][pl.ds(start % half, step)] = part


def down_rows(hidden, weights, order):
    _, width, units = weights.shape
    halved = [part.shape[0] // 2 for part in hidden for _ in range(2)]
    outs = vmem_call(
        down_body,
        [((rows, width), BF) for rows in halved],
        [*hidden, (weights, 2)],
        "down_rows",
        (order,),
        limit=60,
        flops=2 * sum(halved) * width * units,
        moved=2 * width * units + 2 * sum(halved) * (width + units),
    )
    return [(outs[0], outs[1]), (outs[2], outs[3]), (outs[4], outs[5])]


def dot(a, b):
    return jnp.dot(a, b, preferred_element_type=F32)


def dot_t(a, b):
    return lax.dot_general(a, b, (((1,), (1,)), ((), ())), preferred_element_type=F32)


def t_dot(a, b):
    return lax.dot_general(a, b, (((0,), (0,)), ((), ())), preferred_element_type=F32)


def pick(index, low, high):
    return jnp.where(index == 0, low, high)


def vmem_call(
    body, outs, ins, name, order=(), scratch=(), limit=16, flops=0, moved=0, first=None
):
    count, skipped, results, extra = len(ins), len(order), len(outs), len(scratch)
    parts = [value[1] if isinstance(value, tuple) else None for value in ins]
    ins = [value[0] if isinstance(value, tuple) else value for value in ins]

    def kernel(*refs):
        sources, refs = refs[:count], refs[count + skipped :]
        fixed, buffers, sem = refs[: results + extra], refs[results + extra : -1], refs[-1]
        fetches = [
            pltpu.make_async_copy(source if at is None else source.at[at], buffer, sem.at[i])
            for i, (source, at, buffer) in enumerate(zip(sources, parts, buffers))
        ]
        for fetch in fetches:
            fetch.start()
        for fetch in fetches[:first]:
            fetch.wait()

        def rest():
            for fetch in fetches[first:]:
                fetch.wait()

        body(*(() if first is None else (rest,)), *buffers, *fixed)

    return pl.pallas_call(
        kernel,
        out_shape=[jax.ShapeDtypeStruct(shape, dtype) for shape, dtype in outs],
        in_specs=[pl.BlockSpec(memory_space=pl.ANY)] * (count + skipped),
        out_specs=[pl.BlockSpec(memory_space=pltpu.VMEM)] * results,
        scratch_shapes=[
            *scratch,
            *(
                pltpu.VMEM(value.shape if at is None else value.shape[1:], value.dtype)
                for value, at in zip(ins, parts)
            ),
            pltpu.SemaphoreType.DMA((count,)),
        ],
        compiler_params=pltpu.CompilerParams(vmem_limit_bytes=limit * 1024 * 1024),
        cost_estimate=pl.CostEstimate(flops=flops, bytes_accessed=moved, transcendentals=0),
        name=name,
    )(*ins, *order)


def copies_body(block, out):
    for i in range(out.shape[0]):
        out[i] = block[...]


def copies(block, count, *order):
    shape = (count,) + block.shape
    moved = 2 * count * block.size
    return vmem_call(
        copies_body, [(shape, block.dtype)], [block], "copies", order, moved=moved
    )[0]


def arrange_body(own, other, zh, out):
    mine = zh[0:1, 0:1] == 0
    for i in range(3):
        out[2 * i] = jnp.where(mine, own[i], other[i])
        out[2 * i + 1] = jnp.where(mine, other[i], own[i])


def ordered_body(own, other, zh, out):
    mine = zh[0:1, 0:1] == 0
    for i in range(own.shape[0]):
        out[0, i] = jnp.where(mine, own[i], other[i])
        out[1, i] = jnp.where(mine, other[i], own[i])


def ordered(own, other, zh, name, order):
    flag = jnp.full((8, HD), zh, jnp.int32)
    shape = (2,) + own.shape
    return vmem_call(
        ordered_body, [(shape, BF)], [own, other, flag], name, order, moved=8 * own.size
    )[0]


def sum_body(terms, out):
    total = terms[0].astype(F32)
    for i in range(1, terms.shape[0]):
        total = total + terms[i].astype(F32)
    out[...] = total


def summed(terms, *order):
    return vmem_call(
        sum_body, [(terms.shape[1:], F32)], [terms], "summed", order, moved=2 * terms.size
    )[0]


def stack_body(*refs):
    *parts, out = refs
    rows = parts[0].shape[0]
    for i, part in enumerate(parts):
        out[i * rows : (i + 1) * rows] = part[...]


def stacked(parts, *order):
    rows, columns = parts[0].shape
    shape = (len(parts) * rows, columns)
    moved = 4 * shape[0] * columns
    return vmem_call(stack_body, [(shape, BF)], list(parts), "stacked", order, moved=moved)[0]


def row_of(blocks, offset, size):
    count, lanes = blocks.shape
    line = (lanes, count * size)
    at = lax.broadcasted_iota(jnp.int32, line, 1)
    from_lane = lax.broadcasted_iota(jnp.int32, line, 0) - offset
    spots = (lax.rem(at, size) == from_lane).astype(BF)
    values = dot(blocks, spots)
    at = lax.broadcasted_iota(jnp.int32, values.shape, 1)
    owner = lax.broadcasted_iota(jnp.int32, values.shape, 0)
    mine = (at >= owner * size) & (at < (owner + 1) * size)
    return jnp.sum(jnp.where(mine, values, 0.0), axis=0, keepdims=True)


def vectors_body(gains, biases, ranks, attn_out, mlp_out, bias_out):
    attn_out[...] = jnp.broadcast_to(row_of(gains[...], 0, 48), attn_out.shape)
    mlp_out[...] = jnp.broadcast_to(row_of(gains[...], 48, 48), mlp_out.shape)
    full = row_of(biases[...], 0, 64)
    rank = ranks[0:1, 0:1]
    query = key = value = 0.0
    for i in range(4):
        query = query + jnp.where(rank == i, full[:, 384 * i : 384 * (i + 1)], 0.0)
    for i in range(2):
        mine = (rank >= 2 * i) & (rank < 2 * i + 2)
        key = key + jnp.where(mine, full[:, 1536 + HD * i : 1536 + HD * (i + 1)], 0.0)
        value = value + jnp.where(mine, full[:, 1792 + HD * i : 1792 + HD * (i + 1)], 0.0)
    line = jnp.concatenate([query, key, value], axis=1)
    bias_out[...] = jnp.broadcast_to(line, bias_out.shape)


def turn(vectors, cos2, sin2):
    return vectors * cos2 + pltpu.roll(vectors, HD // 2, 1) * sin2


def unpack_table(table, places):
    first, last = table[:, 2 * HD : 2 * HD + 1], table[:, 2 * HD + 1 : 2 * HD + 2]
    keys = places[0:1, :]
    return table[:, :HD], table[:, HD : 2 * HD], (keys >= first) & (keys <= last)


def masked_scores(queries, keys, allowed):
    return jnp.where(allowed, dot_t(queries, keys) * HD ** (-0.5), -1e30)


def attn_forward_body(
    x0, x1, x2, x3, gain, w, bias, table, places,
    n_out, q_out, kv_out, o_out, lse_out,
):
    rows = x0.shape[0]
    for i, x in enumerate((x0, x1, x2, x3)):
        part = x[...].astype(F32)
        scale = lax.rsqrt(jnp.mean(part * part, axis=-1, keepdims=True) + EPSILON)
        n_out[i * rows : (i + 1) * rows] = (part * scale * gain[0:1]).astype(BF)
    qkv = dot(n_out[...], w[...]) + bias[0:1]
    cosines, sines, allowed = unpack_table(table, places)
    keys = turn(qkv[:, 384:512], cosines, sines).astype(BF)
    values = qkv[:, 512:].astype(BF)
    kv_out[:, :HD] = keys
    kv_out[:, HD:] = values
    lses = []
    for h in range(3):
        at = slice(h * HD, (h + 1) * HD)
        queries = turn(qkv[:, at], cosines, sines).astype(BF)
        q_out[:, at] = queries
        scores = masked_scores(queries, keys, allowed)
        peak = jnp.max(scores, axis=-1, keepdims=True)
        shifted = jnp.exp(scores - peak)
        total = jnp.sum(shifted, axis=-1, keepdims=True)
        probs = (shifted / total).astype(BF)
        o_out[:, at] = dot(probs, values).astype(BF)
        lses.append(peak + jnp.log(total))
    lse_out[...] = jnp.concatenate(lses + [jnp.zeros((4 * rows, 125), F32)], axis=1)


def parted(partial, keep, give):
    rows = partial.shape[0] // 4
    keep[0] = partial[:rows].astype(BF)
    give[0] = partial[rows : 2 * rows].astype(BF)
    keep[1] = partial[2 * rows : 3 * rows].astype(BF)
    give[1] = partial[3 * rows :].astype(BF)


def attn_out_body(o, w, keep, give):
    parted(dot_t(o[...], w[...]), keep, give)


def residual_body(x, keep, got, across, gain, h_out, n_out):
    h = x[...].astype(F32) + keep[0].astype(F32) + got[0].astype(F32) + across[...].astype(F32)
    h_out[...] = h
    scale = lax.rsqrt(jnp.mean(h * h, axis=-1, keepdims=True) + EPSILON)
    n_out[...] = (h * scale * gain[0:1]).astype(BF)


def norm_backward(grad, rows, gain):
    scale = lax.rsqrt(jnp.mean(rows * rows, axis=-1, keepdims=True) + EPSILON)
    scaled = grad * gain
    back = scale * scaled - rows * scale**3 * jnp.mean(scaled * rows, axis=-1, keepdims=True)
    return back, jnp.sum(grad * rows * scale, axis=0, keepdims=True)


def ff_back_body(own_a, own_b, got_a, got_b, got_c, h, cot, gain, grad_out, branch_out, gain_out):
    grad = sum(part[...].astype(F32) for part in (own_a, own_b, got_a, got_b, got_c))
    back, gain_out[...] = norm_backward(grad, h[...], gain[0:1])
    total = cot[...].astype(F32) + back
    grad_out[...] = total
    branch_out[...] = total.astype(BF)


def attn_back_body(keep, got, across, x, above, gain, grad_out):
    grad = keep[0].astype(F32) + got[0].astype(F32) + across[...].astype(F32)
    back, _ = norm_backward(grad, x[...].astype(F32), gain[0:1])
    grad_out[...] = above[...] + back


def attn_backward_body(
    rest, b0, b1, b2, b3, wo, x0, x1, x2, x3, w, q, kv, lse, table, places, core,
    query_out, kv_keep, kv_give, keep, give, sums_out, gain_out, bbuf, grads_out,
):
    rows = b0.shape[0]
    for i, part in enumerate((b0, b1, b2, b3)):
        bbuf[i * rows : (i + 1) * rows] = part[...]
    attended_grad = dot(bbuf[...], wo[...]).astype(BF)
    rest()
    keys, values = kv[:, :HD], kv[:, HD:]
    cosines, sines, allowed = unpack_table(table, places)
    sines = -sines
    key_grad = value_grad = 0.0
    for h in range(3):
        at = slice(h * HD, (h + 1) * HD)
        queries, o_grad = q[:, at], attended_grad[:, at]
        probs = jnp.exp(masked_scores(queries, keys, allowed) - lse[:, h : h + 1])
        prob_grad = dot_t(o_grad, values)
        inner = jnp.sum(probs * prob_grad, axis=-1, keepdims=True)
        score_grad = (probs * (prob_grad - inner)).astype(BF)
        query_grad = dot(score_grad, keys) * HD ** (-0.5)
        grads_out[:, at] = turn(query_grad, cosines, sines).astype(BF)
        key_grad = key_grad + t_dot(score_grad, queries)
        value_grad = value_grad + t_dot(probs.astype(BF), o_grad)
    grads_out[:, 384:512] = turn(key_grad * HD ** (-0.5), cosines, sines).astype(BF)
    grads_out[:, 512:] = value_grad.astype(BF)
    grads = grads_out[...]
    query_out[...] = grads[:, :384]
    first = core[0:1, 0:1] == 0
    kv_keep[...] = jnp.where(first, grads[:, 384:512], grads[:, 512:])
    kv_give[...] = jnp.where(first, grads[:, 512:], grads[:, 384:512])
    sums_out[...] = jnp.sum(grads.astype(F32), axis=0, keepdims=True)
    partial = dot_t(grads, w[...])
    parted(partial, keep, give)
    gain_grad = 0.0
    for i, x in enumerate((x0, x1, x2, x3)):
        part = x[...].astype(F32)
        scale = lax.rsqrt(jnp.mean(part * part, axis=-1, keepdims=True) + EPSILON)
        terms = partial[i * rows : (i + 1) * rows] * part * scale
        gain_grad = gain_grad + jnp.sum(terms, axis=0, keepdims=True)
    gain_out[...] = gain_grad


def blocks_of(row, size):
    count = row.shape[1] // size
    at = lax.broadcasted_iota(jnp.int32, (count, row.shape[1]), 1)
    owner = lax.broadcasted_iota(jnp.int32, (count, row.shape[1]), 0)
    mine = (at >= owner * size) & (at < (owner + 1) * size)
    values = jnp.where(mine, row, 0.0).astype(BF)
    at = lax.broadcasted_iota(jnp.int32, (row.shape[1], HD), 0)
    lane = lax.broadcasted_iota(jnp.int32, (row.shape[1], HD), 1)
    return dot(values, (lax.rem(at, size) == lane).astype(BF))


def attn_grads_body(
    rest, b0, b1, b2, b3, attended, normed, query_grad, kv_keep, kv_got, gain_attn, gain_mlp, sums, ranks, out, bbuf, right
):
    size = b0.shape[0]
    for i, part in enumerate((b0, b1, b2, b3)):
        bbuf[i * size : (i + 1) * size] = part[...]
    half = bbuf.shape[1] // 2
    spans = [(slice(i * half, (i + 1) * half), slice(16 * i, 16 * (i + 1))) for i in range(2)]
    for at, blocks in spans:
        grad = t_dot(bbuf[:, at], attended[...]).astype(BF)
        out[blocks, :, 640:] = grad.reshape(16, half // 16, 384)
    rest()
    right[:, :384] = query_grad[...]
    for i, other in enumerate((1, 0, 3, 2)):
        mine, theirs = slice(i * size, (i + 1) * size), slice(other * size, (other + 1) * size)
        total = kv_keep[mine].astype(F32) + kv_got[theirs].astype(F32)
        right[mine, 384:] = total.astype(BF)
    for at, blocks in spans:
        grad = t_dot(normed[:, at], right[...]).astype(BF)
        out[blocks, :, :512] = grad.reshape(16, half // 16, 512)
    rank = ranks[0:1, 0:1]
    parts = [jnp.where(rank == i, sums[:, :384], 0.0) for i in range(4)]
    for start in (384, 512):
        for i in range(2):
            mine = (rank >= 2 * i) & (rank < 2 * i + 2)
            parts.append(jnp.where(mine, sums[:, start : start + HD], 0.0))
    rows_of = (
        blocks_of(gain_attn[...], 48),
        blocks_of(gain_mlp[...], 48),
        blocks_of(jnp.concatenate(parts[:6], axis=1), 56),
        blocks_of(jnp.concatenate(parts[6:], axis=1), 8),
    )
    at = lax.broadcasted_iota(jnp.int32, (32, out.shape[1], HD), 1)
    tail = jnp.zeros((32, out.shape[1], HD), F32)
    for i, values in enumerate(rows_of):
        tail = jnp.where(at == i, values[:, None, :], tail)
    out[:, :, 512:640] = tail.astype(BF)


def shards(
    layer_input,
    q_weight,
    kv_weight,
    o_weight,
    norm_gains,
    qkv_bias,
    gate_up,
    down_weight,
    cotangent,
    lengths,
):
    zh, zl, core = (lax.axis_index(a) for a in ("zh", "zl", "core"))
    rank = 2 * zl + core
    width = layer_input.shape[1]
    rows = layer_input.shape[0]

    small = jnp.concatenate([norm_gains.reshape(-1), qkv_bias, jnp.zeros((216,), BF)])
    vectors = jnp.concatenate([kv_weight.reshape(24, 256), small[None], jnp.zeros((7, 256), BF)])
    got = swap(vectors, "core")
    both = jnp.stack([pick(core, vectors, got), pick(core, got, vectors)])
    small_keep = both[:, 24].reshape(2, 2, HD)
    kv_keep = pick(zl, both[:, :24, :HD], both[:, :24, HD:])
    kv_give = pick(zl, both[:, :24, HD:], both[:, :24, :HD])
    kv_crossed = swap(
        jnp.concatenate([kv_give, small_keep, jnp.zeros((2, 6, HD), BF)], axis=1), "zl"
    )
    kv_got, small_got = kv_crossed[:, :24], kv_crossed[:, 24:26]
    kv_rows = jnp.stack([pick(zl, kv_keep, kv_got), pick(zl, kv_got, kv_keep)])
    kv_rows = kv_rows.reshape(2, 2, 2, 12, HD).transpose(0, 1, 3, 2, 4).reshape(48, 2 * HD)
    small = jnp.stack([pick(zl, small_keep, small_got), pick(zl, small_got, small_keep)])
    small = small.reshape(4, 256)
    gains_row = jnp.concatenate([small[:, :12].reshape(48), small[:, 12:24].reshape(48)])
    bias_row = small[:, 24:40].reshape(64)
    small = jnp.zeros((48, HD), BF).at[0, :96].set(gains_row).at[1, :64].set(bias_row)

    ends = jnp.cumsum(lengths[0])
    ranks = jnp.stack([rank, 2 * zl + 1 - core, 2 * (1 - zl) + core, 2 * (1 - zl) + 1 - core])
    group = 4 * rows
    places = (ranks[:, None] * rows + jnp.arange(rows, dtype=jnp.int32)[None, :]).reshape(group)
    passed = ends[None, :] <= places[:, None]
    starts = jnp.sum(jnp.where(passed, lengths[0][None, :], 0), axis=1)
    inverse = THETA ** (-(2.0 * jnp.arange(HD // 2, dtype=F32)) / HD)
    inverse = jnp.concatenate([inverse, inverse])[None, :]
    angles = (places - starts).astype(F32)[:, None] * inverse
    sign = jnp.where(jnp.arange(HD) < HD // 2, -1.0, 1.0).astype(F32)[None, :]
    lane = jnp.arange(HD)[None, :]
    ranges = jnp.where(lane == 0, starts[:, None], places[:, None]).astype(F32)
    table = jnp.concatenate([jnp.cos(angles), jnp.sin(angles) * sign, ranges], axis=1)
    tables = (table, jnp.broadcast_to(places.astype(F32)[None, :], (8, group)))

    living = (places[:rows] < ends[-1])[:, None]
    cot_local = jnp.where(living, cotangent, jnp.zeros((), BF))
    cot_groups = token_groups(cot_local)

    across = swap(layer_input, "zl")
    group_inputs = (layer_input, swap(layer_input, "core"), across, swap(across, "core"))

    attn_part = jnp.concatenate([q_weight, kv_rows, small, o_weight.T], axis=-1)
    attn_plane = exchange(copies(attn_part, 16), PLANE)
    qkv_plane, o_plane = attn_plane[..., :640], attn_plane[..., 768:]
    small_plane = attn_plane[:, :2, 640:768]
    small_other = swap(small_plane, "zh")
    qkv_other = swap(qkv_plane, "zh")
    o_other = swap(o_plane, "zh")
    waits = (cot_groups[1][1], cot_groups[2][1], group_inputs[3], *tables)
    qkv_full = ordered(qkv_plane, qkv_other, zh, "qkv_weights", waits)
    small = jnp.stack([pick(zh, small_plane, small_other), pick(zh, small_other, small_plane)])
    small = small.reshape(32, 2, HD)
    qkv_full = qkv_full.reshape(width, 640)
    gain_attn, gain_mlp, bias = vmem_call(
        vectors_body,
        [((8, width), F32), ((8, width), F32), ((8, 640), F32)],
        [small[:, 0], small[:, 1], jnp.full((8, HD), rank, jnp.int32)],
        "gains_and_biases",
        limit=16,
    )

    mlp = jnp.concatenate([gate_up, down_weight.T[None]], axis=0)
    mlp = jnp.pad(mlp, ((0, 0), (0, 0), (0, 2 * HALF - mlp.shape[2])))
    mlp_own = pick(zh, mlp[..., :HALF], mlp[..., HALF:])
    mlp_other = swap(pick(zh, mlp[..., HALF:], mlp[..., :HALF]), "zh")
    mlp = vmem_call(
        arrange_body,
        [((6, 48, HALF), BF)],
        [mlp_own, mlp_other, jnp.full((8, HD), zh, jnp.int32)],
        "arranged",
        (kv_crossed,),
        moved=4 * mlp_own.size,
    )[0]
    mlp = lax.all_gather(mlp, PLANE, axis=1, tiled=True)
    mlp = mlp.reshape(3, width, HALF)

    normed_group, queries, kv_rot, attended, lse = vmem_call(
        attn_forward_body,
        [
            ((group, width), BF),
            ((group, 384), BF),
            ((group, 256), BF),
            ((group, 384), BF),
            ((group, 128), F32),
        ],
        [*group_inputs, gain_attn, qkv_full, bias, *tables],
        "attention_forward",
        limit=32,
        flops=2 * group * (width * 640 + 6 * group * HD),
        moved=2 * group * width * 2 + 2 * width * 768,
    )
    o_full = ordered(o_plane, o_other, zh, "o_weights", (attended,)).reshape(width, 384)
    pair = ((2, rows, width), BF)
    keep, give = vmem_call(
        attn_out_body,
        [pair, pair],
        [attended, o_full],
        "attention_out",
        flops=2 * group * width * 384,
        moved=2 * width * 384 + 2 * group * width,
    )
    got = swap(give, "core")
    weights = held(mlp)
    residual, normed_mlp = vmem_call(
        residual_body,
        [((rows, width), F32), ((rows, width), BF)],
        [layer_input, keep, got, swap(add(keep[1], got[1]), "zl"), gain_mlp],
        "residual_norm",
        (weights,),
        moved=10 * rows * width,
    )

    after_rows, before_rows = z_shift(normed_mlp, -1), z_shift(normed_mlp, 1)
    far_rows = z_shift(normed_mlp, 2)
    own = (normed_mlp, swap(normed_mlp, "core"))
    own_out = ff_rows(own, cot_groups[0], weights, cot_local)
    cot_near, cot_far = vmem_call(
        cot_products_body,
        [((4 * rows, HALF), F32), ((2 * rows, HALF), F32)],
        [*cot_groups[1], *cot_groups[2], (mlp, 2)],
        "cotangent_products",
        (own_out[0],),
        flops=12 * rows * width * HALF,
    )
    near = stacked((after_rows, before_rows), cot_near)
    near = (near, swap(near, "core"))
    near_out = ff_rows(near, (cot_near,), weights, own_out[0])
    far_rows = stacked((far_rows,), near_out[0])
    far = (far_rows, swap(far_rows, "core"))
    near_sum = [
        add(mine, swap(others, "core"))
        for mine, others in zip(halves(near_out[3], 0), halves(near_out[4], 0))
    ]
    near_got = (z_shift(near_sum[0], 1), z_shift(near_sum[1], -1))
    far_out = ff_rows(far, (cot_far,), weights, near_sum[1])
    far_sum = add(far_out[3], swap(far_out[4], "core"))
    own_got = swap(own_out[4], "core")
    far_got = z_shift(far_sum, 2)
    results = (own_out, near_out, far_out)
    hidden, gate_grads, up_grads = ([r[i] for r in results] for i in range(3))
    flat_normed = [*own, *near, *far]
    flat_cots = [part for pair in cot_groups for part in pair]
    grad_terms = weight_grads(flat_normed, flat_cots, hidden, gate_grads, up_grads, far_sum)
    residual_grad, branch, gain_mlp_grad = vmem_call(
        ff_back_body,
        [((rows, width), F32), ((rows, width), BF), ((1, width), F32)],
        [own_out[3], own_got, *near_got, far_got, residual, cot_local, gain_mlp],
        "residual_gradient",
        (grad_terms,),
        limit=60,
        flops=10**9 * WEIGHT,
        moved=24 * rows * width,
    )
    mlp_grads = lax.psum_scatter(
        grad_terms.reshape(6, width // 2, HALF), PLANE, scatter_dimension=1, tiled=True
    ).reshape(3, 2, 48, HALF)
    own_grads = lax.dynamic_index_in_dim(mlp_grads, zh, 1, keepdims=False)
    other_grads = swap(lax.dynamic_index_in_dim(mlp_grads, 1 - zh, 1, keepdims=False), "zh")
    own_grads, other_grads = own_grads.astype(F32), other_grads.astype(F32)
    mlp_shard = jnp.concatenate(
        [pick(zh, own_grads, other_grads), pick(zh, other_grads, own_grads)], axis=-1
    )[..., : gate_up.shape[2]]
    gate_up_shard = mlp_shard[:2]
    down_shard = mlp_shard[2].T

    out_pairs = down_rows(hidden, mlp, branch)
    layer_output = (residual + token_sums(out_pairs)).astype(BF)

    across = stacked((swap(branch, "zl"),), out_pairs[0][0])
    branch_group = (branch, swap(branch, "core"), across, swap(across, "core"))
    query_grad, kv_keep, kv_give, keep, give, sums, gain_attn_grad = vmem_call(
        attn_backward_body,
        [
            ((group, 384), BF),
            ((group, HD), BF),
            ((group, HD), BF),
            pair,
            pair,
            ((1, 640), F32),
            ((1, width), F32),
        ],
        [
            *branch_group, o_full, *group_inputs, qkv_full, queries, kv_rot, lse, *tables,
            jnp.full((8, HD), core, jnp.int32),
        ],
        "attention_backward",
        limit=60,
        first=5,
        scratch=[pltpu.VMEM((group, width), BF), pltpu.VMEM((group, 640), BF)],
        flops=2 * group * (width * 1024 + 15 * group * HD),
        moved=4 * group * width + 2 * width * 1024,
    )
    kv_got = swap(kv_give, "core")

    terms = vmem_call(
        attn_grads_body,
        [((32, width // 32, 1024), BF)],
        [
            *branch_group,
            attended,
            normed_group,
            query_grad,
            kv_keep,
            kv_got,
            gain_attn_grad,
            gain_mlp_grad,
            sums,
            jnp.full((8, HD), rank, jnp.int32),
        ],
        "attention_weight_gradients",
        scratch=[pltpu.VMEM((group, width), BF), pltpu.VMEM((group, 512), BF)],
        limit=60,
        first=5,
        flops=2 * group * width * 1024,
        moved=4 * group * width + 2 * width * 1152,
    )[0]
    attn_shard = summed(exchange(terms, DATA))

    got = swap(give, "core")
    across = swap(add(keep[1], got[1]), "zl")
    input_grad = vmem_call(
        attn_back_body,
        [((rows, width), F32)],
        [keep, got, across, layer_input, residual_grad, gain_attn],
        "input_gradient",
        moved=20 * rows * width,
    )[0]

    q_shard = attn_shard[:, :384]
    o_shard = attn_shard[:, 640:].T
    kv_sum = attn_shard[:, 384:512].reshape(2, 2, 12, HD)
    kv_keep = lax.dynamic_index_in_dim(kv_sum, core, 1, keepdims=False)
    kv_give = lax.dynamic_index_in_dim(kv_sum, 1 - core, 1, keepdims=False)
    vectors = attn_shard[:8, 512:640]
    got = swap(jnp.concatenate([kv_give.reshape(24, HD), vectors]), "core")
    kv_got = got[:24].reshape(2, 12, HD)
    vectors = vectors + got[24:]
    kv_sum = jnp.stack([pick(core, kv_keep, kv_got), pick(core, kv_got, kv_keep)], axis=2)
    kv_sum = kv_sum.reshape(2, 24, HD)
    kv_keep = pick(zl, kv_sum[0], kv_sum[1])
    got = swap(jnp.concatenate([pick(zl, kv_sum[1], kv_sum[0]), vectors]), "zl")
    kv_got = got[:24]
    vectors = vectors + got[24:]
    kv_shard = jnp.concatenate([pick(zl, kv_keep, kv_got), pick(zl, kv_got, kv_keep)], axis=-1)
    kv_shard = kv_shard.reshape(12, 2, 2 * HD).transpose(1, 0, 2)

    def own_part(row, size):
        return lax.dynamic_index_in_dim(
            vectors[row, : 4 * size].reshape(4, size), rank, 0, keepdims=False
        )

    return (
        layer_output,
        input_grad,
        q_shard,
        kv_shard,
        o_shard,
        jnp.stack([own_part(0, 12), own_part(1, 12)]),
        own_part(2, 14),
        own_part(3, 2),
        gate_up_shard,
        down_shard,
    )


def solution(mesh):
    fine = Mesh(mesh.devices.reshape(SIZES), AXES)
    dp = ("zh", "y", "x")
    tensor = ("zl", "core")
    every = dp + tensor
    in_specs = (
        P(every, None),
        P(dp, tensor),
        P(None, every, None),
        P(tensor, dp),
        P(None, every),
        P(every),
        P(None, dp, tensor),
        P(tensor, dp),
        P(every, None),
        P(dp, None),
    )
    out_specs = (
        P(every, None),
        P(every, None),
        P(dp, tensor),
        P(None, every, None),
        P(tensor, dp),
        P(None, every),
        P(every),
        P(every),
        P(None, dp, tensor),
        P(tensor, dp),
    )
    return jax.shard_map(shards, mesh=fine, in_specs=in_specs, out_specs=out_specs, check_vma=False)
```
